32 devices in a mesh: dp: 8 (over y, x, core), grp: 4 (over z).
Axes of the slice: x: 2, y: 2, z: 4, core: 2. Of those that a mesh axis runs over, the one named last changes fastest.
Arguments:
- tokens: bfloat16 [8, 12544, 384], P('dp', 'grp'), may hold values from -6 to 6
- cotangent: bfloat16 [8, 12544, 384], P('dp', 'grp'), may hold values from -6 to 6
- attn_master: float32 [598272], P(('dp', 'grp')), as said below
- attn_first: float32 [598272], P(('dp', 'grp')), as said below
- attn_second: float32 [598272], P(('dp', 'grp')), as said below
- mlp_master: float32 [1182464], P(('dp', 'grp')), as said below
- mlp_first: float32 [1182464], P(('dp', 'grp')), as said below
- mlp_second: float32 [1182464], P(('dp', 'grp')), as said below
Outputs:
- output: bfloat16 [8, 12544, 384], P('dp', 'grp')
- input_grad: float32 [8, 12544, 384], P('dp', 'grp')
- attn_first_new: float32 [598272], P(('dp', 'grp'))
- attn_second_new: float32 [598272], P(('dp', 'grp'))
- attn_master_new: float32 [598272], P(('dp', 'grp'))
- mlp_first_new: float32 [1182464], P(('dp', 'grp'))
- mlp_second_new: float32 [1182464], P(('dp', 'grp'))
- mlp_master_new: float32 [1182464], P(('dp', 'grp'))
The draws below stay inside these ranges and needn't reach their ends.
Inputs may be any that keep to these rules, and one draw needn't show every extreme that they name: `attn_master`: entries past the parameters of the layout are zero. `attn_first`: entries past the parameters of the layout are zero. `attn_second`: positive on the parameters of the layout, zero past them. `mlp_master`: entries past the parameters of the layout are zero. `mlp_first`: entries past the parameters of the layout are zero. `mlp_second`: positive on the parameters of the layout, zero past them.
All inputs are finite; a program needn't handle non-finite values.
Results may differ from the reference program's by a relative error of at most 0.012.
Values may be sent and summed in bfloat16 or wider, within the bound.
A program may use at most 320 MiB of HBM per device.

```python
import math
import jax
import jax.numpy as jnp
import numpy as np
from jax import lax

D = 384
HEADS = 12
HDIM = 32
FF = 1536
WIN = 7
STEP = 10
GROUPS = 2
IMAGES = 256
TOKENS_ALL = 100352
FLAT_A = 598272
FLAT_B = 1182464


beta_one = 0.9


beta_two = 0.999


def attn_kinds():
    root_width = D ** (-0.5)
    return [((D, 3 * D), 0.0, root_width, 0.3), ((D, D), 0.0, 4.0 * root_width, 0.3), ((HEADS, (3 * WIN - 2) ** 2), 0.0, 0.5, 1.0), ((HEADS, (2 * WIN - 1) ** 2), 0.0, 0.5, 1.0), ((D,), 1.0, 0.15, 1.0), ((D,), 0.0, 0.3, 1.0), ((D,), 0.0, 0.3, 1.0), ((D,), 0.0, 0.3, 1.0), ((D,), 0.0, 0.3, 1.0)]


def mlp_kinds():
    return [((D, FF), 0.0, D ** (-0.5), 0.3), ((FF, D), 0.0, FF ** (-0.5), 0.6), ((FF,), 0.0, 0.3, 1.0), ((D,), 1.0, 0.15, 1.0), ((D,), 0.0, 0.3, 1.0), ((D,), 0.0, 0.3, 1.0)]


def segment_tables(kinds, total_len):
    centers = np.zeros(total_len, np.float32)
    spreads = np.zeros(total_len, np.float32)
    grad_sizes = np.zeros(total_len, np.float32)
    live_mask = np.zeros(total_len, np.float32)
    offset = 0
    for seg_shape, center, spread, grad_coef in kinds:
        length = int(np.prod(seg_shape))
        centers[offset:offset + length] = center
        spreads[offset:offset + length] = spread
        grad_sizes[offset:offset + length] = grad_coef * np.sqrt(float(TOKENS_ALL))
        live_mask[offset:offset + length] = 1.0
        offset += length
    return (jnp.asarray(centers), jnp.asarray(spreads), jnp.asarray(grad_sizes), jnp.asarray(live_mask))


def draw_attn_master(key, part):
    key = jax.random.fold_in(key, 11)
    centers, spreads, grad_sizes, live_mask = segment_tables(attn_kinds(), FLAT_A)
    noise_vec = jax.random.truncated_normal(key, -3.0, 3.0, (FLAT_A,), jnp.float32)
    return (centers + spreads * noise_vec) * live_mask


def draw_attn_first(key, part):
    key = jax.random.fold_in(key, 12)
    centers, spreads, grad_sizes, live_mask = segment_tables(attn_kinds(), FLAT_A)
    noise_vec = jax.random.truncated_normal(key, -3.0, 3.0, (FLAT_A,), jnp.float32)
    return (1.0 - beta_one) / beta_one * grad_sizes * noise_vec * live_mask


def draw_attn_second(key, part):
    key = jax.random.fold_in(key, 13)
    centers, spreads, grad_sizes, live_mask = segment_tables(attn_kinds(), FLAT_A)
    factor = jax.random.uniform(key, (FLAT_A,), jnp.float32, 1.0, 4.0)
    return (1.0 - beta_two) / beta_two * grad_sizes * grad_sizes * factor * live_mask


def draw_mlp_master(key, part):
    key = jax.random.fold_in(key, 21)
    centers, spreads, grad_sizes, live_mask = segment_tables(mlp_kinds(), FLAT_B)
    noise_vec = jax.random.truncated_normal(key, -3.0, 3.0, (FLAT_B,), jnp.float32)
    return (centers + spreads * noise_vec) * live_mask


def draw_mlp_first(key, part):
    key = jax.random.fold_in(key, 22)
    centers, spreads, grad_sizes, live_mask = segment_tables(mlp_kinds(), FLAT_B)
    noise_vec = jax.random.truncated_normal(key, -3.0, 3.0, (FLAT_B,), jnp.float32)
    return (1.0 - beta_one) / beta_one * grad_sizes * noise_vec * live_mask


def draw_mlp_second(key, part):
    key = jax.random.fold_in(key, 23)
    centers, spreads, grad_sizes, live_mask = segment_tables(mlp_kinds(), FLAT_B)
    factor = jax.random.uniform(key, (FLAT_B,), jnp.float32, 1.0, 4.0)
    return (1.0 - beta_two) / beta_two * grad_sizes * grad_sizes * factor * live_mask


def block_levels(key, dims, shards, smallest, largest):
    def one(dim, shards_of):
        draws = jax.random.uniform(jax.random.fold_in(jax.random.fold_in(key, 6), dim), (shards_of,), jnp.float32, smallest / len(shards), largest / len(shards))
        return jnp.repeat(jnp.exp(draws), dims[dim] // shards_of).reshape((-1,) + (1,) * (len(dims) - dim - 1))

    gain = one(*shards[0])
    for cut in shards[1:]:
        gain = gain * one(*cut)
    return gain


def centred(rng, extent, deviation, bound, split=(), kind=jnp.bfloat16):
    level = block_levels(rng, extent, split, -0.22, 0.18) if split else 1.0
    values = jax.random.normal(rng, extent, jnp.float32) * deviation * level
    return jnp.minimum(jnp.maximum(values, -bound), bound).astype(kind)


def setup_inputs(seed: int = 0) -> dict:
    arg_keys = jax.random.split(jax.random.key(seed), 9)
    tokens = centred(arg_keys[0], (4 * GROUPS, IMAGES * WIN * WIN, D), 1.0, 6.0, ((0, 8), (1, 4)))
    cotangent = centred(arg_keys[1], (4 * GROUPS, IMAGES * WIN * WIN, D), 1.0, 6.0, ((0, 8), (1, 4)))
    attn_master = draw_attn_master(jax.random.fold_in(arg_keys[8], 71), 0)
    attn_first = draw_attn_first(jax.random.fold_in(arg_keys[8], 71), 0)
    attn_second = draw_attn_second(jax.random.fold_in(arg_keys[8], 71), 0)
    mlp_master = draw_mlp_master(jax.random.fold_in(arg_keys[8], 71), 0)
    mlp_first = draw_mlp_first(jax.random.fold_in(arg_keys[8], 71), 0)
    mlp_second = draw_mlp_second(jax.random.fold_in(arg_keys[8], 71), 0)
    return dict(tokens=tokens, cotangent=cotangent, attn_master=attn_master, attn_first=attn_first, attn_second=attn_second, mlp_master=mlp_master, mlp_first=mlp_first, mlp_second=mlp_second)


@jax.custom_vjp
def low(v):
    return lax.optimization_barrier(v.astype(jnp.bfloat16)).astype(jnp.float32)

@jax.custom_vjp
def low_back(v):
    return v

def low_keep(v):
    return (low(v), None)

def low_pass(kept, grad):
    return (grad,)

def back_keep(v):
    return (v, None)

def back_low(kept, grad):
    return (low(grad),)
low.defvjp(low_keep, low_pass)
low_back.defvjp(back_keep, back_low)
highest = lax.Precision.HIGHEST
beta_one = 0.9
beta_two = 0.999
learn_rate = 0.04
decay_rate = 0.05
adam_eps = 1e-08
norm_eps = 1e-05
masked_score = -1e+30

def attn_layout():
    return [('w_qkv', (D, 3 * D)), ('w_proj', (D, D)), ('table_fine', (HEADS, (3 * WIN - 2) ** 2)), ('table_coarse', (HEADS, (2 * WIN - 1) ** 2)), ('ln1_gain', (D,)), ('ln1_shift', (D,)), ('q_bias', (D,)), ('v_bias', (D,)), ('proj_bias', (D,))]

def mlp_layout():
    return [('w_fc1', (D, FF)), ('w_fc2', (FF, D)), ('fc1_bias', (FF,)), ('ln2_gain', (D,)), ('ln2_shift', (D,)), ('fc2_bias', (D,))]

def unpack(flat, layout):
    pieces = {}
    offset = 0
    for seg_name, seg_shape in layout:
        length = int(np.prod(seg_shape))
        pieces[seg_name] = flat[offset:offset + length].reshape(seg_shape)
        offset += length
    return pieces

def layer_norm(values, gain_vec, bias_vec):
    centered = values - lax.optimization_barrier(jnp.mean(values, axis=-1, keepdims=True))
    variance = lax.optimization_barrier(jnp.mean(centered * centered, axis=-1, keepdims=True))
    return centered * lax.rsqrt(variance + norm_eps) * gain_vec + bias_vec

def gelu_tanh(values):
    return jax.nn.gelu(values, approximate=True)

def fine_indices():
    halo_width = WIN // 2
    region = WIN + 2 * halo_width
    span_size = 3 * WIN - 2
    base_off = WIN - 1 + halo_width
    query_row = np.repeat(np.arange(WIN), WIN)
    query_col = np.tile(np.arange(WIN), WIN)
    key_row = np.repeat(np.arange(region), region) - halo_width
    key_col = np.tile(np.arange(region), region) - halo_width
    rows_off = key_row[None, :] - query_row[:, None] + base_off
    cols_off = key_col[None, :] - query_col[:, None] + base_off
    return rows_off * span_size + cols_off

def coarse_indices(row_bit, col_bit):
    span_size = 2 * WIN - 1
    query_row = (WIN * row_bit + np.repeat(np.arange(WIN), WIN)) // 2
    query_col = (WIN * col_bit + np.tile(np.arange(WIN), WIN)) // 2
    key_row = np.repeat(np.arange(WIN), WIN)
    key_col = np.tile(np.arange(WIN), WIN)
    rows_off = key_row[None, :] - query_row[:, None] + WIN - 1
    cols_off = key_col[None, :] - query_col[:, None] + WIN - 1
    return rows_off * span_size + cols_off

def fine_valid(row_bit, col_bit):
    halo_width = WIN // 2
    region = WIN + 2 * halo_width
    places = np.arange(region)
    row_ok = (WIN * row_bit + places >= halo_width) & (WIN * row_bit + places < halo_width + 2 * WIN)
    col_ok = (WIN * col_bit + places >= halo_width) & (WIN * col_bit + places < halo_width + 2 * WIN)
    return (row_ok[:, None] & col_ok[None, :]).reshape(-1)

def block_forward(images, attn_params, mlp_params):
    image_count = images.shape[0]
    halo_width = WIN // 2
    region = WIN + 2 * halo_width
    normed_one = low(layer_norm(images, attn_params['ln1_gain'], attn_params['ln1_shift']))
    projected = jnp.einsum('bijd,de->bije', normed_one, attn_params['w_qkv'], precision=highest)
    queries = low(low_back(projected[..., :D] + attn_params['q_bias']) * HDIM ** (-0.5))
    key_grid = low(low_back(projected[..., D:2 * D]))
    values = low(low_back(projected[..., 2 * D:] + attn_params['v_bias']))
    pooled_keys = low(lax.optimization_barrier(jnp.mean(key_grid.reshape(image_count, WIN, 2, WIN, 2, D), axis=(2, 4)))).reshape(image_count, WIN * WIN, HEADS, HDIM)
    pooled_values = low(lax.optimization_barrier(jnp.mean(values.reshape(image_count, WIN, 2, WIN, 2, D), axis=(2, 4)))).reshape(image_count, WIN * WIN, HEADS, HDIM)
    padding = ((0, 0), (halo_width, halo_width), (halo_width, halo_width), (0, 0))
    padded_keys = jnp.pad(key_grid, padding)
    padded_values = jnp.pad(values, padding)
    fine_bias = attn_params['table_fine'][:, fine_indices()]
    row_parts = []
    for row_bit in range(2):
        col_parts = []
        for col_bit in range(2):
            row_lo = WIN * row_bit
            col_lo = WIN * col_bit
            query_win = queries[:, row_lo:row_lo + WIN, col_lo:col_lo + WIN].reshape(image_count, WIN * WIN, HEADS, HDIM)
            key_fine = padded_keys[:, row_lo:row_lo + region, col_lo:col_lo + region].reshape(image_count, region * region, HEADS, HDIM)
            value_fine = padded_values[:, row_lo:row_lo + region, col_lo:col_lo + region].reshape(image_count, region * region, HEADS, HDIM)
            key_set = jnp.concatenate([key_fine, pooled_keys], axis=1)
            value_set = jnp.concatenate([value_fine, pooled_values], axis=1)
            bias_set = jnp.concatenate([fine_bias, attn_params['table_coarse'][:, coarse_indices(row_bit, col_bit)]], axis=2)
            key_valid = np.concatenate([fine_valid(row_bit, col_bit), np.ones(WIN * WIN, dtype=bool)])
            scores = low_back(jnp.einsum('bqhe,bkhe->bhqk', query_win, key_set, precision=highest) + bias_set)
            scores = jnp.where(key_valid, scores, masked_score)
            row_peak = lax.optimization_barrier(jnp.max(scores, axis=-1, keepdims=True))
            exponent = jnp.exp(scores - row_peak)
            attn_probs = low(exponent / lax.optimization_barrier(jnp.sum(exponent, axis=-1, keepdims=True)))
            mixed_win = low(low_back(jnp.einsum('bhqk,bkhe->bqhe', attn_probs, value_set, precision=highest)))
            col_parts.append(mixed_win.reshape(image_count, WIN, WIN, D))
        row_parts.append(jnp.concatenate(col_parts, axis=2))
    mixed_all = jnp.concatenate(row_parts, axis=1)
    attn_out = low_back(jnp.einsum('bijd,de->bije', mixed_all, attn_params['w_proj'], precision=highest) + attn_params['proj_bias'])
    residual = images + attn_out
    normed_two = low(layer_norm(residual, mlp_params['ln2_gain'], mlp_params['ln2_shift']))
    hidden = low_back(jnp.einsum('bijd,de->bije', normed_two, mlp_params['w_fc1'], precision=highest) + mlp_params['fc1_bias'])
    activated = low(gelu_tanh(hidden))
    return residual + jnp.einsum('bije,ed->bijd', activated, mlp_params['w_fc2'], precision=highest) + mlp_params['fc2_bias']

def to_images(flat_tokens):
    groups_here = flat_tokens.shape[0] // 4
    images = flat_tokens.reshape(groups_here, 2, 2, IMAGES, WIN, WIN, D)
    return images.transpose(0, 3, 1, 4, 2, 5, 6).reshape(groups_here * IMAGES, 2 * WIN, 2 * WIN, D)

def from_images(images):
    groups_here = images.shape[0] // IMAGES
    shaped = images.reshape(groups_here, IMAGES, 2, WIN, 2, WIN, D)
    return shaped.transpose(0, 2, 4, 1, 3, 5, 6).reshape(groups_here * 4, IMAGES * WIN * WIN, D)

def forward(inputs, attn_master, mlp_master):
    attn_params = unpack(low(attn_master), attn_layout())
    mlp_params = unpack(low(mlp_master), mlp_layout())
    images = to_images(inputs)
    total_images = images.shape[0]
    per_block = math.gcd(total_images, 16)
    blocks = images.reshape(total_images // per_block, per_block, 2 * WIN, 2 * WIN, D)

    def run_block(image_blk):
        return block_forward(image_blk, attn_params, mlp_params)
    result = lax.map(jax.checkpoint(run_block), blocks)
    return from_images(result.reshape(total_images, 2 * WIN, 2 * WIN, D))

def adamw(master, first, second, grads):
    first_new = beta_one * first + (1.0 - beta_one) * grads
    second_new = beta_two * second + (1.0 - beta_two) * grads * grads
    first_hat = first_new / (1.0 - beta_one ** STEP)
    second_hat = second_new / (1.0 - beta_two ** STEP)
    master_new = master - learn_rate * (first_hat / (jnp.sqrt(second_hat) + adam_eps) + decay_rate * master)
    return (first_new, second_new, master_new)

def reference(tokens, cotangent, attn_master, attn_first, attn_second, mlp_master, mlp_first, mlp_second):
    result, pull_back = jax.vjp(forward, tokens.astype(jnp.float32), attn_master, mlp_master)
    input_grad, attn_grad, mlp_grad = pull_back(cotangent.astype(jnp.float32))
    attn_new = adamw(attn_master, attn_first, attn_second, attn_grad)
    mlp_new = adamw(mlp_master, mlp_first, mlp_second, mlp_grad)
    return (result.astype(jnp.bfloat16), input_grad, attn_new[0], attn_new[1], attn_new[2], mlp_new[0], mlp_new[1], mlp_new[2])
```

```python
import functools

import jax
import jax.numpy as jnp
import ml_dtypes
import numpy as np
from jax import lax
from jax.experimental import pallas as pl
from jax.experimental.pallas import tpu as pltpu
from jax.sharding import PartitionSpec as P

D = 384
HEADS = 12
HDIM = 32
FF = 1536
WIN = 7
STEP = 10
SEQ = WIN * WIN
HALF = 64
FINE = (3 * WIN - 2) ** 2
COARSE = (2 * WIN - 1) ** 2
KEYS = 192

beta_one = 0.9
beta_two = 0.999
learn_rate = 0.04
decay_rate = 0.05
adam_eps = 1e-08
norm_eps = 1e-05
masked_score = -1e30

F32 = jnp.float32
BF16 = jnp.bfloat16
MESH = pl.DeviceIdType.MESH
VMEM_LIMIT = 56 * 2**20


def token_place(gy, gx):
    window = 2 * (gy // WIN) + gx // WIN
    return window * HALF + (gy % WIN) * WIN + gx % WIN


@functools.cache
def gather_tables(images):
    keys = np.zeros((images, 256, 256), np.float32)
    queries = np.zeros((images, 256, 256), np.float32)
    for i in range(images):
        for gy in range(2 * WIN):
            for gx in range(2 * WIN):
                at = token_place(gy, gx) + i
                key = gy * 14 + gx if gy < 10 else 192 + (gy - 10) * 14 + gx
                keys[i, key, at] = 1.0
                keys[i, 140 + (gy // 2) * WIN + gx // 2, at] = 0.25
                queries[i, (gy // WIN) * 128 + (gy % WIN) * 14 + gx, at] = 1.0
    return (
        keys.astype(ml_dtypes.bfloat16),
        queries.astype(ml_dtypes.bfloat16),
        np.ascontiguousarray(keys.transpose(0, 2, 1)).astype(ml_dtypes.bfloat16),
        np.ascontiguousarray(queries.transpose(0, 2, 1)).astype(ml_dtypes.bfloat16),
    )


@functools.cache
def bias_tables():
    fine = np.zeros((14, 384, 384), np.float32)
    coarse = np.zeros((14, 256, 128), np.float32)
    for qx in range(14):
        for a in range(27):
            for kx in range(14):
                col = kx - qx + 9
                if 4 <= a <= 22 and 0 <= col <= 18:
                    fine[qx, 19 * (a - 4) + col, a * 14 + kx] = 1.0
        for p in range(13):
            for s in range(WIN):
                coarse[qx, 13 * p + s - qx // 2 + 6, p * WIN + s] = 1.0
    mask = np.zeros((2, KEYS, 128), np.float32)
    for half in range(2):
        for q in range(98):
            qx = q % 14
            for e in range(KEYS):
                at = e + 56 * half
                if at < 140:
                    ok = abs_ok(qx, at % 14)
                elif at < 189:
                    ok = True
                elif at < 192:
                    ok = False
                else:
                    ok = at < 248 and abs_ok(qx, (at - 192) % 14)
                mask[half, e, q] = 0.0 if ok else masked_score
    return fine.astype(ml_dtypes.bfloat16), coarse.astype(ml_dtypes.bfloat16), mask


def abs_ok(qx, kx):
    return kx < 10 if qx < WIN else kx >= 4


def bias_runs(half, qy):
    fine = (13 - qy) * 14
    pool = 384 + (6 - qy // 2) * WIN
    if half == 0:
        return [(0, 140, fine), (140, 49, pool)]
    return [(0, 84, fine + 56), (84, 49, pool), (136, 56, fine + 140)]


class Flat:
    def __init__(self, devices, part_a, part_b):
        self.devices = devices
        self.part = (part_a, part_b)
        self.rows = tuple(-(-((p + 126) // 128 + 1) // 8) * 8 for p in self.part)
        self.total = sum(self.rows)
        extra = -self.total % 16
        self.rows = (self.rows[0], self.rows[1] + extra)
        self.total += extra
        self.buffer = tuple(
            -(-(self.start(w, devices - 1) + self.rows[w]) // 8) * 8 for w in range(2)
        )

    def start(self, which, device):
        return device * self.part[which] // 128


def bit_order(n_dp, n_grp):
    dp_bits = [("dp", 2**b) for b in range(n_dp.bit_length() - 1)]
    grp_bits = [("grp", 2**b) for b in reversed(range(n_grp.bit_length() - 1))]
    return dp_bits[1:2] + grp_bits + dp_bits[2:] + dp_bits[:1]


def place_of(order, dp, grp):
    place = 0
    for k, (axis, stride) in enumerate(order):
        place = place + ((dp if axis == "dp" else grp) // stride) % 2 * 2**k
    return place


def partner_of(axis, stride, dp, grp):
    if axis == "dp":
        return (dp + (1 - 2 * ((dp // stride) % 2)) * stride, grp)
    return (dp, grp + (1 - 2 * ((grp // stride) % 2)) * stride)


def greet(order, dp, grp):
    barrier = pltpu.get_barrier_semaphore()
    for axis, stride in order:
        pl.semaphore_signal(
            barrier, inc=1, device_id=partner_of(axis, stride, dp, grp), device_id_type=MESH
        )
    pl.semaphore_wait(barrier, len(order))


def shift_lanes(values, amount, up):
    lane = lax.broadcasted_iota(jnp.int32, values.shape, 1)
    if up:
        turned = pltpu.roll(values, amount, 1)
        return jnp.where(lane >= amount, turned, pltpu.roll(turned, 1, 0))
    turned = pltpu.roll(values, lax.rem(128 - amount, 128), 1)
    return jnp.where(lane < 128 - amount, turned, pltpu.roll(turned, values.shape[0] - 1, 0))


def gather_kernel(flat, order, a_ref, b_ref, out_ref, own, own_sem, send_sems, recv_sems):
    dp, grp = lax.axis_index("dp"), lax.axis_index("grp")
    device = dp * lax.axis_size("grp") + grp
    place = place_of(order, dp, grp)
    parts = [
        shift_lanes(ref[...], lax.rem(device * flat.part[w], 128), True)
        for w, ref in enumerate((a_ref, b_ref))
    ]
    own[...] = jnp.concatenate(parts, axis=0).astype(BF16)
    copy = pltpu.make_async_copy(own, out_ref.at[place], own_sem)
    copy.start()
    greet(order, dp, grp)
    copy.wait()
    for k, (axis, stride) in enumerate(order):
        held = out_ref.at[pl.ds(place // 2**k * 2**k, 2**k)]
        send = pltpu.make_async_remote_copy(
            src_ref=held,
            dst_ref=held,
            send_sem=send_sems.at[k],
            recv_sem=recv_sems.at[k],
            device_id=partner_of(axis, stride, dp, grp),
            device_id_type=MESH,
        )
        send.start()
        send.wait()


def gather_params(flat, order, master_a, master_b):
    padded = [
        jnp.pad(m, (0, flat.rows[w] * 128 - m.shape[0])).reshape(flat.rows[w], 128)
        for w, m in enumerate((master_a, master_b))
    ]
    stages = len(order)
    return pl.pallas_call(
        functools.partial(gather_kernel, flat, order),
        out_shape=jax.ShapeDtypeStruct((flat.devices, flat.total, 128), BF16),
        in_specs=[pl.BlockSpec(memory_space=pltpu.VMEM)] * 2,
        out_specs=pl.BlockSpec(memory_space=pl.ANY),
        scratch_shapes=[
            pltpu.VMEM((flat.total, 128), BF16),
            pltpu.SemaphoreType.DMA,
            pltpu.SemaphoreType.DMA((stages,)),
            pltpu.SemaphoreType.DMA((stages,)),
        ],
        compiler_params=pltpu.CompilerParams(
            collective_id=0, has_side_effects=True, vmem_limit_bytes=VMEM_LIMIT
        ),
        name="gather_params",
    )(*padded)


def sum_kernel(
    flat, order, x_ref, a_ref, b_ref, total, outgoing, arrived, send_sems, recv_sems
):
    dp, grp = lax.axis_index("dp"), lax.axis_index("grp")
    device = dp * lax.axis_size("grp") + grp
    place = place_of(order, dp, grp)
    greet(order, dp, grp)
    stages = len(order)
    for k in reversed(range(stages)):
        axis, stride = order[k]
        size = 2**k
        mine = place // size % 2 * size
        other = size - mine
        if k == stages - 1:
            source = x_ref.at[pl.ds(other, size)]
        else:

            def fill(j, carry):
                outgoing[size + j] = total[other + j].astype(BF16)
                return carry

            lax.fori_loop(0, size, fill, 0)
            source = outgoing.at[pl.ds(size, size)]
        send = pltpu.make_async_remote_copy(
            src_ref=source,
            dst_ref=arrived.at[pl.ds(size, size)],
            send_sem=send_sems.at[k],
            recv_sem=recv_sems.at[k],
            device_id=partner_of(axis, stride, dp, grp),
            device_id_type=MESH,
        )
        send.start()
        send.wait()

        def add(j, carry):
            if k == stages - 1:
                held = x_ref[mine + j].astype(F32)
            else:
                held = total[mine + j]
            total[j] = held + arrived[size + j].astype(F32)
            return carry

        lax.fori_loop(0, size, add, 0)
    result = total[0]
    rows = flat.rows[0]
    for w, (ref, part) in enumerate(((a_ref, result[:rows]), (b_ref, result[rows:]))):
        ref[...] = shift_lanes(part, lax.rem(device * flat.part[w], 128), False)


def sum_grads(flat, order, blocks):
    stages = len(order)
    n = flat.devices
    outs = pl.pallas_call(
        functools.partial(sum_kernel, flat, order),
        out_shape=[jax.ShapeDtypeStruct((r, 128), F32) for r in flat.rows],
        in_specs=[pl.BlockSpec(memory_space=pltpu.VMEM)],
        out_specs=[pl.BlockSpec(memory_space=pltpu.VMEM)] * 2,
        scratch_shapes=[
            pltpu.VMEM((n // 2, flat.total, 128), F32),
            pltpu.VMEM((n // 2, flat.total, 128), BF16),
            pltpu.VMEM((n, flat.total, 128), BF16),
            pltpu.SemaphoreType.DMA((stages,)),
            pltpu.SemaphoreType.DMA((stages,)),
        ],
        compiler_params=pltpu.CompilerParams(
            collective_id=1, has_side_effects=True, vmem_limit_bytes=VMEM_LIMIT
        ),
        name="sum_grads",
    )(blocks)
    return [o.reshape(-1)[: flat.part[w]] for w, o in enumerate(outs)]


def place_list(order, n_dp, n_grp):
    return [place_of(order, d // n_grp, d % n_grp) for d in range(n_dp * n_grp)]


ATTN_VECTORS = (D * 3 * D + D * D + HEADS * FINE + HEADS * COARSE, 5)
TABLE_AT = D * 3 * D + D * D


def prep_kernel(
    flat,
    places,
    parts_ref,
    one_fine,
    one_coarse,
    mask_ref,
    wqkv,
    wproj,
    w1,
    w2,
    vecs,
    bias,
    flat_a,
    flat_b,
    tab_fine,
    tab_coarse,
    shifted,
    turned,
):
    flat_a[...] = jnp.zeros_like(flat_a)
    flat_b[...] = jnp.zeros_like(flat_b)
    for device, place in enumerate(places):
        block = parts_ref[place].astype(F32)
        a_at, b_at = flat.start(0, device), flat.start(1, device)
        a_rows, b_rows = flat.rows
        flat_a[a_at : a_at + a_rows, :] += block[:a_rows]
        flat_b[b_at : b_at + b_rows, :] += block[a_rows:]
    for j in range(9):
        wqkv[:, j * 128 : (j + 1) * 128] = flat_a[pl.ds(j, D, stride=9), :].astype(BF16)
    for j in range(3):
        wproj[:, j * 128 : (j + 1) * 128] = flat_a[pl.ds(3456 + j, D, stride=3), :].astype(BF16)
        w2[:, j * 128 : (j + 1) * 128] = flat_b[pl.ds(4608 + j, FF, stride=3), :].astype(BF16)
    for j in range(12):
        w1[:, j * 128 : (j + 1) * 128] = flat_b[pl.ds(j, D, stride=12), :].astype(BF16)
    vecs[...] = jnp.zeros_like(vecs)
    row, lane = divmod(ATTN_VECTORS[0], 128)
    rows = shift_lanes(flat_a[row : row + 16, :], lane, False)
    for v in range(5):
        for j in range(3):
            vecs[v : v + 1, j * 128 : (j + 1) * 128] = rows[3 * v + j : 3 * v + j + 1]
    for j in range(12):
        vecs[8:9, j * 128 : (j + 1) * 128] = flat_b[9216 + j : 9217 + j, :]
    for v in range(3):
        for j in range(3):
            at = 9228 + 3 * v + j
            vecs[5 + v : 6 + v, j * 128 : (j + 1) * 128] = flat_b[at : at + 1, :]
    tab_fine[...] = jnp.zeros_like(tab_fine)
    tab_coarse[...] = jnp.zeros_like(tab_coarse)
    for ref, first, length in (
        (tab_fine, TABLE_AT, FINE),
        (tab_coarse, TABLE_AT + HEADS * FINE, COARSE),
    ):
        for h in range(HEADS):
            row, lane = divmod(first + h * length, 128)
            count = -(-(lane + length) // 128)
            line = jnp.concatenate(
                [flat_a[row + c : row + c + 1, :] for c in range(count)], axis=1
            )
            ref[h : h + 1, 0:length] = line[:, lane : lane + length]
    for qx in range(14):
        at = slice(qx * 16, qx * 16 + 16)
        moved = dot(tab_fine[...].astype(BF16), one_fine[qx])
        for c in range(3):
            shifted[c, at, :] = moved[:, c * 128 : (c + 1) * 128]
        shifted[3, at, :] = dot(tab_coarse[...].astype(BF16), one_coarse[qx])
    turned[...] = jnp.zeros_like(turned)
    for h in range(HEADS):
        table = jnp.concatenate(
            [shifted[c, pl.ds(h, 14, stride=16), :] for c in range(4)], axis=1
        )
        for half in range(2):
            for y in range(WIN):
                for at, length, source in bias_runs(half, WIN * half + y):
                    turned[half, y * 14 : y * 14 + 14, at : at + length] = table[
                        :, source : source + length
                    ]
            bias[h, half] = turned[half].T[0:KEYS] + mask_ref[half]


def prepare(flat, places, gathered):
    fine, coarse, mask = bias_tables()
    vm = pl.BlockSpec(memory_space=pltpu.VMEM)
    return pl.pallas_call(
        functools.partial(prep_kernel, flat, places),
        out_shape=[
            jax.ShapeDtypeStruct((D, 3 * D), BF16),
            jax.ShapeDtypeStruct((D, D), BF16),
            jax.ShapeDtypeStruct((D, FF), BF16),
            jax.ShapeDtypeStruct((FF, D), BF16),
            jax.ShapeDtypeStruct((16, FF), F32),
            jax.ShapeDtypeStruct((HEADS, 2, KEYS, 128), F32),
        ],
        in_specs=[vm] * 4,
        out_specs=[vm] * 6,
        scratch_shapes=[
            pltpu.VMEM((flat.buffer[0], 128), F32),
            pltpu.VMEM((flat.buffer[1], 128), F32),
            pltpu.VMEM((16, 384), F32),
            pltpu.VMEM((16, 256), F32),
            pltpu.VMEM((4, 14 * 16, 128), F32),
            pltpu.VMEM((2, 128, 256), F32),
        ],
        compiler_params=pltpu.CompilerParams(vmem_limit_bytes=VMEM_LIMIT),
        name="prepare",
    )(gathered, jnp.asarray(fine), jnp.asarray(coarse), jnp.asarray(mask))


def dot(a, b):
    return jnp.dot(a, b, preferred_element_type=F32)


def dot_t(a, b):
    return lax.dot_general(a, b, (((1,), (1,)), ((), ())), preferred_element_type=F32)


def norm_parts(values):
    centered = values - jnp.mean(values, axis=-1, keepdims=True)
    scale = lax.rsqrt(jnp.mean(centered * centered, axis=-1, keepdims=True) + norm_eps)
    return centered * scale, scale


def norm_back(d_normed, xhat, scale, gain):
    dh = d_normed * gain
    return scale * (
        dh
        - jnp.mean(dh, axis=-1, keepdims=True)
        - xhat * jnp.mean(dh * xhat, axis=-1, keepdims=True)
    )


def xor_slot(slot, k):
    low, high = lax.rem(slot, 2), slot // 2
    if k % 2:
        low = 1 - low
    if k // 2:
        high = 1 - high
    return 2 * high + low


def split_copies(slot, refs, whole, sems, rows, outward):
    copies = []
    for k, ref in enumerate(refs):
        part = whole.at[pl.ds(pl.multiple_of(xor_slot(slot, k) * rows, 16), rows)]
        ends = (part, ref) if outward else (ref, part)
        copies.append(pltpu.make_async_copy(*ends, sems.at[k]))
    return copies


def lane_heads(j):
    lane = lax.broadcasted_iota(jnp.int32, (256, 128), 1)
    return (lane // HDIM) == j


def image_rows(ref, i, rows, columns):
    at = pl.multiple_of(48 * i, 16)
    parts = [
        ref[pl.ds(pl.multiple_of(w * rows + at, 16), HALF), columns] for w in range(4)
    ]
    return jnp.concatenate(parts, axis=0)


def put_image_rows(ref, i, rows, columns, values):
    at = 48 * i
    for w in range(4):
        part = values[w * HALF : (w + 1) * HALF]
        first = pl.ds(pl.multiple_of(w * rows + at, 16), 16)
        rest = pl.ds(pl.multiple_of(w * rows + at + 16, 16), HALF - 16)
        held = jnp.where(i > 0, ref[first, columns].astype(F32), 0.0)
        ref[first, columns] = (held + part[:16]).astype(ref.dtype)
        ref[rest, columns] = part[16:].astype(ref.dtype)


def attend_kernel(
    rows,
    slot_ref,
    tok_ref,
    in1,
    in2,
    in3,
    wqkv,
    vecs,
    bias,
    keys_tab,
    query_tab,
    query_back,
    mixed,
    probs,
    qkv,
    x_out,
    x_buf,
    normed,
    mixed_t,
    sems,
    out_sem,
):
    i = pl.program_id(0)
    slot = slot_ref[0]

    @pl.when(i == 0)
    def _():
        own = tok_ref.at[pl.ds(pl.multiple_of(slot * rows, 16), rows)]
        copies = split_copies(slot, (own, in1, in2, in3), x_buf, sems, rows, False)
        for c in copies:
            c.start()
        for c in copies:
            c.wait()
        pltpu.make_async_copy(x_buf, x_out, out_sem).start()

        def project(w, carry):
            base = pl.multiple_of(w * rows, 16)
            step = rows // 7

            def norm(c, inner):
                at = pl.multiple_of(c * step, 16)
                xhat, _ = norm_parts(x_buf[pl.ds(base + at, step), :].astype(F32))
                normed[pl.ds(at, step), :] = (xhat * vecs[0:1, :D] + vecs[1:2, :D]).astype(BF16)
                return inner

            lax.fori_loop(0, 7, norm, 0)
            here = pl.ds(base, rows)
            q = dot(normed[...], wqkv[:, :D]) + vecs[2:3, :D]
            qkv[here, :D] = (q * HDIM ** (-0.5)).astype(BF16)
            qkv[here, D : 2 * D] = dot(normed[...], wqkv[:, D : 2 * D]).astype(BF16)
            v = dot(normed[...], wqkv[:, 2 * D :]) + vecs[3:4, :D]
            qkv[here, 2 * D :] = v.astype(BF16)
            return carry

        lax.fori_loop(0, 4, project, 0)

    q_ext = dot(query_tab[0], image_rows(qkv, i, rows, slice(0, D))).astype(BF16)
    kv_ext = dot(keys_tab[0], image_rows(qkv, i, rows, slice(D, 3 * D)))
    k_ext = kv_ext[:, :D].astype(BF16)
    v_t = kv_ext[:, D:].T.astype(BF16)
    for h in range(HEADS):
        tile = slice(h // 4 * 128, h // 4 * 128 + 128)
        q_head = jnp.where(lane_heads(h % 4), q_ext[:, tile], 0)
        scores = dot_t(k_ext[:, tile], q_head)
        halves = []
        for half in range(2):
            s = scores[56 * half : 56 * half + KEYS, 128 * half : 128 * half + 128] + bias[h, half]
            e = jnp.exp(s - jnp.max(s, axis=0, keepdims=True))
            p = e * (1.0 / jnp.sum(e, axis=0, keepdims=True))
            above, below = 56 * half, 64 - 56 * half
            pieces = [p, jnp.zeros((below, 128), F32)]
            if above:
                pieces = [jnp.zeros((above, 128), F32)] + pieces
            halves.append(jnp.concatenate(pieces, axis=0))
        p = jnp.concatenate(halves, axis=1).astype(BF16)
        probs[0, h] = p
        mixed_t[h * HDIM : (h + 1) * HDIM, :] = dot(
            v_t[h * HDIM : (h + 1) * HDIM, :], p
        ).astype(BF16)
    put_image_rows(mixed, i, rows, slice(None), dot_t(query_back[0], mixed_t[...]))

    @pl.when(i == pl.num_programs(0) - 1)
    def _():
        pltpu.make_async_copy(x_buf, x_out, out_sem).wait()


def attend(slot, tok, arrived, wqkv, vecs, bias, images):
    tokens = tok.shape[0]
    rows = tokens // 4
    keys_tab, query_tab, _, query_back = gather_tables(images)
    vm = pl.BlockSpec(memory_space=pltpu.VMEM)
    hbm = pl.BlockSpec(memory_space=pl.ANY)
    table = pl.BlockSpec((1, 256, 256), lambda i: (i, 0, 0))
    whole = lambda width: pl.BlockSpec((tokens, width), lambda i: (0, 0))
    return pl.pallas_call(
        functools.partial(attend_kernel, rows),
        grid=(images,),
        out_shape=[
            jax.ShapeDtypeStruct((tokens, D), BF16),
            jax.ShapeDtypeStruct((images, HEADS, 256, 256), BF16),
            jax.ShapeDtypeStruct((tokens, 3 * D), BF16),
            jax.ShapeDtypeStruct((tokens, D), BF16),
        ],
        in_specs=[pl.BlockSpec(memory_space=pltpu.SMEM)] + [hbm] * 4 + [vm] * 3 + [table] * 3,
        out_specs=[
            whole(D),
            pl.BlockSpec((1, HEADS, 256, 256), lambda i: (i, 0, 0, 0)),
            whole(3 * D),
            hbm,
        ],
        scratch_shapes=[
            pltpu.VMEM((tokens, D), BF16),
            pltpu.VMEM((rows, D), BF16),
            pltpu.VMEM((D, 256), BF16),
            pltpu.SemaphoreType.DMA((4,)),
            pltpu.SemaphoreType.DMA,
        ],
        compiler_params=pltpu.CompilerParams(vmem_limit_bytes=VMEM_LIMIT),
        name="attend",
    )(slot, tok, *arrived, wqkv, vecs, bias, keys_tab, query_tab, query_back)


GELU_A = float(np.sqrt(2.0 / np.pi))
GELU_B = 0.044715


def mlp_kernel(
    rows,
    slot_ref,
    cot_ref,
    in1,
    in2,
    in3,
    mixed_ref,
    x_ref,
    wproj,
    w1,
    w2,
    vecs,
    out0,
    out1,
    out2,
    out3,
    d_res_ref,
    d_mixed_ref,
    g_w1,
    g_w2t,
    g_proj,
    g_vec,
    g_buf,
    o_buf,
    sems,
):
    i = pl.program_id(0)
    slot = slot_ref[0]
    chunk = mixed_ref.shape[0]

    @pl.when(i == 0)
    def _():
        own = cot_ref.at[pl.ds(pl.multiple_of(slot * rows, 16), rows)]
        copies = split_copies(slot, (own, in1, in2, in3), g_buf, sems, rows, False)
        for c in copies:
            c.start()
        for c in copies:
            c.wait()
        g_w1[...] = jnp.zeros_like(g_w1)
        g_w2t[...] = jnp.zeros_like(g_w2t)
        g_proj[...] = jnp.zeros_like(g_proj)
        g_vec[...] = jnp.zeros_like(g_vec)

    here = pl.ds(pl.multiple_of(i * chunk, 16), chunk)
    mix = mixed_ref[...]
    res = x_ref[...].astype(F32) + dot(mix, wproj[...]) + vecs[4:5, :D]
    xhat, scale = norm_parts(res)
    gain = vecs[5:6, :D]
    normed = (xhat * gain + vecs[6:7, :D]).astype(BF16)
    grad = g_buf[here, :]
    grad_t = grad.T
    normed_t = normed.T
    out = res + vecs[7:8, :D]
    d_normed = jnp.zeros((chunk, D), F32)
    for f in range(3):
        cols = slice(f * 512, f * 512 + 512)
        hidden = dot(normed, w1[:, cols]) + vecs[8:9, cols]
        square = hidden * hidden
        t = jnp.tanh(hidden * (GELU_A + (GELU_A * GELU_B) * square))
        half = 0.5 + 0.5 * t
        act = (hidden * half).astype(BF16)
        slope = half + (0.5 * hidden) * (1.0 - t * t) * (GELU_A + (3 * GELU_A * GELU_B) * square)
        out += dot(act, w2[cols, :])
        d_hidden32 = dot_t(grad, w2[cols, :]) * slope
        d_hidden = d_hidden32.astype(BF16)
        g_vec[0:1, cols] += jnp.sum(d_hidden32, axis=0, keepdims=True)
        d_normed += dot_t(d_hidden, w1[:, cols])
        g_w1[:, cols] += dot(normed_t, d_hidden)
        g_w2t[:, cols] += dot(grad_t, act)
    o_buf[here, :] = out.astype(BF16)
    grad32 = grad.astype(F32)
    d_res = grad32 + norm_back(d_normed, xhat, scale, gain)
    d_res_ref[...] = d_res
    d_attn = d_res.astype(BF16)
    d_mixed_ref[...] = dot_t(d_attn, wproj[...]).astype(BF16)
    g_proj[...] += dot(mix.T, d_attn)
    g_vec[1:2, :D] += jnp.sum(d_normed * xhat, axis=0, keepdims=True)
    g_vec[2:3, :D] += jnp.sum(d_normed, axis=0, keepdims=True)
    g_vec[3:4, :D] += jnp.sum(grad32, axis=0, keepdims=True)
    g_vec[4:5, :D] += jnp.sum(d_res, axis=0, keepdims=True)

    @pl.when(i == pl.num_programs(0) - 1)
    def _():
        copies = split_copies(slot, (out0, out1, out2, out3), o_buf, sems, rows, True)
        for c in copies:
            c.start()
        for c in copies:
            c.wait()


def mlp(slot, cot, arrived, mixed, x, wproj, w1, w2, vecs):
    tokens = x.shape[0]
    rows = tokens // 4
    chunk = tokens // 7
    vm = pl.BlockSpec(memory_space=pltpu.VMEM)
    hbm = pl.BlockSpec(memory_space=pl.ANY)
    tile = pl.BlockSpec((chunk, D), lambda i: (i, 0))
    fixed = lambda *shape: pl.BlockSpec(shape, lambda i: (0, 0))
    return pl.pallas_call(
        functools.partial(mlp_kernel, rows),
        grid=(7,),
        out_shape=[jax.ShapeDtypeStruct((rows, D), BF16)] * 4
        + [
            jax.ShapeDtypeStruct((tokens, D), F32),
            jax.ShapeDtypeStruct((tokens, D), BF16),
            jax.ShapeDtypeStruct((D, FF), F32),
            jax.ShapeDtypeStruct((D, FF), F32),
            jax.ShapeDtypeStruct((D, D), F32),
            jax.ShapeDtypeStruct((8, FF), F32),
        ],
        in_specs=[pl.BlockSpec(memory_space=pltpu.SMEM)] + [hbm] * 4 + [tile] * 2 + [vm] * 4,
        out_specs=[hbm] * 4
        + [tile, tile, fixed(D, FF), fixed(D, FF), fixed(D, D), fixed(8, FF)],
        scratch_shapes=[
            pltpu.VMEM((tokens, D), BF16),
            pltpu.VMEM((tokens, D), BF16),
            pltpu.SemaphoreType.DMA((4,)),
        ],
        compiler_params=pltpu.CompilerParams(vmem_limit_bytes=VMEM_LIMIT),
        name="mlp",
    )(slot, cot, *arrived, mixed, x, wproj, w1, w2, vecs)


def attend_back_kernel(
    rows,
    qkv,
    d_mixed,
    probs,
    keys_tab,
    query_tab,
    keys_back,
    query_back,
    d_qkv,
    g_bias,
    d_query_t,
    d_key_value,
):
    i = pl.program_id(0)

    @pl.when(i == 0)
    def _():
        g_bias[...] = jnp.zeros_like(g_bias)

    q_ext = dot(query_tab[0], image_rows(qkv, i, rows, slice(0, D))).astype(BF16)
    dm_ext = dot(query_tab[0], image_rows(d_mixed, i, rows, slice(None))).astype(BF16)
    kv_ext = dot(keys_tab[0], image_rows(qkv, i, rows, slice(D, 3 * D)))
    k_t = kv_ext[:, :D].T.astype(BF16)
    v_ext = kv_ext[:, D:].astype(BF16)
    for tile_at in range(3):
        tile = slice(tile_at * 128, tile_at * 128 + 128)
        d_key = jnp.zeros((256, 128), F32)
        d_value = jnp.zeros((256, 128), F32)
        for j in range(4):
            h = tile_at * 4 + j
            mine = lane_heads(j)
            q_head = jnp.where(mine, q_ext[:, tile], 0)
            dm_head = jnp.where(mine, dm_ext[:, tile], 0)
            p = probs[0, h]
            d_value += dot(p, dm_head)
            d_probs = dot_t(v_ext[:, tile], dm_head)
            halves = []
            for half in range(2):
                at = (slice(56 * half, 56 * half + KEYS), slice(128 * half, 128 * half + 128))
                p32 = p[:, at[1]].astype(F32)[at[0]]
                dp = d_probs[at]
                ds = p32 * (dp - jnp.sum(p32 * dp, axis=0, keepdims=True))
                g_bias[h, half] += ds
                above, below = 56 * half, 64 - 56 * half
                pieces = [ds, jnp.zeros((below, 128), F32)]
                if above:
                    pieces = [jnp.zeros((above, 128), F32)] + pieces
                halves.append(jnp.concatenate(pieces, axis=0))
            ds = jnp.concatenate(halves, axis=1).astype(BF16)
            d_key += dot(ds, q_head)
            d_query_t[h * HDIM : (h + 1) * HDIM, :] = (
                dot(k_t[h * HDIM : (h + 1) * HDIM, :], ds) * HDIM ** (-0.5)
            ).astype(BF16)
        d_key_value[:, tile] = d_key.astype(BF16)
        d_key_value[:, D + tile_at * 128 : D + tile_at * 128 + 128] = d_value.astype(BF16)
    put_image_rows(d_qkv, i, rows, slice(0, D), dot_t(query_back[0], d_query_t[...]))
    put_image_rows(d_qkv, i, rows, slice(D, 3 * D), dot(keys_back[0], d_key_value[...]))


def attend_back(qkv, d_mixed, probs, images):
    tokens = qkv.shape[0]
    tables = gather_tables(images)
    vm = pl.BlockSpec(memory_space=pltpu.VMEM)
    table = pl.BlockSpec((1, 256, 256), lambda i: (i, 0, 0))
    return pl.pallas_call(
        functools.partial(attend_back_kernel, tokens // 4),
        grid=(images,),
        out_shape=[
            jax.ShapeDtypeStruct((tokens, 3 * D), BF16),
            jax.ShapeDtypeStruct((HEADS, 2, KEYS, 128), F32),
        ],
        in_specs=[vm, vm, pl.BlockSpec((1, HEADS, 256, 256), lambda i: (i, 0, 0, 0))]
        + [table] * 4,
        out_specs=[
            pl.BlockSpec((tokens, 3 * D), lambda i: (0, 0)),
            pl.BlockSpec((HEADS, 2, KEYS, 128), lambda i: (0, 0, 0, 0)),
        ],
        scratch_shapes=[pltpu.VMEM((D, 256), BF16), pltpu.VMEM((256, 2 * D), BF16)],
        compiler_params=pltpu.CompilerParams(vmem_limit_bytes=VMEM_LIMIT),
        name="attend_back",
    )(qkv, d_mixed, probs, *tables)


def input_kernel(
    rows,
    slot_ref,
    d_qkv_ref,
    x_ref,
    d_res_ref,
    wqkv,
    vecs,
    out0,
    out1,
    out2,
    out3,
    g_qkv,
    g_vec,
    o_buf,
    sems,
):
    i = pl.program_id(0)
    slot = slot_ref[0]
    chunk = x_ref.shape[0]

    @pl.when(i == 0)
    def _():
        g_qkv[...] = jnp.zeros_like(g_qkv)
        g_vec[...] = jnp.zeros_like(g_vec)

    xhat, scale = norm_parts(x_ref[...].astype(F32))
    gain = vecs[0:1, :D]
    normed = (xhat * gain + vecs[1:2, :D]).astype(BF16)
    d_qkv = d_qkv_ref[...]
    d_normed = dot_t(d_qkv, wqkv[...])
    d_in = d_res_ref[...] + norm_back(d_normed, xhat, scale, gain)
    o_buf[pl.ds(pl.multiple_of(i * chunk, 16), chunk), :] = d_in.astype(BF16)
    g_qkv[...] += dot(normed.T, d_qkv)
    g_vec[0:1, :] += jnp.sum(d_qkv.astype(F32), axis=0, keepdims=True)
    g_vec[1:2, :D] += jnp.sum(d_normed * xhat, axis=0, keepdims=True)
    g_vec[2:3, :D] += jnp.sum(d_normed, axis=0, keepdims=True)

    @pl.when(i == pl.num_programs(0) - 1)
    def _():
        copies = split_copies(slot, (out0, out1, out2, out3), o_buf, sems, rows, True)
        for c in copies:
            c.start()
        for c in copies:
            c.wait()


def input_back(slot, d_qkv, x, d_res, wqkv, vecs):
    tokens = x.shape[0]
    rows = tokens // 4
    chunk = tokens // 7
    vm = pl.BlockSpec(memory_space=pltpu.VMEM)
    hbm = pl.BlockSpec(memory_space=pl.ANY)
    tile = lambda width: pl.BlockSpec((chunk, width), lambda i: (i, 0))
    return pl.pallas_call(
        functools.partial(input_kernel, rows),
        grid=(7,),
        out_shape=[jax.ShapeDtypeStruct((rows, D), BF16)] * 4
        + [jax.ShapeDtypeStruct((D, 3 * D), F32), jax.ShapeDtypeStruct((8, 3 * D), F32)],
        in_specs=[pl.BlockSpec(memory_space=pltpu.SMEM), tile(3 * D), tile(D), tile(D), vm, vm],
        out_specs=[hbm] * 4
        + [
            pl.BlockSpec((D, 3 * D), lambda i: (0, 0)),
            pl.BlockSpec((8, 3 * D), lambda i: (0, 0)),
        ],
        scratch_shapes=[pltpu.VMEM((tokens, D), BF16), pltpu.SemaphoreType.DMA((4,))],
        compiler_params=pltpu.CompilerParams(vmem_limit_bytes=VMEM_LIMIT),
        name="input_back",
    )(slot, d_qkv, x, d_res, wqkv, vecs)


def pack_kernel(
    flat,
    places,
    one_fine,
    one_coarse,
    g_bias,
    g_qkv,
    g_vec1,
    g_proj,
    g_w1,
    g_w2t,
    g_vec2,
    out,
    flat_a,
    flat_b,
    table,
    shifted,
    line,
):
    flat_a[...] = jnp.zeros_like(flat_a)
    flat_b[...] = jnp.zeros_like(flat_b)
    for j in range(9):
        flat_a[pl.ds(j, D, stride=9), :] = g_qkv[:, j * 128 : (j + 1) * 128]
    for j in range(3):
        flat_a[pl.ds(3456 + j, D, stride=3), :] = g_proj[:, j * 128 : (j + 1) * 128]
        flat_b[pl.ds(4608 + j, FF, stride=3), :] = g_w2t[j * 128 : (j + 1) * 128, :].T
    for j in range(12):
        flat_b[pl.ds(j, D, stride=12), :] = g_w1[:, j * 128 : (j + 1) * 128]
        flat_b[9216 + j : 9217 + j, :] = g_vec2[0:1, j * 128 : (j + 1) * 128]
    for v in range(3):
        for j in range(3):
            at = 9228 + 3 * v + j
            flat_b[at : at + 1, :] = g_vec2[1 + v : 2 + v, j * 128 : (j + 1) * 128]
    vectors = [
        g_vec1[1:2, :D],
        g_vec1[2:3, :D],
        g_vec1[0:1, :D],
        g_vec1[0:1, 2 * D :],
        g_vec2[4:5, :D],
    ]
    pieces = [v[:, j * 128 : (j + 1) * 128] for v in vectors for j in range(3)]
    pieces += [jnp.zeros((1, 128), F32)]
    row, lane = divmod(ATTN_VECTORS[0], 128)
    flat_a[row : row + 16, :] += shift_lanes(jnp.concatenate(pieces, axis=0), lane, True)
    for h in range(HEADS):
        table[...] = jnp.zeros_like(table)
        for half in range(2):
            turned = g_bias[h, half].T
            for y in range(WIN):
                for at, length, source in bias_runs(half, WIN * half + y):
                    table[0:14, source : source + length] += turned[
                        y * 14 : y * 14 + 14, at : at + length
                    ]
        for c in range(4):
            shifted[c, pl.ds(h, 14, stride=16), :] = table[0:14, c * 128 : (c + 1) * 128]
    g_fine = jnp.zeros((16, 384), F32)
    g_coarse = jnp.zeros((16, 256), F32)
    for qx in range(14):
        at = slice(qx * 16, qx * 16 + 16)
        part = jnp.concatenate([shifted[c, at, :] for c in range(4)], axis=1)
        high = part.astype(BF16)
        low = (part - high.astype(F32)).astype(BF16)
        g_fine += dot_t(high[:, :384], one_fine[qx]) + dot_t(low[:, :384], one_fine[qx])
        g_coarse += dot_t(high[:, 384:], one_coarse[qx]) + dot_t(low[:, 384:], one_coarse[qx])
    for value, first, length in (
        (g_fine, TABLE_AT, FINE),
        (g_coarse, TABLE_AT + HEADS * FINE, COARSE),
    ):
        for h in range(HEADS):
            row, lane = divmod(first + h * length, 128)
            count = -(-(lane + length) // 128)
            line[...] = jnp.zeros_like(line)
            line[0:1, lane : lane + length] = value[h : h + 1, :length]
            for c in range(count):
                flat_a[row + c : row + c + 1, :] += line[0:1, c * 128 : (c + 1) * 128]
    for device, place in enumerate(places):
        a_at, b_at = flat.start(0, device), flat.start(1, device)
        out[place] = jnp.concatenate(
            [
                flat_a[a_at : a_at + flat.rows[0], :],
                flat_b[b_at : b_at + flat.rows[1], :],
            ],
            axis=0,
        ).astype(BF16)


def pack(flat, places, g_bias, g_qkv, g_vec1, g_proj, g_w1, g_w2t, g_vec2):
    fine, coarse, _ = bias_tables()
    vm = pl.BlockSpec(memory_space=pltpu.VMEM)
    return pl.pallas_call(
        functools.partial(pack_kernel, flat, places),
        out_shape=jax.ShapeDtypeStruct((flat.devices, flat.total, 128), BF16),
        in_specs=[vm] * 9,
        out_specs=vm,
        scratch_shapes=[
            pltpu.VMEM((flat.buffer[0], 128), F32),
            pltpu.VMEM((flat.buffer[1], 128), F32),
            pltpu.VMEM((16, 512), F32),
            pltpu.VMEM((4, 14 * 16, 128), F32),
            pltpu.VMEM((8, 512), F32),
        ],
        compiler_params=pltpu.CompilerParams(vmem_limit_bytes=VMEM_LIMIT),
        name="pack",
    )(
        jnp.asarray(fine),
        jnp.asarray(coarse),
        g_bias,
        g_qkv,
        g_vec1,
        g_proj,
        g_w1,
        g_w2t,
        g_vec2,
    )


def join_kernel(rows, slot_ref, in0, in1, in2, in3, out):
    for k, ref in enumerate((in0, in1, in2, in3)):
        at = pl.multiple_of(xor_slot(slot_ref[0], k) * rows, 16)
        out[pl.ds(at, rows), :] = ref[...].astype(out.dtype)


def join(slot, parts, dtype):
    rows = parts[0].shape[0]
    vm = pl.BlockSpec(memory_space=pltpu.VMEM)
    return pl.pallas_call(
        functools.partial(join_kernel, rows),
        out_shape=jax.ShapeDtypeStruct((4 * rows, D), dtype),
        in_specs=[pl.BlockSpec(memory_space=pltpu.SMEM)] + [vm] * 4,
        out_specs=vm,
        compiler_params=pltpu.CompilerParams(vmem_limit_bytes=VMEM_LIMIT),
        name="join",
    )(slot, *parts)


def adamw(master, first, second, grads):
    first_new = beta_one * first + (1.0 - beta_one) * grads
    second_new = beta_two * second + (1.0 - beta_two) * grads * grads
    first_hat = first_new / (1.0 - beta_one**STEP)
    second_hat = second_new / (1.0 - beta_two**STEP)
    master_new = master - learn_rate * (
        first_hat / (jnp.sqrt(second_hat) + adam_eps) + decay_rate * master
    )
    return (first_new, second_new, master_new)


def swap(value, k):
    pairs = [(s, s ^ k) for s in range(lax.axis_size("dp"))]
    return lax.ppermute(value, "dp", pairs)


def body(
    tokens, cotangent, attn_master, attn_first, attn_second, mlp_master, mlp_first, mlp_second
):
    n_dp, n_grp = lax.axis_size("dp"), lax.axis_size("grp")
    order = bit_order(n_dp, n_grp)
    places = place_list(order, n_dp, n_grp)
    flat = Flat(n_dp * n_grp, attn_master.shape[0], mlp_master.shape[0])
    slot = lax.rem(lax.axis_index("dp"), 4).astype(jnp.int32)
    slot_arr = slot.reshape(1)
    token_count = tokens.shape[1]
    rows = token_count // 4
    images = rows // SEQ

    def exchanged(array):
        return [
            swap(lax.dynamic_slice_in_dim(array, xor_slot(slot, k) * rows, rows, 0), k)
            for k in (1, 2, 3)
        ]

    tok, cot = tokens[0], cotangent[0]
    tok_in = exchanged(tok)
    cot_in = exchanged(cot)
    gathered = gather_params(flat, order, attn_master, mlp_master)
    wqkv, wproj, w1, w2, vecs, bias = prepare(flat, places, gathered)
    mixed, probs, qkv, x = attend(slot_arr, tok, tok_in, wqkv, vecs, bias, images)
    mlp_out = mlp(slot_arr, cot, cot_in, mixed, x, wproj, w1, w2, vecs)
    out_parts, (d_res, d_mixed, g_w1, g_w2t, g_proj, g_vec2) = mlp_out[:4], mlp_out[4:]
    out_parts = [out_parts[0]] + [swap(out_parts[k], k) for k in (1, 2, 3)]
    d_qkv, g_bias = attend_back(qkv, d_mixed, probs, images)
    back = input_back(slot_arr, d_qkv, x, d_res, wqkv, vecs)
    in_parts, (g_qkv, g_vec1) = back[:4], back[4:]
    in_parts = [in_parts[0]] + [swap(in_parts[k], k) for k in (1, 2, 3)]
    blocks = pack(flat, places, g_bias, g_qkv, g_vec1, g_proj, g_w1, g_w2t, g_vec2)
    grad_a, grad_b = sum_grads(flat, order, blocks)
    attn_new = adamw(attn_master, attn_first, attn_second, grad_a)
    mlp_new = adamw(mlp_master, mlp_first, mlp_second, grad_b)
    output = join(slot_arr, out_parts, BF16)
    input_grad = join(slot_arr, in_parts, F32)
    return (output[None], input_grad[None], *attn_new, *mlp_new)


def solution(mesh):
    flat_spec = P(("dp", "grp"))
    token_spec = P("dp", "grp", None)
    placed = (token_spec, token_spec) + (flat_spec,) * 6
    return jax.shard_map(
        body, mesh=mesh, in_specs=placed, out_specs=placed, check_vma=False
    )
```

```python
import functools

import jax
import jax.numpy as jnp
import ml_dtypes
import numpy as np
from jax import lax
from jax.experimental import pallas as pl
from jax.experimental.pallas import tpu as pltpu
from jax.sharding import PartitionSpec as P

D = 384
HEADS = 12
HDIM = 32
FF = 1536
WIN = 7
STEP = 10
SEQ = WIN * WIN
HALF = 64
FINE = (3 * WIN - 2) ** 2
COARSE = (2 * WIN - 1) ** 2
KEYS = 192

beta_one = 0.9
beta_two = 0.999
learn_rate = 0.04
decay_rate = 0.05
adam_eps = 1e-08
norm_eps = 1e-05
masked_score = -1e30

F32 = jnp.float32
BF16 = jnp.bfloat16
MESH = pl.DeviceIdType.MESH
VMEM_LIMIT = 56 * 2**20


def token_place(gy, gx):
    window = 2 * (gy // WIN) + gx // WIN
    return window * HALF + (gy % WIN) * WIN + gx % WIN


@functools.cache
def gather_tables(images):
    keys = np.zeros((images, 256, 256), np.float32)
    queries = np.zeros((images, 256, 256), np.float32)
    for i in range(images):
        for gy in range(2 * WIN):
            for gx in range(2 * WIN):
                at = token_place(gy, gx) + i
                key = gy * 14 + gx if gy < 10 else 192 + (gy - 10) * 14 + gx
                keys[i, key, at] = 1.0
                keys[i, 140 + (gy // 2) * WIN + gx // 2, at] = 0.25
                queries[i, (gy // WIN) * 128 + (gy % WIN) * 14 + gx, at] = 1.0
    return (
        keys.astype(ml_dtypes.bfloat16),
        queries.astype(ml_dtypes.bfloat16),
        np.ascontiguousarray(keys.transpose(0, 2, 1)).astype(ml_dtypes.bfloat16),
        np.ascontiguousarray(queries.transpose(0, 2, 1)).astype(ml_dtypes.bfloat16),
    )


@functools.cache
def bias_tables():
    fine = np.zeros((14, 384, 384), np.float32)
    coarse = np.zeros((14, 256, 128), np.float32)
    for qx in range(14):
        for a in range(27):
            for kx in range(14):
                col = kx - qx + 9
                if 4 <= a <= 22 and 0 <= col <= 18:
                    fine[qx, 19 * (a - 4) + col, a * 14 + kx] = 1.0
        for p in range(13):
            for s in range(WIN):
                coarse[qx, 13 * p + s - qx // 2 + 6, p * WIN + s] = 1.0
    mask = np.zeros((2, KEYS, 128), np.float32)
    for half in range(2):
        for q in range(98):
            qx = q % 14
            for e in range(KEYS):
                at = e + 56 * half
                if at < 140:
                    ok = abs_ok(qx, at % 14)
                elif at < 189:
                    ok = True
                elif at < 192:
                    ok = False
                else:
                    ok = at < 248 and abs_ok(qx, (at - 192) % 14)
                mask[half, e, q] = 0.0 if ok else masked_score
    return fine.astype(ml_dtypes.bfloat16), coarse.astype(ml_dtypes.bfloat16), mask


def abs_ok(qx, kx):
    return kx < 10 if qx < WIN else kx >= 4


def bias_runs(half, qy):
    fine = (13 - qy) * 14
    pool = 384 + (6 - qy // 2) * WIN
    if half == 0:
        return [(0, 140, fine), (140, 49, pool)]
    return [(0, 84, fine + 56), (84, 49, pool), (136, 56, fine + 140)]


class Flat:
    def __init__(self, devices, part_a, part_b):
        self.devices = devices
        self.part = (part_a, part_b)
        self.rows = tuple(-(-((p + 126) // 128 + 1) // 8) * 8 for p in self.part)
        self.total = sum(self.rows)
        extra = -self.total % 16
        self.rows = (self.rows[0], self.rows[1] + extra)
        self.total += extra
        self.buffer = tuple(
            -(-(self.start(w, devices - 1) + self.rows[w]) // 8) * 8 for w in range(2)
        )

    def start(self, which, device):
        return device * self.part[which] // 128


def bit_order(n_dp, n_grp):
    dp_bits = [("dp", 2**b) for b in range(n_dp.bit_length() - 1)]
    grp_bits = [("grp", 2**b) for b in reversed(range(n_grp.bit_length() - 1))]
    return dp_bits[1:2] + grp_bits + dp_bits[2:] + dp_bits[:1]


def place_of(order, dp, grp):
    place = 0
    for k, (axis, stride) in enumerate(order):
        place = place + ((dp if axis == "dp" else grp) // stride) % 2 * 2**k
    return place


def partner_of(axis, stride, dp, grp):
    if axis == "dp":
        return (dp + (1 - 2 * ((dp // stride) % 2)) * stride, grp)
    return (dp, grp + (1 - 2 * ((grp // stride) % 2)) * stride)


def greet(partners):
    barrier = pltpu.get_barrier_semaphore()
    for partner in partners:
        pl.semaphore_signal(barrier, inc=1, device_id=partner, device_id_type=MESH)
    pl.semaphore_wait(barrier, len(partners))


def cube_partners(order, dp, grp):
    return [partner_of(axis, stride, dp, grp) for axis, stride in order]


def shift_lanes(values, amount, up):
    lane = lax.broadcasted_iota(jnp.int32, values.shape, 1)
    if up:
        turned = pltpu.roll(values, amount, 1)
        return jnp.where(lane >= amount, turned, pltpu.roll(turned, 1, 0))
    turned = pltpu.roll(values, lax.rem(128 - amount, 128), 1)
    return jnp.where(lane < 128 - amount, turned, pltpu.roll(turned, values.shape[0] - 1, 0))


def window_partner(dp, grp, k):
    low, high = dp % 2, dp // 2 % 2
    to = dp
    if k % 2:
        to = to + 1 - 2 * low
    if k // 2:
        to = to + 2 * (1 - 2 * high)
    return (to, grp)


def exchange_copies(source, target, dp, grp, own_sem, send_sems, recv_sems):
    rows = source.shape[0] // 4
    slot = dp % 4
    mine = pl.ds(pl.multiple_of(slot * rows, 16), rows)
    own = pltpu.make_async_copy(source.at[mine], target.at[mine], own_sem)
    sends = []
    for k in (3, 2, 1):
        to, _ = window_partner(dp, grp, k)
        theirs = pl.ds(pl.multiple_of(to % 4 * rows, 16), rows)
        sends.append(
            pltpu.make_async_remote_copy(
                src_ref=source.at[theirs],
                dst_ref=target.at[mine],
                send_sem=send_sems.at[k - 1],
                recv_sem=recv_sems.at[k - 1],
                device_id=(to, grp),
                device_id_type=MESH,
            )
        )
    return [own] + sends


def gather_kernel(
    flat,
    order,
    a_ref,
    b_ref,
    tok_ref,
    out_ref,
    x_ref,
    own,
    own_sem,
    send_sems,
    recv_sems,
    x_sem,
    x_send,
    x_recv,
):
    dp, grp = lax.axis_index("dp"), lax.axis_index("grp")
    device = dp * lax.axis_size("grp") + grp
    place = place_of(order, dp, grp)
    parts = [
        shift_lanes(ref[...], lax.rem(device * flat.part[w], 128), True)
        for w, ref in enumerate((a_ref, b_ref))
    ]
    own[...] = jnp.concatenate(parts, axis=0).astype(BF16)
    copy = pltpu.make_async_copy(own, out_ref.at[place], own_sem)
    copy.start()
    greet(cube_partners(order, dp, grp) + [window_partner(dp, grp, 3)])
    copy.wait()
    exchange = exchange_copies(tok_ref, x_ref, dp, grp, x_sem, x_send, x_recv)
    for k, (axis, stride) in enumerate(order):
        held = out_ref.at[pl.ds(place // 2**k * 2**k, 2**k)]
        send = pltpu.make_async_remote_copy(
            src_ref=held,
            dst_ref=held,
            send_sem=send_sems.at[k],
            recv_sem=recv_sems.at[k],
            device_id=partner_of(axis, stride, dp, grp),
            device_id_type=MESH,
        )
        send.start()
        if k == 0:
            for c in exchange:
                c.start()
        send.wait()
    for c in exchange:
        c.wait()


def gather_params(flat, order, master_a, master_b, tok):
    padded = [
        jnp.pad(m, (0, flat.rows[w] * 128 - m.shape[0])).reshape(flat.rows[w], 128)
        for w, m in enumerate((master_a, master_b))
    ]
    stages = len(order)
    return pl.pallas_call(
        functools.partial(gather_kernel, flat, order),
        out_shape=[
            jax.ShapeDtypeStruct((flat.devices, flat.total, 128), BF16),
            jax.ShapeDtypeStruct(tok.shape, BF16),
        ],
        in_specs=[pl.BlockSpec(memory_space=pltpu.VMEM)] * 2
        + [pl.BlockSpec(memory_space=pl.ANY)],
        out_specs=[pl.BlockSpec(memory_space=pl.ANY)] * 2,
        scratch_shapes=[
            pltpu.VMEM((flat.total, 128), BF16),
            pltpu.SemaphoreType.DMA,
            pltpu.SemaphoreType.DMA((stages,)),
            pltpu.SemaphoreType.DMA((stages,)),
            pltpu.SemaphoreType.DMA,
            pltpu.SemaphoreType.DMA((3,)),
            pltpu.SemaphoreType.DMA((3,)),
        ],
        compiler_params=pltpu.CompilerParams(
            collective_id=0, has_side_effects=True, vmem_limit_bytes=VMEM_LIMIT
        ),
        name="gather_params",
    )(*padded, tok)


def sum_kernel(
    flat, order, x_ref, a_ref, b_ref, total, outgoing, arrived, send_sems, recv_sems
):
    dp, grp = lax.axis_index("dp"), lax.axis_index("grp")
    device = dp * lax.axis_size("grp") + grp
    place = place_of(order, dp, grp)
    greet(cube_partners(order, dp, grp))
    stages = len(order)
    for k in reversed(range(stages)):
        axis, stride = order[k]
        size = 2**k
        mine = place // size % 2 * size
        other = size - mine
        if k == stages - 1:
            source = x_ref.at[pl.ds(other, size)]
        else:

            def fill(j, carry):
                outgoing[size + j] = total[other + j].astype(BF16)
                return carry

            lax.fori_loop(0, size, fill, 0)
            source = outgoing.at[pl.ds(size, size)]
        send = pltpu.make_async_remote_copy(
            src_ref=source,
            dst_ref=arrived.at[pl.ds(size, size)],
            send_sem=send_sems.at[k],
            recv_sem=recv_sems.at[k],
            device_id=partner_of(axis, stride, dp, grp),
            device_id_type=MESH,
        )
        send.start()
        send.wait()

        def add(j, carry):
            if k == stages - 1:
                held = x_ref[mine + j].astype(F32)
            else:
                held = total[mine + j]
            total[j] = held + arrived[size + j].astype(F32)
            return carry

        lax.fori_loop(0, size, add, 0)
    result = total[0]
    rows = flat.rows[0]
    for w, (ref, part) in enumerate(((a_ref, result[:rows]), (b_ref, result[rows:]))):
        ref[...] = shift_lanes(part, lax.rem(device * flat.part[w], 128), False)


def sum_grads(flat, order, blocks):
    stages = len(order)
    n = flat.devices
    outs = pl.pallas_call(
        functools.partial(sum_kernel, flat, order),
        out_shape=[jax.ShapeDtypeStruct((r, 128), F32) for r in flat.rows],
        in_specs=[pl.BlockSpec(memory_space=pltpu.VMEM)],
        out_specs=[pl.BlockSpec(memory_space=pltpu.VMEM)] * 2,
        scratch_shapes=[
            pltpu.VMEM((n // 2, flat.total, 128), F32),
            pltpu.VMEM((n // 2, flat.total, 128), BF16),
            pltpu.VMEM((n, flat.total, 128), BF16),
            pltpu.SemaphoreType.DMA((stages,)),
            pltpu.SemaphoreType.DMA((stages,)),
        ],
        compiler_params=pltpu.CompilerParams(
            collective_id=1, has_side_effects=True, vmem_limit_bytes=VMEM_LIMIT
        ),
        name="sum_grads",
    )(blocks)
    return [o.reshape(-1)[: flat.part[w]] for w, o in enumerate(outs)]


def place_list(order, n_dp, n_grp):
    return [place_of(order, d // n_grp, d % n_grp) for d in range(n_dp * n_grp)]


ATTN_VECTORS = (D * 3 * D + D * D + HEADS * FINE + HEADS * COARSE, 5)
TABLE_AT = D * 3 * D + D * D


def prep_kernel(
    flat,
    places,
    parts_ref,
    one_fine,
    one_coarse,
    mask_ref,
    wqkv,
    wproj,
    w1,
    w2,
    vecs,
    bias,
    flat_a,
    flat_b,
    tab_fine,
    tab_coarse,
    shifted,
    turned,
):
    flat_a[...] = jnp.zeros_like(flat_a)
    flat_b[...] = jnp.zeros_like(flat_b)
    for device, place in enumerate(places):
        block = parts_ref[place].astype(F32)
        a_at, b_at = flat.start(0, device), flat.start(1, device)
        a_rows, b_rows = flat.rows
        flat_a[a_at : a_at + a_rows, :] += block[:a_rows]
        flat_b[b_at : b_at + b_rows, :] += block[a_rows:]
    for j in range(9):
        wqkv[:, j * 128 : (j + 1) * 128] = flat_a[pl.ds(j, D, stride=9), :].astype(BF16)
    for j in range(3):
        wproj[:, j * 128 : (j + 1) * 128] = flat_a[pl.ds(3456 + j, D, stride=3), :].astype(BF16)
        w2[:, j * 128 : (j + 1) * 128] = flat_b[pl.ds(4608 + j, FF, stride=3), :].astype(BF16)
    for j in range(12):
        w1[:, j * 128 : (j + 1) * 128] = flat_b[pl.ds(j, D, stride=12), :].astype(BF16)
    vecs[...] = jnp.zeros_like(vecs)
    row, lane = divmod(ATTN_VECTORS[0], 128)
    rows = shift_lanes(flat_a[row : row + 16, :], lane, False)
    for v in range(5):
        for j in range(3):
            vecs[v : v + 1, j * 128 : (j + 1) * 128] = rows[3 * v + j : 3 * v + j + 1]
    for j in range(12):
        vecs[8:9, j * 128 : (j + 1) * 128] = flat_b[9216 + j : 9217 + j, :]
    for v in range(3):
        for j in range(3):
            at = 9228 + 3 * v + j
            vecs[5 + v : 6 + v, j * 128 : (j + 1) * 128] = flat_b[at : at + 1, :]
    tab_fine[...] = jnp.zeros_like(tab_fine)
    tab_coarse[...] = jnp.zeros_like(tab_coarse)
    for ref, first, length in (
        (tab_fine, TABLE_AT, FINE),
        (tab_coarse, TABLE_AT + HEADS * FINE, COARSE),
    ):
        for h in range(HEADS):
            row, lane = divmod(first + h * length, 128)
            count = -(-(lane + length) // 128)
            line = jnp.concatenate(
                [flat_a[row + c : row + c + 1, :] for c in range(count)], axis=1
            )
            ref[h : h + 1, 0:length] = line[:, lane : lane + length]
    for qx in range(14):
        at = slice(qx * 16, qx * 16 + 16)
        moved = dot(tab_fine[...].astype(BF16), one_fine[qx])
        for c in range(3):
            shifted[c, at, :] = moved[:, c * 128 : (c + 1) * 128]
        shifted[3, at, :] = dot(tab_coarse[...].astype(BF16), one_coarse[qx])
    turned[...] = jnp.zeros_like(turned)
    for h in range(HEADS):
        table = jnp.concatenate(
            [shifted[c, pl.ds(h, 14, stride=16), :] for c in range(4)], axis=1
        )
        for half in range(2):
            for y in range(WIN):
                for at, length, source in bias_runs(half, WIN * half + y):
                    turned[half, y * 14 : y * 14 + 14, at : at + length] = table[
                        :, source : source + length
                    ]
            bias[h, half] = turned[half].T[0:KEYS] + mask_ref[half]


def prepare(flat, places, gathered):
    fine, coarse, mask = bias_tables()
    vm = pl.BlockSpec(memory_space=pltpu.VMEM)
    return pl.pallas_call(
        functools.partial(prep_kernel, flat, places),
        out_shape=[
            jax.ShapeDtypeStruct((D, 3 * D), BF16),
            jax.ShapeDtypeStruct((D, D), BF16),
            jax.ShapeDtypeStruct((D, FF), BF16),
            jax.ShapeDtypeStruct((FF, D), BF16),
            jax.ShapeDtypeStruct((16, FF), F32),
            jax.ShapeDtypeStruct((HEADS, 2, KEYS, 128), F32),
        ],
        in_specs=[vm] * 4,
        out_specs=[vm] * 6,
        scratch_shapes=[
            pltpu.VMEM((flat.buffer[0], 128), F32),
            pltpu.VMEM((flat.buffer[1], 128), F32),
            pltpu.VMEM((16, 384), F32),
            pltpu.VMEM((16, 256), F32),
            pltpu.VMEM((4, 14 * 16, 128), F32),
            pltpu.VMEM((2, 128, 256), F32),
        ],
        compiler_params=pltpu.CompilerParams(vmem_limit_bytes=VMEM_LIMIT),
        name="prepare",
    )(gathered, jnp.asarray(fine), jnp.asarray(coarse), jnp.asarray(mask))


def dot(a, b):
    return jnp.dot(a, b, preferred_element_type=F32)


def dot_t(a, b):
    return lax.dot_general(a, b, (((1,), (1,)), ((), ())), preferred_element_type=F32)


def norm_parts(values):
    centered = values - jnp.mean(values, axis=-1, keepdims=True)
    scale = lax.rsqrt(jnp.mean(centered * centered, axis=-1, keepdims=True) + norm_eps)
    return centered * scale, scale


def norm_back(d_normed, xhat, scale, gain):
    dh = d_normed * gain
    return scale * (
        dh
        - jnp.mean(dh, axis=-1, keepdims=True)
        - xhat * jnp.mean(dh * xhat, axis=-1, keepdims=True)
    )


def xor_slot(slot, k):
    low, high = lax.rem(slot, 2), slot // 2
    if k % 2:
        low = 1 - low
    if k // 2:
        high = 1 - high
    return 2 * high + low


def split_copies(slot, refs, whole, sems, rows, outward):
    copies = []
    for k, ref in enumerate(refs):
        part = whole.at[pl.ds(pl.multiple_of(xor_slot(slot, k) * rows, 16), rows)]
        ends = (part, ref) if outward else (ref, part)
        copies.append(pltpu.make_async_copy(*ends, sems.at[k]))
    return copies


def lane_heads(j):
    lane = lax.broadcasted_iota(jnp.int32, (256, 128), 1)
    return (lane // HDIM) == j


def image_rows(ref, i, rows, columns):
    at = pl.multiple_of(48 * i, 16)
    parts = [
        ref[pl.ds(pl.multiple_of(w * rows + at, 16), HALF), columns] for w in range(4)
    ]
    return jnp.concatenate(parts, axis=0)


def put_image_rows(ref, i, rows, columns, values):
    at = 48 * i
    for w in range(4):
        part = values[w * HALF : (w + 1) * HALF]
        first = pl.ds(pl.multiple_of(w * rows + at, 16), 16)
        rest = pl.ds(pl.multiple_of(w * rows + at + 16, 16), HALF - 16)
        held = jnp.where(i > 0, ref[first, columns].astype(F32), 0.0)
        ref[first, columns] = (held + part[:16]).astype(ref.dtype)
        ref[rest, columns] = part[16:].astype(ref.dtype)


def attend_kernel(
    rows,
    x_buf,
    cot_ref,
    wqkv,
    vecs,
    bias,
    keys_tab,
    query_tab,
    query_back,
    mixed,
    probs,
    qkv,
    cot_out,
    normed,
    mixed_t,
    own_sem,
    send_sems,
    recv_sems,
):
    i = pl.program_id(0)
    dp, grp = lax.axis_index("dp"), lax.axis_index("grp")
    exchange = exchange_copies(cot_ref, cot_out, dp, grp, own_sem, send_sems, recv_sems)

    @pl.when(i == 0)
    def _():
        greet([window_partner(dp, grp, k) for k in (1, 2, 3)])
        for c in exchange:
            c.start()

        def project(w, carry):
            base = pl.multiple_of(w * rows, 16)
            step = rows // 7

            def norm(c, inner):
                at = pl.multiple_of(c * step, 16)
                xhat, _ = norm_parts(x_buf[pl.ds(base + at, step), :].astype(F32))
                normed[pl.ds(at, step), :] = (xhat * vecs[0:1, :D] + vecs[1:2, :D]).astype(BF16)
                return inner

            lax.fori_loop(0, 7, norm, 0)
            here = pl.ds(base, rows)
            q = dot(normed[...], wqkv[:, :D]) + vecs[2:3, :D]
            qkv[here, :D] = (q * HDIM ** (-0.5)).astype(BF16)
            qkv[here, D : 2 * D] = dot(normed[...], wqkv[:, D : 2 * D]).astype(BF16)
            v = dot(normed[...], wqkv[:, 2 * D :]) + vecs[3:4, :D]
            qkv[here, 2 * D :] = v.astype(BF16)
            return carry

        lax.fori_loop(0, 4, project, 0)

    q_ext = dot(query_tab[0], image_rows(qkv, i, rows, slice(0, D))).astype(BF16)
    kv_ext = dot(keys_tab[0], image_rows(qkv, i, rows, slice(D, 3 * D)))
    k_ext = kv_ext[:, :D].astype(BF16)
    v_t = kv_ext[:, D:].T.astype(BF16)
    for h in range(HEADS):
        tile = slice(h // 4 * 128, h // 4 * 128 + 128)
        q_head = jnp.where(lane_heads(h % 4), q_ext[:, tile], 0)
        scores = dot_t(k_ext[:, tile], q_head)
        halves = []
        for half in range(2):
            s = scores[56 * half : 56 * half + KEYS, 128 * half : 128 * half + 128] + bias[h, half]
            e = jnp.exp(s - jnp.max(s, axis=0, keepdims=True))
            p = e * (1.0 / jnp.sum(e, axis=0, keepdims=True))
            above, below = 56 * half, 64 - 56 * half
            pieces = [p, jnp.zeros((below, 128), F32)]
            if above:
                pieces = [jnp.zeros((above, 128), F32)] + pieces
            halves.append(jnp.concatenate(pieces, axis=0))
        p = jnp.concatenate(halves, axis=1).astype(BF16)
        probs[0, h] = p
        mixed_t[h * HDIM : (h + 1) * HDIM, :] = dot(
            v_t[h * HDIM : (h + 1) * HDIM, :], p
        ).astype(BF16)
    put_image_rows(mixed, i, rows, slice(None), dot_t(query_back[0], mixed_t[...]))

    @pl.when(i == pl.num_programs(0) - 1)
    def _():
        for c in exchange:
            c.wait()


def attend(x, cot, wqkv, vecs, bias, images):
    tokens = x.shape[0]
    rows = tokens // 4
    keys_tab, query_tab, _, query_back = gather_tables(images)
    vm = pl.BlockSpec(memory_space=pltpu.VMEM)
    hbm = pl.BlockSpec(memory_space=pl.ANY)
    table = pl.BlockSpec((1, 256, 256), lambda i: (i, 0, 0))
    whole = lambda width: pl.BlockSpec((tokens, width), lambda i: (0, 0))
    return pl.pallas_call(
        functools.partial(attend_kernel, rows),
        grid=(images,),
        out_shape=[
            jax.ShapeDtypeStruct((tokens, D), BF16),
            jax.ShapeDtypeStruct((images, HEADS, 256, 256), BF16),
            jax.ShapeDtypeStruct((tokens, 3 * D), BF16),
            jax.ShapeDtypeStruct((tokens, D), BF16),
        ],
        in_specs=[vm, hbm] + [vm] * 3 + [table] * 3,
        out_specs=[
            whole(D),
            pl.BlockSpec((1, HEADS, 256, 256), lambda i: (i, 0, 0, 0)),
            whole(3 * D),
            hbm,
        ],
        scratch_shapes=[
            pltpu.VMEM((rows, D), BF16),
            pltpu.VMEM((D, 256), BF16),
            pltpu.SemaphoreType.DMA,
            pltpu.SemaphoreType.DMA((3,)),
            pltpu.SemaphoreType.DMA((3,)),
        ],
        compiler_params=pltpu.CompilerParams(
            collective_id=2, has_side_effects=True, vmem_limit_bytes=VMEM_LIMIT
        ),
        name="attend",
    )(x, cot, wqkv, vecs, bias, keys_tab, query_tab, query_back)


GELU_A = float(np.sqrt(2.0 / np.pi))
GELU_B = 0.044715


def mlp_kernel(
    rows,
    slot_ref,
    cot_ref,
    mixed_ref,
    x_ref,
    wproj,
    w1,
    w2,
    vecs,
    out0,
    out1,
    out2,
    out3,
    d_res_ref,
    d_mixed_ref,
    g_w1,
    g_w2t,
    g_proj,
    g_vec,
    o_buf,
    sems,
):
    i = pl.program_id(0)
    slot = slot_ref[0]
    chunk = mixed_ref.shape[0]

    @pl.when(i == 0)
    def _():
        g_w1[...] = jnp.zeros_like(g_w1)
        g_w2t[...] = jnp.zeros_like(g_w2t)
        g_proj[...] = jnp.zeros_like(g_proj)
        g_vec[...] = jnp.zeros_like(g_vec)

    here = pl.ds(pl.multiple_of(i * chunk, 16), chunk)
    mix = mixed_ref[...]
    res = x_ref[...].astype(F32) + dot(mix, wproj[...]) + vecs[4:5, :D]
    xhat, scale = norm_parts(res)
    gain = vecs[5:6, :D]
    normed = (xhat * gain + vecs[6:7, :D]).astype(BF16)
    grad = cot_ref[...]
    grad_t = grad.T
    normed_t = normed.T
    out = res + vecs[7:8, :D]
    d_normed = jnp.zeros((chunk, D), F32)
    for f in range(3):
        cols = slice(f * 512, f * 512 + 512)
        hidden = dot(normed, w1[:, cols]) + vecs[8:9, cols]
        square = hidden * hidden
        t = jnp.tanh(hidden * (GELU_A + (GELU_A * GELU_B) * square))
        half = 0.5 + 0.5 * t
        act = (hidden * half).astype(BF16)
        slope = half + (0.5 * hidden) * (1.0 - t * t) * (GELU_A + (3 * GELU_A * GELU_B) * square)
        out += dot(act, w2[cols, :])
        d_hidden32 = dot_t(grad, w2[cols, :]) * slope
        d_hidden = d_hidden32.astype(BF16)
        g_vec[0:1, cols] += jnp.sum(d_hidden32, axis=0, keepdims=True)
        d_normed += dot_t(d_hidden, w1[:, cols])
        g_w1[:, cols] += dot(normed_t, d_hidden)
        g_w2t[:, cols] += dot(grad_t, act)
    o_buf[here, :] = out.astype(BF16)
    grad32 = grad.astype(F32)
    d_res = grad32 + norm_back(d_normed, xhat, scale, gain)
    d_res_ref[...] = d_res
    d_attn = d_res.astype(BF16)
    d_mixed_ref[...] = dot_t(d_attn, wproj[...]).astype(BF16)
    g_proj[...] += dot(mix.T, d_attn)
    g_vec[1:2, :D] += jnp.sum(d_normed * xhat, axis=0, keepdims=True)
    g_vec[2:3, :D] += jnp.sum(d_normed, axis=0, keepdims=True)
    g_vec[3:4, :D] += jnp.sum(grad32, axis=0, keepdims=True)
    g_vec[4:5, :D] += jnp.sum(d_res, axis=0, keepdims=True)

    @pl.when(i == pl.num_programs(0) - 1)
    def _():
        copies = split_copies(slot, (out0, out1, out2, out3), o_buf, sems, rows, True)
        for c in copies:
            c.start()
        for c in copies:
            c.wait()


def mlp(slot, cot, mixed, x, wproj, w1, w2, vecs):
    tokens = x.shape[0]
    rows = tokens // 4
    chunk = tokens // 7
    vm = pl.BlockSpec(memory_space=pltpu.VMEM)
    hbm = pl.BlockSpec(memory_space=pl.ANY)
    tile = pl.BlockSpec((chunk, D), lambda i: (i, 0))
    fixed = lambda *shape: pl.BlockSpec(shape, lambda i: (0, 0))
    return pl.pallas_call(
        functools.partial(mlp_kernel, rows),
        grid=(7,),
        out_shape=[jax.ShapeDtypeStruct((rows, D), BF16)] * 4
        + [
            jax.ShapeDtypeStruct((tokens, D), F32),
            jax.ShapeDtypeStruct((tokens, D), BF16),
            jax.ShapeDtypeStruct((D, FF), F32),
            jax.ShapeDtypeStruct((D, FF), F32),
            jax.ShapeDtypeStruct((D, D), F32),
            jax.ShapeDtypeStruct((8, FF), F32),
        ],
        in_specs=[pl.BlockSpec(memory_space=pltpu.SMEM)] + [tile] * 3 + [vm] * 4,
        out_specs=[hbm] * 4
        + [tile, tile, fixed(D, FF), fixed(D, FF), fixed(D, D), fixed(8, FF)],
        scratch_shapes=[
            pltpu.VMEM((tokens, D), BF16),
            pltpu.SemaphoreType.DMA((4,)),
        ],
        compiler_params=pltpu.CompilerParams(vmem_limit_bytes=VMEM_LIMIT),
        name="mlp",
    )(slot, cot, mixed, x, wproj, w1, w2, vecs)


def attend_back_kernel(
    rows,
    qkv,
    d_mixed,
    probs,
    keys_tab,
    query_tab,
    keys_back,
    query_back,
    d_qkv,
    g_bias,
    d_query_t,
    d_key_value,
):
    i = pl.program_id(0)

    @pl.when(i == 0)
    def _():
        g_bias[...] = jnp.zeros_like(g_bias)

    q_ext = dot(query_tab[0], image_rows(qkv, i, rows, slice(0, D))).astype(BF16)
    dm_ext = dot(query_tab[0], image_rows(d_mixed, i, rows, slice(None))).astype(BF16)
    kv_ext = dot(keys_tab[0], image_rows(qkv, i, rows, slice(D, 3 * D)))
    k_t = kv_ext[:, :D].T.astype(BF16)
    v_ext = kv_ext[:, D:].astype(BF16)
    for tile_at in range(3):
        tile = slice(tile_at * 128, tile_at * 128 + 128)
        d_key = jnp.zeros((256, 128), F32)
        d_value = jnp.zeros((256, 128), F32)
        for j in range(4):
            h = tile_at * 4 + j
            mine = lane_heads(j)
            q_head = jnp.where(mine, q_ext[:, tile], 0)
            dm_head = jnp.where(mine, dm_ext[:, tile], 0)
            p = probs[0, h]
            d_value += dot(p, dm_head)
            d_probs = dot_t(v_ext[:, tile], dm_head)
            halves = []
            for half in range(2):
                at = (slice(56 * half, 56 * half + KEYS), slice(128 * half, 128 * half + 128))
                p32 = p[:, at[1]].astype(F32)[at[0]]
                dp = d_probs[at]
                ds = p32 * (dp - jnp.sum(p32 * dp, axis=0, keepdims=True))
                g_bias[h, half] += ds
                above, below = 56 * half, 64 - 56 * half
                pieces = [ds, jnp.zeros((below, 128), F32)]
                if above:
                    pieces = [jnp.zeros((above, 128), F32)] + pieces
                halves.append(jnp.concatenate(pieces, axis=0))
            ds = jnp.concatenate(halves, axis=1).astype(BF16)
            d_key += dot(ds, q_head)
            d_query_t[h * HDIM : (h + 1) * HDIM, :] = (
                dot(k_t[h * HDIM : (h + 1) * HDIM, :], ds) * HDIM ** (-0.5)
            ).astype(BF16)
        d_key_value[:, tile] = d_key.astype(BF16)
        d_key_value[:, D + tile_at * 128 : D + tile_at * 128 + 128] = d_value.astype(BF16)
    put_image_rows(d_qkv, i, rows, slice(0, D), dot_t(query_back[0], d_query_t[...]))
    put_image_rows(d_qkv, i, rows, slice(D, 3 * D), dot(keys_back[0], d_key_value[...]))


def attend_back(qkv, d_mixed, probs, images):
    tokens = qkv.shape[0]
    tables = gather_tables(images)
    vm = pl.BlockSpec(memory_space=pltpu.VMEM)
    table = pl.BlockSpec((1, 256, 256), lambda i: (i, 0, 0))
    return pl.pallas_call(
        functools.partial(attend_back_kernel, tokens // 4),
        grid=(images,),
        out_shape=[
            jax.ShapeDtypeStruct((tokens, 3 * D), BF16),
            jax.ShapeDtypeStruct((HEADS, 2, KEYS, 128), F32),
        ],
        in_specs=[vm, vm, pl.BlockSpec((1, HEADS, 256, 256), lambda i: (i, 0, 0, 0))]
        + [table] * 4,
        out_specs=[
            pl.BlockSpec((tokens, 3 * D), lambda i: (0, 0)),
            pl.BlockSpec((HEADS, 2, KEYS, 128), lambda i: (0, 0, 0, 0)),
        ],
        scratch_shapes=[pltpu.VMEM((D, 256), BF16), pltpu.VMEM((256, 2 * D), BF16)],
        compiler_params=pltpu.CompilerParams(vmem_limit_bytes=VMEM_LIMIT),
        name="attend_back",
    )(qkv, d_mixed, probs, *tables)


def input_kernel(
    rows,
    slot_ref,
    d_qkv_ref,
    x_ref,
    d_res_ref,
    wqkv,
    vecs,
    out0,
    out1,
    out2,
    out3,
    g_qkv,
    g_vec,
    o_buf,
    sems,
):
    i = pl.program_id(0)
    slot = slot_ref[0]
    chunk = x_ref.shape[0]

    @pl.when(i == 0)
    def _():
        g_qkv[...] = jnp.zeros_like(g_qkv)
        g_vec[...] = jnp.zeros_like(g_vec)

    xhat, scale = norm_parts(x_ref[...].astype(F32))
    gain = vecs[0:1, :D]
    normed = (xhat * gain + vecs[1:2, :D]).astype(BF16)
    d_qkv = d_qkv_ref[...]
    d_normed = dot_t(d_qkv, wqkv[...])
    d_in = d_res_ref[...] + norm_back(d_normed, xhat, scale, gain)
    o_buf[pl.ds(pl.multiple_of(i * chunk, 16), chunk), :] = d_in.astype(BF16)
    g_qkv[...] += dot(normed.T, d_qkv)
    g_vec[0:1, :] += jnp.sum(d_qkv.astype(F32), axis=0, keepdims=True)
    g_vec[1:2, :D] += jnp.sum(d_normed * xhat, axis=0, keepdims=True)
    g_vec[2:3, :D] += jnp.sum(d_normed, axis=0, keepdims=True)

    @pl.when(i == pl.num_programs(0) - 1)
    def _():
        copies = split_copies(slot, (out0, out1, out2, out3), o_buf, sems, rows, True)
        for c in copies:
            c.start()
        for c in copies:
            c.wait()


def input_back(slot, d_qkv, x, d_res, wqkv, vecs):
    tokens = x.shape[0]
    rows = tokens // 4
    chunk = tokens // 7
    vm = pl.BlockSpec(memory_space=pltpu.VMEM)
    hbm = pl.BlockSpec(memory_space=pl.ANY)
    tile = lambda width: pl.BlockSpec((chunk, width), lambda i: (i, 0))
    return pl.pallas_call(
        functools.partial(input_kernel, rows),
        grid=(7,),
        out_shape=[jax.ShapeDtypeStruct((rows, D), BF16)] * 4
        + [jax.ShapeDtypeStruct((D, 3 * D), F32), jax.ShapeDtypeStruct((8, 3 * D), F32)],
        in_specs=[pl.BlockSpec(memory_space=pltpu.SMEM), tile(3 * D), tile(D), tile(D), vm, vm],
        out_specs=[hbm] * 4
        + [
            pl.BlockSpec((D, 3 * D), lambda i: (0, 0)),
            pl.BlockSpec((8, 3 * D), lambda i: (0, 0)),
        ],
        scratch_shapes=[pltpu.VMEM((tokens, D), BF16), pltpu.SemaphoreType.DMA((4,))],
        compiler_params=pltpu.CompilerParams(vmem_limit_bytes=VMEM_LIMIT),
        name="input_back",
    )(slot, d_qkv, x, d_res, wqkv, vecs)


def pack_kernel(
    flat,
    places,
    one_fine,
    one_coarse,
    g_bias,
    g_qkv,
    g_vec1,
    g_proj,
    g_w1,
    g_w2t,
    g_vec2,
    out,
    flat_a,
    flat_b,
    table,
    shifted,
    line,
):
    flat_a[...] = jnp.zeros_like(flat_a)
    flat_b[...] = jnp.zeros_like(flat_b)
    for j in range(9):
        flat_a[pl.ds(j, D, stride=9), :] = g_qkv[:, j * 128 : (j + 1) * 128]
    for j in range(3):
        flat_a[pl.ds(3456 + j, D, stride=3), :] = g_proj[:, j * 128 : (j + 1) * 128]
        flat_b[pl.ds(4608 + j, FF, stride=3), :] = g_w2t[j * 128 : (j + 1) * 128, :].T
    for j in range(12):
        flat_b[pl.ds(j, D, stride=12), :] = g_w1[:, j * 128 : (j + 1) * 128]
        flat_b[9216 + j : 9217 + j, :] = g_vec2[0:1, j * 128 : (j + 1) * 128]
    for v in range(3):
        for j in range(3):
            at = 9228 + 3 * v + j
            flat_b[at : at + 1, :] = g_vec2[1 + v : 2 + v, j * 128 : (j + 1) * 128]
    vectors = [
        g_vec1[1:2, :D],
        g_vec1[2:3, :D],
        g_vec1[0:1, :D],
        g_vec1[0:1, 2 * D :],
        g_vec2[4:5, :D],
    ]
    pieces = [v[:, j * 128 : (j + 1) * 128] for v in vectors for j in range(3)]
    pieces += [jnp.zeros((1, 128), F32)]
    row, lane = divmod(ATTN_VECTORS[0], 128)
    flat_a[row : row + 16, :] += shift_lanes(jnp.concatenate(pieces, axis=0), lane, True)
    for h in range(HEADS):
        table[...] = jnp.zeros_like(table)
        for half in range(2):
            turned = g_bias[h, half].T
            for y in range(WIN):
                for at, length, source in bias_runs(half, WIN * half + y):
                    table[0:14, source : source + length] += turned[
                        y * 14 : y * 14 + 14, at : at + length
                    ]
        for c in range(4):
            shifted[c, pl.ds(h, 14, stride=16), :] = table[0:14, c * 128 : (c + 1) * 128]
    g_fine = jnp.zeros((16, 384), F32)
    g_coarse = jnp.zeros((16, 256), F32)
    for qx in range(14):
        at = slice(qx * 16, qx * 16 + 16)
        part = jnp.concatenate([shifted[c, at, :] for c in range(4)], axis=1)
        high = part.astype(BF16)
        low = (part - high.astype(F32)).astype(BF16)
        g_fine += dot_t(high[:, :384], one_fine[qx]) + dot_t(low[:, :384], one_fine[qx])
        g_coarse += dot_t(high[:, 384:], one_coarse[qx]) + dot_t(low[:, 384:], one_coarse[qx])
    for value, first, length in (
        (g_fine, TABLE_AT, FINE),
        (g_coarse, TABLE_AT + HEADS * FINE, COARSE),
    ):
        for h in range(HEADS):
            row, lane = divmod(first + h * length, 128)
            count = -(-(lane + length) // 128)
            line[...] = jnp.zeros_like(line)
            line[0:1, lane : lane + length] = value[h : h + 1, :length]
            for c in range(count):
                flat_a[row + c : row + c + 1, :] += line[0:1, c * 128 : (c + 1) * 128]
    for device, place in enumerate(places):
        a_at, b_at = flat.start(0, device), flat.start(1, device)
        out[place] = jnp.concatenate(
            [
                flat_a[a_at : a_at + flat.rows[0], :],
                flat_b[b_at : b_at + flat.rows[1], :],
            ],
            axis=0,
        ).astype(BF16)


def pack(flat, places, g_bias, g_qkv, g_vec1, g_proj, g_w1, g_w2t, g_vec2):
    fine, coarse, _ = bias_tables()
    vm = pl.BlockSpec(memory_space=pltpu.VMEM)
    return pl.pallas_call(
        functools.partial(pack_kernel, flat, places),
        out_shape=jax.ShapeDtypeStruct((flat.devices, flat.total, 128), BF16),
        in_specs=[vm] * 9,
        out_specs=vm,
        scratch_shapes=[
            pltpu.VMEM((flat.buffer[0], 128), F32),
            pltpu.VMEM((flat.buffer[1], 128), F32),
            pltpu.VMEM((16, 512), F32),
            pltpu.VMEM((4, 14 * 16, 128), F32),
            pltpu.VMEM((8, 512), F32),
        ],
        compiler_params=pltpu.CompilerParams(vmem_limit_bytes=VMEM_LIMIT),
        name="pack",
    )(
        jnp.asarray(fine),
        jnp.asarray(coarse),
        g_bias,
        g_qkv,
        g_vec1,
        g_proj,
        g_w1,
        g_w2t,
        g_vec2,
    )


def join_kernel(rows, slot_ref, in0, in1, in2, in3, out):
    for k, ref in enumerate((in0, in1, in2, in3)):
        at = pl.multiple_of(xor_slot(slot_ref[0], k) * rows, 16)
        out[pl.ds(at, rows), :] = ref[...].astype(out.dtype)


def join(slot, parts, dtype):
    rows = parts[0].shape[0]
    vm = pl.BlockSpec(memory_space=pltpu.VMEM)
    return pl.pallas_call(
        functools.partial(join_kernel, rows),
        out_shape=jax.ShapeDtypeStruct((4 * rows, D), dtype),
        in_specs=[pl.BlockSpec(memory_space=pltpu.SMEM)] + [vm] * 4,
        out_specs=vm,
        compiler_params=pltpu.CompilerParams(vmem_limit_bytes=VMEM_LIMIT),
        name="join",
    )(slot, *parts)


def adamw(master, first, second, grads):
    first_new = beta_one * first + (1.0 - beta_one) * grads
    second_new = beta_two * second + (1.0 - beta_two) * grads * grads
    first_hat = first_new / (1.0 - beta_one**STEP)
    second_hat = second_new / (1.0 - beta_two**STEP)
    master_new = master - learn_rate * (
        first_hat / (jnp.sqrt(second_hat) + adam_eps) + decay_rate * master
    )
    return (first_new, second_new, master_new)


def swap(value, k):
    pairs = [(s, s ^ k) for s in range(lax.axis_size("dp"))]
    return lax.ppermute(value, "dp", pairs)


def body(
    tokens, cotangent, attn_master, attn_first, attn_second, mlp_master, mlp_first, mlp_second
):
    n_dp, n_grp = lax.axis_size("dp"), lax.axis_size("grp")
    order = bit_order(n_dp, n_grp)
    places = place_list(order, n_dp, n_grp)
    flat = Flat(n_dp * n_grp, attn_master.shape[0], mlp_master.shape[0])
    slot = lax.rem(lax.axis_index("dp"), 4).astype(jnp.int32)
    slot_arr = slot.reshape(1)
    token_count = tokens.shape[1]
    rows = token_count // 4
    images = rows // SEQ

    gathered, x = gather_params(flat, order, attn_master, mlp_master, tokens[0])
    wqkv, wproj, w1, w2, vecs, bias = prepare(flat, places, gathered)
    mixed, probs, qkv, cot = attend(x, cotangent[0], wqkv, vecs, bias, images)
    mlp_out = mlp(slot_arr, cot, mixed, x, wproj, w1, w2, vecs)
    out_parts, (d_res, d_mixed, g_w1, g_w2t, g_proj, g_vec2) = mlp_out[:4], mlp_out[4:]
    out_parts = [out_parts[0]] + [swap(out_parts[k], k) for k in (1, 2, 3)]
    d_qkv, g_bias = attend_back(qkv, d_mixed, probs, images)
    back = input_back(slot_arr, d_qkv, x, d_res, wqkv, vecs)
    in_parts, (g_qkv, g_vec1) = back[:4], back[4:]
    in_parts = [in_parts[0]] + [swap(in_parts[k], k) for k in (1, 2, 3)]
    blocks = pack(flat, places, g_bias, g_qkv, g_vec1, g_proj, g_w1, g_w2t, g_vec2)
    grad_a, grad_b = sum_grads(flat, order, blocks)
    attn_new = adamw(attn_master, attn_first, attn_second, grad_a)
    mlp_new = adamw(mlp_master, mlp_first, mlp_second, grad_b)
    output = join(slot_arr, out_parts, BF16)
    input_grad = join(slot_arr, in_parts, F32)
    return (output[None], input_grad[None], *attn_new, *mlp_new)


def solution(mesh):
    flat_spec = P(("dp", "grp"))
    token_spec = P("dp", "grp", None)
    placed = (token_spec, token_spec) + (flat_spec,) * 6
    return jax.shard_map(
        body, mesh=mesh, in_specs=placed, out_specs=placed, check_vma=False
    )
```

```python
import functools

import jax
import jax.numpy as jnp
import ml_dtypes
import numpy as np
from jax import lax
from jax.experimental import pallas as pl
from jax.experimental.pallas import tpu as pltpu
from jax.sharding import PartitionSpec as P

D = 384
HEADS = 12
HDIM = 32
FF = 1536
WIN = 7
STEP = 10
SEQ = WIN * WIN
HALF = 64
FINE = (3 * WIN - 2) ** 2
COARSE = (2 * WIN - 1) ** 2
KEYS = 192

beta_one = 0.9
beta_two = 0.999
learn_rate = 0.04
decay_rate = 0.05
adam_eps = 1e-08
norm_eps = 1e-05
masked_score = -1e30

F32 = jnp.float32
BF16 = jnp.bfloat16
MESH = pl.DeviceIdType.MESH
VMEM_LIMIT = 56 * 2**20


def token_place(gy, gx):
    window = 2 * (gy // WIN) + gx // WIN
    return window * HALF + (gy % WIN) * WIN + gx % WIN


@functools.cache
def gather_tables(images):
    keys = np.zeros((images, 256, 256), np.float32)
    queries = np.zeros((images, 256, 256), np.float32)
    for i in range(images):
        for gy in range(2 * WIN):
            for gx in range(2 * WIN):
                at = token_place(gy, gx) + i
                key = gy * 14 + gx if gy < 10 else 192 + (gy - 10) * 14 + gx
                keys[i, key, at] = 1.0
                keys[i, 140 + (gy // 2) * WIN + gx // 2, at] = 0.25
                queries[i, (gy // WIN) * 128 + (gy % WIN) * 14 + gx, at] = 1.0
    return (
        keys.astype(ml_dtypes.bfloat16),
        queries.astype(ml_dtypes.bfloat16),
        np.ascontiguousarray(keys.transpose(0, 2, 1)).astype(ml_dtypes.bfloat16),
        np.ascontiguousarray(queries.transpose(0, 2, 1)).astype(ml_dtypes.bfloat16),
    )


@functools.cache
def bias_tables():
    fine = np.zeros((14, 384, 384), np.float32)
    coarse = np.zeros((14, 256, 128), np.float32)
    for qx in range(14):
        for a in range(27):
            for kx in range(14):
                col = kx - qx + 9
                if 4 <= a <= 22 and 0 <= col <= 18:
                    fine[qx, 19 * (a - 4) + col, a * 14 + kx] = 1.0
        for p in range(13):
            for s in range(WIN):
                coarse[qx, 13 * p + s - qx // 2 + 6, p * WIN + s] = 1.0
    mask = np.zeros((2, KEYS, 128), np.float32)
    for half in range(2):
        for q in range(98):
            qx = q % 14
            for e in range(KEYS):
                at = e + 56 * half
                if at < 140:
                    ok = abs_ok(qx, at % 14)
                elif at < 189:
                    ok = True
                elif at < 192:
                    ok = False
                else:
                    ok = at < 248 and abs_ok(qx, (at - 192) % 14)
                mask[half, e, q] = 0.0 if ok else masked_score
    return fine.astype(ml_dtypes.bfloat16), coarse.astype(ml_dtypes.bfloat16), mask


def abs_ok(qx, kx):
    return kx < 10 if qx < WIN else kx >= 4


def bias_runs(half, qy):
    fine = (13 - qy) * 14
    pool = 384 + (6 - qy // 2) * WIN
    if half == 0:
        return [(0, 140, fine), (140, 49, pool)]
    return [(0, 84, fine + 56), (84, 49, pool), (136, 56, fine + 140)]


class Part:
    def __init__(self, devices, length):
        self.devices = devices
        self.length = length
        self.rows = -(-((length + 126) // 128 + 1) // 16) * 16
        self.buffer = -(-(self.start(devices - 1) + self.rows) // 8) * 8

    def start(self, device):
        return device * self.length // 128

    def lane(self, device):
        return lax.rem(device * self.length, 128)

    def padded(self, vector):
        extra = self.rows * 128 - self.length
        return jnp.pad(vector, (0, extra)).reshape(self.rows, 128)


def bit_order(n_dp, n_grp):
    dp_bits = [("dp", 2**b) for b in range(n_dp.bit_length() - 1)]
    grp_bits = [("grp", 2**b) for b in reversed(range(n_grp.bit_length() - 1))]
    return dp_bits[1:2] + grp_bits + dp_bits[2:] + dp_bits[:1]


def place_of(order, dp, grp):
    place = 0
    for k, (axis, stride) in enumerate(order):
        place = place + ((dp if axis == "dp" else grp) // stride) % 2 * 2**k
    return place


def partner_of(axis, stride, dp, grp):
    if axis == "dp":
        return (dp + (1 - 2 * ((dp // stride) % 2)) * stride, grp)
    return (dp, grp + (1 - 2 * ((grp // stride) % 2)) * stride)


def greet(partners):
    barrier = pltpu.get_barrier_semaphore()
    for partner in partners:
        pl.semaphore_signal(barrier, inc=1, device_id=partner, device_id_type=MESH)
    pl.semaphore_wait(barrier, len(partners))


def cube_partners(order, dp, grp):
    return [partner_of(axis, stride, dp, grp) for axis, stride in order]


def shift_lanes(values, amount, up):
    lane = lax.broadcasted_iota(jnp.int32, values.shape, 1)
    if up:
        turned = pltpu.roll(values, amount, 1)
        return jnp.where(lane >= amount, turned, pltpu.roll(turned, 1, 0))
    turned = pltpu.roll(values, lax.rem(128 - amount, 128), 1)
    return jnp.where(lane < 128 - amount, turned, pltpu.roll(turned, values.shape[0] - 1, 0))


def window_partner(dp, grp, k):
    low, high = dp % 2, dp // 2 % 2
    to = dp
    if k % 2:
        to = to + 1 - 2 * low
    if k // 2:
        to = to + 2 * (1 - 2 * high)
    return (to, grp)


def exchange_copies(source, target, dp, grp, own_sem, send_sems, recv_sems):
    rows = source.shape[0] // 4
    slot = dp % 4
    mine = pl.ds(pl.multiple_of(slot * rows, 16), rows)
    own = pltpu.make_async_copy(source.at[mine], target.at[mine], own_sem)
    sends = []
    for k in (3, 2, 1):
        to, _ = window_partner(dp, grp, k)
        theirs = pl.ds(pl.multiple_of(to % 4 * rows, 16), rows)
        sends.append(
            pltpu.make_async_remote_copy(
                src_ref=source.at[theirs],
                dst_ref=target.at[mine],
                send_sem=send_sems.at[k - 1],
                recv_sem=recv_sems.at[k - 1],
                device_id=(to, grp),
                device_id_type=MESH,
            )
        )
    return [own] + sends


def cube_copy(order, k, source, target, dp, grp, send_sems, recv_sems):
    axis, stride = order[k]
    return pltpu.make_async_remote_copy(
        src_ref=source,
        dst_ref=target,
        send_sem=send_sems.at[k],
        recv_sem=recv_sems.at[k],
        device_id=partner_of(axis, stride, dp, grp),
        device_id_type=MESH,
    )


def gather_copy(order, k, blocks, dp, grp, sems):
    place = place_of(order, dp, grp)
    held = blocks.at[pl.ds(place // 2**k * 2**k, 2**k)]
    return cube_copy(order, k, held, held, dp, grp, *sems)


def own_block(part, master_ref, own):
    device = lax.axis_index("dp") * lax.axis_size("grp") + lax.axis_index("grp")
    own[...] = shift_lanes(master_ref[...], part.lane(device), True).astype(BF16)


class CubeSum:
    def __init__(self, order, blocks, total, outgoing, arrived, sems):
        self.order, self.blocks, self.total = order, blocks, total
        self.outgoing, self.arrived, self.sems = outgoing, arrived, sems
        self.dp, self.grp = lax.axis_index("dp"), lax.axis_index("grp")
        self.place = place_of(order, self.dp, self.grp)
        self.last = len(order) - 1

    def mine(self, k):
        return self.place // 2**k % 2 * 2**k

    def copy(self, k):
        size = 2**k
        if k == self.last:
            source = self.blocks.at[pl.ds(size - self.mine(k), size)]
        else:
            source = self.outgoing.at[pl.ds(size, size)]
        target = self.arrived.at[pl.ds(size, size)]
        return cube_copy(self.order, k, source, target, self.dp, self.grp, *self.sems)

    def start(self, k):
        size = 2**k
        if k < self.last:
            other = size - self.mine(k)

            def fill(j, carry):
                self.outgoing[size + j] = self.total[other + j].astype(BF16)
                return carry

            lax.fori_loop(0, size, fill, 0)
        self.copy(k).start()

    def finish(self, k):
        size, mine = 2**k, self.mine(k)
        self.copy(k).wait()

        def add(j, carry):
            if k == self.last:
                held = self.blocks[mine + j].astype(F32)
            else:
                held = self.total[mine + j]
            self.total[j] = held + self.arrived[size + j].astype(F32)
            return carry

        lax.fori_loop(0, size, add, 0)

    @staticmethod
    def scratch(devices, rows, stages):
        return [
            pltpu.VMEM((devices // 2, rows, 128), F32),
            pltpu.VMEM((devices // 2, rows, 128), BF16),
            pltpu.VMEM((devices, rows, 128), BF16),
            pltpu.SemaphoreType.DMA((stages,)),
            pltpu.SemaphoreType.DMA((stages,)),
        ]


def gather_kernel(
    part, order, a_ref, tok_ref, out_ref, x_ref, own, own_sem, send, recv, x_sem, x_send, x_recv
):
    dp, grp = lax.axis_index("dp"), lax.axis_index("grp")
    own_block(part, a_ref, own)
    copy = pltpu.make_async_copy(own, out_ref.at[place_of(order, dp, grp)], own_sem)
    copy.start()
    greet(cube_partners(order, dp, grp) + [window_partner(dp, grp, 3)])
    copy.wait()
    exchange = exchange_copies(tok_ref, x_ref, dp, grp, x_sem, x_send, x_recv)
    for k in range(len(order)):
        stage = gather_copy(order, k, out_ref, dp, grp, (send, recv))
        stage.start()
        if k == 0:
            for c in exchange:
                c.start()
        stage.wait()
    for c in exchange:
        c.wait()


def gather_params(part, order, master, tok):
    stages = len(order)
    return pl.pallas_call(
        functools.partial(gather_kernel, part, order),
        out_shape=[
            jax.ShapeDtypeStruct((part.devices, part.rows, 128), BF16),
            jax.ShapeDtypeStruct(tok.shape, BF16),
        ],
        in_specs=[
            pl.BlockSpec(memory_space=pltpu.VMEM),
            pl.BlockSpec(memory_space=pl.ANY),
        ],
        out_specs=[pl.BlockSpec(memory_space=pl.ANY)] * 2,
        scratch_shapes=[
            pltpu.VMEM((part.rows, 128), BF16),
            pltpu.SemaphoreType.DMA,
            pltpu.SemaphoreType.DMA((stages,)),
            pltpu.SemaphoreType.DMA((stages,)),
            pltpu.SemaphoreType.DMA,
            pltpu.SemaphoreType.DMA((3,)),
            pltpu.SemaphoreType.DMA((3,)),
        ],
        compiler_params=pltpu.CompilerParams(
            collective_id=0, has_side_effects=True, vmem_limit_bytes=VMEM_LIMIT
        ),
        name="gather_params",
    )(part.padded(master), tok)


def chunk_copies(source, target, first, size, dp, grp, own_sem, send_sems, recv_sems, skip):
    slot = dp % 4
    into = target.at[slot, pl.ds(first, size)]
    rows = pl.ds(first - skip, size)
    copies = [pltpu.make_async_copy(source.at[slot, rows], into, own_sem)]
    for k in (3, 2, 1):
        to, _ = window_partner(dp, grp, k)
        copies.append(
            pltpu.make_async_remote_copy(
                src_ref=source.at[to % 4, rows],
                dst_ref=into,
                send_sem=send_sems.at[k - 1],
                recv_sem=recv_sems.at[k - 1],
                device_id=(to, grp),
                device_id_type=MESH,
            )
        )
    return copies


def sum_kernel(
    part,
    order,
    blocks,
    last_ref,
    dx_ref,
    grad_ref,
    dx_out,
    total,
    outgoing,
    arrived,
    send,
    recv,
    x_sem,
    x_send,
    x_recv,
):
    dp, grp = lax.axis_index("dp"), lax.axis_index("grp")
    greet(cube_partners(order, dp, grp) + [window_partner(dp, grp, 3)])
    cube = CubeSum(order, blocks, total, outgoing, arrived, (send, recv))
    first = dx_ref.shape[1] - last_ref.shape[1]
    exchange = chunk_copies(
        last_ref, dx_out, first, last_ref.shape[1], dp, grp, x_sem, x_send, x_recv, first
    )
    for k in reversed(range(len(order))):
        cube.start(k)
        if k == len(order) - 1:
            for c in exchange:
                c.start()
        cube.finish(k)
    device = dp * lax.axis_size("grp") + grp
    grad_ref[...] = shift_lanes(total[0], part.lane(device), False)
    for c in exchange:
        c.wait()


def sum_grads(part, order, blocks, last, dx):
    stages = len(order)
    hbm = pl.BlockSpec(memory_space=pl.ANY)
    vm = pl.BlockSpec(memory_space=pltpu.VMEM)
    grad, dx = pl.pallas_call(
        functools.partial(sum_kernel, part, order),
        out_shape=[
            jax.ShapeDtypeStruct((part.rows, 128), F32),
            jax.ShapeDtypeStruct(dx.shape, dx.dtype),
        ],
        in_specs=[vm, hbm, hbm],
        out_specs=[vm, hbm],
        input_output_aliases={2: 1},
        scratch_shapes=CubeSum.scratch(part.devices, part.rows, stages)
        + [
            pltpu.SemaphoreType.DMA,
            pltpu.SemaphoreType.DMA((3,)),
            pltpu.SemaphoreType.DMA((3,)),
        ],
        compiler_params=pltpu.CompilerParams(
            collective_id=1, has_side_effects=True, vmem_limit_bytes=VMEM_LIMIT
        ),
        name="sum_grads",
    )(blocks, last, dx)
    return grad.reshape(-1)[: part.length], dx


def place_list(order, n_dp, n_grp):
    return [place_of(order, d // n_grp, d % n_grp) for d in range(n_dp * n_grp)]


ATTN_VECTORS = (D * 3 * D + D * D + HEADS * FINE + HEADS * COARSE, 5)
TABLE_AT = D * 3 * D + D * D


def unflatten(part, places, blocks, flat):
    flat[...] = jnp.zeros_like(flat)
    for device, place in enumerate(places):
        at = part.start(device)
        flat[at : at + part.rows, :] += blocks[place].astype(F32)


def take_matrix(flat, first, target):
    rows, columns = target.shape
    count = columns // 128
    for j in range(count):
        target[:, j * 128 : (j + 1) * 128] = flat[pl.ds(first + j, rows, stride=count), :].astype(
            target.dtype
        )


def put_matrix(flat, first, source):
    rows, columns = source.shape
    count = columns // 128
    for j in range(count):
        flat[pl.ds(first + j, rows, stride=count), :] = source[:, j * 128 : (j + 1) * 128]


TABLES = ((TABLE_AT, FINE), (TABLE_AT + HEADS * FINE, COARSE))


def table_lines():
    for t, (first, length) in enumerate(TABLES):
        for h in range(HEADS):
            row, lane = divmod(first + h * length, 128)
            yield t, h, length, row, lane, -(-(lane + length) // 128)


def prep_kernel(
    part,
    places,
    blocks,
    one_fine,
    one_coarse,
    mask_ref,
    wqkv,
    wproj,
    vecs,
    bias,
    flat,
    tab_fine,
    tab_coarse,
    shifted,
    turned,
):
    unflatten(part, places, blocks, flat)
    take_matrix(flat, 0, wqkv)
    take_matrix(flat, 3456, wproj)
    vecs[...] = jnp.zeros_like(vecs)
    row, lane = divmod(ATTN_VECTORS[0], 128)
    rows = shift_lanes(flat[row : row + 16, :], lane, False)
    for v in range(5):
        for j in range(3):
            vecs[v : v + 1, j * 128 : (j + 1) * 128] = rows[3 * v + j : 3 * v + j + 1]
    tab_fine[...] = jnp.zeros_like(tab_fine)
    tab_coarse[...] = jnp.zeros_like(tab_coarse)
    for t, h, length, row, lane, count in table_lines():
        line = jnp.concatenate([flat[row + c : row + c + 1, :] for c in range(count)], axis=1)
        (tab_fine, tab_coarse)[t][h : h + 1, 0:length] = line[:, lane : lane + length]
    for qx in range(14):
        at = slice(qx * 16, qx * 16 + 16)
        moved = dot(tab_fine[...].astype(BF16), one_fine[qx])
        for c in range(3):
            shifted[c, at, :] = moved[:, c * 128 : (c + 1) * 128]
        shifted[3, at, :] = dot(tab_coarse[...].astype(BF16), one_coarse[qx])
    turned[...] = jnp.zeros_like(turned)
    for h in range(HEADS):
        table = jnp.concatenate(
            [shifted[c, pl.ds(h, 14, stride=16), :] for c in range(4)], axis=1
        )
        for half in range(2):
            for y in range(WIN):
                for at, length, source in bias_runs(half, WIN * half + y):
                    turned[half, y * 14 : y * 14 + 14, at : at + length] = table[
                        :, source : source + length
                    ]
            bias[h, half] = turned[half].T[0:KEYS] + mask_ref[half]


def prepare(part, places, blocks):
    fine, coarse, mask = bias_tables()
    vm = pl.BlockSpec(memory_space=pltpu.VMEM)
    return pl.pallas_call(
        functools.partial(prep_kernel, part, places),
        out_shape=[
            jax.ShapeDtypeStruct((D, 3 * D), BF16),
            jax.ShapeDtypeStruct((D, D), BF16),
            jax.ShapeDtypeStruct((8, D), F32),
            jax.ShapeDtypeStruct((HEADS, 2, KEYS, 128), F32),
        ],
        in_specs=[vm] * 4,
        out_specs=[vm] * 4,
        scratch_shapes=[
            pltpu.VMEM((part.buffer, 128), F32),
            pltpu.VMEM((16, 384), F32),
            pltpu.VMEM((16, 256), F32),
            pltpu.VMEM((4, 14 * 16, 128), F32),
            pltpu.VMEM((2, 128, 256), F32),
        ],
        compiler_params=pltpu.CompilerParams(vmem_limit_bytes=VMEM_LIMIT),
        name="prepare",
    )(blocks, jnp.asarray(fine), jnp.asarray(coarse), jnp.asarray(mask))


def prep_mlp_kernel(part, places, blocks, w1, w2, vecs, flat):
    unflatten(part, places, blocks, flat)
    take_matrix(flat, 0, w1)
    take_matrix(flat, 4608, w2)
    vecs[...] = jnp.zeros_like(vecs)
    for j in range(12):
        vecs[0:1, j * 128 : (j + 1) * 128] = flat[9216 + j : 9217 + j, :]
    for v in range(3):
        for j in range(3):
            at = 9228 + 3 * v + j
            vecs[1 + v : 2 + v, j * 128 : (j + 1) * 128] = flat[at : at + 1, :]


def prepare_mlp(part, places, blocks):
    vm = pl.BlockSpec(memory_space=pltpu.VMEM)
    return pl.pallas_call(
        functools.partial(prep_mlp_kernel, part, places),
        out_shape=[
            jax.ShapeDtypeStruct((D, FF), BF16),
            jax.ShapeDtypeStruct((FF, D), BF16),
            jax.ShapeDtypeStruct((8, FF), F32),
        ],
        in_specs=[vm],
        out_specs=[vm] * 3,
        scratch_shapes=[pltpu.VMEM((part.buffer, 128), F32)],
        compiler_params=pltpu.CompilerParams(vmem_limit_bytes=VMEM_LIMIT),
        name="prepare_mlp",
    )(blocks)


def dot(a, b):
    return jnp.dot(a, b, preferred_element_type=F32)


def dot_t(a, b):
    return lax.dot_general(a, b, (((1,), (1,)), ((), ())), preferred_element_type=F32)


def norm_parts(values):
    centered = values - jnp.mean(values, axis=-1, keepdims=True)
    scale = lax.rsqrt(jnp.mean(centered * centered, axis=-1, keepdims=True) + norm_eps)
    return centered * scale, scale


def norm_back(d_normed, xhat, scale, gain):
    dh = d_normed * gain
    return scale * (
        dh
        - jnp.mean(dh, axis=-1, keepdims=True)
        - xhat * jnp.mean(dh * xhat, axis=-1, keepdims=True)
    )


def lane_heads(j):
    lane = lax.broadcasted_iota(jnp.int32, (256, 128), 1)
    return (lane // HDIM) == j


def image_rows(ref, i, columns):
    at = pl.ds(pl.multiple_of(48 * i, 16), HALF)
    return jnp.concatenate([ref[w, at, columns] for w in range(4)], axis=0)


def put_image_rows(ref, i, columns, values):
    for w in range(4):
        part = values[w * HALF : (w + 1) * HALF]
        first = pl.ds(pl.multiple_of(48 * i, 16), 16)
        rest = pl.ds(pl.multiple_of(48 * i + 16, 16), HALF - 16)
        held = jnp.where(i > 0, ref[w, first, columns].astype(F32), 0.0)
        ref[w, first, columns] = (held + part[:16]).astype(ref.dtype)
        ref[w, rest, columns] = part[16:].astype(ref.dtype)


def spread(halves):
    columns = []
    for half, values in enumerate(halves):
        pieces = [values, jnp.zeros((64 - 56 * half, 128), F32)]
        if half:
            pieces = [jnp.zeros((56, 128), F32)] + pieces
        columns.append(jnp.concatenate(pieces, axis=0))
    return jnp.concatenate(columns, axis=1).astype(BF16)


def half_of(values, half):
    return values[56 * half : 56 * half + KEYS, 128 * half : 128 * half + 128]


def tile_of(h):
    return slice(h // 4 * 128, h // 4 * 128 + 128)


def attend_kernel(
    rows,
    part,
    order,
    x_buf,
    cot_ref,
    master_ref,
    wqkv,
    vecs,
    bias,
    keys_tab,
    query_tab,
    query_back,
    mixed,
    probs,
    ext,
    inverse,
    cot_out,
    blocks,
    normed,
    qkv,
    mixed_t,
    own,
    own_sem,
    send,
    recv,
    cot_sem,
    cot_send,
    cot_recv,
):
    i = pl.program_id(0)
    steps = pl.num_programs(0)
    dp, grp = lax.axis_index("dp"), lax.axis_index("grp")
    exchange = exchange_copies(cot_ref, cot_out, dp, grp, cot_sem, cot_send, cot_recv)
    stages = len(order)

    @pl.when(i == 0)
    def _():
        own_block(part, master_ref, own)
        copy = pltpu.make_async_copy(own, blocks.at[place_of(order, dp, grp)], own_sem)
        copy.start()
        greet(cube_partners(order, dp, grp) + [window_partner(dp, grp, 3)])
        copy.wait()

    for k in range(stages):

        @pl.when(i == k * steps // stages)
        def _(k=k):
            if k:
                gather_copy(order, k - 1, blocks, dp, grp, (send, recv)).wait()
            gather_copy(order, k, blocks, dp, grp, (send, recv)).start()

    @pl.when(i == 0)
    def _():
        for c in exchange:
            c.start()

        def project(w, carry):
            step = rows // 7

            def norm(c, inner):
                at = pl.multiple_of(c * step, 16)
                xhat, _ = norm_parts(x_buf[w, pl.ds(at, step), :].astype(F32))
                normed[pl.ds(at, step), :] = (xhat * vecs[0:1, :D] + vecs[1:2, :D]).astype(BF16)
                return inner

            lax.fori_loop(0, 7, norm, 0)
            q = dot(normed[...], wqkv[:, :D]) + vecs[2:3, :D]
            qkv[w, :, :D] = (q * HDIM ** (-0.5)).astype(BF16)
            qkv[w, :, D : 2 * D] = dot(normed[...], wqkv[:, D : 2 * D]).astype(BF16)
            v = dot(normed[...], wqkv[:, 2 * D :]) + vecs[3:4, :D]
            qkv[w, :, 2 * D :] = v.astype(BF16)
            return carry

        lax.fori_loop(0, 4, project, 0)

    q_ext = dot(query_tab[0], image_rows(qkv, i, slice(0, D))).astype(BF16)
    kv_ext = dot(keys_tab[0], image_rows(qkv, i, slice(D, 3 * D)))
    k_ext = kv_ext[:, :D].astype(BF16)
    v_ext = kv_ext[:, D:]
    v_t = v_ext.T.astype(BF16)
    ext[0, :, :D] = q_ext
    ext[0, :, D : 2 * D] = k_ext
    ext[0, :, 2 * D :] = v_ext.astype(BF16)

    def scores_of(h):
        q_head = jnp.where(lane_heads(h % 4), q_ext[:, tile_of(h)], 0)
        return dot_t(k_ext[:, tile_of(h)], q_head)

    inverse[0, HEADS:16, :] = jnp.zeros((16 - HEADS, 256), F32)
    scores = scores_of(0)
    for h in range(HEADS):
        ahead = scores_of(h + 1) if h + 1 < HEADS else None
        halves, inverses = [], []
        for half in range(2):
            s = half_of(scores, half) + bias[h, half]
            e = jnp.exp(s - jnp.max(s, axis=0, keepdims=True))
            inverses.append(1.0 / jnp.sum(e, axis=0, keepdims=True))
            halves.append(e)
        e = spread(halves)
        inv = jnp.concatenate(inverses, axis=1)
        probs[0, h] = e
        inverse[0, h : h + 1, :] = inv
        mixed_t[h * HDIM : (h + 1) * HDIM, :] = (
            dot(v_t[h * HDIM : (h + 1) * HDIM, :], e) * inv
        ).astype(BF16)
        scores = ahead
    put_image_rows(mixed, i, slice(0, D), dot_t(query_back[0], mixed_t[...]))

    @pl.when(i == steps - 1)
    def _():
        gather_copy(order, stages - 1, blocks, dp, grp, (send, recv)).wait()
        for c in exchange:
            c.wait()


def attend(part, order, x, cot, master, wqkv, vecs, bias, images):
    tokens = x.shape[0]
    stages = len(order)
    rows = tokens // 4
    keys_tab, query_tab, _, query_back = gather_tables(images)
    vm = pl.BlockSpec(memory_space=pltpu.VMEM)
    hbm = pl.BlockSpec(memory_space=pl.ANY)
    table = pl.BlockSpec((1, 256, 256), lambda i: (i, 0, 0))
    return pl.pallas_call(
        functools.partial(attend_kernel, rows, part, order),
        grid=(images,),
        out_shape=[
            jax.ShapeDtypeStruct((4, rows, D), BF16),
            jax.ShapeDtypeStruct((images, HEADS, 256, 256), BF16),
            jax.ShapeDtypeStruct((images, 256, 3 * D), BF16),
            jax.ShapeDtypeStruct((images, 16, 256), F32),
            jax.ShapeDtypeStruct((tokens, D), BF16),
            jax.ShapeDtypeStruct((part.devices, part.rows, 128), BF16),
        ],
        in_specs=[vm, hbm] + [vm] * 4 + [table] * 3,
        out_specs=[
            pl.BlockSpec((4, rows, D), lambda i: (0, 0, 0)),
            pl.BlockSpec((1, HEADS, 256, 256), lambda i: (i, 0, 0, 0)),
            pl.BlockSpec((1, 256, 3 * D), lambda i: (i, 0, 0)),
            pl.BlockSpec((1, 16, 256), lambda i: (i, 0, 0)),
            hbm,
            hbm,
        ],
        scratch_shapes=[
            pltpu.VMEM((rows, D), BF16),
            pltpu.VMEM((4, rows, 3 * D), BF16),
            pltpu.VMEM((D, 256), BF16),
            pltpu.VMEM((part.rows, 128), BF16),
            pltpu.SemaphoreType.DMA,
            pltpu.SemaphoreType.DMA((stages,)),
            pltpu.SemaphoreType.DMA((stages,)),
            pltpu.SemaphoreType.DMA,
            pltpu.SemaphoreType.DMA((3,)),
            pltpu.SemaphoreType.DMA((3,)),
        ],
        compiler_params=pltpu.CompilerParams(
            collective_id=2, has_side_effects=True, vmem_limit_bytes=VMEM_LIMIT
        ),
        name="attend",
    )(
        x.reshape(4, rows, D),
        cot,
        part.padded(master),
        wqkv,
        vecs,
        bias,
        keys_tab,
        query_tab,
        query_back,
    )


GELU_A = float(np.sqrt(2.0 / np.pi))
GELU_B = 0.044715


def mlp_kernel(
    cot_ref,
    mixed_ref,
    x_ref,
    wproj,
    w1,
    w2,
    vecs_a,
    vecs,
    out_ref,
    d_res_ref,
    d_mixed_ref,
    g_w1,
    g_w2t,
    g_proj,
    g_vec,
):
    i = pl.program_id(0)
    chunk = mixed_ref.shape[0]

    @pl.when(i == 0)
    def _():
        g_w1[...] = jnp.zeros_like(g_w1)
        g_w2t[...] = jnp.zeros_like(g_w2t)
        g_proj[...] = jnp.zeros_like(g_proj)
        g_vec[...] = jnp.zeros_like(g_vec)

    mix = mixed_ref[...]
    res = x_ref[...].astype(F32) + dot(mix, wproj[...]) + vecs_a[4:5, :]
    xhat, scale = norm_parts(res)
    gain = vecs[1:2, :D]
    normed = (xhat * gain + vecs[2:3, :D]).astype(BF16)
    grad = cot_ref[...]
    grad_t = grad.T
    normed_t = normed.T
    out = res + vecs[3:4, :D]
    d_normed = jnp.zeros((chunk, D), F32)
    for f in range(3):
        cols = slice(f * 512, f * 512 + 512)
        hidden = dot(normed, w1[:, cols]) + vecs[0:1, cols]
        square = hidden * hidden
        t = jnp.tanh(hidden * (GELU_A + (GELU_A * GELU_B) * square))
        half = 0.5 + 0.5 * t
        act = (hidden * half).astype(BF16)
        slope = half + (0.5 * hidden) * (1.0 - t * t) * (GELU_A + (3 * GELU_A * GELU_B) * square)
        out += dot(act, w2[cols, :])
        d_hidden32 = dot_t(grad, w2[cols, :]) * slope
        d_hidden = d_hidden32.astype(BF16)
        g_vec[0:1, cols] += jnp.sum(d_hidden32, axis=0, keepdims=True)
        d_normed += dot_t(d_hidden, w1[:, cols])
        g_w1[:, cols] += dot(normed_t, d_hidden)
        g_w2t[:, cols] += dot(grad_t, act)
    out_ref[...] = out.astype(BF16)
    grad32 = grad.astype(F32)
    d_res = grad32 + norm_back(d_normed, xhat, scale, gain)
    d_res_ref[...] = d_res
    d_attn = d_res.astype(BF16)
    d_mixed_ref[...] = dot_t(d_attn, wproj[...]).astype(BF16)
    g_proj[...] += dot(mix.T, d_attn)
    g_vec[1:2, :D] += jnp.sum(d_normed * xhat, axis=0, keepdims=True)
    g_vec[2:3, :D] += jnp.sum(d_normed, axis=0, keepdims=True)
    g_vec[3:4, :D] += jnp.sum(grad32, axis=0, keepdims=True)
    g_vec[4:5, :D] += jnp.sum(d_res, axis=0, keepdims=True)


def mlp(cot, mixed, x, wproj, w1, w2, vecs_a, vecs):
    tokens = x.shape[0]
    chunk = tokens // 7
    vm = pl.BlockSpec(memory_space=pltpu.VMEM)
    tile = pl.BlockSpec((chunk, D), lambda i: (i, 0))
    fixed = lambda *shape: pl.BlockSpec(shape, lambda i: (0, 0))
    return pl.pallas_call(
        mlp_kernel,
        grid=(7,),
        out_shape=[
            jax.ShapeDtypeStruct((tokens, D), BF16),
            jax.ShapeDtypeStruct((tokens, D), F32),
            jax.ShapeDtypeStruct((tokens, D), BF16),
            jax.ShapeDtypeStruct((D, FF), F32),
            jax.ShapeDtypeStruct((D, FF), F32),
            jax.ShapeDtypeStruct((D, D), F32),
            jax.ShapeDtypeStruct((8, FF), F32),
        ],
        in_specs=[tile] * 3 + [vm] * 5,
        out_specs=[tile] * 3 + [fixed(D, FF), fixed(D, FF), fixed(D, D), fixed(8, FF)],
        compiler_params=pltpu.CompilerParams(vmem_limit_bytes=VMEM_LIMIT),
        name="mlp",
    )(cot, mixed, x, wproj, w1, w2, vecs_a, vecs)


CHUNK = 192
LAST = 208


def head_tables():
    lanes = np.arange(D) // HDIM
    one = (np.arange(16)[:, None] == lanes[None, :]).astype(np.float32)
    return np.concatenate([one, one], axis=0).astype(ml_dtypes.bfloat16)


def split_float(values):
    high = values.astype(BF16)
    return high, (values - high.astype(F32)).astype(BF16)


def attend_back_kernel(
    part,
    order,
    ext,
    d_mixed,
    mixed,
    probs,
    inverse,
    head_tab,
    keys_back,
    query_tab,
    query_back,
    x_hbm,
    d_res_hbm,
    wqkv,
    vecs,
    blocks,
    out_src,
    g_bias,
    g_qkv,
    g_vec,
    dx_last,
    grad_ref,
    out_ref,
    dx_ref,
    d_query_t,
    d_key_value,
    d_qkv,
    d_in,
    x_buf,
    d_res_buf,
    load_sems,
    total,
    outgoing,
    arrived,
    send,
    recv,
    out_sem,
    out_send,
    out_recv,
    dx_sem0,
    dx_send0,
    dx_recv0,
    dx_sem1,
    dx_send1,
    dx_recv1,
    dx_sem2,
    dx_send2,
    dx_recv2,
):
    i = pl.program_id(0)
    steps = pl.num_programs(0)
    stages = len(order)
    dp, grp = lax.axis_index("dp"), lax.axis_index("grp")
    cube = CubeSum(order, blocks, total, outgoing, arrived, (send, recv))
    exchange = exchange_copies(out_src, out_ref, dp, grp, out_sem, out_send, out_recv)
    dx_sems = (
        (dx_sem0, dx_send0, dx_recv0),
        (dx_sem1, dx_send1, dx_recv1),
        (dx_sem2, dx_send2, dx_recv2),
    )
    loads = [
        pltpu.make_async_copy(x_hbm, x_buf, load_sems.at[0]),
        pltpu.make_async_copy(d_res_hbm, d_res_buf, load_sems.at[1]),
    ]

    def chunk(c):
        return chunk_copies(d_in, dx_ref, CHUNK * c, CHUNK, dp, grp, *dx_sems[c], 0)

    @pl.when(i == 0)
    def _():
        for c in loads:
            c.start()
        g_bias[...] = jnp.zeros_like(g_bias)
        g_qkv[...] = jnp.zeros_like(g_qkv)
        g_vec[...] = jnp.zeros_like(g_vec)
        greet(cube_partners(order, dp, grp) + [window_partner(dp, grp, 3)])

    for k in reversed(range(stages)):

        @pl.when(i == (stages - 1 - k) * steps // stages)
        def _(k=k):
            if k < stages - 1:
                cube.finish(k + 1)
            cube.start(k)

    @pl.when(i == 0)
    def _():
        for c in exchange:
            c.start()

    inv = inverse[0]
    inv_high, inv_low = split_float(inv)
    inv_t = jnp.concatenate([inv_high, inv_low], axis=0).astype(F32).T.astype(BF16)
    dm_rows = image_rows(d_mixed, i, slice(0, D))
    dm_ext = dot(query_tab[0], dm_rows) * dot(inv_t, head_tab[...])
    mixed_ext = dot(query_tab[0], image_rows(mixed, i, slice(0, D)))
    dm_ext = dm_ext.astype(BF16)
    high, low = split_float(dm_ext.astype(F32) * mixed_ext)
    sums = dot_t(head_tab[0:16, :], high) + dot_t(head_tab[0:16, :], low)
    q_ext = ext[0, :, :D]
    k_t = ext[0, :, D : 2 * D].astype(F32).T.astype(BF16)
    v_ext = ext[0, :, 2 * D :]

    def head_inputs(h):
        mine = lane_heads(h % 4)
        q_head = jnp.where(mine, q_ext[:, tile_of(h)], 0)
        dm_head = jnp.where(mine, dm_ext[:, tile_of(h)], 0)
        return q_head, dm_head, dot_t(v_ext[:, tile_of(h)], dm_head)

    current = head_inputs(0)
    for h in range(HEADS):
        q_head, dm_head, d_probs = current
        if h + 1 < HEADS:
            current = head_inputs(h + 1)
        if h % 4 == 0:
            d_key = jnp.zeros((256, 128), F32)
            d_value = jnp.zeros((256, 128), F32)
        e = probs[0, h]
        d_value += dot(e, dm_head)
        halves = []
        for half in range(2):
            lanes = slice(128 * half, 128 * half + 128)
            e32 = e[:, lanes].astype(F32)[56 * half : 56 * half + KEYS]
            ds = e32 * (half_of(d_probs, half) - sums[h : h + 1, lanes])
            g_bias[h, half] += ds
            halves.append(ds)
        ds = spread(halves)
        d_key += dot(ds, q_head)
        d_query_t[h * HDIM : (h + 1) * HDIM, :] = (
            dot(k_t[h * HDIM : (h + 1) * HDIM, :], ds) * HDIM ** (-0.5)
        ).astype(BF16)
        if h % 4 == 3:
            d_key_value[:, tile_of(h)] = d_key.astype(BF16)
            d_key_value[:, D + h // 4 * 128 : D + h // 4 * 128 + 128] = d_value.astype(BF16)
    put_image_rows(d_qkv, i, slice(0, D), dot_t(query_back[0], d_query_t[...]))
    put_image_rows(d_qkv, i, slice(D, 3 * D), dot(keys_back[0], d_key_value[...]))

    @pl.when(i == 3)
    def _():
        for c in loads:
            c.wait()

    @pl.when(lax.rem(i, 4) == 3)
    def _():
        c = i // 4
        at = pl.ds(pl.multiple_of(c * CHUNK, 16), LAST)
        xhat, scale = norm_parts(x_buf[:, at, :].reshape(4 * LAST, D).astype(F32))
        gain = vecs[0:1, :]
        normed = (xhat * gain + vecs[1:2, :]).astype(BF16)
        row = lax.rem(lax.broadcasted_iota(jnp.int32, (4 * LAST, 1), 0), LAST)
        counts = row < jnp.where(i == steps - 1, LAST, CHUNK)
        grads = d_qkv[:, at, :].reshape(4 * LAST, 3 * D)
        grads = jnp.where(counts, grads, 0)
        d_normed = dot_t(grads, wqkv[...])
        result = d_res_buf[:, at, :].reshape(4 * LAST, D) + norm_back(d_normed, xhat, scale, gain)
        result = result.astype(BF16).reshape(4, LAST, D)
        d_in[:, at, :] = result
        dx_last[...] = result
        g_qkv[...] += dot(normed.T, grads)
        g_vec[0:1, :] += jnp.sum(grads.astype(F32), axis=0, keepdims=True)
        g_vec[1:2, :D] += jnp.sum(d_normed * xhat, axis=0, keepdims=True)
        g_vec[2:3, :D] += jnp.sum(d_normed, axis=0, keepdims=True)

    for c in range(3):

        @pl.when(i == 4 * c + 3)
        def _(c=c):
            for copy in chunk(c):
                copy.start()

    @pl.when(i == steps - 1)
    def _():
        cube.finish(0)
        device = dp * lax.axis_size("grp") + grp
        grad_ref[...] = shift_lanes(total[0], part.lane(device), False)
        for c in exchange:
            c.wait()
        for c in range(3):
            for copy in chunk(c):
                copy.wait()


def attend_back(
    part, order, ext, d_mixed, mixed, probs, inverse, x, d_res, wqkv, vecs, blocks, out
):
    images = ext.shape[0]
    tokens = out.shape[0]
    rows = tokens // 4
    stages = len(order)
    _, query_tab, keys_back, query_back = gather_tables(images)
    vm = pl.BlockSpec(memory_space=pltpu.VMEM)
    hbm = pl.BlockSpec(memory_space=pl.ANY)
    table = pl.BlockSpec((1, 256, 256), lambda i: (i, 0, 0))
    by_window = lambda array: array.reshape(4, rows, -1)
    outs = pl.pallas_call(
        functools.partial(attend_back_kernel, part, order),
        grid=(images,),
        out_shape=[
            jax.ShapeDtypeStruct((HEADS, 2, KEYS, 128), F32),
            jax.ShapeDtypeStruct((D, 3 * D), F32),
            jax.ShapeDtypeStruct((8, 3 * D), F32),
            jax.ShapeDtypeStruct((4, LAST, D), BF16),
            jax.ShapeDtypeStruct((part.rows, 128), F32),
            jax.ShapeDtypeStruct((tokens, D), BF16),
            jax.ShapeDtypeStruct((4, rows, D), BF16),
        ],
        in_specs=[
            pl.BlockSpec((1, 256, 3 * D), lambda i: (i, 0, 0)),
            vm,
            vm,
            pl.BlockSpec((1, HEADS, 256, 256), lambda i: (i, 0, 0, 0)),
            pl.BlockSpec((1, 16, 256), lambda i: (i, 0, 0)),
            vm,
        ]
        + [table] * 3
        + [hbm, hbm, vm, vm, vm, hbm],
        out_specs=[
            pl.BlockSpec((HEADS, 2, KEYS, 128), lambda i: (0, 0, 0, 0)),
            pl.BlockSpec((D, 3 * D), lambda i: (0, 0)),
            pl.BlockSpec((8, 3 * D), lambda i: (0, 0)),
            pl.BlockSpec((4, LAST, D), lambda i: (0, 0, 0)),
            pl.BlockSpec((part.rows, 128), lambda i: (0, 0)),
            hbm,
            hbm,
        ],
        scratch_shapes=[
            pltpu.VMEM((D, 256), BF16),
            pltpu.VMEM((256, 2 * D), BF16),
            pltpu.VMEM((4, rows, 3 * D), BF16),
            pltpu.VMEM((4, rows, D), BF16),
            pltpu.VMEM((4, rows, D), BF16),
            pltpu.VMEM((4, rows, D), F32),
            pltpu.SemaphoreType.DMA((2,)),
        ]
        + CubeSum.scratch(part.devices, part.rows, stages)
        + [
            pltpu.SemaphoreType.DMA,
            pltpu.SemaphoreType.DMA((3,)),
            pltpu.SemaphoreType.DMA((3,)),
        ]
        * 4,
        compiler_params=pltpu.CompilerParams(
            collective_id=3, has_side_effects=True, vmem_limit_bytes=VMEM_LIMIT
        ),
        name="attend_back",
    )(
        ext,
        by_window(d_mixed),
        by_window(mixed),
        probs,
        inverse,
        jnp.asarray(head_tables()),
        keys_back,
        query_tab,
        query_back,
        by_window(x),
        by_window(d_res),
        wqkv,
        vecs,
        blocks,
        out,
    )
    grad = outs[4].reshape(-1)[: part.length]
    return (*outs[:4], grad, *outs[5:])


def to_blocks(part, places, flat, out):
    for device, place in enumerate(places):
        at = part.start(device)
        out[place] = flat[at : at + part.rows, :].astype(BF16)


def pack_mlp_kernel(part, places, g_w1, g_w2t, g_vec, out, flat):
    flat[...] = jnp.zeros_like(flat)
    put_matrix(flat, 0, g_w1)
    for j in range(3):
        flat[pl.ds(4608 + j, FF, stride=3), :] = g_w2t[j * 128 : (j + 1) * 128, :].T
    for j in range(12):
        flat[9216 + j : 9217 + j, :] = g_vec[0:1, j * 128 : (j + 1) * 128]
    for v in range(3):
        for j in range(3):
            at = 9228 + 3 * v + j
            flat[at : at + 1, :] = g_vec[1 + v : 2 + v, j * 128 : (j + 1) * 128]
    to_blocks(part, places, flat, out)


def pack_mlp(part, places, g_w1, g_w2t, g_vec):
    vm = pl.BlockSpec(memory_space=pltpu.VMEM)
    return pl.pallas_call(
        functools.partial(pack_mlp_kernel, part, places),
        out_shape=jax.ShapeDtypeStruct((part.devices, part.rows, 128), BF16),
        in_specs=[vm] * 3,
        out_specs=vm,
        scratch_shapes=[pltpu.VMEM((part.buffer, 128), F32)],
        compiler_params=pltpu.CompilerParams(vmem_limit_bytes=VMEM_LIMIT),
        name="pack_mlp",
    )(g_w1, g_w2t, g_vec)


def pack_kernel(
    part,
    places,
    one_fine,
    one_coarse,
    g_bias,
    g_qkv,
    g_vec1,
    g_proj,
    g_vec2,
    out,
    flat,
    table,
    shifted,
    line,
):
    flat[...] = jnp.zeros_like(flat)
    put_matrix(flat, 0, g_qkv)
    put_matrix(flat, 3456, g_proj)
    vectors = [
        g_vec1[1:2, :D],
        g_vec1[2:3, :D],
        g_vec1[0:1, :D],
        g_vec1[0:1, 2 * D :],
        g_vec2[4:5, :D],
    ]
    pieces = [v[:, j * 128 : (j + 1) * 128] for v in vectors for j in range(3)]
    pieces += [jnp.zeros((1, 128), F32)]
    row, lane = divmod(ATTN_VECTORS[0], 128)
    flat[row : row + 16, :] += shift_lanes(jnp.concatenate(pieces, axis=0), lane, True)
    for h in range(HEADS):
        table[...] = jnp.zeros_like(table)
        for half in range(2):
            turned = g_bias[h, half].T
            for y in range(WIN):
                for at, length, source in bias_runs(half, WIN * half + y):
                    table[0:14, source : source + length] += turned[
                        y * 14 : y * 14 + 14, at : at + length
                    ]
        for c in range(4):
            shifted[c, pl.ds(h, 14, stride=16), :] = table[0:14, c * 128 : (c + 1) * 128]
    g_fine = jnp.zeros((16, 384), F32)
    g_coarse = jnp.zeros((16, 256), F32)
    for qx in range(14):
        at = slice(qx * 16, qx * 16 + 16)
        gathered = jnp.concatenate([shifted[c, at, :] for c in range(4)], axis=1)
        high = gathered.astype(BF16)
        low = (gathered - high.astype(F32)).astype(BF16)
        g_fine += dot_t(high[:, :384], one_fine[qx]) + dot_t(low[:, :384], one_fine[qx])
        g_coarse += dot_t(high[:, 384:], one_coarse[qx]) + dot_t(low[:, 384:], one_coarse[qx])
    for t, h, length, row, lane, count in table_lines():
        line[...] = jnp.zeros_like(line)
        line[0:1, lane : lane + length] = (g_fine, g_coarse)[t][h : h + 1, :length]
        for c in range(count):
            flat[row + c : row + c + 1, :] += line[0:1, c * 128 : (c + 1) * 128]
    to_blocks(part, places, flat, out)


def pack(part, places, g_bias, g_qkv, g_vec1, g_proj, g_vec2):
    fine, coarse, _ = bias_tables()
    vm = pl.BlockSpec(memory_space=pltpu.VMEM)
    return pl.pallas_call(
        functools.partial(pack_kernel, part, places),
        out_shape=jax.ShapeDtypeStruct((part.devices, part.rows, 128), BF16),
        in_specs=[vm] * 7,
        out_specs=vm,
        scratch_shapes=[
            pltpu.VMEM((part.buffer, 128), F32),
            pltpu.VMEM((16, 512), F32),
            pltpu.VMEM((4, 14 * 16, 128), F32),
            pltpu.VMEM((8, 512), F32),
        ],
        compiler_params=pltpu.CompilerParams(vmem_limit_bytes=VMEM_LIMIT),
        name="pack",
    )(jnp.asarray(fine), jnp.asarray(coarse), g_bias, g_qkv, g_vec1, g_proj, g_vec2)


def adamw(master, first, second, grads):
    first_new = beta_one * first + (1.0 - beta_one) * grads
    second_new = beta_two * second + (1.0 - beta_two) * grads * grads
    first_hat = first_new / (1.0 - beta_one**STEP)
    second_hat = second_new / (1.0 - beta_two**STEP)
    master_new = master - learn_rate * (
        first_hat / (jnp.sqrt(second_hat) + adam_eps) + decay_rate * master
    )
    return (first_new, second_new, master_new)


def body(
    tokens, cotangent, attn_master, attn_first, attn_second, mlp_master, mlp_first, mlp_second
):
    n_dp, n_grp = lax.axis_size("dp"), lax.axis_size("grp")
    order = bit_order(n_dp, n_grp)
    places = place_list(order, n_dp, n_grp)
    part_a = Part(n_dp * n_grp, attn_master.shape[0])
    part_b = Part(n_dp * n_grp, mlp_master.shape[0])
    images = tokens.shape[1] // 4 // SEQ
    blocks_a, x = gather_params(part_a, order, attn_master, tokens[0])
    wqkv, wproj, vecs_a, bias = prepare(part_a, places, blocks_a)
    mixed, probs, ext, inverse, cot, blocks_b = attend(
        part_b, order, x, cotangent[0], mlp_master, wqkv, vecs_a, bias, images
    )
    mixed = mixed.reshape(-1, D)
    w1, w2, vecs_b = prepare_mlp(part_b, places, blocks_b)
    out, d_res, d_mixed, g_w1, g_w2t, g_proj, g_vec2 = mlp(
        cot, mixed, x, wproj, w1, w2, vecs_a, vecs_b
    )
    sums_b = pack_mlp(part_b, places, g_w1, g_w2t, g_vec2)
    g_bias, g_qkv, g_vec1, dx_last, grad_b, output, dx = attend_back(
        part_b,
        order,
        ext,
        d_mixed,
        mixed,
        probs,
        inverse,
        x,
        d_res,
        wqkv,
        vecs_a,
        sums_b,
        out,
    )
    sums_a = pack(part_a, places, g_bias, g_qkv, g_vec1, g_proj, g_vec2)
    grad_a, dx = sum_grads(part_a, order, sums_a, dx_last, dx)
    attn_new = adamw(attn_master, attn_first, attn_second, grad_a)
    mlp_new = adamw(mlp_master, mlp_first, mlp_second, grad_b)
    input_grad = dx.reshape(-1, D).astype(F32)
    return (output[None], input_grad[None], *attn_new, *mlp_new)


def solution(mesh):
    flat_spec = P(("dp", "grp"))
    token_spec = P("dp", "grp", None)
    placed = (token_spec, token_spec) + (flat_spec,) * 6
    return jax.shard_map(
        body, mesh=mesh, in_specs=placed, out_specs=placed, check_vma=False
    )
```

```python
import functools

import jax
import jax.numpy as jnp
import ml_dtypes
import numpy as np
from jax import lax
from jax.experimental import pallas as pl
from jax.experimental.pallas import tpu as pltpu
from jax.sharding import PartitionSpec as P

D = 384
HEADS = 12
HDIM = 32
FF = 1536
WIN = 7
STEP = 10
SEQ = WIN * WIN
HALF = 64
FINE = (3 * WIN - 2) ** 2
COARSE = (2 * WIN - 1) ** 2
KEYS = 192

beta_one = 0.9
beta_two = 0.999
learn_rate = 0.04
decay_rate = 0.05
adam_eps = 1e-08
norm_eps = 1e-05
masked_score = -1e30

F32 = jnp.float32
BF16 = jnp.bfloat16
MESH = pl.DeviceIdType.MESH
VMEM_LIMIT = 56 * 2**20


def token_place(gy, gx):
    window = 2 * (gy // WIN) + gx // WIN
    return window * HALF + (gy % WIN) * WIN + gx % WIN


@functools.cache
def gather_tables(images):
    keys = np.zeros((images, 256, 256), np.float32)
    queries = np.zeros((images, 256, 256), np.float32)
    for i in range(images):
        for gy in range(2 * WIN):
            for gx in range(2 * WIN):
                at = token_place(gy, gx) + i
                key = gy * 14 + gx if gy < 10 else 192 + (gy - 10) * 14 + gx
                keys[i, key, at] = 1.0
                keys[i, 140 + (gy // 2) * WIN + gx // 2, at] = 0.25
                queries[i, (gy // WIN) * 128 + (gy % WIN) * 14 + gx, at] = 1.0
    return (
        keys.astype(ml_dtypes.bfloat16),
        queries.astype(ml_dtypes.bfloat16),
        np.ascontiguousarray(keys.transpose(0, 2, 1)).astype(ml_dtypes.bfloat16),
        np.ascontiguousarray(queries.transpose(0, 2, 1)).astype(ml_dtypes.bfloat16),
    )


@functools.cache
def bias_tables():
    fine = np.zeros((384, 384), np.float32)
    coarse = np.zeros((256, 128), np.float32)
    for a in range(4, 23):
        for kx in range(14):
            fine[19 * (a - 4) + kx + 9, a * 14 + kx] = 1.0
    for p in range(13):
        for x in range(WIN):
            coarse[13 * p + x + 6, p * WIN + x] = 1.0
    mask = np.zeros((2, KEYS, 128), np.float32)
    for half in range(2):
        for q in range(98):
            qx = q % 14
            for e in range(KEYS):
                at = e + 56 * half
                if at < 140:
                    ok = abs_ok(qx, at % 14)
                elif at < 189:
                    ok = True
                elif at < 192:
                    ok = False
                else:
                    ok = at < 248 and abs_ok(qx, (at - 192) % 14)
                mask[half, e, q] = 0.0 if ok else masked_score
    return fine.astype(ml_dtypes.bfloat16), coarse.astype(ml_dtypes.bfloat16), mask


def abs_ok(qx, kx):
    return kx < 10 if qx < WIN else kx >= 4


def bias_runs(half, qy):
    fine = (13 - qy) * 14
    pool = 384 + (6 - qy // 2) * WIN
    if half == 0:
        return [(0, 140, fine), (140, 49, pool)]
    return [(0, 84, fine + 56), (84, 49, pool), (136, 56, fine + 140)]


class Part:
    def __init__(self, devices, length):
        self.devices = devices
        self.length = length
        self.rows = -(-((length + 126) // 128 + 1) // 16) * 16
        self.buffer = -(-(self.start(devices - 1) + self.rows) // 8) * 8

    def start(self, device):
        return device * self.length // 128

    def lane(self, device):
        return lax.rem(device * self.length, 128)

    def padded(self, vector):
        extra = self.rows * 128 - self.length
        return jnp.pad(vector, (0, extra)).reshape(self.rows, 128)


GATHER_STEPS = 16
SUM_STEPS = 15


def bit_order(n_dp, n_grp):
    dp_bits = [("dp", 2**b) for b in range(n_dp.bit_length() - 1)]
    grp_bits = [("grp", 2**b) for b in reversed(range(n_grp.bit_length() - 1))]
    return dp_bits[1:2] + grp_bits + dp_bits[2:] + dp_bits[:1]


def stage_weights(order):
    weights = []
    for k, (axis, stride) in enumerate(order):
        relative = 0.35 if (axis, stride) == ("dp", 1) else 2 if (axis == "grp" and stride > 1) else 1
        weights.append(relative * 2**k)
    return weights


def starts_of(weights, steps):
    done, starts = 0.0, []
    for weight in weights:
        starts.append(min(int(np.ceil(steps * done / sum(weights))), steps - 1))
        done += weight
    return starts


def place_of(order, dp, grp):
    place = 0
    for k, (axis, stride) in enumerate(order):
        place = place + ((dp if axis == "dp" else grp) // stride) % 2 * 2**k
    return place


def partner_of(axis, stride, dp, grp):
    if axis == "dp":
        return (dp + (1 - 2 * ((dp // stride) % 2)) * stride, grp)
    return (dp, grp + (1 - 2 * ((grp // stride) % 2)) * stride)


def greet(partners):
    barrier = pltpu.get_barrier_semaphore()
    for partner in partners:
        pl.semaphore_signal(barrier, inc=1, device_id=partner, device_id_type=MESH)
    pl.semaphore_wait(barrier, len(partners))


def cube_partners(order, dp, grp):
    return [partner_of(axis, stride, dp, grp) for axis, stride in order]


def shift_lanes(values, amount, up):
    lane = lax.broadcasted_iota(jnp.int32, values.shape, 1)
    if up:
        turned = pltpu.roll(values, amount, 1)
        return jnp.where(lane >= amount, turned, pltpu.roll(turned, 1, 0))
    turned = pltpu.roll(values, lax.rem(128 - amount, 128), 1)
    return jnp.where(lane < 128 - amount, turned, pltpu.roll(turned, values.shape[0] - 1, 0))


def window_partner(dp, grp, k):
    low, high = dp % 2, dp // 2 % 2
    to = dp
    if k % 2:
        to = to + 1 - 2 * low
    if k // 2:
        to = to + 2 * (1 - 2 * high)
    return (to, grp)


def exchange_copies(source, target, dp, grp, own_sem, send_sems, recv_sems):
    rows = source.shape[0] // 4
    slot = dp % 4
    mine = pl.ds(pl.multiple_of(slot * rows, 16), rows)
    own = pltpu.make_async_copy(source.at[mine], target.at[mine], own_sem)
    sends = []
    for k in (3, 2, 1):
        to, _ = window_partner(dp, grp, k)
        theirs = pl.ds(pl.multiple_of(to % 4 * rows, 16), rows)
        sends.append(
            pltpu.make_async_remote_copy(
                src_ref=source.at[theirs],
                dst_ref=target.at[mine],
                send_sem=send_sems.at[k - 1],
                recv_sem=recv_sems.at[k - 1],
                device_id=(to, grp),
                device_id_type=MESH,
            )
        )
    return [own] + sends


def cube_copy(order, k, source, target, dp, grp, send_sems, recv_sems):
    axis, stride = order[k]
    return pltpu.make_async_remote_copy(
        src_ref=source,
        dst_ref=target,
        send_sem=send_sems.at[k],
        recv_sem=recv_sems.at[k],
        device_id=partner_of(axis, stride, dp, grp),
        device_id_type=MESH,
    )


def gather_copy(order, k, blocks, dp, grp, sems):
    place = place_of(order, dp, grp)
    held = blocks.at[pl.ds(place // 2**k * 2**k, 2**k)]
    return cube_copy(order, k, held, held, dp, grp, *sems)


def own_block(part, master_ref, own):
    device = lax.axis_index("dp") * lax.axis_size("grp") + lax.axis_index("grp")
    own[...] = shift_lanes(master_ref[...], part.lane(device), True).astype(BF16)


class CubeSum:
    def __init__(self, order, blocks, total, outgoing, arrived, sems):
        self.order, self.blocks, self.total = order, blocks, total
        self.outgoing, self.arrived, self.sems = outgoing, arrived, sems
        self.dp, self.grp = lax.axis_index("dp"), lax.axis_index("grp")
        self.place = place_of(order, self.dp, self.grp)
        self.last = len(order) - 1

    def mine(self, k):
        return self.place // 2**k % 2 * 2**k

    def copy(self, k):
        size = 2**k
        if k == self.last:
            source = self.blocks.at[pl.ds(size - self.mine(k), size)]
        else:
            source = self.outgoing.at[pl.ds(size, size)]
        target = self.arrived.at[pl.ds(size, size)]
        return cube_copy(self.order, k, source, target, self.dp, self.grp, *self.sems)

    def start(self, k):
        size = 2**k
        if k < self.last:
            other = size - self.mine(k)

            def fill(j, carry):
                self.outgoing[size + j] = self.total[other + j].astype(BF16)
                return carry

            lax.fori_loop(0, size, fill, 0)
        self.copy(k).start()

    def finish(self, k):
        size, mine = 2**k, self.mine(k)
        self.copy(k).wait()

        def add(j, carry):
            if k == self.last:
                held = self.blocks[mine + j].astype(F32)
            else:
                held = self.total[mine + j]
            self.total[j] = held + self.arrived[size + j].astype(F32)
            return carry

        lax.fori_loop(0, size, add, 0)

    @staticmethod
    def scratch(devices, rows, stages):
        return [
            pltpu.VMEM((devices // 2, rows, 128), F32),
            pltpu.VMEM((devices // 2, rows, 128), BF16),
            pltpu.VMEM((devices, rows, 128), BF16),
            pltpu.SemaphoreType.DMA((stages,)),
            pltpu.SemaphoreType.DMA((stages,)),
        ]


def gather_kernel(
    part, order, a_ref, tok_ref, out_ref, x_ref, own, own_sem, send, recv, x_sem, x_send, x_recv
):
    dp, grp = lax.axis_index("dp"), lax.axis_index("grp")
    own_block(part, a_ref, own)
    copy = pltpu.make_async_copy(own, out_ref.at[place_of(order, dp, grp)], own_sem)
    copy.start()
    greet(cube_partners(order, dp, grp) + [window_partner(dp, grp, 3)])
    copy.wait()
    exchange = exchange_copies(tok_ref, x_ref, dp, grp, x_sem, x_send, x_recv)
    for k in range(len(order)):
        stage = gather_copy(order, k, out_ref, dp, grp, (send, recv))
        stage.start()
        if k == 0:
            for c in exchange:
                c.start()
        stage.wait()
    for c in exchange:
        c.wait()


def gather_params(part, order, master, tok):
    stages = len(order)
    return pl.pallas_call(
        functools.partial(gather_kernel, part, order),
        out_shape=[
            jax.ShapeDtypeStruct((part.devices, part.rows, 128), BF16),
            jax.ShapeDtypeStruct(tok.shape, BF16),
        ],
        in_specs=[
            pl.BlockSpec(memory_space=pltpu.VMEM),
            pl.BlockSpec(memory_space=pl.ANY),
        ],
        out_specs=[pl.BlockSpec(memory_space=pl.ANY)] * 2,
        scratch_shapes=[
            pltpu.VMEM((part.rows, 128), BF16),
            pltpu.SemaphoreType.DMA,
            pltpu.SemaphoreType.DMA((stages,)),
            pltpu.SemaphoreType.DMA((stages,)),
            pltpu.SemaphoreType.DMA,
            pltpu.SemaphoreType.DMA((3,)),
            pltpu.SemaphoreType.DMA((3,)),
        ],
        compiler_params=pltpu.CompilerParams(
            collective_id=0, has_side_effects=True, vmem_limit_bytes=VMEM_LIMIT
        ),
        name="gather_params",
    )(part.padded(master), tok)


def chunk_copies(source, target, first, size, dp, grp, own_sem, send_sems, recv_sems, skip):
    slot = dp % 4
    into = target.at[slot, pl.ds(first, size)]
    rows = pl.ds(first - skip, size)
    copies = [pltpu.make_async_copy(source.at[slot, rows], into, own_sem)]
    for k in (3, 2, 1):
        to, _ = window_partner(dp, grp, k)
        copies.append(
            pltpu.make_async_remote_copy(
                src_ref=source.at[to % 4, rows],
                dst_ref=into,
                send_sem=send_sems.at[k - 1],
                recv_sem=recv_sems.at[k - 1],
                device_id=(to, grp),
                device_id_type=MESH,
            )
        )
    return copies


def sum_kernel(
    part,
    order,
    blocks,
    last_ref,
    dx_ref,
    grad_ref,
    dx_out,
    total,
    outgoing,
    arrived,
    send,
    recv,
    x_sem,
    x_send,
    x_recv,
):
    dp, grp = lax.axis_index("dp"), lax.axis_index("grp")
    greet(cube_partners(order, dp, grp) + [window_partner(dp, grp, 3)])
    cube = CubeSum(order, blocks, total, outgoing, arrived, (send, recv))
    first = dx_ref.shape[1] - last_ref.shape[1]
    exchange = chunk_copies(
        last_ref, dx_out, first, last_ref.shape[1], dp, grp, x_sem, x_send, x_recv, first
    )
    for k in reversed(range(len(order))):
        cube.start(k)
        if k == len(order) - 1:
            for c in exchange:
                c.start()
        cube.finish(k)
    device = dp * lax.axis_size("grp") + grp
    grad_ref[...] = shift_lanes(total[0], part.lane(device), False)
    for c in exchange:
        c.wait()


def sum_grads(part, order, blocks, last, dx):
    stages = len(order)
    hbm = pl.BlockSpec(memory_space=pl.ANY)
    vm = pl.BlockSpec(memory_space=pltpu.VMEM)
    grad, dx = pl.pallas_call(
        functools.partial(sum_kernel, part, order),
        out_shape=[
            jax.ShapeDtypeStruct((part.rows, 128), F32),
            jax.ShapeDtypeStruct(dx.shape, dx.dtype),
        ],
        in_specs=[vm, hbm, hbm],
        out_specs=[vm, hbm],
        input_output_aliases={2: 1},
        scratch_shapes=CubeSum.scratch(part.devices, part.rows, stages)
        + [
            pltpu.SemaphoreType.DMA,
            pltpu.SemaphoreType.DMA((3,)),
            pltpu.SemaphoreType.DMA((3,)),
        ],
        compiler_params=pltpu.CompilerParams(
            collective_id=1, has_side_effects=True, vmem_limit_bytes=VMEM_LIMIT
        ),
        name="sum_grads",
    )(blocks, last, dx)
    return grad.reshape(-1)[: part.length], dx


def place_list(order, n_dp, n_grp):
    return [place_of(order, d // n_grp, d % n_grp) for d in range(n_dp * n_grp)]


ATTN_VECTORS = (D * 3 * D + D * D + HEADS * FINE + HEADS * COARSE, 5)
TABLE_AT = D * 3 * D + D * D


def unflatten(part, places, blocks, flat):
    flat[...] = jnp.zeros_like(flat)
    for device, place in enumerate(places):
        at = part.start(device)
        flat[at : at + part.rows, :] += blocks[place].astype(F32)


def take_matrix(flat, first, target):
    rows, columns = target.shape
    count = columns // 128
    for j in range(count):
        target[:, j * 128 : (j + 1) * 128] = flat[pl.ds(first + j, rows, stride=count), :].astype(
            target.dtype
        )


def put_matrix(flat, first, source):
    rows, columns = source.shape
    count = columns // 128
    for j in range(count):
        flat[pl.ds(first + j, rows, stride=count), :] = source[:, j * 128 : (j + 1) * 128]


TABLES = ((TABLE_AT, FINE), (TABLE_AT + HEADS * FINE, COARSE))


def table_lines():
    for t, (first, length) in enumerate(TABLES):
        for h in range(HEADS):
            row, lane = divmod(first + h * length, 128)
            yield t, h, length, row, lane, -(-(lane + length) // 128)


def prep_kernel(
    part,
    places,
    blocks,
    one_fine,
    one_coarse,
    mask_ref,
    wqkv,
    wproj,
    vecs,
    bias,
    flat,
    tab_fine,
    tab_coarse,
    shifted,
    turned,
):
    unflatten(part, places, blocks, flat)
    take_matrix(flat, 0, wqkv)
    take_matrix(flat, 3456, wproj)
    vecs[...] = jnp.zeros_like(vecs)
    row, lane = divmod(ATTN_VECTORS[0], 128)
    rows = shift_lanes(flat[row : row + 16, :], lane, False)
    for v in range(5):
        for j in range(3):
            vecs[v : v + 1, j * 128 : (j + 1) * 128] = rows[3 * v + j : 3 * v + j + 1]
    tab_fine[...] = jnp.zeros_like(tab_fine)
    tab_coarse[...] = jnp.zeros_like(tab_coarse)
    for t, h, length, row, lane, count in table_lines():
        line = jnp.concatenate([flat[row + c : row + c + 1, :] for c in range(count)], axis=1)
        (tab_fine, tab_coarse)[t][h : h + 1, 0:length] = line[:, lane : lane + length]
    fine, coarse = tab_fine[...], tab_coarse[...]
    fine = jnp.concatenate([pltpu.roll(fine, qx, 1) for qx in range(14)], axis=0)
    coarse = jnp.concatenate([pltpu.roll(coarse, qx // 2, 1) for qx in range(14)], axis=0)
    fine = dot(fine.astype(BF16), one_fine[...])
    for c in range(3):
        shifted[c] = fine[:, c * 128 : (c + 1) * 128]
    shifted[3] = dot(coarse.astype(BF16), one_coarse[...])
    turned[...] = jnp.zeros_like(turned)
    for h in range(HEADS):
        table = jnp.concatenate(
            [shifted[c, pl.ds(h, 14, stride=16), :] for c in range(4)], axis=1
        )
        for half in range(2):
            for y in range(WIN):
                for at, length, source in bias_runs(half, WIN * half + y):
                    turned[half, y * 14 : y * 14 + 14, at : at + length] = table[
                        :, source : source + length
                    ]
            bias[h, half] = turned[half].T[0:KEYS] + mask_ref[half]


def prepare(part, places, blocks):
    fine, coarse, mask = bias_tables()
    vm = pl.BlockSpec(memory_space=pltpu.VMEM)
    return pl.pallas_call(
        functools.partial(prep_kernel, part, places),
        out_shape=[
            jax.ShapeDtypeStruct((D, 3 * D), BF16),
            jax.ShapeDtypeStruct((D, D), BF16),
            jax.ShapeDtypeStruct((8, D), F32),
            jax.ShapeDtypeStruct((HEADS, 2, KEYS, 128), F32),
        ],
        in_specs=[vm] * 4,
        out_specs=[vm] * 4,
        scratch_shapes=[
            pltpu.VMEM((part.buffer, 128), F32),
            pltpu.VMEM((16, 384), F32),
            pltpu.VMEM((16, 256), F32),
            pltpu.VMEM((4, 14 * 16, 128), F32),
            pltpu.VMEM((2, 128, 256), F32),
        ],
        compiler_params=pltpu.CompilerParams(vmem_limit_bytes=VMEM_LIMIT),
        name="prepare",
    )(blocks, jnp.asarray(fine), jnp.asarray(coarse), jnp.asarray(mask))


def prep_mlp_kernel(part, places, blocks, w1, w2, vecs, flat):
    unflatten(part, places, blocks, flat)
    take_matrix(flat, 0, w1)
    take_matrix(flat, 4608, w2)
    vecs[...] = jnp.zeros_like(vecs)
    for j in range(12):
        vecs[0:1, j * 128 : (j + 1) * 128] = flat[9216 + j : 9217 + j, :]
    for v in range(3):
        for j in range(3):
            at = 9228 + 3 * v + j
            vecs[1 + v : 2 + v, j * 128 : (j + 1) * 128] = flat[at : at + 1, :]


def prepare_mlp(part, places, blocks):
    vm = pl.BlockSpec(memory_space=pltpu.VMEM)
    return pl.pallas_call(
        functools.partial(prep_mlp_kernel, part, places),
        out_shape=[
            jax.ShapeDtypeStruct((D, FF), BF16),
            jax.ShapeDtypeStruct((FF, D), BF16),
            jax.ShapeDtypeStruct((8, FF), F32),
        ],
        in_specs=[vm],
        out_specs=[vm] * 3,
        scratch_shapes=[pltpu.VMEM((part.buffer, 128), F32)],
        compiler_params=pltpu.CompilerParams(vmem_limit_bytes=VMEM_LIMIT),
        name="prepare_mlp",
    )(blocks)


def dot(a, b):
    return jnp.dot(a, b, preferred_element_type=F32)


def dot_t(a, b):
    return lax.dot_general(a, b, (((1,), (1,)), ((), ())), preferred_element_type=F32)


def norm_parts(values):
    centered = values - jnp.mean(values, axis=-1, keepdims=True)
    scale = lax.rsqrt(jnp.mean(centered * centered, axis=-1, keepdims=True) + norm_eps)
    return centered * scale, scale


def norm_back(d_normed, xhat, scale, gain):
    dh = d_normed * gain
    return scale * (
        dh
        - jnp.mean(dh, axis=-1, keepdims=True)
        - xhat * jnp.mean(dh * xhat, axis=-1, keepdims=True)
    )


def image_rows(ref, i, columns):
    at = pl.ds(pl.multiple_of(48 * i, 16), HALF)
    return jnp.concatenate([ref[w, at, columns] for w in range(4)], axis=0)


def put_image_rows(ref, i, columns, values):
    for w in range(4):
        part = values[w * HALF : (w + 1) * HALF]
        first = pl.ds(pl.multiple_of(48 * i, 16), 16)
        rest = pl.ds(pl.multiple_of(48 * i + 16, 16), HALF - 16)
        held = jnp.where(i > 0, ref[w, first, columns].astype(F32), 0.0)
        ref[w, first, columns] = (held + part[:16]).astype(ref.dtype)
        ref[w, rest, columns] = part[16:].astype(ref.dtype)


def spread(halves):
    columns = []
    for half, values in enumerate(halves):
        pieces = [values, jnp.zeros((64 - 56 * half, 128), F32)]
        if half:
            pieces = [jnp.zeros((56, 128), F32)] + pieces
        columns.append(jnp.concatenate(pieces, axis=0))
    return jnp.concatenate(columns, axis=1).astype(BF16)


def only_head(turned, h):
    pieces = [jnp.zeros((HDIM, 256), BF16)] * 4
    pieces[h % 4] = turned[h * HDIM : (h + 1) * HDIM, :]
    return jnp.concatenate(pieces, axis=0)


def half_of(values, half):
    return values[56 * half : 56 * half + KEYS, 128 * half : 128 * half + 128]


def tile_of(h):
    return slice(h // 4 * 128, h // 4 * 128 + 128)


def attend_kernel(
    rows,
    part,
    order,
    x_buf,
    cot_ref,
    master_ref,
    wqkv,
    vecs,
    bias,
    keys_tab,
    query_tab,
    query_back,
    mixed,
    probs,
    query_out,
    key_out,
    value_out,
    mixed_out,
    inverse,
    cot_out,
    blocks,
    normed,
    qkv,
    own,
    own_sem,
    send,
    recv,
    cot_sem,
    cot_send,
    cot_recv,
):
    i = pl.program_id(0)
    steps = pl.num_programs(0)
    dp, grp = lax.axis_index("dp"), lax.axis_index("grp")
    exchange = exchange_copies(cot_ref, cot_out, dp, grp, cot_sem, cot_send, cot_recv)
    stages = len(order)

    @pl.when(i == 0)
    def _():
        own_block(part, master_ref, own)
        copy = pltpu.make_async_copy(own, blocks.at[place_of(order, dp, grp)], own_sem)
        copy.start()
        greet(cube_partners(order, dp, grp) + [window_partner(dp, grp, 3)])
        copy.wait()

    for k, start in enumerate(starts_of(stage_weights(order), GATHER_STEPS)):

        @pl.when(i == start)
        def _(k=k):
            if k:
                gather_copy(order, k - 1, blocks, dp, grp, (send, recv)).wait()
            gather_copy(order, k, blocks, dp, grp, (send, recv)).start()

    @pl.when(i == 0)
    def _():
        for c in exchange:
            c.start()

        step = rows // 7

        def norm(w):
            for c in range(7):
                at = slice(c * step, (c + 1) * step)
                xhat, _ = norm_parts(x_buf[w, at, :].astype(F32))
                normed[w % 2, at, :] = (xhat * vecs[0:1, :] + vecs[1:2, :]).astype(BF16)

        norm(0)
        for w in range(4):
            q = dot(normed[w % 2], wqkv[:, :D]) + vecs[2:3, :]
            qkv[w, :, :D] = (q * HDIM ** (-0.5)).astype(BF16)
            if w < 3:
                norm(w + 1)
            qkv[w, :, D : 2 * D] = dot(normed[w % 2], wqkv[:, D : 2 * D]).astype(BF16)
            v = dot(normed[w % 2], wqkv[:, 2 * D :]) + vecs[3:4, :]
            qkv[w, :, 2 * D :] = v.astype(BF16)

    q_ext = dot(query_tab[0], image_rows(qkv, i, slice(0, D)))
    kv_ext = dot(keys_tab[0], image_rows(qkv, i, slice(D, 3 * D)))
    q_t = q_ext.T.astype(BF16)
    k_ext = kv_ext[:, :D].astype(BF16)
    v_t = kv_ext[:, D:].T.astype(BF16)
    query_out[0] = q_t
    key_out[0] = kv_ext[:, :D].T.astype(BF16)
    value_out[0] = kv_ext[:, D:].astype(BF16)
    inverse[0, HEADS:16, :] = jnp.zeros((16 - HEADS, 256), F32)

    def scores_of(h):
        heads = jnp.concatenate([only_head(q_t, h), only_head(q_t, h + 1)], axis=1)
        return dot(k_ext[:, tile_of(h)], heads)

    def softmax(scores, h):
        halves, inverses = [], []
        for half in range(2):
            s = half_of(scores, half) + bias[h, half]
            e = jnp.exp(s - jnp.max(s, axis=0, keepdims=True))
            inverses.append(1.0 / jnp.sum(e, axis=0, keepdims=True))
            halves.append(e)
        e = spread(halves)
        inv = jnp.concatenate(inverses, axis=1)
        probs[0, h] = e
        inverse[0, h : h + 1, :] = inv
        return e, inv

    def mix(h, e, inv):
        own = slice(h * HDIM, (h + 1) * HDIM)
        mixed_out[0, own, :] = (dot(v_t[own, :], e) * inv).astype(BF16)

    ahead = scores_of(0)
    waiting = []
    for h in range(0, HEADS, 2):
        now = ahead
        if h + 2 < HEADS:
            ahead = scores_of(h + 2)
        for c in range(2):
            waiting.append((h + c, *softmax(now[:, c * 256 : (c + 1) * 256], h + c)))
        while len(waiting) > 1:
            mix(*waiting.pop(0))
    for last in waiting:
        mix(*last)
    put_image_rows(mixed, i, slice(0, D), dot_t(query_back[0], mixed_out[0]))

    @pl.when(i == steps - 1)
    def _():
        gather_copy(order, stages - 1, blocks, dp, grp, (send, recv)).wait()
        for c in exchange:
            c.wait()


def attend(part, order, x, cot, master, wqkv, vecs, bias, images):
    tokens = x.shape[0]
    stages = len(order)
    rows = tokens // 4
    keys_tab, query_tab, _, query_back = gather_tables(images)
    vm = pl.BlockSpec(memory_space=pltpu.VMEM)
    hbm = pl.BlockSpec(memory_space=pl.ANY)
    image = lambda *shape: pl.BlockSpec((1, *shape), lambda i: (i, 0, 0))
    table = image(256, 256)
    return pl.pallas_call(
        functools.partial(attend_kernel, rows, part, order),
        grid=(images,),
        out_shape=[
            jax.ShapeDtypeStruct((4, rows, D), BF16),
            jax.ShapeDtypeStruct((images, HEADS, 256, 256), BF16),
            jax.ShapeDtypeStruct((images, D, 256), BF16),
            jax.ShapeDtypeStruct((images, D, 256), BF16),
            jax.ShapeDtypeStruct((images, 256, D), BF16),
            jax.ShapeDtypeStruct((images, D, 256), BF16),
            jax.ShapeDtypeStruct((images, 16, 256), F32),
            jax.ShapeDtypeStruct((tokens, D), BF16),
            jax.ShapeDtypeStruct((part.devices, part.rows, 128), BF16),
        ],
        in_specs=[vm, hbm] + [vm] * 4 + [table] * 3,
        out_specs=[
            pl.BlockSpec((4, rows, D), lambda i: (0, 0, 0)),
            pl.BlockSpec((1, HEADS, 256, 256), lambda i: (i, 0, 0, 0)),
            image(D, 256),
            image(D, 256),
            image(256, D),
            image(D, 256),
            image(16, 256),
            hbm,
            hbm,
        ],
        scratch_shapes=[
            pltpu.VMEM((2, rows, D), BF16),
            pltpu.VMEM((4, rows, 3 * D), BF16),
            pltpu.VMEM((part.rows, 128), BF16),
            pltpu.SemaphoreType.DMA,
            pltpu.SemaphoreType.DMA((stages,)),
            pltpu.SemaphoreType.DMA((stages,)),
            pltpu.SemaphoreType.DMA,
            pltpu.SemaphoreType.DMA((3,)),
            pltpu.SemaphoreType.DMA((3,)),
        ],
        compiler_params=pltpu.CompilerParams(
            collective_id=2, has_side_effects=True, vmem_limit_bytes=VMEM_LIMIT
        ),
        name="attend",
    )(
        x.reshape(4, rows, D),
        cot,
        part.padded(master),
        wqkv,
        vecs,
        bias,
        keys_tab,
        query_tab,
        query_back,
    )


GELU_A = float(np.sqrt(2.0 / np.pi))
GELU_B = 0.044715


def mlp_kernel(
    cot_ref,
    mixed_ref,
    x_ref,
    wproj,
    w1,
    w2,
    vecs_a,
    vecs,
    out_ref,
    d_res_ref,
    d_mixed_ref,
    g_w1,
    g_w2t,
    g_proj,
    g_vec,
):
    i = pl.program_id(0)
    chunk = mixed_ref.shape[0]

    @pl.when(i == 0)
    def _():
        g_w1[...] = jnp.zeros_like(g_w1)
        g_w2t[...] = jnp.zeros_like(g_w2t)
        g_proj[...] = jnp.zeros_like(g_proj)
        g_vec[...] = jnp.zeros_like(g_vec)

    mix = mixed_ref[...]
    res = x_ref[...].astype(F32) + dot(mix, wproj[...]) + vecs_a[4:5, :]
    xhat, scale = norm_parts(res)
    gain = vecs[1:2, :D]
    normed = (xhat * gain + vecs[2:3, :D]).astype(BF16)
    grad = cot_ref[...]
    grad_t = grad.T
    normed_t = normed.T
    out = res + vecs[3:4, :D]
    d_normed = jnp.zeros((chunk, D), F32)
    for f in range(3):
        cols = slice(f * 512, f * 512 + 512)
        hidden = dot(normed, w1[:, cols]) + vecs[0:1, cols]
        square = hidden * hidden
        t = jnp.tanh(hidden * (GELU_A + (GELU_A * GELU_B) * square))
        half = 0.5 + 0.5 * t
        act = (hidden * half).astype(BF16)
        slope = half + (0.5 * hidden) * (1.0 - t * t) * (GELU_A + (3 * GELU_A * GELU_B) * square)
        out += dot(act, w2[cols, :])
        d_hidden32 = dot_t(grad, w2[cols, :]) * slope
        d_hidden = d_hidden32.astype(BF16)
        g_vec[0:1, cols] += jnp.sum(d_hidden32, axis=0, keepdims=True)
        d_normed += dot_t(d_hidden, w1[:, cols])
        g_w1[:, cols] += dot(normed_t, d_hidden)
        g_w2t[:, cols] += dot(grad_t, act)
    out_ref[...] = out.astype(BF16)
    grad32 = grad.astype(F32)
    d_res = grad32 + norm_back(d_normed, xhat, scale, gain)
    d_res_ref[...] = d_res
    d_attn = d_res.astype(BF16)
    d_mixed_ref[...] = dot_t(d_attn, wproj[...]).astype(BF16)
    g_proj[...] += dot(mix.T, d_attn)
    g_vec[1:2, :D] += jnp.sum(d_normed * xhat, axis=0, keepdims=True)
    g_vec[2:3, :D] += jnp.sum(d_normed, axis=0, keepdims=True)
    g_vec[3:4, :D] += jnp.sum(grad32, axis=0, keepdims=True)
    g_vec[4:5, :D] += jnp.sum(d_res, axis=0, keepdims=True)


def mlp(cot, mixed, x, wproj, w1, w2, vecs_a, vecs):
    tokens = x.shape[0]
    chunk = tokens // 7
    vm = pl.BlockSpec(memory_space=pltpu.VMEM)
    tile = pl.BlockSpec((chunk, D), lambda i: (i, 0))
    fixed = lambda *shape: pl.BlockSpec(shape, lambda i: (0, 0))
    return pl.pallas_call(
        mlp_kernel,
        grid=(7,),
        out_shape=[
            jax.ShapeDtypeStruct((tokens, D), BF16),
            jax.ShapeDtypeStruct((tokens, D), F32),
            jax.ShapeDtypeStruct((tokens, D), BF16),
            jax.ShapeDtypeStruct((D, FF), F32),
            jax.ShapeDtypeStruct((D, FF), F32),
            jax.ShapeDtypeStruct((D, D), F32),
            jax.ShapeDtypeStruct((8, FF), F32),
        ],
        in_specs=[tile] * 3 + [vm] * 5,
        out_specs=[tile] * 3 + [fixed(D, FF), fixed(D, FF), fixed(D, D), fixed(8, FF)],
        compiler_params=pltpu.CompilerParams(vmem_limit_bytes=VMEM_LIMIT),
        name="mlp",
    )(cot, mixed, x, wproj, w1, w2, vecs_a, vecs)


CHUNK = 192
LAST = 208


def split_float(values):
    high = values.astype(BF16)
    return high, (values - high.astype(F32)).astype(BF16)


def attend_back_kernel(
    part,
    order,
    q_ref,
    k_ref,
    v_ref,
    mixed_ref,
    d_mixed,
    probs,
    inverse,
    keys_back,
    query_tab,
    query_back,
    x_hbm,
    d_res_hbm,
    wqkv,
    vecs,
    blocks,
    out_src,
    g_bias,
    g_qkv,
    g_vec,
    dx_last,
    grad_ref,
    out_ref,
    dx_ref,
    d_query_t,
    d_key_value_t,
    d_qkv,
    d_in,
    x_buf,
    d_res_buf,
    load_sems,
    total,
    outgoing,
    arrived,
    send,
    recv,
    out_sem,
    out_send,
    out_recv,
    dx_sem0,
    dx_send0,
    dx_recv0,
    dx_sem1,
    dx_send1,
    dx_recv1,
    dx_sem2,
    dx_send2,
    dx_recv2,
):
    i = pl.program_id(0)
    steps = pl.num_programs(0)
    stages = len(order)
    dp, grp = lax.axis_index("dp"), lax.axis_index("grp")
    cube = CubeSum(order, blocks, total, outgoing, arrived, (send, recv))
    exchange = exchange_copies(out_src, out_ref, dp, grp, out_sem, out_send, out_recv)
    dx_sems = (
        (dx_sem0, dx_send0, dx_recv0),
        (dx_sem1, dx_send1, dx_recv1),
        (dx_sem2, dx_send2, dx_recv2),
    )
    loads = [
        pltpu.make_async_copy(x_hbm, x_buf, load_sems.at[0]),
        pltpu.make_async_copy(d_res_hbm, d_res_buf, load_sems.at[1]),
    ]

    def chunk(c):
        return chunk_copies(d_in, dx_ref, CHUNK * c, CHUNK, dp, grp, *dx_sems[c], 0)

    @pl.when(i == 0)
    def _():
        for c in loads:
            c.start()
        g_bias[...] = jnp.zeros_like(g_bias)
        g_qkv[...] = jnp.zeros_like(g_qkv)
        g_vec[...] = jnp.zeros_like(g_vec)
        greet(cube_partners(order, dp, grp) + [window_partner(dp, grp, 3)])

    starts = starts_of(stage_weights(order)[::-1], SUM_STEPS)
    for k, start in zip(reversed(range(stages)), starts):

        @pl.when(i == start)
        def _(k=k):
            if k < stages - 1:
                cube.finish(k + 1)
            cube.start(k)

    @pl.when(i == 0)
    def _():
        for c in exchange:
            c.start()

    dm_t = dot(query_tab[0], image_rows(d_mixed, i, slice(0, D))).T
    spread_heads = lambda ref: jnp.concatenate(
        [jnp.broadcast_to(ref[h : h + 1], (HDIM, 256)) for h in range(HEADS)], axis=0
    )
    dm_t = (dm_t * spread_heads(inverse[0])).astype(BF16)
    products = dm_t.astype(F32) * mixed_ref[0].astype(F32)
    q_t, k_t, v_ext = q_ref[0], k_ref[0], v_ref[0]

    def d_probs_of(h):
        heads = jnp.concatenate([only_head(dm_t, h), only_head(dm_t, h + 1)], axis=1)
        return dot(v_ext[:, tile_of(h)], heads)

    def softmax_back(d_probs, h):
        e = probs[0, h]
        own = slice(h * HDIM, (h + 1) * HDIM)
        sums = jnp.sum(products[own], axis=0, keepdims=True)
        halves = []
        for half in range(2):
            lanes = slice(128 * half, 128 * half + 128)
            e32 = e[:, lanes].astype(F32)[56 * half : 56 * half + KEYS]
            ds = e32 * (half_of(d_probs, half) - sums[:, lanes])
            g_bias[h, half] += ds
            halves.append(ds)
        return spread(halves)

    def gather_back(h, ds):
        own = slice(h * HDIM, (h + 1) * HDIM)
        d_query_t[own, :] = (dot(k_t[own, :], ds) * HDIM ** (-0.5)).astype(BF16)
        d_key_value_t[own, :] = dot_t(q_t[own, :], ds).astype(BF16)
        d_key_value_t[D + h * HDIM : D + (h + 1) * HDIM, :] = dot_t(
            dm_t[own, :], probs[0, h]
        ).astype(BF16)

    ahead = d_probs_of(0)
    waiting = []
    for h in range(0, HEADS, 2):
        now = ahead
        if h + 2 < HEADS:
            ahead = d_probs_of(h + 2)
        for c in range(2):
            waiting.append((h + c, softmax_back(now[:, c * 256 : (c + 1) * 256], h + c)))
        while len(waiting) > 1:
            gather_back(*waiting.pop(0))
    for last in waiting:
        gather_back(*last)
    put_image_rows(d_qkv, i, slice(0, D), dot_t(query_back[0], d_query_t[...]))
    put_image_rows(d_qkv, i, slice(D, 3 * D), dot_t(keys_back[0], d_key_value_t[...]))

    @pl.when(i == 3)
    def _():
        for c in loads:
            c.wait()

    @pl.when(lax.rem(i, 4) == 3)
    def _():
        c = i // 4
        at = pl.ds(pl.multiple_of(c * CHUNK, 16), LAST)
        xhat, scale = norm_parts(x_buf[:, at, :].reshape(4 * LAST, D).astype(F32))
        gain = vecs[0:1, :]
        normed = (xhat * gain + vecs[1:2, :]).astype(BF16)
        row = lax.rem(lax.broadcasted_iota(jnp.int32, (4 * LAST, 1), 0), LAST)
        counts = row < jnp.where(i == steps - 1, LAST, CHUNK)
        grads = d_qkv[:, at, :].reshape(4 * LAST, 3 * D)
        grads = jnp.where(counts, grads, 0)
        d_normed = dot_t(grads, wqkv[...])
        result = d_res_buf[:, at, :].reshape(4 * LAST, D) + norm_back(d_normed, xhat, scale, gain)
        result = result.astype(BF16).reshape(4, LAST, D)
        d_in[:, at, :] = result
        dx_last[...] = result
        g_qkv[...] += dot(normed.T, grads)
        g_vec[0:1, :] += jnp.sum(grads.astype(F32), axis=0, keepdims=True)
        g_vec[1:2, :D] += jnp.sum(d_normed * xhat, axis=0, keepdims=True)
        g_vec[2:3, :D] += jnp.sum(d_normed, axis=0, keepdims=True)

    for c in range(3):

        @pl.when(i == 4 * c + 3)
        def _(c=c):
            for copy in chunk(c):
                copy.start()

    @pl.when(i == steps - 1)
    def _():
        cube.finish(0)
        device = dp * lax.axis_size("grp") + grp
        grad_ref[...] = shift_lanes(total[0], part.lane(device), False)
        for c in exchange:
            c.wait()
        for c in range(3):
            for copy in chunk(c):
                copy.wait()


def attend_back(
    part, order, saved, d_mixed, probs, inverse, x, d_res, wqkv, vecs, blocks, out
):
    images = probs.shape[0]
    tokens = out.shape[0]
    rows = tokens // 4
    stages = len(order)
    _, query_tab, keys_back, query_back = gather_tables(images)
    vm = pl.BlockSpec(memory_space=pltpu.VMEM)
    hbm = pl.BlockSpec(memory_space=pl.ANY)
    image = lambda *shape: pl.BlockSpec((1, *shape), lambda i: (i, 0, 0))
    table = image(256, 256)
    by_window = lambda array: array.reshape(4, rows, -1)
    outs = pl.pallas_call(
        functools.partial(attend_back_kernel, part, order),
        grid=(images,),
        out_shape=[
            jax.ShapeDtypeStruct((HEADS, 2, KEYS, 128), F32),
            jax.ShapeDtypeStruct((D, 3 * D), F32),
            jax.ShapeDtypeStruct((8, 3 * D), F32),
            jax.ShapeDtypeStruct((4, LAST, D), BF16),
            jax.ShapeDtypeStruct((part.rows, 128), F32),
            jax.ShapeDtypeStruct((tokens, D), BF16),
            jax.ShapeDtypeStruct((4, rows, D), BF16),
        ],
        in_specs=[
            image(D, 256),
            image(D, 256),
            image(256, D),
            image(D, 256),
            vm,
            pl.BlockSpec((1, HEADS, 256, 256), lambda i: (i, 0, 0, 0)),
            image(16, 256),
        ]
        + [table] * 3
        + [hbm, hbm, vm, vm, vm, hbm],
        out_specs=[
            pl.BlockSpec((HEADS, 2, KEYS, 128), lambda i: (0, 0, 0, 0)),
            pl.BlockSpec((D, 3 * D), lambda i: (0, 0)),
            pl.BlockSpec((8, 3 * D), lambda i: (0, 0)),
            pl.BlockSpec((4, LAST, D), lambda i: (0, 0, 0)),
            pl.BlockSpec((part.rows, 128), lambda i: (0, 0)),
            hbm,
            hbm,
        ],
        scratch_shapes=[
            pltpu.VMEM((D, 256), BF16),
            pltpu.VMEM((2 * D, 256), BF16),
            pltpu.VMEM((4, rows, 3 * D), BF16),
            pltpu.VMEM((4, rows, D), BF16),
            pltpu.VMEM((4, rows, D), BF16),
            pltpu.VMEM((4, rows, D), F32),
            pltpu.SemaphoreType.DMA((2,)),
        ]
        + CubeSum.scratch(part.devices, part.rows, stages)
        + [
            pltpu.SemaphoreType.DMA,
            pltpu.SemaphoreType.DMA((3,)),
            pltpu.SemaphoreType.DMA((3,)),
        ]
        * 4,
        compiler_params=pltpu.CompilerParams(
            collective_id=3, has_side_effects=True, vmem_limit_bytes=VMEM_LIMIT
        ),
        name="attend_back",
    )(
        *saved,
        by_window(d_mixed),
        probs,
        inverse,
        keys_back,
        query_tab,
        query_back,
        by_window(x),
        by_window(d_res),
        wqkv,
        vecs,
        blocks,
        out,
    )
    grad = outs[4].reshape(-1)[: part.length]
    return (*outs[:4], grad, *outs[5:])


def to_blocks(part, places, flat, out):
    for device, place in enumerate(places):
        at = part.start(device)
        out[place] = flat[at : at + part.rows, :].astype(BF16)


def pack_mlp_kernel(part, places, g_w1, g_w2t, g_vec, out, flat):
    flat[...] = jnp.zeros_like(flat)
    put_matrix(flat, 0, g_w1)
    for j in range(3):
        flat[pl.ds(4608 + j, FF, stride=3), :] = g_w2t[j * 128 : (j + 1) * 128, :].T
    for j in range(12):
        flat[9216 + j : 9217 + j, :] = g_vec[0:1, j * 128 : (j + 1) * 128]
    for v in range(3):
        for j in range(3):
            at = 9228 + 3 * v + j
            flat[at : at + 1, :] = g_vec[1 + v : 2 + v, j * 128 : (j + 1) * 128]
    to_blocks(part, places, flat, out)


def pack_mlp(part, places, g_w1, g_w2t, g_vec):
    vm = pl.BlockSpec(memory_space=pltpu.VMEM)
    return pl.pallas_call(
        functools.partial(pack_mlp_kernel, part, places),
        out_shape=jax.ShapeDtypeStruct((part.devices, part.rows, 128), BF16),
        in_specs=[vm] * 3,
        out_specs=vm,
        scratch_shapes=[pltpu.VMEM((part.buffer, 128), F32)],
        compiler_params=pltpu.CompilerParams(vmem_limit_bytes=VMEM_LIMIT),
        name="pack_mlp",
    )(g_w1, g_w2t, g_vec)


def pack_kernel(
    part,
    places,
    one_fine,
    one_coarse,
    g_bias,
    g_qkv,
    g_vec1,
    g_proj,
    g_vec2,
    out,
    flat,
    table,
    shifted,
    line,
):
    flat[...] = jnp.zeros_like(flat)
    put_matrix(flat, 0, g_qkv)
    put_matrix(flat, 3456, g_proj)
    vectors = [
        g_vec1[1:2, :D],
        g_vec1[2:3, :D],
        g_vec1[0:1, :D],
        g_vec1[0:1, 2 * D :],
        g_vec2[4:5, :D],
    ]
    pieces = [v[:, j * 128 : (j + 1) * 128] for v in vectors for j in range(3)]
    pieces += [jnp.zeros((1, 128), F32)]
    row, lane = divmod(ATTN_VECTORS[0], 128)
    flat[row : row + 16, :] += shift_lanes(jnp.concatenate(pieces, axis=0), lane, True)
    for h in range(HEADS):
        table[...] = jnp.zeros_like(table)
        for half in range(2):
            turned = g_bias[h, half].T
            for y in range(WIN):
                for at, length, source in bias_runs(half, WIN * half + y):
                    table[0:14, source : source + length] += turned[
                        y * 14 : y * 14 + 14, at : at + length
                    ]
        for c in range(4):
            shifted[c, pl.ds(h, 14, stride=16), :] = table[0:14, c * 128 : (c + 1) * 128]
    high, low = split_float(jnp.concatenate([shifted[c] for c in range(3)], axis=1))
    moved_fine = dot_t(high, one_fine[...]) + dot_t(low, one_fine[...])
    high, low = split_float(shifted[3])
    moved_coarse = dot_t(high, one_coarse[...]) + dot_t(low, one_coarse[...])
    g_fine = jnp.zeros((16, 384), F32)
    g_coarse = jnp.zeros((16, 256), F32)
    for qx in range(14):
        at = slice(qx * 16, qx * 16 + 16)
        g_fine += pltpu.roll(moved_fine[at], (384 - qx) % 384, 1)
        g_coarse += pltpu.roll(moved_coarse[at], (256 - qx // 2) % 256, 1)
    for t, h, length, row, lane, count in table_lines():
        line[...] = jnp.zeros_like(line)
        line[0:1, lane : lane + length] = (g_fine, g_coarse)[t][h : h + 1, :length]
        for c in range(count):
            flat[row + c : row + c + 1, :] += line[0:1, c * 128 : (c + 1) * 128]
    to_blocks(part, places, flat, out)


def pack(part, places, g_bias, g_qkv, g_vec1, g_proj, g_vec2):
    fine, coarse, _ = bias_tables()
    vm = pl.BlockSpec(memory_space=pltpu.VMEM)
    return pl.pallas_call(
        functools.partial(pack_kernel, part, places),
        out_shape=jax.ShapeDtypeStruct((part.devices, part.rows, 128), BF16),
        in_specs=[vm] * 7,
        out_specs=vm,
        scratch_shapes=[
            pltpu.VMEM((part.buffer, 128), F32),
            pltpu.VMEM((16, 512), F32),
            pltpu.VMEM((4, 14 * 16, 128), F32),
            pltpu.VMEM((8, 512), F32),
        ],
        compiler_params=pltpu.CompilerParams(vmem_limit_bytes=VMEM_LIMIT),
        name="pack",
    )(jnp.asarray(fine), jnp.asarray(coarse), g_bias, g_qkv, g_vec1, g_proj, g_vec2)


def adamw(master, first, second, grads):
    first_new = beta_one * first + (1.0 - beta_one) * grads
    second_new = beta_two * second + (1.0 - beta_two) * grads * grads
    first_hat = first_new / (1.0 - beta_one**STEP)
    second_hat = second_new / (1.0 - beta_two**STEP)
    master_new = master - learn_rate * (
        first_hat / (jnp.sqrt(second_hat) + adam_eps) + decay_rate * master
    )
    return (first_new, second_new, master_new)


def body(
    tokens, cotangent, attn_master, attn_first, attn_second, mlp_master, mlp_first, mlp_second
):
    n_dp, n_grp = lax.axis_size("dp"), lax.axis_size("grp")
    order = bit_order(n_dp, n_grp)
    places = place_list(order, n_dp, n_grp)
    part_a = Part(n_dp * n_grp, attn_master.shape[0])
    part_b = Part(n_dp * n_grp, mlp_master.shape[0])
    images = tokens.shape[1] // 4 // SEQ
    blocks_a, x = gather_params(part_a, order, attn_master, tokens[0])
    wqkv, wproj, vecs_a, bias = prepare(part_a, places, blocks_a)
    mixed, probs, *saved, inverse, cot, blocks_b = attend(
        part_b, order, x, cotangent[0], mlp_master, wqkv, vecs_a, bias, images
    )
    mixed = mixed.reshape(-1, D)
    w1, w2, vecs_b = prepare_mlp(part_b, places, blocks_b)
    out, d_res, d_mixed, g_w1, g_w2t, g_proj, g_vec2 = mlp(
        cot, mixed, x, wproj, w1, w2, vecs_a, vecs_b
    )
    sums_b = pack_mlp(part_b, places, g_w1, g_w2t, g_vec2)
    g_bias, g_qkv, g_vec1, dx_last, grad_b, output, dx = attend_back(
        part_b,
        order,
        saved,
        d_mixed,
        probs,
        inverse,
        x,
        d_res,
        wqkv,
        vecs_a,
        sums_b,
        out,
    )
    sums_a = pack(part_a, places, g_bias, g_qkv, g_vec1, g_proj, g_vec2)
    grad_a, dx = sum_grads(part_a, order, sums_a, dx_last, dx)
    attn_new = adamw(attn_master, attn_first, attn_second, grad_a)
    mlp_new = adamw(mlp_master, mlp_first, mlp_second, grad_b)
    input_grad = dx.reshape(-1, D).astype(F32)
    return (output[None], input_grad[None], *attn_new, *mlp_new)


def solution(mesh):
    flat_spec = P(("dp", "grp"))
    token_spec = P("dp", "grp", None)
    placed = (token_spec, token_spec) + (flat_spec,) * 6
    return jax.shard_map(
        body, mesh=mesh, in_specs=placed, out_specs=placed, check_vma=False
    )
```

```python
import functools

import jax
import jax.numpy as jnp
import ml_dtypes
import numpy as np
from jax import lax
from jax.experimental import pallas as pl
from jax.experimental.pallas import tpu as pltpu
from jax.sharding import PartitionSpec as P

D = 384
HEADS = 12
HDIM = 32
FF = 1536
WIN = 7
STEP = 10
SEQ = WIN * WIN
HALF = 64
FINE = (3 * WIN - 2) ** 2
COARSE = (2 * WIN - 1) ** 2
KEYS = 192

beta_one = 0.9
beta_two = 0.999
learn_rate = 0.04
decay_rate = 0.05
adam_eps = 1e-08
norm_eps = 1e-05
masked_score = -1e30

F32 = jnp.float32
BF16 = jnp.bfloat16
MESH = pl.DeviceIdType.MESH
VMEM_LIMIT = 56 * 2**20


def token_place(gy, gx):
    window = 2 * (gy // WIN) + gx // WIN
    return window * HALF + (gy % WIN) * WIN + gx % WIN


@functools.cache
def gather_tables(images):
    keys = np.zeros((images, 256, 256), np.float32)
    queries = np.zeros((images, 256, 256), np.float32)
    for i in range(images):
        for gy in range(2 * WIN):
            for gx in range(2 * WIN):
                at = token_place(gy, gx) + i
                key = gy * 14 + gx if gy < 10 else 192 + (gy - 10) * 14 + gx
                keys[i, key, at] = 1.0
                keys[i, 140 + (gy // 2) * WIN + gx // 2, at] = 0.25
                queries[i, (gy // WIN) * 128 + (gy % WIN) * 14 + gx, at] = 1.0
    return (
        keys.astype(ml_dtypes.bfloat16),
        queries.astype(ml_dtypes.bfloat16),
        np.ascontiguousarray(keys.transpose(0, 2, 1)).astype(ml_dtypes.bfloat16),
        np.ascontiguousarray(queries.transpose(0, 2, 1)).astype(ml_dtypes.bfloat16),
    )


@functools.cache
def bias_tables():
    fine = np.zeros((384, 384), np.float32)
    coarse = np.zeros((256, 128), np.float32)
    for a in range(4, 23):
        for kx in range(14):
            fine[19 * (a - 4) + kx + 9, a * 14 + kx] = 1.0
    for p in range(13):
        for x in range(WIN):
            coarse[13 * p + x + 6, p * WIN + x] = 1.0
    mask = np.zeros((2, KEYS, 128), np.float32)
    for half in range(2):
        for q in range(98):
            qx = q % 14
            for e in range(KEYS):
                at = e + 56 * half
                if at < 140:
                    ok = abs_ok(qx, at % 14)
                elif at < 189:
                    ok = True
                elif at < 192:
                    ok = False
                else:
                    ok = at < 248 and abs_ok(qx, (at - 192) % 14)
                mask[half, e, q] = 0.0 if ok else masked_score
    return fine.astype(ml_dtypes.bfloat16), coarse.astype(ml_dtypes.bfloat16), mask


def abs_ok(qx, kx):
    return kx < 10 if qx < WIN else kx >= 4


def bias_runs(half, qy):
    fine = (13 - qy) * 14
    pool = 384 + (6 - qy // 2) * WIN
    if half == 0:
        return [(0, 140, fine), (140, 49, pool)]
    return [(0, 84, fine + 56), (84, 49, pool), (136, 56, fine + 140)]


class Part:
    def __init__(self, devices, length):
        self.devices = devices
        self.length = length
        self.rows = -(-((length + 126) // 128 + 1) // 16) * 16
        self.buffer = -(-(self.start(devices - 1) + self.rows) // 8) * 8

    def start(self, device):
        return device * self.length // 128

    def lane(self, device):
        return lax.rem(device * self.length, 128)

    def padded(self, vector):
        extra = self.rows * 128 - self.length
        return jnp.pad(vector, (0, extra)).reshape(self.rows, 128)


GATHER_STEPS = 12
SUM_STEPS = 15


def bit_order(n_dp, n_grp):
    dp_bits = [("dp", 2**b) for b in range(n_dp.bit_length() - 1)]
    grp_bits = [("grp", 2**b) for b in reversed(range(n_grp.bit_length() - 1))]
    return dp_bits[1:2] + grp_bits + dp_bits[2:] + dp_bits[:1]


def stage_weights(order):
    weights = []
    for k, (axis, stride) in enumerate(order):
        relative = 0.35 if (axis, stride) == ("dp", 1) else 2 if (axis == "grp" and stride > 1) else 1
        weights.append(relative * 2**k)
    return weights


def starts_of(weights, steps):
    done, starts = 0.0, []
    for weight in weights:
        starts.append(min(int(np.ceil(steps * done / sum(weights))), steps - 1))
        done += weight
    return starts


def place_of(order, dp, grp):
    place = 0
    for k, (axis, stride) in enumerate(order):
        place = place + ((dp if axis == "dp" else grp) // stride) % 2 * 2**k
    return place


def partner_of(axis, stride, dp, grp):
    if axis == "dp":
        return (dp + (1 - 2 * ((dp // stride) % 2)) * stride, grp)
    return (dp, grp + (1 - 2 * ((grp // stride) % 2)) * stride)


def greet(partners):
    barrier = pltpu.get_barrier_semaphore()
    for partner in partners:
        pl.semaphore_signal(barrier, inc=1, device_id=partner, device_id_type=MESH)
    pl.semaphore_wait(barrier, len(partners))


def cube_partners(order, dp, grp):
    return [partner_of(axis, stride, dp, grp) for axis, stride in order]


def shift_lanes(values, amount, up):
    lane = lax.broadcasted_iota(jnp.int32, values.shape, 1)
    if up:
        turned = pltpu.roll(values, amount, 1)
        return jnp.where(lane >= amount, turned, pltpu.roll(turned, 1, 0))
    turned = pltpu.roll(values, lax.rem(128 - amount, 128), 1)
    return jnp.where(lane < 128 - amount, turned, pltpu.roll(turned, values.shape[0] - 1, 0))


def window_partner(dp, grp, k):
    low, high = dp % 2, dp // 2 % 2
    to = dp
    if k % 2:
        to = to + 1 - 2 * low
    if k // 2:
        to = to + 2 * (1 - 2 * high)
    return (to, grp)


def exchange_copies(source, target, dp, grp, own_sem, send_sems, recv_sems):
    rows = source.shape[0] // 4
    slot = dp % 4
    mine = pl.ds(pl.multiple_of(slot * rows, 16), rows)
    own = pltpu.make_async_copy(source.at[mine], target.at[mine], own_sem)
    sends = []
    for k in (3, 2, 1):
        to, _ = window_partner(dp, grp, k)
        theirs = pl.ds(pl.multiple_of(to % 4 * rows, 16), rows)
        sends.append(
            pltpu.make_async_remote_copy(
                src_ref=source.at[theirs],
                dst_ref=target.at[mine],
                send_sem=send_sems.at[k - 1],
                recv_sem=recv_sems.at[k - 1],
                device_id=(to, grp),
                device_id_type=MESH,
            )
        )
    return [own] + sends


def cube_copy(order, k, source, target, dp, grp, send_sems, recv_sems):
    axis, stride = order[k]
    return pltpu.make_async_remote_copy(
        src_ref=source,
        dst_ref=target,
        send_sem=send_sems.at[k],
        recv_sem=recv_sems.at[k],
        device_id=partner_of(axis, stride, dp, grp),
        device_id_type=MESH,
    )


def gather_copy(order, k, blocks, dp, grp, sems):
    place = place_of(order, dp, grp)
    held = blocks.at[pl.ds(place // 2**k * 2**k, 2**k)]
    return cube_copy(order, k, held, held, dp, grp, *sems)


class CubeSum:
    def __init__(self, order, blocks, total, outgoing, arrived, sems):
        self.order, self.blocks, self.total = order, blocks, total
        self.outgoing, self.arrived, self.sems = outgoing, arrived, sems
        self.dp, self.grp = lax.axis_index("dp"), lax.axis_index("grp")
        self.place = place_of(order, self.dp, self.grp)
        self.last = len(order) - 1

    def mine(self, k):
        return self.place // 2**k % 2 * 2**k

    def copy(self, k):
        size = 2**k
        if k == self.last:
            source = self.blocks.at[pl.ds(size - self.mine(k), size)]
        else:
            source = self.outgoing.at[pl.ds(size, size)]
        target = self.arrived.at[pl.ds(size, size)]
        return cube_copy(self.order, k, source, target, self.dp, self.grp, *self.sems)

    def start(self, k):
        size = 2**k
        if k < self.last:
            other = size - self.mine(k)

            def fill(j, carry):
                self.outgoing[size + j] = self.total[other + j].astype(BF16)
                return carry

            lax.fori_loop(0, size, fill, 0)
        self.copy(k).start()

    def finish(self, k):
        size, mine = 2**k, self.mine(k)
        self.copy(k).wait()

        def add(j, carry):
            if k == self.last:
                held = self.blocks[mine + j].astype(F32)
            else:
                held = self.total[mine + j]
            self.total[j] = held + self.arrived[size + j].astype(F32)
            return carry

        lax.fori_loop(0, size, add, 0)

    @staticmethod
    def scratch(devices, rows, stages):
        return [
            pltpu.VMEM((devices // 2, rows, 128), F32),
            pltpu.VMEM((devices // 2, rows, 128), BF16),
            pltpu.VMEM((devices, rows, 128), BF16),
            pltpu.SemaphoreType.DMA((stages,)),
            pltpu.SemaphoreType.DMA((stages,)),
        ]


def chunk_copies(source, target, first, size, dp, grp, own_sem, send_sems, recv_sems, skip):
    slot = dp % 4
    into = target.at[slot, pl.ds(first, size)]
    rows = pl.ds(first - skip, size)
    copies = [pltpu.make_async_copy(source.at[slot, rows], into, own_sem)]
    for k in (3, 2, 1):
        to, _ = window_partner(dp, grp, k)
        copies.append(
            pltpu.make_async_remote_copy(
                src_ref=source.at[to % 4, rows],
                dst_ref=into,
                send_sem=send_sems.at[k - 1],
                recv_sem=recv_sems.at[k - 1],
                device_id=(to, grp),
                device_id_type=MESH,
            )
        )
    return copies


def sum_kernel(
    part,
    order,
    blocks,
    last_ref,
    dx_ref,
    grad_ref,
    dx_out,
    total,
    outgoing,
    arrived,
    send,
    recv,
    x_sem,
    x_send,
    x_recv,
):
    dp, grp = lax.axis_index("dp"), lax.axis_index("grp")
    greet(cube_partners(order, dp, grp) + [window_partner(dp, grp, 3)])
    cube = CubeSum(order, blocks, total, outgoing, arrived, (send, recv))
    first = dx_ref.shape[1] - last_ref.shape[1]
    exchange = chunk_copies(
        last_ref, dx_out, first, last_ref.shape[1], dp, grp, x_sem, x_send, x_recv, first
    )
    for k in reversed(range(len(order))):
        cube.start(k)
        if k == len(order) - 1:
            for c in exchange:
                c.start()
        cube.finish(k)
    device = dp * lax.axis_size("grp") + grp
    grad_ref[...] = shift_lanes(total[0], part.lane(device), False)
    for c in exchange:
        c.wait()


def sum_grads(part, order, blocks, last, dx):
    stages = len(order)
    hbm = pl.BlockSpec(memory_space=pl.ANY)
    vm = pl.BlockSpec(memory_space=pltpu.VMEM)
    grad, dx = pl.pallas_call(
        functools.partial(sum_kernel, part, order),
        out_shape=[
            jax.ShapeDtypeStruct((part.rows, 128), F32),
            jax.ShapeDtypeStruct(dx.shape, dx.dtype),
        ],
        in_specs=[vm, hbm, hbm],
        out_specs=[vm, hbm],
        input_output_aliases={2: 1},
        scratch_shapes=CubeSum.scratch(part.devices, part.rows, stages)
        + [
            pltpu.SemaphoreType.DMA,
            pltpu.SemaphoreType.DMA((3,)),
            pltpu.SemaphoreType.DMA((3,)),
        ],
        compiler_params=pltpu.CompilerParams(
            collective_id=1, has_side_effects=True, vmem_limit_bytes=VMEM_LIMIT
        ),
        name="sum_grads",
    )(blocks, last, dx)
    return grad.reshape(-1)[: part.length], dx


def place_list(order, n_dp, n_grp):
    return [place_of(order, d // n_grp, d % n_grp) for d in range(n_dp * n_grp)]


ATTN_VECTORS = (D * 3 * D + D * D + HEADS * FINE + HEADS * COARSE, 5)
TABLE_AT = D * 3 * D + D * D


def unflatten(part, places, blocks, flat):
    for device, place in enumerate(places):
        at = part.start(device)
        block = blocks[place].astype(F32)
        first = block[0:1] + flat[at : at + 1, :] if device else block[0:1]
        flat[at : at + part.rows, :] = block
        flat[at : at + 1, :] = first


def take_matrix(flat, first, target):
    rows, columns = target.shape
    count = columns // 128
    for j in range(count):
        target[:, j * 128 : (j + 1) * 128] = flat[pl.ds(first + j, rows, stride=count), :].astype(
            target.dtype
        )


def put_matrix(flat, first, source):
    rows, columns = source.shape
    count = columns // 128
    for j in range(count):
        flat[pl.ds(first + j, rows, stride=count), :] = source[:, j * 128 : (j + 1) * 128]


TABLES = ((TABLE_AT, FINE), (TABLE_AT + HEADS * FINE, COARSE))


def table_lines():
    for t, (first, length) in enumerate(TABLES):
        for h in range(HEADS):
            row, lane = divmod(first + h * length, 128)
            yield t, h, length, row, lane, -(-(lane + length) // 128)


def prepare(
    part, places, blocks, one_fine, one_coarse, mask_ref,
    wqkv, wproj, vecs, bias, flat, tab_fine, tab_coarse, shifted, turned,
):
    unflatten(part, places, blocks, flat)
    take_matrix(flat, 0, wqkv)
    take_matrix(flat, 3456, wproj)
    row, lane = divmod(ATTN_VECTORS[0], 128)
    rows = shift_lanes(flat[row : row + 16, :], lane, False)
    for v in range(5):
        for j in range(3):
            vecs[v : v + 1, j * 128 : (j + 1) * 128] = rows[3 * v + j : 3 * v + j + 1]
    tab_fine[...] = jnp.zeros_like(tab_fine)
    tab_coarse[...] = jnp.zeros_like(tab_coarse)
    for t, h, length, row, lane, count in table_lines():
        line = jnp.concatenate([flat[row + c : row + c + 1, :] for c in range(count)], axis=1)
        (tab_fine, tab_coarse)[t][h : h + 1, 0:length] = line[:, lane : lane + length]
    fine, coarse = tab_fine[...], tab_coarse[...]
    fine = jnp.concatenate([pltpu.roll(fine, qx, 1) for qx in range(14)], axis=0)
    coarse = jnp.concatenate([pltpu.roll(coarse, qx // 2, 1) for qx in range(14)], axis=0)
    fine = dot(fine.astype(BF16), one_fine[...])
    for c in range(3):
        shifted[c] = fine[:, c * 128 : (c + 1) * 128]
    shifted[3] = dot(coarse.astype(BF16), one_coarse[...])
    turned[...] = jnp.zeros_like(turned)
    for h in range(HEADS):
        table = jnp.concatenate(
            [shifted[c, pl.ds(h, 14, stride=16), :] for c in range(4)], axis=1
        )
        for half in range(2):
            for y in range(WIN):
                for at, length, source in bias_runs(half, WIN * half + y):
                    turned[half, y * 14 : y * 14 + 14, at : at + length] = table[
                        :, source : source + length
                    ]
            bias[h, half] = turned[half].T[0:KEYS] + mask_ref[half]


def early_stages(order):
    return 1 + sum(axis == "grp" for axis, _ in order)


def gather_kernel(
    part_a,
    part_b,
    order,
    places,
    a_ref,
    b_ref,
    one_fine,
    one_coarse,
    mask_ref,
    tok_ref,
    wqkv,
    wproj,
    vecs,
    bias,
    x_ref,
    blocks_b,
    blocks_a,
    own,
    flat,
    tab_fine,
    tab_coarse,
    shifted,
    turned,
    own_sem,
    send_a,
    recv_a,
    send_b,
    recv_b,
    x_sem,
    x_send,
    x_recv,
):
    dp, grp = lax.axis_index("dp"), lax.axis_index("grp")
    place = place_of(order, dp, grp)
    device = dp * lax.axis_size("grp") + grp
    own[...] = shift_lanes(b_ref[...], part_b.lane(device), True).astype(BF16)
    copy = pltpu.make_async_copy(own, blocks_b.at[place], own_sem)
    copy.start()
    blocks_a[place] = shift_lanes(a_ref[...], part_a.lane(device), True).astype(BF16)
    vecs[...] = jnp.zeros_like(vecs)
    greet(cube_partners(order, dp, grp) + [window_partner(dp, grp, 3)])
    copy.wait()
    exchange = exchange_copies(tok_ref, x_ref, dp, grp, x_sem, x_send, x_recv)
    first = [
        gather_copy(order, k, blocks_a, dp, grp, (send_a, recv_a)) for k in range(len(order))
    ]
    early = early_stages(order)
    second = [gather_copy(order, k, blocks_b, dp, grp, (send_b, recv_b)) for k in range(early)]
    for k, stage in enumerate(first):
        stage.start()
        if k == 0:
            second[0].start()
            for c in exchange:
                c.start()
        if early <= k < 2 * early:
            second[k - early].wait()
            if k - early + 1 < early:
                second[k - early + 1].start()
        stage.wait()
    prepare(
        part_a, places, blocks_a, one_fine, one_coarse, mask_ref,
        wqkv, wproj, vecs, bias, flat, tab_fine, tab_coarse, shifted, turned,
    )
    for k in range(len(order) - early, early):
        second[k].wait()
        if k + 1 < early:
            second[k + 1].start()
    for c in exchange:
        c.wait()


def gather_params(part_a, part_b, order, places, master_a, master_b, tok):
    stages = len(order)
    early = early_stages(order)
    fine, coarse, mask = bias_tables()
    vm = pl.BlockSpec(memory_space=pltpu.VMEM)
    hbm = pl.BlockSpec(memory_space=pl.ANY)
    return pl.pallas_call(
        functools.partial(gather_kernel, part_a, part_b, order, places),
        out_shape=[
            jax.ShapeDtypeStruct((D, 3 * D), BF16),
            jax.ShapeDtypeStruct((D, D), BF16),
            jax.ShapeDtypeStruct((8, D), F32),
            jax.ShapeDtypeStruct((HEADS, 2, KEYS, 128), F32),
            jax.ShapeDtypeStruct(tok.shape, BF16),
            jax.ShapeDtypeStruct((part_b.devices, part_b.rows, 128), BF16),
        ],
        in_specs=[vm] * 5 + [hbm],
        out_specs=[vm] * 4 + [hbm] * 2,
        scratch_shapes=[
            pltpu.VMEM((part_a.devices, part_a.rows, 128), BF16),
            pltpu.VMEM((part_b.rows, 128), BF16),
            pltpu.VMEM((part_a.buffer, 128), F32),
            pltpu.VMEM((16, 384), F32),
            pltpu.VMEM((16, 256), F32),
            pltpu.VMEM((4, 14 * 16, 128), F32),
            pltpu.VMEM((2, 128, 256), F32),
            pltpu.SemaphoreType.DMA,
            pltpu.SemaphoreType.DMA((stages,)),
            pltpu.SemaphoreType.DMA((stages,)),
            pltpu.SemaphoreType.DMA((early,)),
            pltpu.SemaphoreType.DMA((early,)),
            pltpu.SemaphoreType.DMA,
            pltpu.SemaphoreType.DMA((3,)),
            pltpu.SemaphoreType.DMA((3,)),
        ],
        compiler_params=pltpu.CompilerParams(
            collective_id=0, has_side_effects=True, vmem_limit_bytes=VMEM_LIMIT
        ),
        name="gather_params",
    )(
        part_a.padded(master_a),
        part_b.padded(master_b),
        jnp.asarray(fine),
        jnp.asarray(coarse),
        jnp.asarray(mask),
        tok,
    )


def dot(a, b):
    return jnp.dot(a, b, preferred_element_type=F32)


def dot_t(a, b):
    return lax.dot_general(a, b, (((1,), (1,)), ((), ())), preferred_element_type=F32)


def norm_parts(values):
    centered = values - jnp.mean(values, axis=-1, keepdims=True)
    scale = lax.rsqrt(jnp.mean(centered * centered, axis=-1, keepdims=True) + norm_eps)
    return centered * scale, scale


def norm_back(d_normed, xhat, scale, gain):
    dh = d_normed * gain
    return scale * (
        dh
        - jnp.mean(dh, axis=-1, keepdims=True)
        - xhat * jnp.mean(dh * xhat, axis=-1, keepdims=True)
    )


def image_rows(ref, i, columns):
    at = pl.ds(pl.multiple_of(48 * i, 16), HALF)
    return jnp.concatenate([ref[w, at, columns] for w in range(4)], axis=0)


def put_image_rows(ref, i, columns, values):
    for w in range(4):
        part = values[w * HALF : (w + 1) * HALF]
        first = pl.ds(pl.multiple_of(48 * i, 16), 16)
        rest = pl.ds(pl.multiple_of(48 * i + 16, 16), HALF - 16)
        held = jnp.where(i > 0, ref[w, first, columns].astype(F32), 0.0)
        ref[w, first, columns] = (held + part[:16]).astype(ref.dtype)
        ref[w, rest, columns] = part[16:].astype(ref.dtype)


def spread(halves):
    columns = []
    for half, values in enumerate(halves):
        pieces = [values, jnp.zeros((64 - 56 * half, 128), F32)]
        if half:
            pieces = [jnp.zeros((56, 128), F32)] + pieces
        columns.append(jnp.concatenate(pieces, axis=0))
    return jnp.concatenate(columns, axis=1).astype(BF16)


def only_head(turned, h):
    pieces = [jnp.zeros((HDIM, 256), BF16)] * 4
    pieces[h % 4] = turned[h * HDIM : (h + 1) * HDIM, :]
    return jnp.concatenate(pieces, axis=0)


def half_of(values, half):
    return values[56 * half : 56 * half + KEYS, 128 * half : 128 * half + 128]


def tile_of(h):
    return slice(h // 4 * 128, h // 4 * 128 + 128)


def attend_kernel(
    rows,
    order,
    x_buf,
    cot_ref,
    blocks_in,
    wqkv,
    vecs,
    bias,
    keys_tab,
    query_tab,
    query_back,
    mixed,
    probs,
    query_out,
    key_out,
    value_out,
    mixed_out,
    inverse,
    cot_out,
    blocks,
    normed,
    qkv,
    send,
    recv,
    cot_sem,
    cot_send,
    cot_recv,
):
    i = pl.program_id(0)
    steps = pl.num_programs(0)
    dp, grp = lax.axis_index("dp"), lax.axis_index("grp")
    exchange = exchange_copies(cot_ref, cot_out, dp, grp, cot_sem, cot_send, cot_recv)
    early = early_stages(order)
    late = [
        gather_copy(order, k, blocks, dp, grp, (send, recv)) for k in range(early, len(order))
    ]

    @pl.when(i == 0)
    def _():
        greet(cube_partners(order, dp, grp) + [window_partner(dp, grp, 3)])

    for k, start in enumerate(starts_of(stage_weights(order)[early:], GATHER_STEPS)):

        @pl.when(i == start)
        def _(k=k):
            if k:
                late[k - 1].wait()
            late[k].start()

    @pl.when(i == 0)
    def _():
        for c in exchange:
            c.start()

        step = rows // 7

        def norm(w):
            for c in range(7):
                at = slice(c * step, (c + 1) * step)
                xhat, _ = norm_parts(x_buf[w, at, :].astype(F32))
                normed[w % 2, at, :] = (xhat * vecs[0:1, :] + vecs[1:2, :]).astype(BF16)

        norm(0)
        for w in range(4):
            q = dot(normed[w % 2], wqkv[:, :D]) + vecs[2:3, :]
            qkv[w, :, :D] = (q * HDIM ** (-0.5)).astype(BF16)
            if w < 3:
                norm(w + 1)
            qkv[w, :, D : 2 * D] = dot(normed[w % 2], wqkv[:, D : 2 * D]).astype(BF16)
            v = dot(normed[w % 2], wqkv[:, 2 * D :]) + vecs[3:4, :]
            qkv[w, :, 2 * D :] = v.astype(BF16)

    q_ext = dot(query_tab[0], image_rows(qkv, i, slice(0, D)))
    kv_ext = dot(keys_tab[0], image_rows(qkv, i, slice(D, 3 * D)))
    q_t = q_ext.T.astype(BF16)
    k_ext = kv_ext[:, :D].astype(BF16)
    v_t = kv_ext[:, D:].T.astype(BF16)
    query_out[0] = q_t
    key_out[0] = kv_ext[:, :D].T.astype(BF16)
    value_out[0] = kv_ext[:, D:].astype(BF16)
    inverse[0, HEADS:16, :] = jnp.zeros((16 - HEADS, 256), F32)

    def scores_of(h):
        heads = jnp.concatenate([only_head(q_t, h), only_head(q_t, h + 1)], axis=1)
        return dot(k_ext[:, tile_of(h)], heads)

    def softmax(scores, h):
        halves, inverses = [], []
        for half in range(2):
            s = half_of(scores, half) + bias[h, half]
            e = jnp.exp(s - jnp.max(s, axis=0, keepdims=True))
            inverses.append(1.0 / jnp.sum(e, axis=0, keepdims=True))
            halves.append(e)
        e = spread(halves)
        inv = jnp.concatenate(inverses, axis=1)
        probs[0, h] = e
        inverse[0, h : h + 1, :] = inv
        return e, inv

    def mix(h, e, inv):
        own = slice(h * HDIM, (h + 1) * HDIM)
        mixed_out[0, own, :] = (dot(v_t[own, :], e) * inv).astype(BF16)

    ahead = scores_of(0)
    waiting = []
    for h in range(0, HEADS, 2):
        now = ahead
        if h + 2 < HEADS:
            ahead = scores_of(h + 2)
        for c in range(2):
            waiting.append((h + c, *softmax(now[:, c * 256 : (c + 1) * 256], h + c)))
        while len(waiting) > 1:
            mix(*waiting.pop(0))
    for last in waiting:
        mix(*last)
    put_image_rows(mixed, i, slice(0, D), dot_t(query_back[0], mixed_out[0]))

    @pl.when(i == steps - 1)
    def _():
        late[-1].wait()
        for c in exchange:
            c.wait()


def attend(order, x, cot, blocks, wqkv, vecs, bias, images):
    tokens = x.shape[0]
    stages = len(order)
    rows = tokens // 4
    keys_tab, query_tab, _, query_back = gather_tables(images)
    vm = pl.BlockSpec(memory_space=pltpu.VMEM)
    hbm = pl.BlockSpec(memory_space=pl.ANY)
    image = lambda *shape: pl.BlockSpec((1, *shape), lambda i: (i, 0, 0))
    table = image(256, 256)
    return pl.pallas_call(
        functools.partial(attend_kernel, rows, order),
        grid=(images,),
        out_shape=[
            jax.ShapeDtypeStruct((4, rows, D), BF16),
            jax.ShapeDtypeStruct((images, HEADS, 256, 256), BF16),
            jax.ShapeDtypeStruct((images, D, 256), BF16),
            jax.ShapeDtypeStruct((images, D, 256), BF16),
            jax.ShapeDtypeStruct((images, 256, D), BF16),
            jax.ShapeDtypeStruct((images, D, 256), BF16),
            jax.ShapeDtypeStruct((images, 16, 256), F32),
            jax.ShapeDtypeStruct((tokens, D), BF16),
            jax.ShapeDtypeStruct(blocks.shape, BF16),
        ],
        in_specs=[vm, hbm, hbm] + [vm] * 3 + [table] * 3,
        out_specs=[
            pl.BlockSpec((4, rows, D), lambda i: (0, 0, 0)),
            pl.BlockSpec((1, HEADS, 256, 256), lambda i: (i, 0, 0, 0)),
            image(D, 256),
            image(D, 256),
            image(256, D),
            image(D, 256),
            image(16, 256),
            hbm,
            hbm,
        ],
        scratch_shapes=[
            pltpu.VMEM((2, rows, D), BF16),
            pltpu.VMEM((4, rows, 3 * D), BF16),
            pltpu.SemaphoreType.DMA((stages,)),
            pltpu.SemaphoreType.DMA((stages,)),
            pltpu.SemaphoreType.DMA,
            pltpu.SemaphoreType.DMA((3,)),
            pltpu.SemaphoreType.DMA((3,)),
        ],
        input_output_aliases={2: 8},
        compiler_params=pltpu.CompilerParams(
            collective_id=2, has_side_effects=True, vmem_limit_bytes=VMEM_LIMIT
        ),
        name="attend",
    )(
        x.reshape(4, rows, D),
        cot,
        blocks,
        wqkv,
        vecs,
        bias,
        keys_tab,
        query_tab,
        query_back,
    )


GELU_A = float(np.sqrt(2.0 / np.pi))
GELU_B = 0.044715


def unpack_mlp(part, places, blocks, flat, w1, w2, vecs):
    unflatten(part, places, blocks, flat)
    take_matrix(flat, 0, w1)
    take_matrix(flat, 4608, w2)
    for j in range(12):
        vecs[0:1, j * 128 : (j + 1) * 128] = flat[9216 + j : 9217 + j, :]
    for v in range(3):
        for j in range(3):
            at = 9228 + 3 * v + j
            vecs[1 + v : 2 + v, j * 128 : (j + 1) * 128] = flat[at : at + 1, :]


def pack_mlp(part, places, g_w1, g_w2t, g_vec, flat, out):
    put_matrix(flat, 0, g_w1)
    for j in range(3):
        flat[pl.ds(4608 + j, FF, stride=3), :] = g_w2t[j * 128 : (j + 1) * 128, :].T
    for j in range(12):
        flat[9216 + j : 9217 + j, :] = g_vec[0:1, j * 128 : (j + 1) * 128]
    for v in range(3):
        for j in range(3):
            at = 9228 + 3 * v + j
            flat[at : at + 1, :] = g_vec[1 + v : 2 + v, j * 128 : (j + 1) * 128]
    flat[9237:, :] = jnp.zeros((flat.shape[0] - 9237, 128), F32)
    to_blocks(part, places, flat, out)


def mlp_kernel(
    part,
    places,
    cot_ref,
    mixed_ref,
    x_ref,
    wproj,
    vecs_a,
    blocks,
    out_ref,
    d_res_ref,
    d_mixed_ref,
    sums,
    g_proj,
    g_vec,
    w1,
    w2,
    vecs,
    g_w1,
    g_w2t,
    flat,
):
    i = pl.program_id(0)

    @pl.when(i == 0)
    def _():
        unpack_mlp(part, places, blocks, flat, w1, w2, vecs)
        g_w1[...] = jnp.zeros_like(g_w1)
        g_w2t[...] = jnp.zeros_like(g_w2t)
        g_proj[...] = jnp.zeros_like(g_proj)
        g_vec[...] = jnp.zeros_like(g_vec)

    mix = mixed_ref[...]
    grad = cot_ref[...]
    columns = [slice(0, FF // 2), slice(FF // 2, FF)]
    res = x_ref[...].astype(F32) + dot(mix, wproj[...]) + vecs_a[4:5, :]
    d_act = dot_t(grad, w2[columns[0], :])
    xhat, scale = norm_parts(res)
    gain = vecs[1:2, :D]
    normed = (xhat * gain + vecs[2:3, :D]).astype(BF16)
    grad_t = grad.T
    normed_t = normed.T
    hidden = dot(normed, w1[:, columns[0]])
    out, d_normed = res + vecs[3:4, :D], None
    for f, cols in enumerate(columns):
        value, d_value = hidden + vecs[0:1, cols], d_act
        if f == 0:
            hidden = dot(normed, w1[:, columns[f + 1]])
            d_act = dot_t(grad, w2[columns[f + 1], :])
        square = value * value
        t = jnp.tanh(value * (GELU_A + (GELU_A * GELU_B) * square))
        half = 0.5 + 0.5 * t
        act = (value * half).astype(BF16)
        slope = half + (0.5 * value) * (1.0 - t * t) * (GELU_A + (3 * GELU_A * GELU_B) * square)
        d_hidden32 = d_value * slope
        d_hidden = d_hidden32.astype(BF16)
        g_vec[0:1, cols] += jnp.sum(d_hidden32, axis=0, keepdims=True)
        out += dot(act, w2[cols, :])
        back = dot_t(d_hidden, w1[:, cols])
        d_normed = back if d_normed is None else d_normed + back
        g_w1[:, cols] += dot(normed_t, d_hidden)
        g_w2t[:, cols] += dot(grad_t, act)
    out_ref[...] = out.astype(BF16)
    grad32 = grad.astype(F32)
    d_res = grad32 + norm_back(d_normed, xhat, scale, gain)
    d_res_ref[...] = d_res
    d_attn = d_res.astype(BF16)
    d_mixed_ref[...] = dot_t(d_attn, wproj[...]).astype(BF16)
    g_proj[...] += dot(mix.T, d_attn)
    g_vec[1:2, :D] += jnp.sum(d_normed * xhat, axis=0, keepdims=True)
    g_vec[2:3, :D] += jnp.sum(d_normed, axis=0, keepdims=True)
    g_vec[3:4, :D] += jnp.sum(grad32, axis=0, keepdims=True)
    g_vec[4:5, :D] += jnp.sum(d_res, axis=0, keepdims=True)

    @pl.when(i == pl.num_programs(0) - 1)
    def _():
        pack_mlp(part, places, g_w1, g_w2t, g_vec, flat, sums)


def mlp(part, places, cot, mixed, x, wproj, vecs_a, blocks):
    tokens = x.shape[0]
    chunk = tokens // 7
    vm = pl.BlockSpec(memory_space=pltpu.VMEM)
    tile = pl.BlockSpec((chunk, D), lambda i: (i, 0))
    fixed = lambda *shape: pl.BlockSpec(shape, lambda i: (0,) * len(shape))
    return pl.pallas_call(
        functools.partial(mlp_kernel, part, places),
        grid=(7,),
        out_shape=[
            jax.ShapeDtypeStruct((tokens, D), BF16),
            jax.ShapeDtypeStruct((tokens, D), F32),
            jax.ShapeDtypeStruct((tokens, D), BF16),
            jax.ShapeDtypeStruct((part.devices, part.rows, 128), BF16),
            jax.ShapeDtypeStruct((D, D), F32),
            jax.ShapeDtypeStruct((8, FF), F32),
        ],
        in_specs=[tile] * 3 + [vm] * 3,
        out_specs=[tile] * 3 + [fixed(part.devices, part.rows, 128), fixed(D, D), fixed(8, FF)],
        scratch_shapes=[
            pltpu.VMEM((D, FF), BF16),
            pltpu.VMEM((FF, D), BF16),
            pltpu.VMEM((8, FF), F32),
            pltpu.VMEM((D, FF), F32),
            pltpu.VMEM((D, FF), F32),
            pltpu.VMEM((part.buffer, 128), F32),
        ],
        compiler_params=pltpu.CompilerParams(vmem_limit_bytes=VMEM_LIMIT),
        name="mlp",
    )(cot, mixed, x, wproj, vecs_a, blocks)


CHUNK = 192
LAST = 208


def split_float(values):
    high = values.astype(BF16)
    return high, (values - high.astype(F32)).astype(BF16)


def attend_back_kernel(
    part,
    order,
    q_ref,
    k_ref,
    v_ref,
    mixed_ref,
    d_mixed,
    probs,
    inverse,
    keys_back,
    query_tab,
    query_back,
    x_hbm,
    d_res_hbm,
    wqkv,
    vecs,
    blocks,
    out_src,
    g_bias,
    g_qkv,
    g_vec,
    dx_last,
    grad_ref,
    out_ref,
    dx_ref,
    d_query_t,
    d_key_value_t,
    d_qkv,
    d_in,
    x_buf,
    d_res_buf,
    load_sems,
    total,
    outgoing,
    arrived,
    send,
    recv,
    out_sem,
    out_send,
    out_recv,
    dx_sem0,
    dx_send0,
    dx_recv0,
    dx_sem1,
    dx_send1,
    dx_recv1,
    dx_sem2,
    dx_send2,
    dx_recv2,
):
    i = pl.program_id(0)
    steps = pl.num_programs(0)
    stages = len(order)
    dp, grp = lax.axis_index("dp"), lax.axis_index("grp")
    cube = CubeSum(order, blocks, total, outgoing, arrived, (send, recv))
    exchange = exchange_copies(out_src, out_ref, dp, grp, out_sem, out_send, out_recv)
    dx_sems = (
        (dx_sem0, dx_send0, dx_recv0),
        (dx_sem1, dx_send1, dx_recv1),
        (dx_sem2, dx_send2, dx_recv2),
    )
    loads = [
        pltpu.make_async_copy(x_hbm, x_buf, load_sems.at[0]),
        pltpu.make_async_copy(d_res_hbm, d_res_buf, load_sems.at[1]),
    ]

    def chunk(c):
        return chunk_copies(d_in, dx_ref, CHUNK * c, CHUNK, dp, grp, *dx_sems[c], 0)

    @pl.when(i == 0)
    def _():
        for c in loads:
            c.start()
        g_bias[...] = jnp.zeros_like(g_bias)
        g_qkv[...] = jnp.zeros_like(g_qkv)
        g_vec[...] = jnp.zeros_like(g_vec)
        greet(cube_partners(order, dp, grp) + [window_partner(dp, grp, 3)])

    starts = starts_of(stage_weights(order)[::-1], SUM_STEPS)
    for k, start in zip(reversed(range(stages)), starts):

        @pl.when(i == start)
        def _(k=k):
            if k < stages - 1:
                cube.finish(k + 1)
            cube.start(k)

    @pl.when(i == 0)
    def _():
        for c in exchange:
            c.start()

    dm_t = dot(query_tab[0], image_rows(d_mixed, i, slice(0, D))).T
    spread_heads = lambda ref: jnp.concatenate(
        [jnp.broadcast_to(ref[h : h + 1], (HDIM, 256)) for h in range(HEADS)], axis=0
    )
    dm_t = (dm_t * spread_heads(inverse[0])).astype(BF16)
    products = dm_t.astype(F32) * mixed_ref[0].astype(F32)
    q_t, k_t, v_ext = q_ref[0], k_ref[0], v_ref[0]

    def d_probs_of(h):
        heads = jnp.concatenate([only_head(dm_t, h), only_head(dm_t, h + 1)], axis=1)
        return dot(v_ext[:, tile_of(h)], heads)

    def softmax_back(d_probs, h):
        e = probs[0, h]
        own = slice(h * HDIM, (h + 1) * HDIM)
        sums = jnp.sum(products[own], axis=0, keepdims=True)
        halves = []
        for half in range(2):
            lanes = slice(128 * half, 128 * half + 128)
            e32 = e[:, lanes].astype(F32)[56 * half : 56 * half + KEYS]
            ds = e32 * (half_of(d_probs, half) - sums[:, lanes])
            g_bias[h, half] += ds
            halves.append(ds)
        return spread(halves)

    def gather_back(h, ds):
        own = slice(h * HDIM, (h + 1) * HDIM)
        d_query_t[own, :] = (dot(k_t[own, :], ds) * HDIM ** (-0.5)).astype(BF16)
        d_key_value_t[own, :] = dot_t(q_t[own, :], ds).astype(BF16)
        d_key_value_t[D + h * HDIM : D + (h + 1) * HDIM, :] = dot_t(
            dm_t[own, :], probs[0, h]
        ).astype(BF16)

    ahead = d_probs_of(0)
    waiting = []
    for h in range(0, HEADS, 2):
        now = ahead
        if h + 2 < HEADS:
            ahead = d_probs_of(h + 2)
        for c in range(2):
            waiting.append((h + c, softmax_back(now[:, c * 256 : (c + 1) * 256], h + c)))
        while len(waiting) > 1:
            gather_back(*waiting.pop(0))
    for last in waiting:
        gather_back(*last)
    put_image_rows(d_qkv, i, slice(0, D), dot_t(query_back[0], d_query_t[...]))
    put_image_rows(d_qkv, i, slice(D, 3 * D), dot_t(keys_back[0], d_key_value_t[...]))

    @pl.when(i == 3)
    def _():
        for c in loads:
            c.wait()

    @pl.when(lax.rem(i, 4) == 3)
    def _():
        c = i // 4
        at = pl.ds(pl.multiple_of(c * CHUNK, 16), LAST)
        xhat, scale = norm_parts(x_buf[:, at, :].reshape(4 * LAST, D).astype(F32))
        gain = vecs[0:1, :]
        normed = (xhat * gain + vecs[1:2, :]).astype(BF16)
        row = lax.rem(lax.broadcasted_iota(jnp.int32, (4 * LAST, 1), 0), LAST)
        counts = row < jnp.where(i == steps - 1, LAST, CHUNK)
        grads = d_qkv[:, at, :].reshape(4 * LAST, 3 * D)
        grads = jnp.where(counts, grads, 0)
        d_normed = dot_t(grads, wqkv[...])
        result = d_res_buf[:, at, :].reshape(4 * LAST, D) + norm_back(d_normed, xhat, scale, gain)
        result = result.astype(BF16).reshape(4, LAST, D)
        d_in[:, at, :] = result
        dx_last[...] = result
        g_qkv[...] += dot(normed.T, grads)
        g_vec[0:1, :] += jnp.sum(grads.astype(F32), axis=0, keepdims=True)
        g_vec[1:2, :D] += jnp.sum(d_normed * xhat, axis=0, keepdims=True)
        g_vec[2:3, :D] += jnp.sum(d_normed, axis=0, keepdims=True)

    for c in range(3):

        @pl.when(i == 4 * c + 3)
        def _(c=c):
            for copy in chunk(c):
                copy.start()

    @pl.when(i == steps - 1)
    def _():
        cube.finish(0)
        device = dp * lax.axis_size("grp") + grp
        grad_ref[...] = shift_lanes(total[0], part.lane(device), False)
        for c in exchange:
            c.wait()
        for c in range(3):
            for copy in chunk(c):
                copy.wait()


def attend_back(
    part, order, saved, d_mixed, probs, inverse, x, d_res, wqkv, vecs, blocks, out
):
    images = probs.shape[0]
    tokens = out.shape[0]
    rows = tokens // 4
    stages = len(order)
    _, query_tab, keys_back, query_back = gather_tables(images)
    vm = pl.BlockSpec(memory_space=pltpu.VMEM)
    hbm = pl.BlockSpec(memory_space=pl.ANY)
    image = lambda *shape: pl.BlockSpec((1, *shape), lambda i: (i, 0, 0))
    table = image(256, 256)
    by_window = lambda array: array.reshape(4, rows, -1)
    outs = pl.pallas_call(
        functools.partial(attend_back_kernel, part, order),
        grid=(images,),
        out_shape=[
            jax.ShapeDtypeStruct((HEADS, 2, KEYS, 128), F32),
            jax.ShapeDtypeStruct((D, 3 * D), F32),
            jax.ShapeDtypeStruct((8, 3 * D), F32),
            jax.ShapeDtypeStruct((4, LAST, D), BF16),
            jax.ShapeDtypeStruct((part.rows, 128), F32),
            jax.ShapeDtypeStruct((tokens, D), BF16),
            jax.ShapeDtypeStruct((4, rows, D), BF16),
        ],
        in_specs=[
            image(D, 256),
            image(D, 256),
            image(256, D),
            image(D, 256),
            vm,
            pl.BlockSpec((1, HEADS, 256, 256), lambda i: (i, 0, 0, 0)),
            image(16, 256),
        ]
        + [table] * 3
        + [hbm, hbm, vm, vm, vm, hbm],
        out_specs=[
            pl.BlockSpec((HEADS, 2, KEYS, 128), lambda i: (0, 0, 0, 0)),
            pl.BlockSpec((D, 3 * D), lambda i: (0, 0)),
            pl.BlockSpec((8, 3 * D), lambda i: (0, 0)),
            pl.BlockSpec((4, LAST, D), lambda i: (0, 0, 0)),
            pl.BlockSpec((part.rows, 128), lambda i: (0, 0)),
            hbm,
            hbm,
        ],
        scratch_shapes=[
            pltpu.VMEM((D, 256), BF16),
            pltpu.VMEM((2 * D, 256), BF16),
            pltpu.VMEM((4, rows, 3 * D), BF16),
            pltpu.VMEM((4, rows, D), BF16),
            pltpu.VMEM((4, rows, D), BF16),
            pltpu.VMEM((4, rows, D), F32),
            pltpu.SemaphoreType.DMA((2,)),
        ]
        + CubeSum.scratch(part.devices, part.rows, stages)
        + [
            pltpu.SemaphoreType.DMA,
            pltpu.SemaphoreType.DMA((3,)),
            pltpu.SemaphoreType.DMA((3,)),
        ]
        * 4,
        compiler_params=pltpu.CompilerParams(
            collective_id=3, has_side_effects=True, vmem_limit_bytes=VMEM_LIMIT
        ),
        name="attend_back",
    )(
        *saved,
        by_window(d_mixed),
        probs,
        inverse,
        keys_back,
        query_tab,
        query_back,
        by_window(x),
        by_window(d_res),
        wqkv,
        vecs,
        blocks,
        out,
    )
    grad = outs[4].reshape(-1)[: part.length]
    return (*outs[:4], grad, *outs[5:])


def to_blocks(part, places, flat, out):
    for device, place in enumerate(places):
        at = part.start(device)
        out[place] = flat[at : at + part.rows, :].astype(BF16)


def pack_kernel(
    part,
    places,
    one_fine,
    one_coarse,
    g_bias,
    g_qkv,
    g_vec1,
    g_proj,
    g_vec2,
    out,
    flat,
    table,
    shifted,
    line,
):
    flat[...] = jnp.zeros_like(flat)
    put_matrix(flat, 0, g_qkv)
    put_matrix(flat, 3456, g_proj)
    vectors = [
        g_vec1[1:2, :D],
        g_vec1[2:3, :D],
        g_vec1[0:1, :D],
        g_vec1[0:1, 2 * D :],
        g_vec2[4:5, :D],
    ]
    pieces = [v[:, j * 128 : (j + 1) * 128] for v in vectors for j in range(3)]
    pieces += [jnp.zeros((1, 128), F32)]
    row, lane = divmod(ATTN_VECTORS[0], 128)
    flat[row : row + 16, :] += shift_lanes(jnp.concatenate(pieces, axis=0), lane, True)
    for h in range(HEADS):
        table[...] = jnp.zeros_like(table)
        for half in range(2):
            turned = g_bias[h, half].T
            for y in range(WIN):
                for at, length, source in bias_runs(half, WIN * half + y):
                    table[0:14, source : source + length] += turned[
                        y * 14 : y * 14 + 14, at : at + length
                    ]
        for c in range(4):
            shifted[c, pl.ds(h, 14, stride=16), :] = table[0:14, c * 128 : (c + 1) * 128]
    high, low = split_float(jnp.concatenate([shifted[c] for c in range(3)], axis=1))
    moved_fine = dot_t(high, one_fine[...]) + dot_t(low, one_fine[...])
    high, low = split_float(shifted[3])
    moved_coarse = dot_t(high, one_coarse[...]) + dot_t(low, one_coarse[...])
    g_fine = jnp.zeros((16, 384), F32)
    g_coarse = jnp.zeros((16, 256), F32)
    for qx in range(14):
        at = slice(qx * 16, qx * 16 + 16)
        g_fine += pltpu.roll(moved_fine[at], (384 - qx) % 384, 1)
        g_coarse += pltpu.roll(moved_coarse[at], (256 - qx // 2) % 256, 1)
    for t, h, length, row, lane, count in table_lines():
        line[...] = jnp.zeros_like(line)
        line[0:1, lane : lane + length] = (g_fine, g_coarse)[t][h : h + 1, :length]
        for c in range(count):
            flat[row + c : row + c + 1, :] += line[0:1, c * 128 : (c + 1) * 128]
    to_blocks(part, places, flat, out)


def pack(part, places, g_bias, g_qkv, g_vec1, g_proj, g_vec2):
    fine, coarse, _ = bias_tables()
    vm = pl.BlockSpec(memory_space=pltpu.VMEM)
    return pl.pallas_call(
        functools.partial(pack_kernel, part, places),
        out_shape=jax.ShapeDtypeStruct((part.devices, part.rows, 128), BF16),
        in_specs=[vm] * 7,
        out_specs=vm,
        scratch_shapes=[
            pltpu.VMEM((part.buffer, 128), F32),
            pltpu.VMEM((16, 512), F32),
            pltpu.VMEM((4, 14 * 16, 128), F32),
            pltpu.VMEM((8, 512), F32),
        ],
        compiler_params=pltpu.CompilerParams(vmem_limit_bytes=VMEM_LIMIT),
        name="pack",
    )(jnp.asarray(fine), jnp.asarray(coarse), g_bias, g_qkv, g_vec1, g_proj, g_vec2)


def adamw(master, first, second, grads):
    first_new = beta_one * first + (1.0 - beta_one) * grads
    second_new = beta_two * second + (1.0 - beta_two) * grads * grads
    first_hat = first_new / (1.0 - beta_one**STEP)
    second_hat = second_new / (1.0 - beta_two**STEP)
    master_new = master - learn_rate * (
        first_hat / (jnp.sqrt(second_hat) + adam_eps) + decay_rate * master
    )
    return (first_new, second_new, master_new)


def body(
    tokens, cotangent, attn_master, attn_first, attn_second, mlp_master, mlp_first, mlp_second
):
    n_dp, n_grp = lax.axis_size("dp"), lax.axis_size("grp")
    order = bit_order(n_dp, n_grp)
    places = place_list(order, n_dp, n_grp)
    part_a = Part(n_dp * n_grp, attn_master.shape[0])
    part_b = Part(n_dp * n_grp, mlp_master.shape[0])
    images = tokens.shape[1] // 4 // SEQ
    wqkv, wproj, vecs_a, bias, x, blocks_b = gather_params(
        part_a, part_b, order, places, attn_master, mlp_master, tokens[0]
    )
    mixed, probs, *saved, inverse, cot, blocks_b = attend(
        order, x, cotangent[0], blocks_b, wqkv, vecs_a, bias, images
    )
    mixed = mixed.reshape(-1, D)
    out, d_res, d_mixed, sums_b, g_proj, g_vec2 = mlp(
        part_b, places, cot, mixed, x, wproj, vecs_a, blocks_b
    )
    g_bias, g_qkv, g_vec1, dx_last, grad_b, output, dx = attend_back(
        part_b,
        order,
        saved,
        d_mixed,
        probs,
        inverse,
        x,
        d_res,
        wqkv,
        vecs_a,
        sums_b,
        out,
    )
    sums_a = pack(part_a, places, g_bias, g_qkv, g_vec1, g_proj, g_vec2)
    grad_a, dx = sum_grads(part_a, order, sums_a, dx_last, dx)
    attn_new = adamw(attn_master, attn_first, attn_second, grad_a)
    mlp_new = adamw(mlp_master, mlp_first, mlp_second, grad_b)
    input_grad = dx.reshape(-1, D).astype(F32)
    return (output[None], input_grad[None], *attn_new, *mlp_new)


def solution(mesh):
    flat_spec = P(("dp", "grp"))
    token_spec = P("dp", "grp", None)
    placed = (token_spec, token_spec) + (flat_spec,) * 6
    return jax.shard_map(
        body, mesh=mesh, in_specs=placed, out_specs=placed, check_vma=False
    )
```

```python
import functools

import jax
import jax.numpy as jnp
import ml_dtypes
import numpy as np
from jax import lax
from jax.experimental import pallas as pl
from jax.experimental.pallas import tpu as pltpu
from jax.sharding import PartitionSpec as P

D = 384
HEADS = 12
HDIM = 32
FF = 1536
WIN = 7
STEP = 10
SEQ = WIN * WIN
HALF = 64
FINE = (3 * WIN - 2) ** 2
COARSE = (2 * WIN - 1) ** 2
KEYS = 192

beta_one = 0.9
beta_two = 0.999
learn_rate = 0.04
decay_rate = 0.05
adam_eps = 1e-08
norm_eps = 1e-05
masked_score = -1e30

F32 = jnp.float32
BF16 = jnp.bfloat16
MESH = pl.DeviceIdType.MESH
VMEM_LIMIT = 60 * 2**20


def token_place(gy, gx):
    window = 2 * (gy // WIN) + gx // WIN
    return window * HALF + (gy % WIN) * WIN + gx % WIN


@functools.cache
def gather_tables(images):
    keys = np.zeros((images, 256, 256), np.float32)
    queries = np.zeros((images, 256, 256), np.float32)
    for i in range(images):
        for gy in range(2 * WIN):
            for gx in range(2 * WIN):
                at = token_place(gy, gx) + i
                key = gy * 14 + gx if gy < 10 else 192 + (gy - 10) * 14 + gx
                keys[i, key, at] = 1.0
                keys[i, 140 + (gy // 2) * WIN + gx // 2, at] = 0.25
                queries[i, (gy // WIN) * 128 + (gy % WIN) * 14 + gx, at] = 1.0
    return (
        keys.astype(ml_dtypes.bfloat16),
        queries.astype(ml_dtypes.bfloat16),
        np.ascontiguousarray(keys.transpose(0, 2, 1)).astype(ml_dtypes.bfloat16),
        np.ascontiguousarray(queries.transpose(0, 2, 1)).astype(ml_dtypes.bfloat16),
    )


@functools.cache
def bias_tables():
    fine = np.zeros((384, 384), np.float32)
    coarse = np.zeros((256, 128), np.float32)
    for a in range(4, 23):
        for kx in range(14):
            fine[19 * (a - 4) + kx + 9, a * 14 + kx] = 1.0
    for p in range(13):
        for x in range(WIN):
            coarse[13 * p + x + 6, p * WIN + x] = 1.0
    mask = np.zeros((2, KEYS, 128), np.float32)
    for half in range(2):
        for q in range(98):
            qx = q % 14
            for e in range(KEYS):
                at = e + 56 * half
                if at < 140:
                    ok = abs_ok(qx, at % 14)
                elif at < 189:
                    ok = True
                elif at < 192:
                    ok = False
                else:
                    ok = at < 248 and abs_ok(qx, (at - 192) % 14)
                mask[half, e, q] = 0.0 if ok else masked_score
    return fine.astype(ml_dtypes.bfloat16), coarse.astype(ml_dtypes.bfloat16), mask


def abs_ok(qx, kx):
    return kx < 10 if qx < WIN else kx >= 4


def bias_runs(half, qy):
    fine = (13 - qy) * 14
    pool = 384 + (6 - qy // 2) * WIN
    if half == 0:
        return [(0, 140, fine), (140, 49, pool)]
    return [(0, 84, fine + 56), (84, 49, pool), (136, 56, fine + 140)]


class Part:
    def __init__(self, devices, length):
        self.devices = devices
        self.length = length
        self.rows = -(-((length + 126) // 128 + 1) // 16) * 16
        self.buffer = -(-(self.start(devices - 1) + self.rows) // 8) * 8

    def start(self, device):
        return device * self.length // 128

    def lane(self, device):
        return lax.rem(device * self.length, 128)

    def split(self, share):
        first = max(16, min(self.rows - 16, round(self.rows * share / 16) * 16))
        return first, self.rows - first

    def padded(self, vector):
        extra = self.rows * 128 - self.length
        return jnp.pad(vector, (0, extra)).reshape(self.rows, 128)


GATHER_SHARE = 0.7
SUM_SHARE = 0.5
GATHER_STEPS = 12
SUM_STEPS = 16


def bit_order(n_dp, n_grp):
    dp_bits = [("dp", 2**b) for b in range(n_dp.bit_length() - 1)]
    grp_bits = [("grp", 2**b) for b in reversed(range(n_grp.bit_length() - 1))]
    return dp_bits[1:2] + grp_bits + dp_bits[2:] + dp_bits[:1]


def other_order(order):
    grp_bits = [stage for stage in order if stage[0] == "grp"]
    dp_bits = [stage for stage in order if stage[0] == "dp"]
    return dp_bits[:-1] + grp_bits + dp_bits[-1:]


def stage_weights(order):
    weights = []
    for k, (axis, stride) in enumerate(order):
        relative = 0.35 if (axis, stride) == ("dp", 1) else 2 if (axis == "grp" and stride > 1) else 1
        weights.append(relative * 2**k)
    return weights


def starts_of(weights, steps):
    done, starts = 0.0, []
    for weight in weights:
        starts.append(min(int(np.ceil(steps * done / sum(weights))), steps - 1))
        done += weight
    return starts


def place_of(order, dp, grp):
    place = 0
    for k, (axis, stride) in enumerate(order):
        place = place + ((dp if axis == "dp" else grp) // stride) % 2 * 2**k
    return place


def partner_of(axis, stride, dp, grp):
    if axis == "dp":
        return (dp + (1 - 2 * ((dp // stride) % 2)) * stride, grp)
    return (dp, grp + (1 - 2 * ((grp // stride) % 2)) * stride)


def greet(partners):
    barrier = pltpu.get_barrier_semaphore()
    for partner in partners:
        pl.semaphore_signal(barrier, inc=1, device_id=partner, device_id_type=MESH)
    pl.semaphore_wait(barrier, len(partners))


def cube_partners(order, dp, grp):
    return [partner_of(axis, stride, dp, grp) for axis, stride in order]


def shift_lanes(values, amount, up):
    lane = lax.broadcasted_iota(jnp.int32, values.shape, 1)
    if up:
        turned = pltpu.roll(values, amount, 1)
        return jnp.where(lane >= amount, turned, pltpu.roll(turned, 1, 0))
    turned = pltpu.roll(values, lax.rem(128 - amount, 128), 1)
    return jnp.where(lane < 128 - amount, turned, pltpu.roll(turned, values.shape[0] - 1, 0))


def window_partner(dp, grp, k):
    low, high = dp % 2, dp // 2 % 2
    to = dp
    if k % 2:
        to = to + 1 - 2 * low
    if k // 2:
        to = to + 2 * (1 - 2 * high)
    return (to, grp)


def exchange_copies(source, target, dp, grp, own_sem, send_sems, recv_sems):
    rows = source.shape[0] // 4
    slot = dp % 4
    mine = pl.ds(pl.multiple_of(slot * rows, 16), rows)
    own = pltpu.make_async_copy(source.at[mine], target.at[mine], own_sem)
    sends = []
    for k in (3, 2, 1):
        to, _ = window_partner(dp, grp, k)
        theirs = pl.ds(pl.multiple_of(to % 4 * rows, 16), rows)
        sends.append(
            pltpu.make_async_remote_copy(
                src_ref=source.at[theirs],
                dst_ref=target.at[mine],
                send_sem=send_sems.at[k - 1],
                recv_sem=recv_sems.at[k - 1],
                device_id=(to, grp),
                device_id_type=MESH,
            )
        )
    return [own] + sends


def cube_copy(order, k, source, target, dp, grp, send_sems, recv_sems):
    axis, stride = order[k]
    return pltpu.make_async_remote_copy(
        src_ref=source,
        dst_ref=target,
        send_sem=send_sems.at[k],
        recv_sem=recv_sems.at[k],
        device_id=partner_of(axis, stride, dp, grp),
        device_id_type=MESH,
    )


def gather_copy(order, k, blocks, dp, grp, sems):
    place = place_of(order, dp, grp)
    held = blocks.at[pl.ds(place // 2**k * 2**k, 2**k)]
    return cube_copy(order, k, held, held, dp, grp, *sems)


class CubeSum:
    def __init__(self, order, blocks, total, outgoing, arrived, sems):
        self.order, self.blocks, self.total = order, blocks, total
        self.outgoing, self.arrived, self.sems = outgoing, arrived, sems
        self.dp, self.grp = lax.axis_index("dp"), lax.axis_index("grp")
        self.place = place_of(order, self.dp, self.grp)
        self.last = len(order) - 1

    def mine(self, k):
        return self.place // 2**k % 2 * 2**k

    def copy(self, k):
        size = 2**k
        if k == self.last:
            source = self.blocks.at[pl.ds(size - self.mine(k), size)]
        else:
            source = self.outgoing.at[pl.ds(size, size)]
        target = self.arrived.at[pl.ds(size, size)]
        return cube_copy(self.order, k, source, target, self.dp, self.grp, *self.sems)

    def start(self, k):
        self.copy(k).start()

    def finish(self, k):
        size, mine = 2**k, self.mine(k)
        self.copy(k).wait()

        def added(j):
            if k == self.last:
                held = self.blocks[mine + j].astype(F32)
            else:
                held = self.total[mine + j]
            return held + self.arrived[size + j].astype(F32)

        keep = size // 2 if k else 1
        kept = self.mine(k - 1) if k else 0

        def add(j, carry):
            value = added(kept + j)
            if k:
                self.outgoing[keep + j] = added(keep - kept + j).astype(BF16)
            self.total[kept + j] = value
            return carry

        lax.fori_loop(0, keep, add, 0)

    @staticmethod
    def scratch(devices, rows, stages):
        return [
            pltpu.VMEM((devices // 2, rows, 128), F32),
            pltpu.VMEM((devices // 2, rows, 128), BF16),
            pltpu.VMEM((devices, rows, 128), BF16),
            pltpu.SemaphoreType.DMA((stages,)),
            pltpu.SemaphoreType.DMA((stages,)),
        ]


def chunk_copies(source, target, first, size, dp, grp, own_sem, send_sems, recv_sems, skip):
    slot = dp % 4
    into = target.at[slot, pl.ds(first, size)]
    rows = pl.ds(first - skip, size)
    copies = [pltpu.make_async_copy(source.at[slot, rows], into, own_sem)]
    for k in (3, 2, 1):
        to, _ = window_partner(dp, grp, k)
        copies.append(
            pltpu.make_async_remote_copy(
                src_ref=source.at[to % 4, rows],
                dst_ref=into,
                send_sem=send_sems.at[k - 1],
                recv_sem=recv_sems.at[k - 1],
                device_id=(to, grp),
                device_id_type=MESH,
            )
        )
    return copies


def place_list(order, n_dp, n_grp):
    return [place_of(order, d // n_grp, d % n_grp) for d in range(n_dp * n_grp)]


ATTN_VECTORS = (D * 3 * D + D * D + HEADS * FINE + HEADS * COARSE, 5)
TABLE_AT = D * 3 * D + D * D


def unflatten(part, chains, flat):
    for device in range(part.devices):
        at = part.start(device)
        pieces = [blocks[places[device]].astype(F32) for places, blocks in chains]
        block = jnp.concatenate(pieces, axis=0) if len(pieces) > 1 else pieces[0]
        first = block[0:1] + flat[at : at + 1, :] if device else block[0:1]
        flat[at : at + part.rows, :] = block
        flat[at : at + 1, :] = first


def take_matrix(flat, first, target):
    rows, columns = target.shape
    count = columns // 128
    for j in range(count):
        target[:, j * 128 : (j + 1) * 128] = flat[pl.ds(first + j, rows, stride=count), :].astype(
            target.dtype
        )


def put_matrix(flat, first, source):
    rows, columns = source.shape
    count = columns // 128
    for j in range(count):
        flat[pl.ds(first + j, rows, stride=count), :] = source[:, j * 128 : (j + 1) * 128]


TABLES = ((TABLE_AT, FINE), (TABLE_AT + HEADS * FINE, COARSE))


def table_lines():
    for t, (first, length) in enumerate(TABLES):
        for h in range(HEADS):
            row, lane = divmod(first + h * length, 128)
            yield t, h, length, row, lane, -(-(lane + length) // 128)


def prepare(
    part, chains, one_fine, one_coarse, mask_ref,
    wqkv, wproj, vecs, bias, flat, tab_fine, tab_coarse, shifted, turned,
):
    unflatten(part, chains, flat)
    take_matrix(flat, 0, wqkv)
    take_matrix(flat, 3456, wproj)
    row, lane = divmod(ATTN_VECTORS[0], 128)
    rows = shift_lanes(flat[row : row + 16, :], lane, False)
    for v in range(5):
        for j in range(3):
            vecs[v : v + 1, j * 128 : (j + 1) * 128] = rows[3 * v + j : 3 * v + j + 1]
    tab_fine[...] = jnp.zeros_like(tab_fine)
    tab_coarse[...] = jnp.zeros_like(tab_coarse)
    for t, h, length, row, lane, count in table_lines():
        line = jnp.concatenate([flat[row + c : row + c + 1, :] for c in range(count)], axis=1)
        (tab_fine, tab_coarse)[t][h : h + 1, 0:length] = line[:, lane : lane + length]
    fine, coarse = tab_fine[...], tab_coarse[...]
    fine = jnp.concatenate([pltpu.roll(fine, qx, 1) for qx in range(14)], axis=0)
    coarse = jnp.concatenate([pltpu.roll(coarse, qx // 2, 1) for qx in range(14)], axis=0)
    fine = dot(fine.astype(BF16), one_fine[...])
    for c in range(3):
        shifted[c] = fine[:, c * 128 : (c + 1) * 128]
    shifted[3] = dot(coarse.astype(BF16), one_coarse[...])
    turned[...] = jnp.zeros_like(turned)
    for h in range(HEADS):
        table = jnp.concatenate(
            [shifted[c, pl.ds(h, 14, stride=16), :] for c in range(4)], axis=1
        )
        for half in range(2):
            for y in range(WIN):
                for at, length, source in bias_runs(half, WIN * half + y):
                    turned[half, y * 14 : y * 14 + 14, at : at + length] = table[
                        :, source : source + length
                    ]
            bias[h, half] = turned[half].T[0:KEYS] + mask_ref[half]


def early_stages(order):
    return 1 + sum(axis == "grp" for axis, _ in order)


def gather_kernel(
    part_a,
    part_b,
    order,
    chain_places,
    a_ref,
    b_ref,
    one_fine,
    one_coarse,
    mask_ref,
    tok_ref,
    wqkv,
    wproj,
    vecs,
    bias,
    x_ref,
    blocks_b,
    blocks_a1,
    blocks_a2,
    own,
    flat,
    tab_fine,
    tab_coarse,
    shifted,
    turned,
    own_sem,
    send_a1,
    recv_a1,
    send_a2,
    recv_a2,
    send_b,
    recv_b,
    x_sem,
    x_send,
    x_recv,
):
    dp, grp = lax.axis_index("dp"), lax.axis_index("grp")
    place = place_of(order, dp, grp)
    device = dp * lax.axis_size("grp") + grp
    own[...] = shift_lanes(b_ref[...], part_b.lane(device), True).astype(BF16)
    copy = pltpu.make_async_copy(own, blocks_b.at[place], own_sem)
    copy.start()
    mine = shift_lanes(a_ref[...], part_a.lane(device), True)
    orders = (order, other_order(order))
    chains = ((blocks_a1, (send_a1, recv_a1)), (blocks_a2, (send_a2, recv_a2)))
    at = 0
    for chain_order, (blocks, _) in zip(orders, chains):
        blocks[place_of(chain_order, dp, grp)] = mine[at : at + blocks.shape[1]].astype(BF16)
        at += blocks.shape[1]
    vecs[...] = jnp.zeros_like(vecs)
    greet(cube_partners(order, dp, grp) + [window_partner(dp, grp, 3)])
    copy.wait()
    exchange = exchange_copies(tok_ref, x_ref, dp, grp, x_sem, x_send, x_recv)
    first = [
        [
            gather_copy(chain_order, k, blocks, dp, grp, sems)
            for chain_order, (blocks, sems) in zip(orders, chains)
        ]
        for k in range(len(order))
    ]
    early = early_stages(order)
    second = [gather_copy(order, k, blocks_b, dp, grp, (send_b, recv_b)) for k in range(early)]
    for k, stage in enumerate(first):
        for c in stage:
            c.start()
        if k == 0:
            second[0].start()
            for c in exchange:
                c.start()
        if early <= k < 2 * early:
            second[k - early].wait()
            if k - early + 1 < early:
                second[k - early + 1].start()
        for c in stage:
            c.wait()
    prepare(
        part_a, list(zip(chain_places, (blocks_a1, blocks_a2))), one_fine, one_coarse, mask_ref,
        wqkv, wproj, vecs, bias, flat, tab_fine, tab_coarse, shifted, turned,
    )
    for k in range(len(order) - early, early):
        second[k].wait()
        if k + 1 < early:
            second[k + 1].start()
    for c in exchange:
        c.wait()


def gather_params(part_a, part_b, order, chain_places, master_a, master_b, tok):
    stages = len(order)
    rows = part_a.split(GATHER_SHARE)
    early = early_stages(order)
    fine, coarse, mask = bias_tables()
    vm = pl.BlockSpec(memory_space=pltpu.VMEM)
    hbm = pl.BlockSpec(memory_space=pl.ANY)
    return pl.pallas_call(
        functools.partial(gather_kernel, part_a, part_b, order, chain_places),
        out_shape=[
            jax.ShapeDtypeStruct((D, 3 * D), BF16),
            jax.ShapeDtypeStruct((D, D), BF16),
            jax.ShapeDtypeStruct((8, D), F32),
            jax.ShapeDtypeStruct((HEADS, 2, KEYS, 128), F32),
            jax.ShapeDtypeStruct(tok.shape, BF16),
            jax.ShapeDtypeStruct((part_b.devices, part_b.rows, 128), BF16),
        ],
        in_specs=[vm] * 5 + [hbm],
        out_specs=[vm] * 4 + [hbm] * 2,
        scratch_shapes=[
            pltpu.VMEM((part_a.devices, rows[0], 128), BF16),
            pltpu.VMEM((part_a.devices, rows[1], 128), BF16),
            pltpu.VMEM((part_b.rows, 128), BF16),
            pltpu.VMEM((part_a.buffer, 128), F32),
            pltpu.VMEM((16, 384), F32),
            pltpu.VMEM((16, 256), F32),
            pltpu.VMEM((4, 14 * 16, 128), F32),
            pltpu.VMEM((2, 128, 256), F32),
            pltpu.SemaphoreType.DMA,
            pltpu.SemaphoreType.DMA((stages,)),
            pltpu.SemaphoreType.DMA((stages,)),
            pltpu.SemaphoreType.DMA((stages,)),
            pltpu.SemaphoreType.DMA((stages,)),
            pltpu.SemaphoreType.DMA((early,)),
            pltpu.SemaphoreType.DMA((early,)),
            pltpu.SemaphoreType.DMA,
            pltpu.SemaphoreType.DMA((3,)),
            pltpu.SemaphoreType.DMA((3,)),
        ],
        compiler_params=pltpu.CompilerParams(
            collective_id=0, has_side_effects=True, vmem_limit_bytes=VMEM_LIMIT
        ),
        name="gather_params",
    )(
        part_a.padded(master_a),
        part_b.padded(master_b),
        jnp.asarray(fine),
        jnp.asarray(coarse),
        jnp.asarray(mask),
        tok,
    )


def dot(a, b):
    return jnp.dot(a, b, preferred_element_type=F32)


def dot_t(a, b):
    return lax.dot_general(a, b, (((1,), (1,)), ((), ())), preferred_element_type=F32)


def norm_parts(values):
    centered = values - jnp.mean(values, axis=-1, keepdims=True)
    scale = lax.rsqrt(jnp.mean(centered * centered, axis=-1, keepdims=True) + norm_eps)
    return centered * scale, scale


def norm_back(d_normed, xhat, scale, gain):
    dh = d_normed * gain
    return scale * (
        dh
        - jnp.mean(dh, axis=-1, keepdims=True)
        - xhat * jnp.mean(dh * xhat, axis=-1, keepdims=True)
    )


def image_rows(ref, i, columns):
    at = pl.ds(pl.multiple_of(48 * i, 16), HALF)
    return jnp.concatenate([ref[w, at, columns] for w in range(4)], axis=0)


def put_image_rows(ref, i, columns, values):
    for w in range(4):
        part = values[w * HALF : (w + 1) * HALF]
        first = pl.ds(pl.multiple_of(48 * i, 16), 16)
        rest = pl.ds(pl.multiple_of(48 * i + 16, 16), HALF - 16)
        held = jnp.where(i > 0, ref[w, first, columns].astype(F32), 0.0)
        ref[w, first, columns] = (held + part[:16]).astype(ref.dtype)
        ref[w, rest, columns] = part[16:].astype(ref.dtype)


def spread(halves):
    columns = []
    for half, values in enumerate(halves):
        pieces = [values, jnp.zeros((64 - 56 * half, 128), F32)]
        if half:
            pieces = [jnp.zeros((56, 128), F32)] + pieces
        columns.append(jnp.concatenate(pieces, axis=0))
    return jnp.concatenate(columns, axis=1).astype(BF16)


def only_head(turned, h):
    pieces = [jnp.zeros((HDIM, 256), BF16)] * 4
    pieces[h % 4] = turned[h * HDIM : (h + 1) * HDIM, :]
    return jnp.concatenate(pieces, axis=0)


def half_of(values, half):
    return values[56 * half : 56 * half + KEYS, 128 * half : 128 * half + 128]


def tile_of(h):
    return slice(h // 4 * 128, h // 4 * 128 + 128)


def attend_kernel(
    rows,
    order,
    x_buf,
    cot_ref,
    blocks_in,
    wqkv,
    vecs,
    bias,
    keys_tab,
    query_tab,
    query_back,
    mixed,
    probs,
    query_out,
    key_out,
    value_out,
    mixed_out,
    inverse,
    cot_out,
    blocks,
    normed,
    qkv,
    send,
    recv,
    cot_sem,
    cot_send,
    cot_recv,
):
    i = pl.program_id(0)
    steps = pl.num_programs(0)
    dp, grp = lax.axis_index("dp"), lax.axis_index("grp")
    exchange = exchange_copies(cot_ref, cot_out, dp, grp, cot_sem, cot_send, cot_recv)
    early = early_stages(order)
    late = [
        gather_copy(order, k, blocks, dp, grp, (send, recv)) for k in range(early, len(order))
    ]

    @pl.when(i == 0)
    def _():
        greet(cube_partners(order, dp, grp) + [window_partner(dp, grp, 3)])

    for k, start in enumerate(starts_of(stage_weights(order)[early:], GATHER_STEPS)):

        @pl.when(i == start)
        def _(k=k):
            if k:
                late[k - 1].wait()
            late[k].start()

    @pl.when(i == 0)
    def _():
        for c in exchange:
            c.start()

        step = rows // 7

        def norm(w):
            for c in range(7):
                at = slice(c * step, (c + 1) * step)
                xhat, _ = norm_parts(x_buf[w, at, :].astype(F32))
                normed[w % 2, at, :] = (xhat * vecs[0:1, :] + vecs[1:2, :]).astype(BF16)

        norm(0)
        for w in range(4):
            q = dot(normed[w % 2], wqkv[:, :D]) + vecs[2:3, :]
            qkv[w, :, :D] = (q * HDIM ** (-0.5)).astype(BF16)
            if w < 3:
                norm(w + 1)
            qkv[w, :, D : 2 * D] = dot(normed[w % 2], wqkv[:, D : 2 * D]).astype(BF16)
            v = dot(normed[w % 2], wqkv[:, 2 * D :]) + vecs[3:4, :]
            qkv[w, :, 2 * D :] = v.astype(BF16)

    q_ext = dot(query_tab[0], image_rows(qkv, i, slice(0, D)))
    kv_ext = dot(keys_tab[0], image_rows(qkv, i, slice(D, 3 * D)))
    q_t = q_ext.T.astype(BF16)
    k_ext = kv_ext[:, :D].astype(BF16)
    v_t = kv_ext[:, D:].T.astype(BF16)
    query_out[0] = q_t
    key_out[0] = kv_ext[:, :D].T.astype(BF16)
    value_out[0] = kv_ext[:, D:].astype(BF16)
    inverse[0, HEADS:16, :] = jnp.zeros((16 - HEADS, 256), F32)

    def scores_of(h):
        heads = jnp.concatenate([only_head(q_t, h), only_head(q_t, h + 1)], axis=1)
        return dot(k_ext[:, tile_of(h)], heads)

    def softmax(scores, h):
        halves, inverses = [], []
        for half in range(2):
            s = half_of(scores, half) + bias[h, half]
            e = jnp.exp(s - jnp.max(s, axis=0, keepdims=True))
            inverses.append(1.0 / jnp.sum(e, axis=0, keepdims=True))
            halves.append(e)
        e = spread(halves)
        inv = jnp.concatenate(inverses, axis=1)
        probs[0, h] = e
        inverse[0, h : h + 1, :] = inv
        return e, inv

    def mix(h, e, inv):
        own = slice(h * HDIM, (h + 1) * HDIM)
        mixed_out[0, own, :] = (dot(v_t[own, :], e) * inv).astype(BF16)

    ahead = scores_of(0)
    waiting = []
    for h in range(0, HEADS, 2):
        now = ahead
        if h + 2 < HEADS:
            ahead = scores_of(h + 2)
        for c in range(2):
            waiting.append((h + c, *softmax(now[:, c * 256 : (c + 1) * 256], h + c)))
        while len(waiting) > 1:
            mix(*waiting.pop(0))
    for last in waiting:
        mix(*last)
    put_image_rows(mixed, i, slice(0, D), dot_t(query_back[0], mixed_out[0]))

    @pl.when(i == steps - 1)
    def _():
        late[-1].wait()
        for c in exchange:
            c.wait()


def attend(order, x, cot, blocks, wqkv, vecs, bias, images):
    tokens = x.shape[0]
    stages = len(order)
    rows = tokens // 4
    keys_tab, query_tab, _, query_back = gather_tables(images)
    vm = pl.BlockSpec(memory_space=pltpu.VMEM)
    hbm = pl.BlockSpec(memory_space=pl.ANY)
    image = lambda *shape: pl.BlockSpec((1, *shape), lambda i: (i, 0, 0))
    table = image(256, 256)
    return pl.pallas_call(
        functools.partial(attend_kernel, rows, order),
        grid=(images,),
        out_shape=[
            jax.ShapeDtypeStruct((4, rows, D), BF16),
            jax.ShapeDtypeStruct((images, HEADS, 256, 256), BF16),
            jax.ShapeDtypeStruct((images, D, 256), BF16),
            jax.ShapeDtypeStruct((images, D, 256), BF16),
            jax.ShapeDtypeStruct((images, 256, D), BF16),
            jax.ShapeDtypeStruct((images, D, 256), BF16),
            jax.ShapeDtypeStruct((images, 16, 256), F32),
            jax.ShapeDtypeStruct((tokens, D), BF16),
            jax.ShapeDtypeStruct(blocks.shape, BF16),
        ],
        in_specs=[vm, hbm, hbm] + [vm] * 3 + [table] * 3,
        out_specs=[
            pl.BlockSpec((4, rows, D), lambda i: (0, 0, 0)),
            pl.BlockSpec((1, HEADS, 256, 256), lambda i: (i, 0, 0, 0)),
            image(D, 256),
            image(D, 256),
            image(256, D),
            image(D, 256),
            image(16, 256),
            hbm,
            hbm,
        ],
        scratch_shapes=[
            pltpu.VMEM((2, rows, D), BF16),
            pltpu.VMEM((4, rows, 3 * D), BF16),
            pltpu.SemaphoreType.DMA((stages,)),
            pltpu.SemaphoreType.DMA((stages,)),
            pltpu.SemaphoreType.DMA,
            pltpu.SemaphoreType.DMA((3,)),
            pltpu.SemaphoreType.DMA((3,)),
        ],
        input_output_aliases={2: 8},
        compiler_params=pltpu.CompilerParams(
            collective_id=2, has_side_effects=True, vmem_limit_bytes=VMEM_LIMIT
        ),
        name="attend",
    )(
        x.reshape(4, rows, D),
        cot,
        blocks,
        wqkv,
        vecs,
        bias,
        keys_tab,
        query_tab,
        query_back,
    )


GELU_A = float(np.sqrt(2.0 / np.pi))
GELU_B = 0.044715


def unpack_mlp(part, places, blocks, flat, w1, w2, vecs):
    unflatten(part, [(places, blocks)], flat)
    take_matrix(flat, 0, w1)
    take_matrix(flat, 4608, w2)
    for j in range(12):
        vecs[0:1, j * 128 : (j + 1) * 128] = flat[9216 + j : 9217 + j, :]
    for v in range(3):
        for j in range(3):
            at = 9228 + 3 * v + j
            vecs[1 + v : 2 + v, j * 128 : (j + 1) * 128] = flat[at : at + 1, :]


def pack_mlp(part, places, g_w1, g_w2t, g_vec, flat, out):
    put_matrix(flat, 0, g_w1)
    for j in range(3):
        flat[pl.ds(4608 + j, FF, stride=3), :] = g_w2t[j * 128 : (j + 1) * 128, :].T
    for j in range(12):
        flat[9216 + j : 9217 + j, :] = g_vec[0:1, j * 128 : (j + 1) * 128]
    for v in range(3):
        for j in range(3):
            at = 9228 + 3 * v + j
            flat[at : at + 1, :] = g_vec[1 + v : 2 + v, j * 128 : (j + 1) * 128]
    flat[9237:, :] = jnp.zeros((flat.shape[0] - 9237, 128), F32)
    to_blocks(part, [(places, out)], flat)


def mlp_kernel(
    part,
    places,
    cot_ref,
    mixed_ref,
    x_ref,
    wproj,
    vecs_a,
    blocks,
    out_ref,
    d_res_ref,
    d_mixed_ref,
    sums,
    g_proj,
    g_vec,
    w1,
    w2,
    vecs,
    g_w1,
    g_w2t,
    flat,
):
    i = pl.program_id(0)

    @pl.when(i == 0)
    def _():
        unpack_mlp(part, places, blocks, flat, w1, w2, vecs)
        g_w1[...] = jnp.zeros_like(g_w1)
        g_w2t[...] = jnp.zeros_like(g_w2t)
        g_proj[...] = jnp.zeros_like(g_proj)
        g_vec[...] = jnp.zeros_like(g_vec)

    mix = mixed_ref[...]
    grad = cot_ref[...]
    columns = [slice(0, FF // 2), slice(FF // 2, FF)]
    res = x_ref[...].astype(F32) + dot(mix, wproj[...]) + vecs_a[4:5, :]
    d_act = dot_t(grad, w2[columns[0], :])
    xhat, scale = norm_parts(res)
    gain = vecs[1:2, :D]
    normed = (xhat * gain + vecs[2:3, :D]).astype(BF16)
    grad_t = grad.T
    normed_t = normed.T
    hidden = dot(normed, w1[:, columns[0]])
    out, d_normed = res + vecs[3:4, :D], None
    for f, cols in enumerate(columns):
        value, d_value = hidden + vecs[0:1, cols], d_act
        if f == 0:
            hidden = dot(normed, w1[:, columns[f + 1]])
            d_act = dot_t(grad, w2[columns[f + 1], :])
        square = value * value
        t = jnp.tanh(value * (GELU_A + (GELU_A * GELU_B) * square))
        half = 0.5 + 0.5 * t
        act = (value * half).astype(BF16)
        slope = half + (0.5 * value) * (1.0 - t * t) * (GELU_A + (3 * GELU_A * GELU_B) * square)
        d_hidden32 = d_value * slope
        d_hidden = d_hidden32.astype(BF16)
        g_vec[0:1, cols] += jnp.sum(d_hidden32, axis=0, keepdims=True)
        out += dot(act, w2[cols, :])
        back = dot_t(d_hidden, w1[:, cols])
        d_normed = back if d_normed is None else d_normed + back
        g_w1[:, cols] += dot(normed_t, d_hidden)
        g_w2t[:, cols] += dot(grad_t, act)
    out_ref[...] = out.astype(BF16)
    grad32 = grad.astype(F32)
    d_res = grad32 + norm_back(d_normed, xhat, scale, gain)
    d_res_ref[...] = d_res
    d_attn = d_res.astype(BF16)
    d_mixed_ref[...] = dot_t(d_attn, wproj[...]).astype(BF16)
    g_proj[...] += dot(mix.T, d_attn)
    g_vec[1:2, :D] += jnp.sum(d_normed * xhat, axis=0, keepdims=True)
    g_vec[2:3, :D] += jnp.sum(d_normed, axis=0, keepdims=True)
    g_vec[3:4, :D] += jnp.sum(grad32, axis=0, keepdims=True)
    g_vec[4:5, :D] += jnp.sum(d_res, axis=0, keepdims=True)

    @pl.when(i == pl.num_programs(0) - 1)
    def _():
        pack_mlp(part, places, g_w1, g_w2t, g_vec, flat, sums)


def mlp(part, places, cot, mixed, x, wproj, vecs_a, blocks):
    tokens = x.shape[0]
    chunk = tokens // 7
    vm = pl.BlockSpec(memory_space=pltpu.VMEM)
    tile = pl.BlockSpec((chunk, D), lambda i: (i, 0))
    fixed = lambda *shape: pl.BlockSpec(shape, lambda i: (0,) * len(shape))
    return pl.pallas_call(
        functools.partial(mlp_kernel, part, places),
        grid=(7,),
        out_shape=[
            jax.ShapeDtypeStruct((tokens, D), BF16),
            jax.ShapeDtypeStruct((tokens, D), F32),
            jax.ShapeDtypeStruct((tokens, D), BF16),
            jax.ShapeDtypeStruct((part.devices, part.rows, 128), BF16),
            jax.ShapeDtypeStruct((D, D), F32),
            jax.ShapeDtypeStruct((8, FF), F32),
        ],
        in_specs=[tile] * 3 + [vm] * 3,
        out_specs=[tile] * 3 + [fixed(part.devices, part.rows, 128), fixed(D, D), fixed(8, FF)],
        scratch_shapes=[
            pltpu.VMEM((D, FF), BF16),
            pltpu.VMEM((FF, D), BF16),
            pltpu.VMEM((8, FF), F32),
            pltpu.VMEM((D, FF), F32),
            pltpu.VMEM((D, FF), F32),
            pltpu.VMEM((part.buffer, 128), F32),
        ],
        compiler_params=pltpu.CompilerParams(vmem_limit_bytes=VMEM_LIMIT),
        name="mlp",
    )(cot, mixed, x, wproj, vecs_a, blocks)


CHUNK = 192
LAST = 208


def split_float(values):
    high = values.astype(BF16)
    return high, (values - high.astype(F32)).astype(BF16)


def attend_back_kernel(
    part_a,
    part,
    order,
    chain_places,
    q_ref,
    k_ref,
    v_ref,
    mixed_ref,
    d_mixed,
    probs,
    inverse,
    keys_back,
    query_tab,
    query_back,
    x_hbm,
    d_res_hbm,
    wqkv,
    vecs,
    blocks,
    out_src,
    g_proj,
    g_vec2,
    one_fine,
    one_coarse,
    grad_a_ref,
    grad_ref,
    out_ref,
    dx_ref,
    g_bias,
    g_qkv,
    g_vec,
    flat,
    table,
    shifted,
    line,
    d_query_t,
    d_key_value_t,
    d_qkv,
    d_in,
    x_buf,
    d_res_buf,
    load_sems,
    total,
    outgoing,
    arrived,
    send,
    recv,
    out_sem,
    out_send,
    out_recv,
    dx_sem0,
    dx_send0,
    dx_recv0,
    dx_sem1,
    dx_send1,
    dx_recv1,
    dx_sem2,
    dx_send2,
    dx_recv2,
    dx_sem3,
    dx_send3,
    dx_recv3,
    *chain_scratch,
):
    i = pl.program_id(0)
    steps = pl.num_programs(0)
    stages = len(order)
    dp, grp = lax.axis_index("dp"), lax.axis_index("grp")
    cube = CubeSum(order, blocks, total, outgoing, arrived, (send, recv))
    exchange = exchange_copies(out_src, out_ref, dp, grp, out_sem, out_send, out_recv)
    dx_sems = (
        (dx_sem0, dx_send0, dx_recv0),
        (dx_sem1, dx_send1, dx_recv1),
        (dx_sem2, dx_send2, dx_recv2),
        (dx_sem3, dx_send3, dx_recv3),
    )
    loads = [
        pltpu.make_async_copy(x_hbm, x_buf, load_sems.at[0]),
        pltpu.make_async_copy(d_res_hbm, d_res_buf, load_sems.at[1]),
    ]

    def chunk(c):
        size = LAST if c == 3 else CHUNK
        return chunk_copies(d_in, dx_ref, CHUNK * c, size, dp, grp, *dx_sems[c], 0)

    @pl.when(i == 0)
    def _():
        for c in loads:
            c.start()
        g_bias[...] = jnp.zeros_like(g_bias)
        g_qkv[...] = jnp.zeros_like(g_qkv)
        g_vec[...] = jnp.zeros_like(g_vec)
        greet(cube_partners(order, dp, grp) + [window_partner(dp, grp, 3)])

    starts = starts_of(stage_weights(order)[::-1], SUM_STEPS)
    for k, start in zip(reversed(range(stages)), starts):

        @pl.when(i == start)
        def _(k=k):
            if k < stages - 1:
                cube.finish(k + 1)
            cube.start(k)

    @pl.when(i == min(SUM_STEPS, steps - 1))
    def _():
        cube.finish(0)

    @pl.when(i == 0)
    def _():
        for c in exchange:
            c.start()

    dm_t = dot(query_tab[0], image_rows(d_mixed, i, slice(0, D))).T
    spread_heads = lambda ref: jnp.concatenate(
        [jnp.broadcast_to(ref[h : h + 1], (HDIM, 256)) for h in range(HEADS)], axis=0
    )
    dm_t = (dm_t * spread_heads(inverse[0])).astype(BF16)
    products = dm_t.astype(F32) * mixed_ref[0].astype(F32)
    q_t, k_t, v_ext = q_ref[0], k_ref[0], v_ref[0]

    def d_probs_of(h):
        heads = jnp.concatenate([only_head(dm_t, h), only_head(dm_t, h + 1)], axis=1)
        return dot(v_ext[:, tile_of(h)], heads)

    def softmax_back(d_probs, h):
        e = probs[0, h]
        own = slice(h * HDIM, (h + 1) * HDIM)
        sums = jnp.sum(products[own], axis=0, keepdims=True)
        halves = []
        for half in range(2):
            lanes = slice(128 * half, 128 * half + 128)
            e32 = e[:, lanes].astype(F32)[56 * half : 56 * half + KEYS]
            ds = e32 * (half_of(d_probs, half) - sums[:, lanes])
            g_bias[h, half] += ds
            halves.append(ds)
        return spread(halves)

    def gather_back(h, ds):
        own = slice(h * HDIM, (h + 1) * HDIM)
        d_query_t[own, :] = (dot(k_t[own, :], ds) * HDIM ** (-0.5)).astype(BF16)
        d_key_value_t[own, :] = dot_t(q_t[own, :], ds).astype(BF16)
        d_key_value_t[D + h * HDIM : D + (h + 1) * HDIM, :] = dot_t(
            dm_t[own, :], probs[0, h]
        ).astype(BF16)

    ahead = d_probs_of(0)
    waiting = []
    for h in range(0, HEADS, 2):
        now = ahead
        if h + 2 < HEADS:
            ahead = d_probs_of(h + 2)
        for c in range(2):
            waiting.append((h + c, softmax_back(now[:, c * 256 : (c + 1) * 256], h + c)))
        while len(waiting) > 1:
            gather_back(*waiting.pop(0))
    for last in waiting:
        gather_back(*last)
    put_image_rows(d_qkv, i, slice(0, D), dot_t(query_back[0], d_query_t[...]))
    put_image_rows(d_qkv, i, slice(D, 3 * D), dot_t(keys_back[0], d_key_value_t[...]))

    @pl.when(i == 3)
    def _():
        for c in loads:
            c.wait()

    @pl.when(lax.rem(i, 4) == 3)
    def _():
        c = i // 4
        at = pl.ds(pl.multiple_of(c * CHUNK, 16), LAST)
        xhat, scale = norm_parts(x_buf[:, at, :].reshape(4 * LAST, D).astype(F32))
        gain = vecs[0:1, :]
        normed = (xhat * gain + vecs[1:2, :]).astype(BF16)
        row = lax.rem(lax.broadcasted_iota(jnp.int32, (4 * LAST, 1), 0), LAST)
        counts = row < jnp.where(i == steps - 1, LAST, CHUNK)
        grads = d_qkv[:, at, :].reshape(4 * LAST, 3 * D)
        grads = jnp.where(counts, grads, 0)
        d_normed = dot_t(grads, wqkv[...])
        result = d_res_buf[:, at, :].reshape(4 * LAST, D) + norm_back(d_normed, xhat, scale, gain)
        result = result.astype(BF16).reshape(4, LAST, D)
        d_in[:, at, :] = result
        g_qkv[...] += dot(normed.T, grads)
        g_vec[0:1, :] += jnp.sum(grads.astype(F32), axis=0, keepdims=True)
        g_vec[1:2, :D] += jnp.sum(d_normed * xhat, axis=0, keepdims=True)
        g_vec[2:3, :D] += jnp.sum(d_normed, axis=0, keepdims=True)

    for c in range(4):

        @pl.when(i == 4 * c + 3)
        def _(c=c):
            for copy in chunk(c):
                copy.start()

    @pl.when(i == steps - 1)
    def _():
        device = dp * lax.axis_size("grp") + grp
        grad_ref[...] = shift_lanes(total[0], part.lane(device), False)
        half = len(chain_scratch) // 2
        sums = (chain_scratch[0], chain_scratch[half])
        pack(
            part_a, list(zip(chain_places, sums)), one_fine, one_coarse,
            g_bias, g_qkv, g_vec, g_proj, g_vec2, flat, table, shifted, line,
        )
        cubes = []
        for c, chain_order in enumerate((order, other_order(order))):
            own, *buffers, sent, received = chain_scratch[c * half : (c + 1) * half]
            cubes.append(CubeSum(chain_order, own, *buffers, (sent, received)))
        for k in reversed(range(stages)):
            for chain in cubes:
                chain.start(k)
            for chain in cubes:
                chain.finish(k)
        grad_a = jnp.concatenate([chain.total[0] for chain in cubes], axis=0)
        grad_a_ref[...] = shift_lanes(grad_a, part_a.lane(device), False)
        for c in exchange:
            c.wait()
        for c in range(4):
            for copy in chunk(c):
                copy.wait()


def attend_back(
    part_a, part, order, chain_places, saved, d_mixed, probs, inverse, x, d_res, wqkv, vecs, blocks,
    out, g_proj, g_vec2,
):
    images = probs.shape[0]
    tokens = out.shape[0]
    rows = tokens // 4
    stages = len(order)
    _, query_tab, keys_back, query_back = gather_tables(images)
    fine, coarse, _ = bias_tables()
    vm = pl.BlockSpec(memory_space=pltpu.VMEM)
    hbm = pl.BlockSpec(memory_space=pl.ANY)
    image = lambda *shape: pl.BlockSpec((1, *shape), lambda i: (i, 0, 0))
    by_window = lambda array: array.reshape(4, rows, -1)
    chain_scratch = []
    for count in part_a.split(SUM_SHARE):
        chain_scratch.append(pltpu.VMEM((part.devices, count, 128), BF16))
        chain_scratch += CubeSum.scratch(part.devices, count, stages)
    grad_a, grad_b, output, dx = pl.pallas_call(
        functools.partial(attend_back_kernel, part_a, part, order, chain_places),
        grid=(images,),
        out_shape=[
            jax.ShapeDtypeStruct((part_a.rows, 128), F32),
            jax.ShapeDtypeStruct((part.rows, 128), F32),
            jax.ShapeDtypeStruct((tokens, D), BF16),
            jax.ShapeDtypeStruct((4, rows, D), BF16),
        ],
        in_specs=[
            image(D, 256),
            image(D, 256),
            image(256, D),
            image(D, 256),
            vm,
            pl.BlockSpec((1, HEADS, 256, 256), lambda i: (i, 0, 0, 0)),
            image(16, 256),
        ]
        + [image(256, 256)] * 3
        + [hbm, hbm, vm, vm, vm, hbm, vm, vm, vm, vm],
        out_specs=[
            pl.BlockSpec((part_a.rows, 128), lambda i: (0, 0)),
            pl.BlockSpec((part.rows, 128), lambda i: (0, 0)),
            hbm,
            hbm,
        ],
        scratch_shapes=[
            pltpu.VMEM((HEADS, 2, KEYS, 128), F32),
            pltpu.VMEM((D, 3 * D), F32),
            pltpu.VMEM((8, 3 * D), F32),
            pltpu.VMEM((part_a.buffer, 128), F32),
            pltpu.VMEM((16, 512), F32),
            pltpu.VMEM((4, 14 * 16, 128), F32),
            pltpu.VMEM((8, 512), F32),
            pltpu.VMEM((D, 256), BF16),
            pltpu.VMEM((2 * D, 256), BF16),
            pltpu.VMEM((4, rows, 3 * D), BF16),
            pltpu.VMEM((4, rows, D), BF16),
            pltpu.VMEM((4, rows, D), BF16),
            pltpu.VMEM((4, rows, D), F32),
            pltpu.SemaphoreType.DMA((2,)),
        ]
        + CubeSum.scratch(part.devices, part.rows, stages)
        + [
            pltpu.SemaphoreType.DMA,
            pltpu.SemaphoreType.DMA((3,)),
            pltpu.SemaphoreType.DMA((3,)),
        ]
        * 5
        + chain_scratch,
        compiler_params=pltpu.CompilerParams(
            collective_id=3, has_side_effects=True, vmem_limit_bytes=VMEM_LIMIT
        ),
        name="attend_back",
    )(
        *saved,
        by_window(d_mixed),
        probs,
        inverse,
        keys_back,
        query_tab,
        query_back,
        by_window(x),
        by_window(d_res),
        wqkv,
        vecs,
        blocks,
        out,
        g_proj,
        g_vec2,
        jnp.asarray(fine),
        jnp.asarray(coarse),
    )
    grad_a = grad_a.reshape(-1)[: part_a.length]
    grad_b = grad_b.reshape(-1)[: part.length]
    return grad_a, grad_b, output, dx


def to_blocks(part, chains, flat):
    for device in range(part.devices):
        at = part.start(device)
        for places, out in chains:
            out[places[device]] = flat[at : at + out.shape[1], :].astype(BF16)
            at += out.shape[1]


def pack(
    part, chains, one_fine, one_coarse,
    g_bias, g_qkv, g_vec1, g_proj, g_vec2, flat, table, shifted, line,
):
    row, lane = divmod(ATTN_VECTORS[0], 128)
    flat[4608:, :] = jnp.zeros((flat.shape[0] - 4608, 128), F32)
    put_matrix(flat, 0, g_qkv)
    put_matrix(flat, 3456, g_proj)
    vectors = [
        g_vec1[1:2, :D],
        g_vec1[2:3, :D],
        g_vec1[0:1, :D],
        g_vec1[0:1, 2 * D :],
        g_vec2[4:5, :D],
    ]
    pieces = [v[:, j * 128 : (j + 1) * 128] for v in vectors for j in range(3)]
    pieces += [jnp.zeros((1, 128), F32)]
    flat[row : row + 16, :] += shift_lanes(jnp.concatenate(pieces, axis=0), lane, True)
    for h in range(HEADS):
        table[...] = jnp.zeros_like(table)
        for half in range(2):
            turned = g_bias[h, half].T
            for y in range(WIN):
                for at, length, source in bias_runs(half, WIN * half + y):
                    table[0:14, source : source + length] += turned[
                        y * 14 : y * 14 + 14, at : at + length
                    ]
        for c in range(4):
            shifted[c, pl.ds(h, 14, stride=16), :] = table[0:14, c * 128 : (c + 1) * 128]
    high, low = split_float(jnp.concatenate([shifted[c] for c in range(3)], axis=1))
    moved_fine = dot_t(high, one_fine[...]) + dot_t(low, one_fine[...])
    high, low = split_float(shifted[3])
    moved_coarse = dot_t(high, one_coarse[...]) + dot_t(low, one_coarse[...])
    g_fine = jnp.zeros((16, 384), F32)
    g_coarse = jnp.zeros((16, 256), F32)
    for qx in range(14):
        at = slice(qx * 16, qx * 16 + 16)
        g_fine += pltpu.roll(moved_fine[at], (384 - qx) % 384, 1)
        g_coarse += pltpu.roll(moved_coarse[at], (256 - qx // 2) % 256, 1)
    for t, h, length, row, lane, count in table_lines():
        line[...] = jnp.zeros_like(line)
        line[0:1, lane : lane + length] = (g_fine, g_coarse)[t][h : h + 1, :length]
        for c in range(count):
            flat[row + c : row + c + 1, :] += line[0:1, c * 128 : (c + 1) * 128]
    to_blocks(part, chains, flat)


def adamw(master, first, second, grads):
    first_new = beta_one * first + (1.0 - beta_one) * grads
    second_new = beta_two * second + (1.0 - beta_two) * grads * grads
    first_hat = first_new / (1.0 - beta_one**STEP)
    second_hat = second_new / (1.0 - beta_two**STEP)
    master_new = master - learn_rate * (
        first_hat / (jnp.sqrt(second_hat) + adam_eps) + decay_rate * master
    )
    return (first_new, second_new, master_new)


def body(
    tokens, cotangent, attn_master, attn_first, attn_second, mlp_master, mlp_first, mlp_second
):
    n_dp, n_grp = lax.axis_size("dp"), lax.axis_size("grp")
    order = bit_order(n_dp, n_grp)
    chain_places = [place_list(o, n_dp, n_grp) for o in (order, other_order(order))]
    part_a = Part(n_dp * n_grp, attn_master.shape[0])
    part_b = Part(n_dp * n_grp, mlp_master.shape[0])
    images = tokens.shape[1] // 4 // SEQ
    wqkv, wproj, vecs_a, bias, x, blocks_b = gather_params(
        part_a, part_b, order, chain_places, attn_master, mlp_master, tokens[0]
    )
    mixed, probs, *saved, inverse, cot, blocks_b = attend(
        order, x, cotangent[0], blocks_b, wqkv, vecs_a, bias, images
    )
    mixed = mixed.reshape(-1, D)
    out, d_res, d_mixed, sums_b, g_proj, g_vec2 = mlp(
        part_b, chain_places[0], cot, mixed, x, wproj, vecs_a, blocks_b
    )
    grad_a, grad_b, output, dx = attend_back(
        part_a, part_b, order, chain_places, saved, d_mixed, probs, inverse, x, d_res, wqkv,
        vecs_a, sums_b, out, g_proj, g_vec2,
    )
    attn_new = adamw(attn_master, attn_first, attn_second, grad_a)
    mlp_new = adamw(mlp_master, mlp_first, mlp_second, grad_b)
    input_grad = dx.reshape(-1, D).astype(F32)
    return (output[None], input_grad[None], *attn_new, *mlp_new)


def solution(mesh):
    flat_spec = P(("dp", "grp"))
    token_spec = P("dp", "grp", None)
    placed = (token_spec, token_spec) + (flat_spec,) * 6
    return jax.shard_map(
        body, mesh=mesh, in_specs=placed, out_specs=placed, check_vma=False
    )
```

```python
import functools
import itertools

import jax
import jax.numpy as jnp
import ml_dtypes
import numpy as np
from jax import lax
from jax.experimental import pallas as pl
from jax.experimental.pallas import tpu as pltpu
from jax.sharding import PartitionSpec as P

D = 384
HEADS = 12
HDIM = 32
FF = 1536
WIN = 7
STEP = 10
SEQ = WIN * WIN
HALF = 64
FINE = (3 * WIN - 2) ** 2
COARSE = (2 * WIN - 1) ** 2
KEYS = 192

beta_one = 0.9
beta_two = 0.999
learn_rate = 0.04
decay_rate = 0.05
adam_eps = 1e-08
norm_eps = 1e-05
masked_score = -1e30

F32 = jnp.float32
BF16 = jnp.bfloat16
MESH = pl.DeviceIdType.MESH
VMEM_LIMIT = 58 * 2**20


def token_place(gy, gx):
    window = 2 * (gy // WIN) + gx // WIN
    return window * HALF + (gy % WIN) * WIN + gx % WIN


@functools.cache
def gather_tables(images):
    keys = np.zeros((images, 256, 256), np.float32)
    queries = np.zeros((images, 256, 256), np.float32)
    for i in range(images):
        for gy in range(2 * WIN):
            for gx in range(2 * WIN):
                at = token_place(gy, gx) + i
                key = gy * 14 + gx if gy < 10 else 192 + (gy - 10) * 14 + gx
                keys[i, key, at] = 1.0
                keys[i, 140 + (gy // 2) * WIN + gx // 2, at] = 0.25
                queries[i, (gy // WIN) * 128 + (gy % WIN) * 14 + gx, at] = 1.0
    return (
        keys.astype(ml_dtypes.bfloat16),
        queries.astype(ml_dtypes.bfloat16),
        np.ascontiguousarray(keys.transpose(0, 2, 1)).astype(ml_dtypes.bfloat16),
        np.ascontiguousarray(queries.transpose(0, 2, 1)).astype(ml_dtypes.bfloat16),
    )


@functools.cache
def bias_tables():
    fine = np.zeros((384, 384), np.float32)
    coarse = np.zeros((256, 128), np.float32)
    for a in range(4, 23):
        for kx in range(14):
            fine[19 * (a - 4) + kx + 9, a * 14 + kx] = 1.0
    for p in range(13):
        for x in range(WIN):
            coarse[13 * p + x + 6, p * WIN + x] = 1.0
    mask = np.zeros((2, KEYS, 128), np.float32)
    for half in range(2):
        for q in range(98):
            qx = q % 14
            for e in range(KEYS):
                at = e + 56 * half
                if at < 140:
                    ok = abs_ok(qx, at % 14)
                elif at < 189:
                    ok = True
                elif at < 192:
                    ok = False
                else:
                    ok = at < 248 and abs_ok(qx, (at - 192) % 14)
                mask[half, e, q] = 0.0 if ok else masked_score
    return fine.astype(ml_dtypes.bfloat16), coarse.astype(ml_dtypes.bfloat16), mask


def abs_ok(qx, kx):
    return kx < 10 if qx < WIN else kx >= 4


def bias_runs(half, qy):
    fine = (13 - qy) * 14
    pool = 384 + (6 - qy // 2) * WIN
    if half == 0:
        return [(0, 140, fine), (140, 49, pool)]
    return [(0, 84, fine + 56), (84, 49, pool), (136, 56, fine + 140)]


class Part:
    def __init__(self, devices, length):
        self.devices = devices
        self.length = length
        self.rows = -(-((length + 126) // 128 + 1) // 16) * 16
        self.buffer = -(-(self.start(devices - 1) + self.rows) // 8) * 8

    def start(self, device):
        return device * self.length // 128

    def lane(self, device):
        return lax.rem(device * self.length, 128)

    def split(self, share):
        first = max(16, min(self.rows - 16, round(self.rows * share / 16) * 16))
        return first, self.rows - first

    def padded(self, vector):
        extra = self.rows * 128 - self.length
        return jnp.pad(vector, (0, extra)).reshape(self.rows, 128)


GATHER_SHARE = 0.7
SUM_SHARE = 0.5
GATHER_STEPS = 7
SUM_STEPS = 12


def bit_order(n_dp, n_grp):
    dp_bits = [("dp", 2**b) for b in range(n_dp.bit_length() - 1)]
    grp_bits = [("grp", 2**b) for b in reversed(range(n_grp.bit_length() - 1))]
    return dp_bits[1:2] + grp_bits + dp_bits[2:] + dp_bits[:1]


def other_order(order):
    grp_bits = [stage for stage in order if stage[0] == "grp"]
    dp_bits = [stage for stage in order if stage[0] == "dp"]
    return dp_bits[:-1] + grp_bits + dp_bits[-1:]


def stage_weights(order):
    weights = []
    for k, (axis, stride) in enumerate(order):
        relative = 0.35 if (axis, stride) == ("dp", 1) else 2 if (axis == "grp" and stride > 1) else 1
        weights.append(relative * 2**k)
    return weights


def starts_of(weights, steps):
    done, starts = 0.0, []
    for weight in weights:
        starts.append(int(steps * done / sum(weights)))
        done += weight
    return starts


def place_of(order, dp, grp):
    place = 0
    for k, (axis, stride) in enumerate(order):
        place = place + ((dp if axis == "dp" else grp) // stride) % 2 * 2**k
    return place


def partner_of(axis, stride, dp, grp):
    if axis == "dp":
        return (dp + (1 - 2 * ((dp // stride) % 2)) * stride, grp)
    return (dp, grp + (1 - 2 * ((grp // stride) % 2)) * stride)


def greet(partners):
    barrier = pltpu.get_barrier_semaphore()
    for partner in partners:
        pl.semaphore_signal(barrier, inc=1, device_id=partner, device_id_type=MESH)
    pl.semaphore_wait(barrier, len(partners))


def cube_partners(order, dp, grp):
    return [partner_of(axis, stride, dp, grp) for axis, stride in order]


def shift_lanes(values, amount, up):
    lane = lax.broadcasted_iota(jnp.int32, values.shape, 1)
    if up:
        turned = pltpu.roll(values, amount, 1)
        return jnp.where(lane >= amount, turned, pltpu.roll(turned, 1, 0))
    turned = pltpu.roll(values, lax.rem(128 - amount, 128), 1)
    return jnp.where(lane < 128 - amount, turned, pltpu.roll(turned, values.shape[0] - 1, 0))


def window_partner(dp, grp, k):
    low, high = dp % 2, dp // 2 % 2
    to = dp
    if k % 2:
        to = to + 1 - 2 * low
    if k // 2:
        to = to + 2 * (1 - 2 * high)
    return (to, grp)


def exchange_copies(source, target, dp, grp, own_sem, send_sems, recv_sems):
    rows = source.shape[0] // 4
    slot = dp % 4
    mine = pl.ds(pl.multiple_of(slot * rows, 16), rows)
    own = pltpu.make_async_copy(source.at[mine], target.at[mine], own_sem)
    sends = []
    for k in (3, 2, 1):
        to, _ = window_partner(dp, grp, k)
        theirs = pl.ds(pl.multiple_of(to % 4 * rows, 16), rows)
        sends.append(
            pltpu.make_async_remote_copy(
                src_ref=source.at[theirs],
                dst_ref=target.at[mine],
                send_sem=send_sems.at[k - 1],
                recv_sem=recv_sems.at[k - 1],
                device_id=(to, grp),
                device_id_type=MESH,
            )
        )
    return [own] + sends


def cube_copy(order, k, source, target, dp, grp, send_sems, recv_sems):
    axis, stride = order[k]
    return pltpu.make_async_remote_copy(
        src_ref=source,
        dst_ref=target,
        send_sem=send_sems.at[k],
        recv_sem=recv_sems.at[k],
        device_id=partner_of(axis, stride, dp, grp),
        device_id_type=MESH,
    )


def gather_copy(order, k, blocks, dp, grp, sems):
    place = place_of(order, dp, grp)
    held = blocks.at[pl.ds(place // 2**k * 2**k, 2**k)]
    return cube_copy(order, k, held, held, dp, grp, *sems)


class CubeSum:
    def __init__(self, order, blocks, total, outgoing, arrived, sems):
        self.order, self.blocks, self.total = order, blocks, total
        self.outgoing, self.arrived, self.sems = outgoing, arrived, sems
        self.dp, self.grp = lax.axis_index("dp"), lax.axis_index("grp")
        self.place = place_of(order, self.dp, self.grp)
        self.last = len(order) - 1

    def mine(self, k):
        return self.place // 2**k % 2 * 2**k

    def copy(self, k):
        size = 2**k
        if k == self.last:
            source = self.blocks.at[pl.ds(size - self.mine(k), size)]
        else:
            source = self.outgoing.at[pl.ds(size, size)]
        target = self.arrived.at[pl.ds(size, size)]
        return cube_copy(self.order, k, source, target, self.dp, self.grp, *self.sems)

    def start(self, k):
        self.copy(k).start()

    def finish(self, k):
        size, mine = 2**k, self.mine(k)
        self.copy(k).wait()

        def added(j):
            if k == self.last:
                held = self.blocks[mine + j].astype(F32)
            else:
                held = self.total[mine + j]
            return held + self.arrived[size + j].astype(F32)

        keep = size // 2 if k else 1
        kept = self.mine(k - 1) if k else 0

        def add(j, carry):
            value = added(kept + j)
            if k:
                self.outgoing[keep + j] = added(keep - kept + j).astype(BF16)
            self.total[kept + j] = value
            return carry

        lax.fori_loop(0, keep, add, 0)

    @staticmethod
    def scratch(devices, rows, stages):
        return [
            pltpu.VMEM((devices // 2, rows, 128), F32),
            pltpu.VMEM((devices // 2, rows, 128), BF16),
            pltpu.VMEM((devices, rows, 128), BF16),
            pltpu.SemaphoreType.DMA((stages,)),
            pltpu.SemaphoreType.DMA((stages,)),
        ]


def chunk_copies(source, target, first, size, dp, grp, own_sem, send_sems, recv_sems, skip):
    slot = dp % 4
    into = target.at[slot, pl.ds(first, size)]
    rows = pl.ds(first - skip, size)
    copies = [pltpu.make_async_copy(source.at[slot, rows], into, own_sem)]
    for k in (3, 2, 1):
        to, _ = window_partner(dp, grp, k)
        copies.append(
            pltpu.make_async_remote_copy(
                src_ref=source.at[to % 4, rows],
                dst_ref=into,
                send_sem=send_sems.at[k - 1],
                recv_sem=recv_sems.at[k - 1],
                device_id=(to, grp),
                device_id_type=MESH,
            )
        )
    return copies


def place_list(order, n_dp, n_grp):
    return [place_of(order, d // n_grp, d % n_grp) for d in range(n_dp * n_grp)]


ATTN_VECTORS = (D * 3 * D + D * D + HEADS * FINE + HEADS * COARSE, 5)
TABLE_AT = D * 3 * D + D * D


def unflatten(part, chains, flat):
    for device in range(part.devices):
        at = part.start(device)
        pieces = [blocks[places[device]].astype(F32) for places, blocks in chains]
        block = jnp.concatenate(pieces, axis=0) if len(pieces) > 1 else pieces[0]
        first = block[0:1] + flat[at : at + 1, :] if device else block[0:1]
        flat[at : at + part.rows, :] = block
        flat[at : at + 1, :] = first


def take_matrix(flat, first, target):
    rows, columns = target.shape
    count = columns // 128
    for j in range(count):
        target[:, j * 128 : (j + 1) * 128] = flat[pl.ds(first + j, rows, stride=count), :].astype(
            target.dtype
        )


def put_matrix(flat, first, source):
    rows, columns = source.shape
    count = columns // 128
    for j in range(count):
        flat[pl.ds(first + j, rows, stride=count), :] = source[:, j * 128 : (j + 1) * 128]


TABLES = ((TABLE_AT, FINE), (TABLE_AT + HEADS * FINE, COARSE))


def table_lines():
    for t, (first, length) in enumerate(TABLES):
        for h in range(HEADS):
            row, lane = divmod(first + h * length, 128)
            yield t, h, length, row, lane, -(-(lane + length) // 128)


def prepare(
    part, chains, one_fine, one_coarse, mask_ref,
    wqkv, wproj, vecs, bias, flat, tab_fine, tab_coarse, shifted, turned,
):
    unflatten(part, chains, flat)
    take_matrix(flat, 0, wqkv)
    take_matrix(flat, 3456, wproj)
    row, lane = divmod(ATTN_VECTORS[0], 128)
    rows = shift_lanes(flat[row : row + 16, :], lane, False)
    for v in range(5):
        for j in range(3):
            vecs[v : v + 1, j * 128 : (j + 1) * 128] = rows[3 * v + j : 3 * v + j + 1]
    tab_fine[...] = jnp.zeros_like(tab_fine)
    tab_coarse[...] = jnp.zeros_like(tab_coarse)
    for t, h, length, row, lane, count in table_lines():
        line = jnp.concatenate([flat[row + c : row + c + 1, :] for c in range(count)], axis=1)
        (tab_fine, tab_coarse)[t][h : h + 1, 0:length] = line[:, lane : lane + length]
    fine, coarse = tab_fine[...], tab_coarse[...]
    fine = jnp.concatenate([pltpu.roll(fine, qx, 1) for qx in range(14)], axis=0)
    coarse = jnp.concatenate([pltpu.roll(coarse, qx // 2, 1) for qx in range(14)], axis=0)
    fine = dot(fine.astype(BF16), one_fine[...])
    for c in range(3):
        shifted[c] = fine[:, c * 128 : (c + 1) * 128]
    shifted[3] = dot(coarse.astype(BF16), one_coarse[...])
    turned[...] = jnp.zeros_like(turned)
    for h in range(HEADS):
        table = jnp.concatenate(
            [shifted[c, pl.ds(h, 14, stride=16), :] for c in range(4)], axis=1
        )
        for half in range(2):
            for y in range(WIN):
                for at, length, source in bias_runs(half, WIN * half + y):
                    turned[half, y * 14 : y * 14 + 14, at : at + length] = table[
                        :, source : source + length
                    ]
            bias[h, half] = turned[half].T[0:KEYS] + mask_ref[half]


def early_stages(order):
    return 1 + sum(axis == "grp" for axis, _ in order)


def gather_kernel(
    part_a,
    part_b,
    order,
    chain_places,
    a_ref,
    b_ref,
    one_fine,
    one_coarse,
    mask_ref,
    tok_ref,
    wqkv,
    wproj,
    vecs,
    bias,
    x_ref,
    blocks_b,
    blocks_a1,
    blocks_a2,
    own,
    flat,
    tab_fine,
    tab_coarse,
    shifted,
    turned,
    own_sem,
    send_a1,
    recv_a1,
    send_a2,
    recv_a2,
    send_b,
    recv_b,
    x_sem,
    x_send,
    x_recv,
):
    dp, grp = lax.axis_index("dp"), lax.axis_index("grp")
    place = place_of(order, dp, grp)
    device = dp * lax.axis_size("grp") + grp
    own[...] = shift_lanes(b_ref[...], part_b.lane(device), True).astype(BF16)
    copy = pltpu.make_async_copy(own, blocks_b.at[place], own_sem)
    copy.start()
    mine = shift_lanes(a_ref[...], part_a.lane(device), True)
    orders = (order, other_order(order))
    chains = ((blocks_a1, (send_a1, recv_a1)), (blocks_a2, (send_a2, recv_a2)))
    at = 0
    for chain_order, (blocks, _) in zip(orders, chains):
        blocks[place_of(chain_order, dp, grp)] = mine[at : at + blocks.shape[1]].astype(BF16)
        at += blocks.shape[1]
    vecs[...] = jnp.zeros_like(vecs)
    greet(cube_partners(order, dp, grp) + [window_partner(dp, grp, 3)])
    copy.wait()
    exchange = exchange_copies(tok_ref, x_ref, dp, grp, x_sem, x_send, x_recv)
    first = [
        [
            gather_copy(chain_order, k, blocks, dp, grp, sems)
            for chain_order, (blocks, sems) in zip(orders, chains)
        ]
        for k in range(len(order))
    ]
    early = early_stages(order)
    second = [gather_copy(order, k, blocks_b, dp, grp, (send_b, recv_b)) for k in range(early)]
    for k, stage in enumerate(first):
        for c in stage:
            c.start()
        if k == 0:
            second[0].start()
            for c in exchange:
                c.start()
        if early <= k < 2 * early:
            second[k - early].wait()
            if k - early + 1 < early:
                second[k - early + 1].start()
        for c in stage:
            c.wait()
    prepare(
        part_a, list(zip(chain_places, (blocks_a1, blocks_a2))), one_fine, one_coarse, mask_ref,
        wqkv, wproj, vecs, bias, flat, tab_fine, tab_coarse, shifted, turned,
    )
    for k in range(len(order) - early, early):
        second[k].wait()
        if k + 1 < early:
            second[k + 1].start()
    for c in exchange:
        c.wait()


def gather_params(part_a, part_b, order, chain_places, master_a, master_b, tok):
    stages = len(order)
    rows = part_a.split(GATHER_SHARE)
    early = early_stages(order)
    fine, coarse, mask = bias_tables()
    vm = pl.BlockSpec(memory_space=pltpu.VMEM)
    hbm = pl.BlockSpec(memory_space=pl.ANY)
    return pl.pallas_call(
        functools.partial(gather_kernel, part_a, part_b, order, chain_places),
        out_shape=[
            jax.ShapeDtypeStruct((D, 3 * D), BF16),
            jax.ShapeDtypeStruct((D, D), BF16),
            jax.ShapeDtypeStruct((8, D), F32),
            jax.ShapeDtypeStruct((HEADS, 2, KEYS, 128), F32),
            jax.ShapeDtypeStruct(tok.shape, BF16),
            jax.ShapeDtypeStruct((part_b.devices, part_b.rows, 128), BF16),
        ],
        in_specs=[vm] * 5 + [hbm],
        out_specs=[vm] * 4 + [hbm] * 2,
        scratch_shapes=[
            pltpu.VMEM((part_a.devices, rows[0], 128), BF16),
            pltpu.VMEM((part_a.devices, rows[1], 128), BF16),
            pltpu.VMEM((part_b.rows, 128), BF16),
            pltpu.VMEM((part_a.buffer, 128), F32),
            pltpu.VMEM((16, 384), F32),
            pltpu.VMEM((16, 256), F32),
            pltpu.VMEM((4, 14 * 16, 128), F32),
            pltpu.VMEM((2, 128, 256), F32),
            pltpu.SemaphoreType.DMA,
            pltpu.SemaphoreType.DMA((stages,)),
            pltpu.SemaphoreType.DMA((stages,)),
            pltpu.SemaphoreType.DMA((stages,)),
            pltpu.SemaphoreType.DMA((stages,)),
            pltpu.SemaphoreType.DMA((early,)),
            pltpu.SemaphoreType.DMA((early,)),
            pltpu.SemaphoreType.DMA,
            pltpu.SemaphoreType.DMA((3,)),
            pltpu.SemaphoreType.DMA((3,)),
        ],
        compiler_params=pltpu.CompilerParams(
            collective_id=0, has_side_effects=True, vmem_limit_bytes=VMEM_LIMIT
        ),
        name="gather_params",
    )(
        part_a.padded(master_a),
        part_b.padded(master_b),
        jnp.asarray(fine),
        jnp.asarray(coarse),
        jnp.asarray(mask),
        tok,
    )


def dot(a, b):
    return jnp.dot(a, b, preferred_element_type=F32)


def dot_t(a, b):
    return lax.dot_general(a, b, (((1,), (1,)), ((), ())), preferred_element_type=F32)


def norm_parts(values):
    centered = values - jnp.mean(values, axis=-1, keepdims=True)
    scale = lax.rsqrt(jnp.mean(centered * centered, axis=-1, keepdims=True) + norm_eps)
    return centered * scale, scale


def norm_back(d_normed, xhat, scale, gain):
    dh = d_normed * gain
    return scale * (
        dh
        - jnp.mean(dh, axis=-1, keepdims=True)
        - xhat * jnp.mean(dh * xhat, axis=-1, keepdims=True)
    )


def image_rows(ref, i, columns):
    at = pl.ds(pl.multiple_of(48 * i, 16), HALF)
    return jnp.concatenate([ref[w, at, columns] for w in range(4)], axis=0)


def put_image_rows(ref, i, columns, values):
    for w in range(4):
        part = values[w * HALF : (w + 1) * HALF]
        first = pl.ds(pl.multiple_of(48 * i, 16), 16)
        rest = pl.ds(pl.multiple_of(48 * i + 16, 16), HALF - 16)
        held = jnp.where(i > 0, ref[w, first, columns].astype(F32), 0.0)
        ref[w, first, columns] = (held + part[:16]).astype(ref.dtype)
        ref[w, rest, columns] = part[16:].astype(ref.dtype)


def spread(halves):
    columns = []
    for half, values in enumerate(halves):
        pieces = [values, jnp.zeros((64 - 56 * half, 128), F32)]
        if half:
            pieces = [jnp.zeros((56, 128), F32)] + pieces
        columns.append(jnp.concatenate(pieces, axis=0))
    return jnp.concatenate(columns, axis=1).astype(BF16)


def only_head(turned, h):
    pieces = [jnp.zeros((HDIM, 256), BF16)] * 4
    pieces[h % 4] = turned[h * HDIM : (h + 1) * HDIM, :]
    return jnp.concatenate(pieces, axis=0)


def half_of(values, half):
    return values[56 * half : 56 * half + KEYS, 128 * half : 128 * half + 128]


def tile_of(h):
    return slice(h // 4 * 128, h // 4 * 128 + 128)


def interleave(first, second):
    for _ in itertools.zip_longest(first, second):
        pass


def attend_kernel(
    rows,
    order,
    x_buf,
    cot_ref,
    blocks_in,
    wqkv,
    vecs,
    bias,
    keys_tab,
    query_tab,
    query_back,
    mixed,
    probs,
    query_out,
    key_out,
    value_out,
    mixed_out,
    inverse,
    cot_out,
    blocks,
    normed,
    qkv,
    send,
    recv,
    cot_sem,
    cot_send,
    cot_recv,
):
    i = pl.program_id(0)
    steps = pl.num_programs(0)
    dp, grp = lax.axis_index("dp"), lax.axis_index("grp")
    exchange = exchange_copies(cot_ref, cot_out, dp, grp, cot_sem, cot_send, cot_recv)
    early = early_stages(order)
    late = [
        gather_copy(order, k, blocks, dp, grp, (send, recv)) for k in range(early, len(order))
    ]

    @pl.when(i == 0)
    def _():
        greet(cube_partners(order, dp, grp) + [window_partner(dp, grp, 3)])

    for k, start in enumerate(starts_of(stage_weights(order)[early:], GATHER_STEPS)):

        @pl.when(i == start)
        def _(k=k):
            if k:
                late[k - 1].wait()
            late[k].start()

    @pl.when(i == 0)
    def _():
        for c in exchange:
            c.start()

        step = rows // 7

        def norm(w):
            for c in range(7):
                at = slice(c * step, (c + 1) * step)
                xhat, _ = norm_parts(x_buf[w, at, :].astype(F32))
                normed[w % 2, at, :] = (xhat * vecs[0:1, :] + vecs[1:2, :]).astype(BF16)

        norm(0)
        for w in range(4):
            q = dot(normed[w % 2], wqkv[:, :D]) + vecs[2:3, :]
            qkv[w, :, :D] = (q * HDIM ** (-0.5)).astype(BF16)
            if w < 3:
                norm(w + 1)
            qkv[w, :, D : 2 * D] = dot(normed[w % 2], wqkv[:, D : 2 * D]).astype(BF16)
            v = dot(normed[w % 2], wqkv[:, 2 * D :]) + vecs[3:4, :]
            qkv[w, :, 2 * D :] = v.astype(BF16)

    def image(b):
        at = 2 * i + b
        q_ext = dot(query_tab[b], image_rows(qkv, at, slice(0, D)))
        kv_ext = dot(keys_tab[b], image_rows(qkv, at, slice(D, 3 * D)))
        q_t = q_ext.T.astype(BF16)
        k_ext = kv_ext[:, :D].astype(BF16)
        v_t = kv_ext[:, D:].T.astype(BF16)
        query_out[b] = q_t
        key_out[b] = kv_ext[:, :D].T.astype(BF16)
        value_out[b] = kv_ext[:, D:].astype(BF16)
        inverse[b, HEADS:16, :] = jnp.zeros((16 - HEADS, 256), F32)

        def scores_of(h):
            heads = jnp.concatenate([only_head(q_t, h), only_head(q_t, h + 1)], axis=1)
            return dot(k_ext[:, tile_of(h)], heads)

        def softmax(scores, h):
            halves, inverses = [], []
            for half in range(2):
                s = half_of(scores, half) + bias[h, half]
                e = jnp.exp(s - jnp.max(s, axis=0, keepdims=True))
                inverses.append(1.0 / jnp.sum(e, axis=0, keepdims=True))
                halves.append(e)
            e = spread(halves)
            inv = jnp.concatenate(inverses, axis=1)
            probs[b, h] = e
            inverse[b, h : h + 1, :] = inv
            return e, inv

        def mix(h, e, inv):
            own = slice(h * HDIM, (h + 1) * HDIM)
            mixed_out[b, own, :] = (dot(v_t[own, :], e) * inv).astype(BF16)

        ahead = scores_of(0)
        yield
        waiting = []
        for h in range(0, HEADS, 2):
            now = ahead
            if h + 2 < HEADS:
                ahead = scores_of(h + 2)
            for c in range(2):
                waiting.append((h + c, *softmax(now[:, c * 256 : (c + 1) * 256], h + c)))
            while len(waiting) > 1:
                mix(*waiting.pop(0))
            yield
        for last in waiting:
            mix(*last)
        yield
        put_image_rows(mixed, at, slice(0, D), dot_t(query_back[b], mixed_out[b]))

    interleave(image(0), image(1))

    @pl.when(i == steps - 1)
    def _():
        late[-1].wait()
        for c in exchange:
            c.wait()


def attend(order, x, cot, blocks, wqkv, vecs, bias, images):
    tokens = x.shape[0]
    stages = len(order)
    rows = tokens // 4
    keys_tab, query_tab, _, query_back = gather_tables(images)
    vm = pl.BlockSpec(memory_space=pltpu.VMEM)
    hbm = pl.BlockSpec(memory_space=pl.ANY)
    image = lambda *shape: pl.BlockSpec((2, *shape), lambda i: (i, 0, 0))
    table = image(256, 256)
    return pl.pallas_call(
        functools.partial(attend_kernel, rows, order),
        grid=(images // 2,),
        out_shape=[
            jax.ShapeDtypeStruct((4, rows, D), BF16),
            jax.ShapeDtypeStruct((images, HEADS, 256, 256), BF16),
            jax.ShapeDtypeStruct((images, D, 256), BF16),
            jax.ShapeDtypeStruct((images, D, 256), BF16),
            jax.ShapeDtypeStruct((images, 256, D), BF16),
            jax.ShapeDtypeStruct((images, D, 256), BF16),
            jax.ShapeDtypeStruct((images, 16, 256), F32),
            jax.ShapeDtypeStruct((tokens, D), BF16),
            jax.ShapeDtypeStruct(blocks.shape, BF16),
        ],
        in_specs=[vm, hbm, hbm] + [vm] * 3 + [table] * 3,
        out_specs=[
            pl.BlockSpec((4, rows, D), lambda i: (0, 0, 0)),
            pl.BlockSpec((2, HEADS, 256, 256), lambda i: (i, 0, 0, 0)),
            image(D, 256),
            image(D, 256),
            image(256, D),
            image(D, 256),
            image(16, 256),
            hbm,
            hbm,
        ],
        scratch_shapes=[
            pltpu.VMEM((2, rows, D), BF16),
            pltpu.VMEM((4, rows, 3 * D), BF16),
            pltpu.SemaphoreType.DMA((stages,)),
            pltpu.SemaphoreType.DMA((stages,)),
            pltpu.SemaphoreType.DMA,
            pltpu.SemaphoreType.DMA((3,)),
            pltpu.SemaphoreType.DMA((3,)),
        ],
        input_output_aliases={2: 8},
        compiler_params=pltpu.CompilerParams(
            collective_id=2, has_side_effects=True, vmem_limit_bytes=VMEM_LIMIT
        ),
        name="attend",
    )(
        x.reshape(4, rows, D),
        cot,
        blocks,
        wqkv,
        vecs,
        bias,
        keys_tab,
        query_tab,
        query_back,
    )


GELU_A = float(np.sqrt(2.0 / np.pi))
GELU_B = 0.044715


def unpack_mlp(part, places, blocks, flat, w1, w2, vecs):
    unflatten(part, [(places, blocks)], flat)
    take_matrix(flat, 0, w1)
    take_matrix(flat, 4608, w2)
    for j in range(12):
        vecs[0:1, j * 128 : (j + 1) * 128] = flat[9216 + j : 9217 + j, :]
    for v in range(3):
        for j in range(3):
            at = 9228 + 3 * v + j
            vecs[1 + v : 2 + v, j * 128 : (j + 1) * 128] = flat[at : at + 1, :]


def pack_mlp(part, chains, g_w1, g_w2t, g_vec, flat):
    put_matrix(flat, 0, g_w1)
    for j in range(3):
        flat[pl.ds(4608 + j, FF, stride=3), :] = g_w2t[j * 128 : (j + 1) * 128, :].T
    for j in range(12):
        flat[9216 + j : 9217 + j, :] = g_vec[0:1, j * 128 : (j + 1) * 128]
    for v in range(3):
        for j in range(3):
            at = 9228 + 3 * v + j
            flat[at : at + 1, :] = g_vec[1 + v : 2 + v, j * 128 : (j + 1) * 128]
    flat[9237:, :] = jnp.zeros((flat.shape[0] - 9237, 128), F32)
    to_blocks(part, chains, flat)


def mlp_kernel(
    part,
    chain_places,
    cot_ref,
    mixed_ref,
    x_ref,
    wproj,
    vecs_a,
    blocks,
    out_ref,
    d_res_ref,
    d_mixed_ref,
    sums1,
    sums2,
    g_proj,
    g_vec,
    w1,
    w2,
    vecs,
    g_w1,
    g_w2t,
    flat,
):
    i = pl.program_id(0)

    @pl.when(i == 0)
    def _():
        unpack_mlp(part, chain_places[0], blocks, flat, w1, w2, vecs)
        g_w1[...] = jnp.zeros_like(g_w1)
        g_w2t[...] = jnp.zeros_like(g_w2t)
        g_proj[...] = jnp.zeros_like(g_proj)
        g_vec[...] = jnp.zeros_like(g_vec)

    mix = mixed_ref[...]
    grad = cot_ref[...]
    columns = [slice(0, FF // 2), slice(FF // 2, FF)]
    res = x_ref[...].astype(F32) + dot(mix, wproj[...]) + vecs_a[4:5, :]
    d_act = dot_t(grad, w2[columns[0], :])
    xhat, scale = norm_parts(res)
    gain = vecs[1:2, :D]
    normed = (xhat * gain + vecs[2:3, :D]).astype(BF16)
    grad_t = grad.T
    normed_t = normed.T
    hidden = dot(normed, w1[:, columns[0]])
    out, d_normed = res + vecs[3:4, :D], None
    for f, cols in enumerate(columns):
        value, d_value = hidden + vecs[0:1, cols], d_act
        if f == 0:
            hidden = dot(normed, w1[:, columns[f + 1]])
            d_act = dot_t(grad, w2[columns[f + 1], :])
        square = value * value
        t = jnp.tanh(value * (GELU_A + (GELU_A * GELU_B) * square))
        half = 0.5 + 0.5 * t
        act = (value * half).astype(BF16)
        slope = half + (0.5 * value) * (1.0 - t * t) * (GELU_A + (3 * GELU_A * GELU_B) * square)
        d_hidden32 = d_value * slope
        d_hidden = d_hidden32.astype(BF16)
        g_vec[0:1, cols] += jnp.sum(d_hidden32, axis=0, keepdims=True)
        out += dot(act, w2[cols, :])
        back = dot_t(d_hidden, w1[:, cols])
        d_normed = back if d_normed is None else d_normed + back
        g_w1[:, cols] += dot(normed_t, d_hidden)
        g_w2t[:, cols] += dot(grad_t, act)
    out_ref[...] = out.astype(BF16)
    grad32 = grad.astype(F32)
    d_res = grad32 + norm_back(d_normed, xhat, scale, gain)
    d_res_ref[...] = d_res
    d_attn = d_res.astype(BF16)
    d_mixed_ref[...] = dot_t(d_attn, wproj[...]).astype(BF16)
    g_proj[...] += dot(mix.T, d_attn)
    g_vec[1:2, :D] += jnp.sum(d_normed * xhat, axis=0, keepdims=True)
    g_vec[2:3, :D] += jnp.sum(d_normed, axis=0, keepdims=True)
    g_vec[3:4, :D] += jnp.sum(grad32, axis=0, keepdims=True)
    g_vec[4:5, :D] += jnp.sum(d_res, axis=0, keepdims=True)

    @pl.when(i == pl.num_programs(0) - 1)
    def _():
        pack_mlp(part, list(zip(chain_places, (sums1, sums2))), g_w1, g_w2t, g_vec, flat)


def mlp(part, chain_places, cot, mixed, x, wproj, vecs_a, blocks):
    sums = [(part.devices, rows, 128) for rows in part.split(SUM_SHARE)]
    tokens = x.shape[0]
    chunk = tokens // 7
    vm = pl.BlockSpec(memory_space=pltpu.VMEM)
    tile = pl.BlockSpec((chunk, D), lambda i: (i, 0))
    fixed = lambda *shape: pl.BlockSpec(shape, lambda i: (0,) * len(shape))
    return pl.pallas_call(
        functools.partial(mlp_kernel, part, chain_places),
        grid=(7,),
        out_shape=[
            jax.ShapeDtypeStruct((tokens, D), BF16),
            jax.ShapeDtypeStruct((tokens, D), F32),
            jax.ShapeDtypeStruct((tokens, D), BF16),
            jax.ShapeDtypeStruct(sums[0], BF16),
            jax.ShapeDtypeStruct(sums[1], BF16),
            jax.ShapeDtypeStruct((D, D), F32),
            jax.ShapeDtypeStruct((8, FF), F32),
        ],
        in_specs=[tile] * 3 + [vm] * 3,
        out_specs=[tile] * 3 + [fixed(*sums[0]), fixed(*sums[1]), fixed(D, D), fixed(8, FF)],
        scratch_shapes=[
            pltpu.VMEM((D, FF), BF16),
            pltpu.VMEM((FF, D), BF16),
            pltpu.VMEM((8, FF), F32),
            pltpu.VMEM((D, FF), F32),
            pltpu.VMEM((D, FF), F32),
            pltpu.VMEM((part.buffer, 128), F32),
        ],
        compiler_params=pltpu.CompilerParams(vmem_limit_bytes=VMEM_LIMIT),
        name="mlp",
    )(cot, mixed, x, wproj, vecs_a, blocks)


def row_chunks(rows, steps):
    after = [steps * 3 // 8, steps * 5 // 8, steps * 7 // 8, steps]
    ends = [rows * done // steps // 16 * 16 for done in after]
    return [
        (done - 1, first, end - first) for done, first, end in zip(after, [0] + ends[:-1], ends)
    ]


def split_float(values):
    high = values.astype(BF16)
    return high, (values - high.astype(F32)).astype(BF16)


def attend_back_kernel(
    part_a,
    part,
    order,
    chain_places,
    images,
    q_ref,
    k_ref,
    v_ref,
    mixed_ref,
    d_mixed,
    probs,
    inverse,
    keys_back,
    query_tab,
    query_back,
    x_hbm,
    d_res_hbm,
    wqkv,
    vecs,
    blocks1,
    blocks2,
    out_src,
    g_proj,
    g_vec2,
    one_fine,
    one_coarse,
    grad_a_ref,
    grad_ref,
    out_ref,
    dx_ref,
    g_bias,
    g_qkv,
    g_vec,
    flat,
    table,
    shifted,
    line,
    d_query_t,
    d_key_value_t,
    d_qkv,
    d_in,
    x_buf,
    d_res_buf,
    load_sems,
    out_sem,
    out_send,
    out_recv,
    dx_sem0,
    dx_send0,
    dx_recv0,
    dx_sem1,
    dx_send1,
    dx_recv1,
    dx_sem2,
    dx_send2,
    dx_recv2,
    dx_sem3,
    dx_send3,
    dx_recv3,
    *chain_scratch,
):
    i = pl.program_id(0)
    steps = pl.num_programs(0)
    stages = len(order)
    dp, grp = lax.axis_index("dp"), lax.axis_index("grp")
    orders = (order, other_order(order))

    sums_a, arrived_a, sems_a = chain_scratch[:2], chain_scratch[2:4], chain_scratch[4:8]
    cubes_a, cubes_b = [], []
    for c, blocks in enumerate((blocks1, blocks2)):
        total, outgoing, arrived, *sems = chain_scratch[8 + 5 * c : 13 + 5 * c]
        cubes_b.append(CubeSum(orders[c], blocks, total, outgoing, arrived, sems))
        rows = pl.ds(0, arrived_a[c].shape[1])
        local = (total.at[:, rows], outgoing.at[:, rows])
        cubes_a.append(
            CubeSum(orders[c], sums_a[c], *local, arrived_a[c], sems_a[2 * c : 2 * c + 2])
        )
    def put_result(p, cubes, ref):
        device = dp * lax.axis_size("grp") + grp
        result = jnp.concatenate([cube.total[0] for cube in cubes], axis=0)
        ref[...] = shift_lanes(result, p.lane(device), False)

    exchange = exchange_copies(out_src, out_ref, dp, grp, out_sem, out_send, out_recv)
    dx_sems = (
        (dx_sem0, dx_send0, dx_recv0),
        (dx_sem1, dx_send1, dx_recv1),
        (dx_sem2, dx_send2, dx_recv2),
        (dx_sem3, dx_send3, dx_recv3),
    )
    loads = [
        pltpu.make_async_copy(x_hbm, x_buf, load_sems.at[0]),
        pltpu.make_async_copy(d_res_hbm, d_res_buf, load_sems.at[1]),
    ]

    chunks = row_chunks(d_in.shape[1], images)

    def chunk(c):
        return chunk_copies(d_in, dx_ref, *chunks[c][1:], dp, grp, *dx_sems[c], 0)

    @pl.when(i == 0)
    def _():
        for c in loads:
            c.start()
        g_bias[...] = jnp.zeros_like(g_bias)
        g_qkv[...] = jnp.zeros_like(g_qkv)
        g_vec[...] = jnp.zeros_like(g_vec)
        greet(cube_partners(order, dp, grp) + [window_partner(dp, grp, 3)])

    starts = starts_of(stage_weights(order)[::-1], SUM_STEPS)
    for k, start in zip(reversed(range(stages)), starts):

        @pl.when(i == start)
        def _(k=k):
            for cube in cubes_b:
                if k < stages - 1:
                    cube.finish(k + 1)
                cube.start(k)

    @pl.when(i == steps - 1)
    def _():
        for cube in cubes_b:
            cube.finish(0)
        put_result(part, cubes_b, grad_ref)

    @pl.when(i == 0)
    def _():
        for c in exchange:
            c.start()

    def image(b):
        at = i
        dm_t = dot(query_tab[b], image_rows(d_mixed, at, slice(0, D))).T
        scales = [jnp.broadcast_to(inverse[b, h : h + 1, :], (HDIM, 256)) for h in range(HEADS)]
        dm_t = (dm_t * jnp.concatenate(scales, axis=0)).astype(BF16)
        products = dm_t.astype(F32) * mixed_ref[b].astype(F32)
        q_t, k_t, v_ext = q_ref[b], k_ref[b], v_ref[b]

        def d_probs_of(h):
            heads = jnp.concatenate([only_head(dm_t, h), only_head(dm_t, h + 1)], axis=1)
            return dot(v_ext[:, tile_of(h)], heads)

        def softmax_back(d_probs, h):
            e = probs[b, h]
            own = slice(h * HDIM, (h + 1) * HDIM)
            sums = jnp.sum(products[own], axis=0, keepdims=True)
            halves = []
            for half in range(2):
                lanes = slice(128 * half, 128 * half + 128)
                e32 = e[:, lanes].astype(F32)[56 * half : 56 * half + KEYS]
                ds = e32 * (half_of(d_probs, half) - sums[:, lanes])
                g_bias[h, half] += ds
                halves.append(ds)
            return spread(halves)

        def gather_back(h, ds):
            own = slice(h * HDIM, (h + 1) * HDIM)
            values = slice(D + h * HDIM, D + (h + 1) * HDIM)
            d_query_t[b, own, :] = (dot(k_t[own, :], ds) * HDIM ** (-0.5)).astype(BF16)
            d_key_value_t[b, own, :] = dot_t(q_t[own, :], ds).astype(BF16)
            d_key_value_t[b, values, :] = dot_t(dm_t[own, :], probs[b, h]).astype(BF16)

        ahead = d_probs_of(0)
        yield
        waiting = []
        for h in range(0, HEADS, 2):
            now = ahead
            if h + 2 < HEADS:
                ahead = d_probs_of(h + 2)
            for c in range(2):
                waiting.append((h + c, softmax_back(now[:, c * 256 : (c + 1) * 256], h + c)))
            while len(waiting) > 1:
                gather_back(*waiting.pop(0))
            yield
        for last in waiting:
            gather_back(*last)
        yield
        put_image_rows(d_qkv, at, slice(0, D), dot_t(query_back[b], d_query_t[b]))
        put_image_rows(d_qkv, at, slice(D, 3 * D), dot_t(keys_back[b], d_key_value_t[b]))

    for _ in image(0):
        pass

    @pl.when(i == 3)
    def _():
        for c in loads:
            c.wait()

    def finish_rows(first, size):
        at = slice(first, first + size)
        xhat, scale = norm_parts(x_buf[:, at, :].reshape(4 * size, D).astype(F32))
        gain = vecs[0:1, :]
        normed = (xhat * gain + vecs[1:2, :]).astype(BF16)
        grads = d_qkv[:, at, :].reshape(4 * size, 3 * D)
        d_normed = dot_t(grads, wqkv[...])
        result = d_res_buf[:, at, :].reshape(4 * size, D) + norm_back(d_normed, xhat, scale, gain)
        d_in[:, at, :] = result.astype(BF16).reshape(4, size, D)
        g_qkv[...] += dot(normed.T, grads)
        g_vec[0:1, :] += jnp.sum(grads.astype(F32), axis=0, keepdims=True)
        g_vec[1:2, :D] += jnp.sum(d_normed * xhat, axis=0, keepdims=True)
        g_vec[2:3, :D] += jnp.sum(d_normed, axis=0, keepdims=True)

    for c, (step, first, size) in enumerate(chunks):

        @pl.when(i == step)
        def _(c=c, first=first, size=size):
            finish_rows(first, size)
            for copy in chunk(c):
                copy.start()

    @pl.when(i == steps - 1)
    def _():
        pack(
            part_a, list(zip(chain_places, sums_a)), one_fine, one_coarse,
            g_bias, g_qkv, g_vec, g_proj, g_vec2, flat, table, shifted, line,
        )
        for k in reversed(range(stages)):
            for cube in cubes_a:
                cube.start(k)
            for cube in cubes_a:
                cube.finish(k)
        put_result(part_a, cubes_a, grad_a_ref)
        for c in exchange:
            c.wait()
        for c in range(4):
            for copy in chunk(c):
                copy.wait()


def attend_back(
    part_a, part, order, chain_places, saved, d_mixed, probs, inverse, x, d_res, wqkv, vecs, blocks,
    out, g_proj, g_vec2,
):
    images = probs.shape[0]
    tokens = out.shape[0]
    rows = tokens // 4
    stages = len(order)
    _, query_tab, keys_back, query_back = gather_tables(images)
    fine, coarse, _ = bias_tables()
    vm = pl.BlockSpec(memory_space=pltpu.VMEM)
    hbm = pl.BlockSpec(memory_space=pl.ANY)
    image = lambda *shape: pl.BlockSpec((1, *shape), lambda i: (i, 0, 0))
    by_window = lambda array: array.reshape(4, rows, -1)
    chain_scratch = [
        pltpu.VMEM((part.devices, count, 128), BF16) for count in part_a.split(SUM_SHARE)
    ]
    chain_scratch += chain_scratch
    chain_scratch += [pltpu.SemaphoreType.DMA((stages,))] * 4
    for count in part.split(SUM_SHARE):
        chain_scratch += CubeSum.scratch(part.devices, count, stages)
    grad_a, grad_b, output, dx = pl.pallas_call(
        functools.partial(attend_back_kernel, part_a, part, order, chain_places, images),
        grid=(images,),
        out_shape=[
            jax.ShapeDtypeStruct((part_a.rows, 128), F32),
            jax.ShapeDtypeStruct((part.rows, 128), F32),
            jax.ShapeDtypeStruct((tokens, D), BF16),
            jax.ShapeDtypeStruct((4, rows, D), BF16),
        ],
        in_specs=[
            image(D, 256),
            image(D, 256),
            image(256, D),
            image(D, 256),
            vm,
            pl.BlockSpec((1, HEADS, 256, 256), lambda i: (i, 0, 0, 0)),
            image(16, 256),
        ]
        + [image(256, 256)] * 3
        + [hbm, hbm, vm, vm, vm, vm, hbm, vm, vm, vm, vm],
        out_specs=[
            pl.BlockSpec((part_a.rows, 128), lambda i: (0, 0)),
            pl.BlockSpec((part.rows, 128), lambda i: (0, 0)),
            hbm,
            hbm,
        ],
        scratch_shapes=[
            pltpu.VMEM((HEADS, 2, KEYS, 128), F32),
            pltpu.VMEM((D, 3 * D), F32),
            pltpu.VMEM((8, 3 * D), F32),
            pltpu.VMEM((part_a.buffer, 128), F32),
            pltpu.VMEM((16, 512), F32),
            pltpu.VMEM((4, 14 * 16, 128), F32),
            pltpu.VMEM((8, 512), F32),
            pltpu.VMEM((1, D, 256), BF16),
            pltpu.VMEM((1, 2 * D, 256), BF16),
            pltpu.VMEM((4, rows, 3 * D), BF16),
            pltpu.VMEM((4, rows, D), BF16),
            pltpu.VMEM((4, rows, D), BF16),
            pltpu.VMEM((4, rows, D), F32),
            pltpu.SemaphoreType.DMA((2,)),
        ]
        + [
            pltpu.SemaphoreType.DMA,
            pltpu.SemaphoreType.DMA((3,)),
            pltpu.SemaphoreType.DMA((3,)),
        ]
        * 5
        + chain_scratch,
        compiler_params=pltpu.CompilerParams(
            collective_id=3, has_side_effects=True, vmem_limit_bytes=VMEM_LIMIT
        ),
        name="attend_back",
    )(
        *saved,
        by_window(d_mixed),
        probs,
        inverse,
        keys_back,
        query_tab,
        query_back,
        by_window(x),
        by_window(d_res),
        wqkv,
        vecs,
        *blocks,
        out,
        g_proj,
        g_vec2,
        jnp.asarray(fine),
        jnp.asarray(coarse),
    )
    grad_a = grad_a.reshape(-1)[: part_a.length]
    grad_b = grad_b.reshape(-1)[: part.length]
    return grad_a, grad_b, output, dx


def to_blocks(part, chains, flat):
    for device in range(part.devices):
        at = part.start(device)
        for places, out in chains:
            out[places[device]] = flat[at : at + out.shape[1], :].astype(BF16)
            at += out.shape[1]


def pack(
    part, chains, one_fine, one_coarse,
    g_bias, g_qkv, g_vec1, g_proj, g_vec2, flat, table, shifted, line,
):
    row, lane = divmod(ATTN_VECTORS[0], 128)
    flat[4608:, :] = jnp.zeros((flat.shape[0] - 4608, 128), F32)
    put_matrix(flat, 0, g_qkv)
    put_matrix(flat, 3456, g_proj)
    vectors = [
        g_vec1[1:2, :D],
        g_vec1[2:3, :D],
        g_vec1[0:1, :D],
        g_vec1[0:1, 2 * D :],
        g_vec2[4:5, :D],
    ]
    pieces = [v[:, j * 128 : (j + 1) * 128] for v in vectors for j in range(3)]
    pieces += [jnp.zeros((1, 128), F32)]
    flat[row : row + 16, :] += shift_lanes(jnp.concatenate(pieces, axis=0), lane, True)
    for h in range(HEADS):
        table[...] = jnp.zeros_like(table)
        for half in range(2):
            turned = g_bias[h, half].T
            for y in range(WIN):
                for at, length, source in bias_runs(half, WIN * half + y):
                    table[0:14, source : source + length] += turned[
                        y * 14 : y * 14 + 14, at : at + length
                    ]
        for c in range(4):
            shifted[c, pl.ds(h, 14, stride=16), :] = table[0:14, c * 128 : (c + 1) * 128]
    high, low = split_float(jnp.concatenate([shifted[c] for c in range(3)], axis=1))
    moved_fine = dot_t(high, one_fine[...]) + dot_t(low, one_fine[...])
    high, low = split_float(shifted[3])
    moved_coarse = dot_t(high, one_coarse[...]) + dot_t(low, one_coarse[...])
    g_fine = jnp.zeros((16, 384), F32)
    g_coarse = jnp.zeros((16, 256), F32)
    for qx in range(14):
        at = slice(qx * 16, qx * 16 + 16)
        g_fine += pltpu.roll(moved_fine[at], (384 - qx) % 384, 1)
        g_coarse += pltpu.roll(moved_coarse[at], (256 - qx // 2) % 256, 1)
    for t, h, length, row, lane, count in table_lines():
        line[...] = jnp.zeros_like(line)
        line[0:1, lane : lane + length] = (g_fine, g_coarse)[t][h : h + 1, :length]
        for c in range(count):
            flat[row + c : row + c + 1, :] += line[0:1, c * 128 : (c + 1) * 128]
    to_blocks(part, chains, flat)


def adamw(master, first, second, grads):
    first_new = beta_one * first + (1.0 - beta_one) * grads
    second_new = beta_two * second + (1.0 - beta_two) * grads * grads
    first_hat = first_new / (1.0 - beta_one**STEP)
    second_hat = second_new / (1.0 - beta_two**STEP)
    master_new = master - learn_rate * (
        first_hat / (jnp.sqrt(second_hat) + adam_eps) + decay_rate * master
    )
    return (first_new, second_new, master_new)


def body(
    tokens, cotangent, attn_master, attn_first, attn_second, mlp_master, mlp_first, mlp_second
):
    n_dp, n_grp = lax.axis_size("dp"), lax.axis_size("grp")
    order = bit_order(n_dp, n_grp)
    chain_places = [place_list(o, n_dp, n_grp) for o in (order, other_order(order))]
    part_a = Part(n_dp * n_grp, attn_master.shape[0])
    part_b = Part(n_dp * n_grp, mlp_master.shape[0])
    images = tokens.shape[1] // 4 // SEQ
    wqkv, wproj, vecs_a, bias, x, blocks_b = gather_params(
        part_a, part_b, order, chain_places, attn_master, mlp_master, tokens[0]
    )
    mixed, probs, *saved, inverse, cot, blocks_b = attend(
        order, x, cotangent[0], blocks_b, wqkv, vecs_a, bias, images
    )
    mixed = mixed.reshape(-1, D)
    out, d_res, d_mixed, *sums_b, g_proj, g_vec2 = mlp(
        part_b, chain_places, cot, mixed, x, wproj, vecs_a, blocks_b
    )
    grad_a, grad_b, output, dx = attend_back(
        part_a, part_b, order, chain_places, saved, d_mixed, probs, inverse, x, d_res, wqkv,
        vecs_a, sums_b, out, g_proj, g_vec2,
    )
    attn_new = adamw(attn_master, attn_first, attn_second, grad_a)
    mlp_new = adamw(mlp_master, mlp_first, mlp_second, grad_b)
    input_grad = dx.reshape(-1, D).astype(F32)
    return (output[None], input_grad[None], *attn_new, *mlp_new)


def solution(mesh):
    flat_spec = P(("dp", "grp"))
    token_spec = P("dp", "grp", None)
    placed = (token_spec, token_spec) + (flat_spec,) * 6
    return jax.shard_map(
        body, mesh=mesh, in_specs=placed, out_specs=placed, check_vma=False
    )
```

```python
import functools
import itertools

import jax
import jax.numpy as jnp
import ml_dtypes
import numpy as np
from jax import lax
from jax.experimental import pallas as pl
from jax.experimental.pallas import tpu as pltpu
from jax.sharding import PartitionSpec as P

D = 384
HEADS = 12
HDIM = 32
FF = 1536
WIN = 7
STEP = 10
SEQ = WIN * WIN
HALF = 64
FINE = (3 * WIN - 2) ** 2
COARSE = (2 * WIN - 1) ** 2
KEYS = 192

beta_one = 0.9
beta_two = 0.999
learn_rate = 0.04
decay_rate = 0.05
adam_eps = 1e-08
norm_eps = 1e-05
masked_score = -1e30

F32 = jnp.float32
BF16 = jnp.bfloat16
MESH = pl.DeviceIdType.MESH
VMEM_LIMIT = 58 * 2**20


def token_place(gy, gx):
    window = 2 * (gy // WIN) + gx // WIN
    return window * HALF + (gy % WIN) * WIN + gx % WIN


@functools.cache
def gather_tables(images):
    keys = np.zeros((images, 256, 256), np.float32)
    queries = np.zeros((images, 256, 256), np.float32)
    for i in range(images):
        for gy in range(2 * WIN):
            for gx in range(2 * WIN):
                at = token_place(gy, gx) + i
                key = gy * 14 + gx if gy < 10 else 192 + (gy - 10) * 14 + gx
                keys[i, key, at] = 1.0
                keys[i, 140 + (gy // 2) * WIN + gx // 2, at] = 0.25
                queries[i, (gy // WIN) * 128 + (gy % WIN) * 14 + gx, at] = 1.0
    return (
        keys.astype(ml_dtypes.bfloat16),
        queries.astype(ml_dtypes.bfloat16),
        np.ascontiguousarray(keys.transpose(0, 2, 1)).astype(ml_dtypes.bfloat16),
        np.ascontiguousarray(queries.transpose(0, 2, 1)).astype(ml_dtypes.bfloat16),
    )


@functools.cache
def bias_tables():
    fine = np.zeros((384, 384), np.float32)
    coarse = np.zeros((256, 128), np.float32)
    for a in range(4, 23):
        for kx in range(14):
            fine[19 * (a - 4) + kx + 9, a * 14 + kx] = 1.0
    for p in range(13):
        for x in range(WIN):
            coarse[13 * p + x + 6, p * WIN + x] = 1.0
    mask = np.zeros((2, KEYS, 128), np.float32)
    for half in range(2):
        for q in range(98):
            qx = q % 14
            for e in range(KEYS):
                at = e + 56 * half
                if at < 140:
                    ok = abs_ok(qx, at % 14)
                elif at < 189:
                    ok = True
                elif at < 192:
                    ok = False
                else:
                    ok = at < 248 and abs_ok(qx, (at - 192) % 14)
                mask[half, e, q] = 0.0 if ok else masked_score
    return fine.astype(ml_dtypes.bfloat16), coarse.astype(ml_dtypes.bfloat16), mask


def abs_ok(qx, kx):
    return kx < 10 if qx < WIN else kx >= 4


def bias_runs(half, qy):
    fine = (13 - qy) * 14
    pool = 384 + (6 - qy // 2) * WIN
    if half == 0:
        return [(0, 140, fine), (140, 49, pool)]
    return [(0, 84, fine + 56), (84, 49, pool), (136, 56, fine + 140)]


class Part:
    def __init__(self, devices, length):
        self.devices = devices
        self.length = length
        self.rows = -(-((length + 126) // 128 + 1) // 16) * 16
        self.buffer = -(-(self.start(devices - 1) + self.rows) // 8) * 8

    def start(self, device):
        return device * self.length // 128

    def lane(self, device):
        return lax.rem(device * self.length, 128)

    def split(self, share):
        first = max(16, min(self.rows - 16, round(self.rows * share / 16) * 16))
        return first, self.rows - first

    def padded(self, vector):
        extra = self.rows * 128 - self.length
        return jnp.pad(vector, (0, extra)).reshape(self.rows, 128)


GATHER_SHARE = 0.7
SUM_SHARE = 0.5
GATHER_STEPS = 7
SUM_STEPS = 12


def bit_order(n_dp, n_grp):
    dp_bits = [("dp", 2**b) for b in range(n_dp.bit_length() - 1)]
    grp_bits = [("grp", 2**b) for b in reversed(range(n_grp.bit_length() - 1))]
    return dp_bits[1:2] + grp_bits + dp_bits[2:] + dp_bits[:1]


def other_order(order):
    grp_bits = [stage for stage in order if stage[0] == "grp"]
    dp_bits = [stage for stage in order if stage[0] == "dp"]
    return dp_bits[:-1] + grp_bits + dp_bits[-1:]


def stage_weights(order):
    weights = []
    for k, (axis, stride) in enumerate(order):
        relative = 0.35 if (axis, stride) == ("dp", 1) else 2 if (axis == "grp" and stride > 1) else 1
        weights.append(relative * 2**k)
    return weights


def starts_of(weights, steps):
    done, starts = 0.0, []
    for weight in weights:
        starts.append(int(steps * done / sum(weights)))
        done += weight
    return starts


def place_of(order, dp, grp):
    place = 0
    for k, (axis, stride) in enumerate(order):
        place = place + ((dp if axis == "dp" else grp) // stride) % 2 * 2**k
    return place


def partner_of(axis, stride, dp, grp):
    if axis == "dp":
        return (dp + (1 - 2 * ((dp // stride) % 2)) * stride, grp)
    return (dp, grp + (1 - 2 * ((grp // stride) % 2)) * stride)


def greet(partners):
    barrier = pltpu.get_barrier_semaphore()
    for partner in partners:
        pl.semaphore_signal(barrier, inc=1, device_id=partner, device_id_type=MESH)
    pl.semaphore_wait(barrier, len(partners))


def cube_partners(order, dp, grp):
    return [partner_of(axis, stride, dp, grp) for axis, stride in order]


def shift_lanes(values, amount, up):
    lane = lax.broadcasted_iota(jnp.int32, values.shape, 1)
    if up:
        turned = pltpu.roll(values, amount, 1)
        return jnp.where(lane >= amount, turned, pltpu.roll(turned, 1, 0))
    turned = pltpu.roll(values, lax.rem(128 - amount, 128), 1)
    return jnp.where(lane < 128 - amount, turned, pltpu.roll(turned, values.shape[0] - 1, 0))


def window_partner(dp, grp, k):
    low, high = dp % 2, dp // 2 % 2
    to = dp
    if k % 2:
        to = to + 1 - 2 * low
    if k // 2:
        to = to + 2 * (1 - 2 * high)
    return (to, grp)


def exchange_copies(source, target, dp, grp, own_sem, send_sems, recv_sems):
    rows = source.shape[0] // 4
    slot = dp % 4
    mine = pl.ds(pl.multiple_of(slot * rows, 16), rows)
    own = pltpu.make_async_copy(source.at[mine], target.at[mine], own_sem)
    sends = []
    for k in (3, 2, 1):
        to, _ = window_partner(dp, grp, k)
        theirs = pl.ds(pl.multiple_of(to % 4 * rows, 16), rows)
        sends.append(
            pltpu.make_async_remote_copy(
                src_ref=source.at[theirs],
                dst_ref=target.at[mine],
                send_sem=send_sems.at[k - 1],
                recv_sem=recv_sems.at[k - 1],
                device_id=(to, grp),
                device_id_type=MESH,
            )
        )
    return [own] + sends


def cube_copy(order, k, source, target, dp, grp, send_sems, recv_sems):
    axis, stride = order[k]
    return pltpu.make_async_remote_copy(
        src_ref=source,
        dst_ref=target,
        send_sem=send_sems.at[k],
        recv_sem=recv_sems.at[k],
        device_id=partner_of(axis, stride, dp, grp),
        device_id_type=MESH,
    )


def gather_copy(order, k, blocks, dp, grp, sems):
    place = place_of(order, dp, grp)
    held = blocks.at[pl.ds(place // 2**k * 2**k, 2**k)]
    return cube_copy(order, k, held, held, dp, grp, *sems)


class CubeSum:
    def __init__(self, order, blocks, total, outgoing, arrived, sems):
        self.order, self.blocks, self.total = order, blocks, total
        self.outgoing, self.arrived, self.sems = outgoing, arrived, sems
        self.dp, self.grp = lax.axis_index("dp"), lax.axis_index("grp")
        self.place = place_of(order, self.dp, self.grp)
        self.last = len(order) - 1

    def mine(self, k):
        return self.place // 2**k % 2 * 2**k

    def copy(self, k):
        size = 2**k
        if k == self.last:
            source = self.blocks.at[pl.ds(size - self.mine(k), size)]
        else:
            source = self.outgoing.at[pl.ds(size, size)]
        target = self.arrived.at[pl.ds(size, size)]
        return cube_copy(self.order, k, source, target, self.dp, self.grp, *self.sems)

    def start(self, k):
        self.copy(k).start()

    def finish(self, k):
        size, mine = 2**k, self.mine(k)
        self.copy(k).wait()

        def added(j):
            if k == self.last:
                held = self.blocks[mine + j].astype(F32)
            else:
                held = self.total[mine + j]
            return held + self.arrived[size + j].astype(F32)

        keep = size // 2 if k else 1
        kept = self.mine(k - 1) if k else 0

        def add(j, carry):
            value = added(kept + j)
            if k:
                self.outgoing[keep + j] = added(keep - kept + j).astype(BF16)
            self.total[kept + j] = value
            return carry

        lax.fori_loop(0, keep, add, 0)

    @staticmethod
    def scratch(devices, rows, stages):
        return [
            pltpu.VMEM((devices // 2, rows, 128), F32),
            pltpu.VMEM((devices // 2, rows, 128), BF16),
            pltpu.VMEM((devices, rows, 128), BF16),
            pltpu.SemaphoreType.DMA((stages,)),
            pltpu.SemaphoreType.DMA((stages,)),
        ]


def chunk_copies(source, target, first, size, dp, grp, own_sem, send_sems, recv_sems, skip):
    slot = dp % 4
    into = target.at[slot, pl.ds(first, size)]
    rows = pl.ds(first - skip, size)
    copies = [pltpu.make_async_copy(source.at[slot, rows], into, own_sem)]
    for k in (3, 2, 1):
        to, _ = window_partner(dp, grp, k)
        copies.append(
            pltpu.make_async_remote_copy(
                src_ref=source.at[to % 4, rows],
                dst_ref=into,
                send_sem=send_sems.at[k - 1],
                recv_sem=recv_sems.at[k - 1],
                device_id=(to, grp),
                device_id_type=MESH,
            )
        )
    return copies


def place_list(order, n_dp, n_grp):
    return [place_of(order, d // n_grp, d % n_grp) for d in range(n_dp * n_grp)]


ATTN_VECTORS = (D * 3 * D + D * D + HEADS * FINE + HEADS * COARSE, 5)
TABLE_AT = D * 3 * D + D * D


def unflatten(part, chains, flat):
    for device in range(part.devices):
        at = part.start(device)
        pieces = [blocks[places[device]].astype(F32) for places, blocks in chains]
        block = jnp.concatenate(pieces, axis=0) if len(pieces) > 1 else pieces[0]
        first = block[0:1] + flat[at : at + 1, :] if device else block[0:1]
        flat[at : at + part.rows, :] = block
        flat[at : at + 1, :] = first


def take_matrix(flat, first, target):
    rows, columns = target.shape
    count = columns // 128
    for j in range(count):
        target[:, j * 128 : (j + 1) * 128] = flat[pl.ds(first + j, rows, stride=count), :].astype(
            target.dtype
        )


def put_matrix(flat, first, source):
    rows, columns = source.shape
    count = columns // 128
    for j in range(count):
        flat[pl.ds(first + j, rows, stride=count), :] = source[:, j * 128 : (j + 1) * 128]


TABLES = ((TABLE_AT, FINE), (TABLE_AT + HEADS * FINE, COARSE))


def table_lines():
    for t, (first, length) in enumerate(TABLES):
        for h in range(HEADS):
            row, lane = divmod(first + h * length, 128)
            yield t, h, length, row, lane, -(-(lane + length) // 128)


def prepare(
    part, chains, one_fine, one_coarse, mask_ref,
    wqkv, wproj, vecs, bias, flat, tab_fine, tab_coarse, shifted, turned,
):
    unflatten(part, chains, flat)
    take_matrix(flat, 0, wqkv)
    take_matrix(flat, 3456, wproj)
    row, lane = divmod(ATTN_VECTORS[0], 128)
    rows = shift_lanes(flat[row : row + 16, :], lane, False)
    for v in range(5):
        for j in range(3):
            vecs[v : v + 1, j * 128 : (j + 1) * 128] = rows[3 * v + j : 3 * v + j + 1]
    tab_fine[...] = jnp.zeros_like(tab_fine)
    tab_coarse[...] = jnp.zeros_like(tab_coarse)
    for t, h, length, row, lane, count in table_lines():
        line = jnp.concatenate([flat[row + c : row + c + 1, :] for c in range(count)], axis=1)
        (tab_fine, tab_coarse)[t][h : h + 1, 0:length] = line[:, lane : lane + length]
    fine, coarse = tab_fine[...], tab_coarse[...]
    fine = jnp.concatenate([pltpu.roll(fine, qx, 1) for qx in range(14)], axis=0)
    coarse = jnp.concatenate([pltpu.roll(coarse, qx // 2, 1) for qx in range(14)], axis=0)
    fine = dot(fine.astype(BF16), one_fine[...])
    for c in range(3):
        shifted[c] = fine[:, c * 128 : (c + 1) * 128]
    shifted[3] = dot(coarse.astype(BF16), one_coarse[...])
    turned[...] = jnp.zeros_like(turned)
    for h in range(HEADS):
        table = jnp.concatenate(
            [shifted[c, pl.ds(h, 14, stride=16), :] for c in range(4)], axis=1
        )
        for half in range(2):
            for y in range(WIN):
                for at, length, source in bias_runs(half, WIN * half + y):
                    turned[half, y * 14 : y * 14 + 14, at : at + length] = table[
                        :, source : source + length
                    ]
            bias[h, half] = turned[half].T[0:KEYS] + mask_ref[half]


def early_stages(order):
    return 1 + sum(axis == "grp" for axis, _ in order)


def gather_kernel(
    part_a,
    part_b,
    order,
    chain_places,
    a_ref,
    b_ref,
    one_fine,
    one_coarse,
    mask_ref,
    tok_ref,
    wqkv,
    wproj,
    vecs,
    bias,
    x_ref,
    blocks_b,
    blocks_a1,
    blocks_a2,
    own,
    flat,
    tab_fine,
    tab_coarse,
    shifted,
    turned,
    own_sem,
    send_a1,
    recv_a1,
    send_a2,
    recv_a2,
    send_b,
    recv_b,
    x_sem,
    x_send,
    x_recv,
):
    dp, grp = lax.axis_index("dp"), lax.axis_index("grp")
    place = place_of(order, dp, grp)
    device = dp * lax.axis_size("grp") + grp
    own[...] = shift_lanes(b_ref[...], part_b.lane(device), True).astype(BF16)
    copy = pltpu.make_async_copy(own, blocks_b.at[place], own_sem)
    copy.start()
    mine = shift_lanes(a_ref[...], part_a.lane(device), True)
    orders = (order, other_order(order))
    chains = ((blocks_a1, (send_a1, recv_a1)), (blocks_a2, (send_a2, recv_a2)))
    at = 0
    for chain_order, (blocks, _) in zip(orders, chains):
        blocks[place_of(chain_order, dp, grp)] = mine[at : at + blocks.shape[1]].astype(BF16)
        at += blocks.shape[1]
    vecs[...] = jnp.zeros_like(vecs)
    greet(cube_partners(order, dp, grp) + [window_partner(dp, grp, 3)])
    copy.wait()
    exchange = exchange_copies(tok_ref, x_ref, dp, grp, x_sem, x_send, x_recv)
    first = [
        [
            gather_copy(chain_order, k, blocks, dp, grp, sems)
            for chain_order, (blocks, sems) in zip(orders, chains)
        ]
        for k in range(len(order))
    ]
    early = early_stages(order)
    second = [gather_copy(order, k, blocks_b, dp, grp, (send_b, recv_b)) for k in range(early)]
    for k, stage in enumerate(first):
        for c in stage:
            c.start()
        if k == 0:
            second[0].start()
            for c in exchange:
                c.start()
        if early <= k < 2 * early:
            second[k - early].wait()
            if k - early + 1 < early:
                second[k - early + 1].start()
        for c in stage:
            c.wait()
    prepare(
        part_a, list(zip(chain_places, (blocks_a1, blocks_a2))), one_fine, one_coarse, mask_ref,
        wqkv, wproj, vecs, bias, flat, tab_fine, tab_coarse, shifted, turned,
    )
    for k in range(len(order) - early, early):
        second[k].wait()
        if k + 1 < early:
            second[k + 1].start()
    for c in exchange:
        c.wait()


def gather_params(part_a, part_b, order, chain_places, master_a, master_b, tok):
    stages = len(order)
    rows = part_a.split(GATHER_SHARE)
    early = early_stages(order)
    fine, coarse, mask = bias_tables()
    vm = pl.BlockSpec(memory_space=pltpu.VMEM)
    hbm = pl.BlockSpec(memory_space=pl.ANY)
    return pl.pallas_call(
        functools.partial(gather_kernel, part_a, part_b, order, chain_places),
        out_shape=[
            jax.ShapeDtypeStruct((D, 3 * D), BF16),
            jax.ShapeDtypeStruct((D, D), BF16),
            jax.ShapeDtypeStruct((8, D), F32),
            jax.ShapeDtypeStruct((HEADS, 2, KEYS, 128), F32),
            jax.ShapeDtypeStruct(tok.shape, BF16),
            jax.ShapeDtypeStruct((part_b.devices, part_b.rows, 128), BF16),
        ],
        in_specs=[vm] * 5 + [hbm],
        out_specs=[vm] * 4 + [hbm] * 2,
        scratch_shapes=[
            pltpu.VMEM((part_a.devices, rows[0], 128), BF16),
            pltpu.VMEM((part_a.devices, rows[1], 128), BF16),
            pltpu.VMEM((part_b.rows, 128), BF16),
            pltpu.VMEM((part_a.buffer, 128), F32),
            pltpu.VMEM((16, 384), F32),
            pltpu.VMEM((16, 256), F32),
            pltpu.VMEM((4, 14 * 16, 128), F32),
            pltpu.VMEM((2, 128, 256), F32),
            pltpu.SemaphoreType.DMA,
            pltpu.SemaphoreType.DMA((stages,)),
            pltpu.SemaphoreType.DMA((stages,)),
            pltpu.SemaphoreType.DMA((stages,)),
            pltpu.SemaphoreType.DMA((stages,)),
            pltpu.SemaphoreType.DMA((early,)),
            pltpu.SemaphoreType.DMA((early,)),
            pltpu.SemaphoreType.DMA,
            pltpu.SemaphoreType.DMA((3,)),
            pltpu.SemaphoreType.DMA((3,)),
        ],
        compiler_params=pltpu.CompilerParams(
            collective_id=0, has_side_effects=True, vmem_limit_bytes=VMEM_LIMIT
        ),
        name="gather_params",
    )(
        part_a.padded(master_a),
        part_b.padded(master_b),
        jnp.asarray(fine),
        jnp.asarray(coarse),
        jnp.asarray(mask),
        tok,
    )


def dot(a, b):
    return jnp.dot(a, b, preferred_element_type=F32)


def dot_t(a, b):
    return lax.dot_general(a, b, (((1,), (1,)), ((), ())), preferred_element_type=F32)


def norm_parts(values):
    centered = values - jnp.mean(values, axis=-1, keepdims=True)
    scale = lax.rsqrt(jnp.mean(centered * centered, axis=-1, keepdims=True) + norm_eps)
    return centered * scale, scale


def norm_back(d_normed, xhat, scale, gain):
    dh = d_normed * gain
    return scale * (
        dh
        - jnp.mean(dh, axis=-1, keepdims=True)
        - xhat * jnp.mean(dh * xhat, axis=-1, keepdims=True)
    )


def image_rows(ref, i, columns):
    at = pl.ds(pl.multiple_of(48 * i, 16), HALF)
    return jnp.concatenate([ref[w, at, columns] for w in range(4)], axis=0)


def put_image_rows(ref, i, columns, values):
    for w in range(4):
        part = values[w * HALF : (w + 1) * HALF]
        first = pl.ds(pl.multiple_of(48 * i, 16), 16)
        rest = pl.ds(pl.multiple_of(48 * i + 16, 16), HALF - 16)
        held = jnp.where(i > 0, ref[w, first, columns].astype(F32), 0.0)
        ref[w, first, columns] = (held + part[:16]).astype(ref.dtype)
        ref[w, rest, columns] = part[16:].astype(ref.dtype)


def spread(halves):
    columns = []
    for half, values in enumerate(halves):
        pieces = [values, jnp.zeros((64 - 56 * half, 128), F32)]
        if half:
            pieces = [jnp.zeros((56, 128), F32)] + pieces
        columns.append(jnp.concatenate(pieces, axis=0))
    return jnp.concatenate(columns, axis=1).astype(BF16)


def only_head(turned, h):
    pieces = [jnp.zeros((HDIM, 256), BF16)] * 4
    pieces[h % 4] = turned[h * HDIM : (h + 1) * HDIM, :]
    return jnp.concatenate(pieces, axis=0)


def half_of(values, half):
    return values[56 * half : 56 * half + KEYS, 128 * half : 128 * half + 128]


def tile_of(h):
    return slice(h // 4 * 128, h // 4 * 128 + 128)


def interleave(first, second):
    for _ in itertools.zip_longest(first, second):
        pass


def attend_kernel(
    rows,
    order,
    x_buf,
    cot_ref,
    blocks_in,
    wqkv,
    vecs,
    bias,
    keys_tab,
    query_tab,
    query_back,
    mixed,
    probs,
    query_out,
    key_out,
    value_out,
    mixed_out,
    inverse,
    cot_out,
    blocks,
    normed,
    qkv,
    send,
    recv,
    cot_sem,
    cot_send,
    cot_recv,
):
    i = pl.program_id(0)
    steps = pl.num_programs(0)
    dp, grp = lax.axis_index("dp"), lax.axis_index("grp")
    exchange = exchange_copies(cot_ref, cot_out, dp, grp, cot_sem, cot_send, cot_recv)
    early = early_stages(order)
    late = [
        gather_copy(order, k, blocks, dp, grp, (send, recv)) for k in range(early, len(order))
    ]

    @pl.when(i == 0)
    def _():
        greet(cube_partners(order, dp, grp) + [window_partner(dp, grp, 3)])

    for k, start in enumerate(starts_of(stage_weights(order)[early:], GATHER_STEPS)):

        @pl.when(i == start)
        def _(k=k):
            if k:
                late[k - 1].wait()
            late[k].start()

    @pl.when(i == 0)
    def _():
        for c in exchange:
            c.start()

        step = rows // 7

        def norm(w):
            for c in range(7):
                at = slice(c * step, (c + 1) * step)
                xhat, _ = norm_parts(x_buf[w, at, :].astype(F32))
                normed[w % 2, at, :] = (xhat * vecs[0:1, :] + vecs[1:2, :]).astype(BF16)

        norm(0)
        for w in range(4):
            q = dot(normed[w % 2], wqkv[:, :D]) + vecs[2:3, :]
            qkv[w, :, :D] = (q * HDIM ** (-0.5)).astype(BF16)
            if w < 3:
                norm(w + 1)
            qkv[w, :, D : 2 * D] = dot(normed[w % 2], wqkv[:, D : 2 * D]).astype(BF16)
            v = dot(normed[w % 2], wqkv[:, 2 * D :]) + vecs[3:4, :]
            qkv[w, :, 2 * D :] = v.astype(BF16)

    def image(b):
        at = 2 * i + b
        q_ext = dot(query_tab[b], image_rows(qkv, at, slice(0, D)))
        kv_ext = dot(keys_tab[b], image_rows(qkv, at, slice(D, 3 * D)))
        q_t = q_ext.T.astype(BF16)
        k_ext = kv_ext[:, :D].astype(BF16)
        v_t = kv_ext[:, D:].T.astype(BF16)
        query_out[b] = q_t
        key_out[b] = kv_ext[:, :D].T.astype(BF16)
        value_out[b] = kv_ext[:, D:].astype(BF16)
        inverse[b, HEADS:16, :] = jnp.zeros((16 - HEADS, 256), F32)

        def scores_of(h):
            heads = jnp.concatenate([only_head(q_t, h), only_head(q_t, h + 1)], axis=1)
            return dot(k_ext[:, tile_of(h)], heads)

        def softmax(scores, h):
            halves, inverses = [], []
            for half in range(2):
                s = half_of(scores, half) + bias[h, half]
                e = jnp.exp(s - jnp.max(s, axis=0, keepdims=True))
                inverses.append(1.0 / jnp.sum(e, axis=0, keepdims=True))
                halves.append(e)
            e = spread(halves)
            inv = jnp.concatenate(inverses, axis=1)
            probs[b, h] = e
            inverse[b, h : h + 1, :] = inv
            return e, inv

        def mix(h, e, inv):
            own = slice(h * HDIM, (h + 1) * HDIM)
            mixed_out[b, own, :] = (dot(v_t[own, :], e) * inv).astype(BF16)

        ahead = scores_of(0)
        yield
        waiting = []
        for h in range(0, HEADS, 2):
            now = ahead
            if h + 2 < HEADS:
                ahead = scores_of(h + 2)
            for c in range(2):
                waiting.append((h + c, *softmax(now[:, c * 256 : (c + 1) * 256], h + c)))
            while len(waiting) > 1:
                mix(*waiting.pop(0))
            yield
        for last in waiting:
            mix(*last)
        yield
        put_image_rows(mixed, at, slice(0, D), dot_t(query_back[b], mixed_out[b]))

    interleave(image(0), image(1))

    @pl.when(i == steps - 1)
    def _():
        late[-1].wait()
        for c in exchange:
            c.wait()


def attend(order, x, cot, blocks, wqkv, vecs, bias, images):
    tokens = x.shape[0]
    stages = len(order)
    rows = tokens // 4
    keys_tab, query_tab, _, query_back = gather_tables(images)
    vm = pl.BlockSpec(memory_space=pltpu.VMEM)
    hbm = pl.BlockSpec(memory_space=pl.ANY)
    image = lambda *shape: pl.BlockSpec((2, *shape), lambda i: (i, 0, 0))
    table = image(256, 256)
    return pl.pallas_call(
        functools.partial(attend_kernel, rows, order),
        grid=(images // 2,),
        out_shape=[
            jax.ShapeDtypeStruct((4, rows, D), BF16),
            jax.ShapeDtypeStruct((images, HEADS, 256, 256), BF16),
            jax.ShapeDtypeStruct((images, D, 256), BF16),
            jax.ShapeDtypeStruct((images, D, 256), BF16),
            jax.ShapeDtypeStruct((images, 256, D), BF16),
            jax.ShapeDtypeStruct((images, D, 256), BF16),
            jax.ShapeDtypeStruct((images, 16, 256), F32),
            jax.ShapeDtypeStruct((tokens, D), BF16),
            jax.ShapeDtypeStruct(blocks.shape, BF16),
        ],
        in_specs=[vm, hbm, hbm] + [vm] * 3 + [table] * 3,
        out_specs=[
            pl.BlockSpec((4, rows, D), lambda i: (0, 0, 0)),
            pl.BlockSpec((2, HEADS, 256, 256), lambda i: (i, 0, 0, 0)),
            image(D, 256),
            image(D, 256),
            image(256, D),
            image(D, 256),
            image(16, 256),
            hbm,
            hbm,
        ],
        scratch_shapes=[
            pltpu.VMEM((2, rows, D), BF16),
            pltpu.VMEM((4, rows, 3 * D), BF16),
            pltpu.SemaphoreType.DMA((stages,)),
            pltpu.SemaphoreType.DMA((stages,)),
            pltpu.SemaphoreType.DMA,
            pltpu.SemaphoreType.DMA((3,)),
            pltpu.SemaphoreType.DMA((3,)),
        ],
        input_output_aliases={2: 8},
        compiler_params=pltpu.CompilerParams(
            collective_id=2, has_side_effects=True, vmem_limit_bytes=VMEM_LIMIT
        ),
        name="attend",
    )(
        x.reshape(4, rows, D),
        cot,
        blocks,
        wqkv,
        vecs,
        bias,
        keys_tab,
        query_tab,
        query_back,
    )


GELU_A = float(np.sqrt(2.0 / np.pi))
GELU_B = 0.044715


def unpack_mlp(part, places, blocks, flat, w1, w2, vecs):
    unflatten(part, [(places, blocks)], flat)
    take_matrix(flat, 0, w1)
    take_matrix(flat, 4608, w2)
    for j in range(12):
        vecs[0:1, j * 128 : (j + 1) * 128] = flat[9216 + j : 9217 + j, :]
    for v in range(3):
        for j in range(3):
            at = 9228 + 3 * v + j
            vecs[1 + v : 2 + v, j * 128 : (j + 1) * 128] = flat[at : at + 1, :]


def pack_mlp(part, chains, g_w1, g_w2t, g_vec, flat):
    put_matrix(flat, 0, g_w1)
    for j in range(3):
        flat[pl.ds(4608 + j, FF, stride=3), :] = g_w2t[j * 128 : (j + 1) * 128, :].T
    for j in range(12):
        flat[9216 + j : 9217 + j, :] = g_vec[0:1, j * 128 : (j + 1) * 128]
    for v in range(3):
        for j in range(3):
            at = 9228 + 3 * v + j
            flat[at : at + 1, :] = g_vec[1 + v : 2 + v, j * 128 : (j + 1) * 128]
    flat[9237:, :] = jnp.zeros((flat.shape[0] - 9237, 128), F32)
    to_blocks(part, chains, flat)


def mlp_kernel(
    part,
    chain_places,
    cot_ref,
    mixed_ref,
    x_ref,
    wproj,
    vecs_a,
    blocks,
    out_ref,
    d_res_ref,
    d_mixed_ref,
    sums1,
    sums2,
    g_proj,
    g_vec,
    w1,
    w2,
    vecs,
    g_w1,
    g_w2t,
    flat,
):
    i = pl.program_id(0)

    @pl.when(i == 0)
    def _():
        unpack_mlp(part, chain_places[0], blocks, flat, w1, w2, vecs)
        g_w1[...] = jnp.zeros_like(g_w1)
        g_w2t[...] = jnp.zeros_like(g_w2t)
        g_proj[...] = jnp.zeros_like(g_proj)
        g_vec[...] = jnp.zeros_like(g_vec)

    mix = mixed_ref[...]
    grad = cot_ref[...]
    columns = [slice(0, FF // 2), slice(FF // 2, FF)]
    res = x_ref[...].astype(F32) + dot(mix, wproj[...]) + vecs_a[4:5, :]
    d_act = dot_t(grad, w2[columns[0], :])
    xhat, scale = norm_parts(res)
    gain = vecs[1:2, :D]
    normed = (xhat * gain + vecs[2:3, :D]).astype(BF16)
    grad_t = grad.T
    normed_t = normed.T
    hidden = dot(normed, w1[:, columns[0]])
    out, d_normed = res + vecs[3:4, :D], None
    for f, cols in enumerate(columns):
        value, d_value = hidden + vecs[0:1, cols], d_act
        if f == 0:
            hidden = dot(normed, w1[:, columns[f + 1]])
            d_act = dot_t(grad, w2[columns[f + 1], :])
        square = value * value
        t = jnp.tanh(value * (GELU_A + (GELU_A * GELU_B) * square))
        half = 0.5 + 0.5 * t
        act = (value * half).astype(BF16)
        slope = half + (0.5 * value) * (1.0 - t * t) * (GELU_A + (3 * GELU_A * GELU_B) * square)
        d_hidden32 = d_value * slope
        d_hidden = d_hidden32.astype(BF16)
        g_vec[0:1, cols] += jnp.sum(d_hidden32, axis=0, keepdims=True)
        out += dot(act, w2[cols, :])
        back = dot_t(d_hidden, w1[:, cols])
        d_normed = back if d_normed is None else d_normed + back
        g_w1[:, cols] += dot(normed_t, d_hidden)
        g_w2t[:, cols] += dot(grad_t, act)
    out_ref[...] = out.astype(BF16)
    grad32 = grad.astype(F32)
    d_res = grad32 + norm_back(d_normed, xhat, scale, gain)
    d_res_ref[...] = d_res
    d_attn = d_res.astype(BF16)
    d_mixed_ref[...] = dot_t(d_attn, wproj[...]).astype(BF16)
    g_proj[...] += dot(mix.T, d_attn)
    g_vec[1:2, :D] += jnp.sum(d_normed * xhat, axis=0, keepdims=True)
    g_vec[2:3, :D] += jnp.sum(d_normed, axis=0, keepdims=True)
    g_vec[3:4, :D] += jnp.sum(grad32, axis=0, keepdims=True)
    g_vec[4:5, :D] += jnp.sum(d_res, axis=0, keepdims=True)

    @pl.when(i == pl.num_programs(0) - 1)
    def _():
        pack_mlp(part, list(zip(chain_places, (sums1, sums2))), g_w1, g_w2t, g_vec, flat)


def mlp(part, chain_places, cot, mixed, x, wproj, vecs_a, blocks):
    sums = [(part.devices, rows, 128) for rows in part.split(SUM_SHARE)]
    tokens = x.shape[0]
    chunk = tokens // 7
    vm = pl.BlockSpec(memory_space=pltpu.VMEM)
    tile = pl.BlockSpec((chunk, D), lambda i: (i, 0))
    fixed = lambda *shape: pl.BlockSpec(shape, lambda i: (0,) * len(shape))
    return pl.pallas_call(
        functools.partial(mlp_kernel, part, chain_places),
        grid=(7,),
        out_shape=[
            jax.ShapeDtypeStruct((tokens, D), BF16),
            jax.ShapeDtypeStruct((tokens, D), F32),
            jax.ShapeDtypeStruct((tokens, D), BF16),
            jax.ShapeDtypeStruct(sums[0], BF16),
            jax.ShapeDtypeStruct(sums[1], BF16),
            jax.ShapeDtypeStruct((D, D), F32),
            jax.ShapeDtypeStruct((8, FF), F32),
        ],
        in_specs=[tile] * 3 + [vm] * 3,
        out_specs=[tile] * 3 + [fixed(*sums[0]), fixed(*sums[1]), fixed(D, D), fixed(8, FF)],
        scratch_shapes=[
            pltpu.VMEM((D, FF), BF16),
            pltpu.VMEM((FF, D), BF16),
            pltpu.VMEM((8, FF), F32),
            pltpu.VMEM((D, FF), F32),
            pltpu.VMEM((D, FF), F32),
            pltpu.VMEM((part.buffer, 128), F32),
        ],
        compiler_params=pltpu.CompilerParams(vmem_limit_bytes=VMEM_LIMIT),
        name="mlp",
    )(cot, mixed, x, wproj, vecs_a, blocks)


def row_chunks(rows, steps):
    after = [steps * 3 // 8, steps * 5 // 8, steps * 7 // 8, steps]
    ends = [rows * done // steps // 16 * 16 for done in after]
    return [
        (done - 1, first, end - first) for done, first, end in zip(after, [0] + ends[:-1], ends)
    ]


def split_float(values):
    high = values.astype(BF16)
    return high, (values - high.astype(F32)).astype(BF16)


def attend_back_kernel(
    part_a,
    part,
    order,
    chain_places,
    images,
    q_ref,
    k_ref,
    v_ref,
    mixed_ref,
    d_mixed,
    probs,
    inverse,
    keys_back,
    query_tab,
    query_back,
    x_hbm,
    d_res_hbm,
    wqkv,
    vecs,
    blocks1,
    blocks2,
    out_src,
    g_proj,
    g_vec2,
    one_fine,
    one_coarse,
    grad_a_ref,
    grad_ref,
    out_ref,
    dx_ref,
    g_bias,
    g_qkv,
    g_vec,
    flat,
    table,
    shifted,
    line,
    d_query_t,
    d_key_value_t,
    d_qkv,
    d_in,
    x_buf,
    d_res_buf,
    load_sems,
    out_sem,
    out_send,
    out_recv,
    dx_sem0,
    dx_send0,
    dx_recv0,
    dx_sem1,
    dx_send1,
    dx_recv1,
    dx_sem2,
    dx_send2,
    dx_recv2,
    dx_sem3,
    dx_send3,
    dx_recv3,
    *chain_scratch,
):
    i = pl.program_id(0)
    steps = pl.num_programs(0)
    stages = len(order)
    dp, grp = lax.axis_index("dp"), lax.axis_index("grp")
    orders = (order, other_order(order))

    sums_a, arrived_a, sems_a = chain_scratch[:2], chain_scratch[2:4], chain_scratch[4:8]
    cubes_a, cubes_b = [], []
    for c, blocks in enumerate((blocks1, blocks2)):
        total, outgoing, arrived, *sems = chain_scratch[8 + 5 * c : 13 + 5 * c]
        cubes_b.append(CubeSum(orders[c], blocks, total, outgoing, arrived, sems))
        rows = pl.ds(0, arrived_a[c].shape[1])
        local = (total.at[:, rows], outgoing.at[:, rows])
        cubes_a.append(
            CubeSum(orders[c], sums_a[c], *local, arrived_a[c], sems_a[2 * c : 2 * c + 2])
        )
    def put_result(p, cubes, ref):
        device = dp * lax.axis_size("grp") + grp
        result = jnp.concatenate([cube.total[0] for cube in cubes], axis=0)
        ref[...] = shift_lanes(result, p.lane(device), False)

    exchange = exchange_copies(out_src, out_ref, dp, grp, out_sem, out_send, out_recv)
    dx_sems = (
        (dx_sem0, dx_send0, dx_recv0),
        (dx_sem1, dx_send1, dx_recv1),
        (dx_sem2, dx_send2, dx_recv2),
        (dx_sem3, dx_send3, dx_recv3),
    )
    loads = [
        pltpu.make_async_copy(x_hbm, x_buf, load_sems.at[0]),
        pltpu.make_async_copy(d_res_hbm, d_res_buf, load_sems.at[1]),
    ]

    chunks = row_chunks(d_in.shape[1], images)

    def chunk(c):
        return chunk_copies(d_in, dx_ref, *chunks[c][1:], dp, grp, *dx_sems[c], 0)

    @pl.when(i == 0)
    def _():
        for c in loads:
            c.start()
        g_bias[...] = jnp.zeros_like(g_bias)
        g_qkv[...] = jnp.zeros_like(g_qkv)
        g_vec[...] = jnp.zeros_like(g_vec)
        greet(cube_partners(order, dp, grp) + [window_partner(dp, grp, 3)])

    starts = starts_of(stage_weights(order)[::-1], SUM_STEPS)
    for k, start in zip(reversed(range(stages)), starts):

        @pl.when(i == start)
        def _(k=k):
            for cube in cubes_b:
                if k < stages - 1:
                    cube.finish(k + 1)
                cube.start(k)

    @pl.when(i == steps - 1)
    def _():
        for cube in cubes_b:
            cube.finish(0)
        put_result(part, cubes_b, grad_ref)

    @pl.when(i == 0)
    def _():
        for c in exchange:
            c.start()

    def image(b):
        at = i
        dm_t = dot(query_tab[b], image_rows(d_mixed, at, slice(0, D))).T
        scales = [jnp.broadcast_to(inverse[b, h : h + 1, :], (HDIM, 256)) for h in range(HEADS)]
        dm_t = (dm_t * jnp.concatenate(scales, axis=0)).astype(BF16)
        products = dm_t.astype(F32) * mixed_ref[b].astype(F32)
        q_t, k_t, v_ext = q_ref[b], k_ref[b], v_ref[b]

        def d_probs_of(h):
            heads = jnp.concatenate([only_head(dm_t, h), only_head(dm_t, h + 1)], axis=1)
            return dot(v_ext[:, tile_of(h)], heads)

        def softmax_back(d_probs, h):
            e = probs[b, h]
            own = slice(h * HDIM, (h + 1) * HDIM)
            sums = jnp.sum(products[own], axis=0, keepdims=True)
            halves = []
            for half in range(2):
                lanes = slice(128 * half, 128 * half + 128)
                e32 = e[:, lanes].astype(F32)[56 * half : 56 * half + KEYS]
                ds = e32 * (half_of(d_probs, half) - sums[:, lanes])
                g_bias[h, half] += ds
                halves.append(ds)
            return spread(halves)

        def gather_back(h, ds):
            own = slice(h * HDIM, (h + 1) * HDIM)
            values = slice(D + h * HDIM, D + (h + 1) * HDIM)
            d_query_t[b, own, :] = (dot(k_t[own, :], ds) * HDIM ** (-0.5)).astype(BF16)
            d_key_value_t[b, own, :] = dot_t(q_t[own, :], ds).astype(BF16)
            d_key_value_t[b, values, :] = dot_t(dm_t[own, :], probs[b, h]).astype(BF16)

        ahead = d_probs_of(0)
        yield
        waiting = []
        for h in range(0, HEADS, 2):
            now = ahead
            if h + 2 < HEADS:
                ahead = d_probs_of(h + 2)
            for c in range(2):
                waiting.append((h + c, softmax_back(now[:, c * 256 : (c + 1) * 256], h + c)))
            while len(waiting) > 1:
                gather_back(*waiting.pop(0))
            yield
        for last in waiting:
            gather_back(*last)
        yield
        put_image_rows(d_qkv, at, slice(0, D), dot_t(query_back[b], d_query_t[b]))
        put_image_rows(d_qkv, at, slice(D, 3 * D), dot_t(keys_back[b], d_key_value_t[b]))

    for _ in image(0):
        pass

    @pl.when(i == 3)
    def _():
        for c in loads:
            c.wait()

    def finish_rows(first, size):
        at = slice(first, first + size)
        xhat, scale = norm_parts(x_buf[:, at, :].reshape(4 * size, D).astype(F32))
        gain = vecs[0:1, :]
        normed = (xhat * gain + vecs[1:2, :]).astype(BF16)
        grads = d_qkv[:, at, :].reshape(4 * size, 3 * D)
        d_normed = dot_t(grads, wqkv[...])
        result = d_res_buf[:, at, :].reshape(4 * size, D) + norm_back(d_normed, xhat, scale, gain)
        d_in[:, at, :] = result.astype(BF16).reshape(4, size, D)
        g_qkv[...] += dot(normed.T, grads)
        g_vec[0:1, :] += jnp.sum(grads.astype(F32), axis=0, keepdims=True)
        g_vec[1:2, :D] += jnp.sum(d_normed * xhat, axis=0, keepdims=True)
        g_vec[2:3, :D] += jnp.sum(d_normed, axis=0, keepdims=True)

    for c, (step, first, size) in enumerate(chunks):

        @pl.when(i == step)
        def _(c=c, first=first, size=size):
            finish_rows(first, size)
            if c < 3:
                for copy in chunk(c):
                    copy.start()

    @pl.when(i == steps - 1)
    def _():
        pack(
            part_a, list(zip(chain_places, sums_a)), one_fine, one_coarse,
            g_bias, g_qkv, g_vec, g_proj, g_vec2, flat, table, shifted, line,
        )
        for k in reversed(range(stages)):
            for cube in cubes_a:
                cube.start(k)
            if k == stages - 1:
                for copy in chunk(3):
                    copy.start()
            for cube in cubes_a:
                cube.finish(k)
        put_result(part_a, cubes_a, grad_a_ref)
        for c in exchange:
            c.wait()
        for c in range(4):
            for copy in chunk(c):
                copy.wait()


def attend_back(
    part_a, part, order, chain_places, saved, d_mixed, probs, inverse, x, d_res, wqkv, vecs, blocks,
    out, g_proj, g_vec2,
):
    images = probs.shape[0]
    tokens = out.shape[0]
    rows = tokens // 4
    stages = len(order)
    _, query_tab, keys_back, query_back = gather_tables(images)
    fine, coarse, _ = bias_tables()
    vm = pl.BlockSpec(memory_space=pltpu.VMEM)
    hbm = pl.BlockSpec(memory_space=pl.ANY)
    image = lambda *shape: pl.BlockSpec((1, *shape), lambda i: (i, 0, 0))
    by_window = lambda array: array.reshape(4, rows, -1)
    chain_scratch = [
        pltpu.VMEM((part.devices, count, 128), BF16) for count in part_a.split(SUM_SHARE)
    ]
    chain_scratch += chain_scratch
    chain_scratch += [pltpu.SemaphoreType.DMA((stages,))] * 4
    for count in part.split(SUM_SHARE):
        chain_scratch += CubeSum.scratch(part.devices, count, stages)
    grad_a, grad_b, output, dx = pl.pallas_call(
        functools.partial(attend_back_kernel, part_a, part, order, chain_places, images),
        grid=(images,),
        out_shape=[
            jax.ShapeDtypeStruct((part_a.rows, 128), F32),
            jax.ShapeDtypeStruct((part.rows, 128), F32),
            jax.ShapeDtypeStruct((tokens, D), BF16),
            jax.ShapeDtypeStruct((4, rows, D), BF16),
        ],
        in_specs=[
            image(D, 256),
            image(D, 256),
            image(256, D),
            image(D, 256),
            vm,
            pl.BlockSpec((1, HEADS, 256, 256), lambda i: (i, 0, 0, 0)),
            image(16, 256),
        ]
        + [image(256, 256)] * 3
        + [hbm, hbm, vm, vm, vm, vm, hbm, vm, vm, vm, vm],
        out_specs=[
            pl.BlockSpec((part_a.rows, 128), lambda i: (0, 0)),
            pl.BlockSpec((part.rows, 128), lambda i: (0, 0)),
            hbm,
            hbm,
        ],
        scratch_shapes=[
            pltpu.VMEM((HEADS, 2, KEYS, 128), F32),
            pltpu.VMEM((D, 3 * D), F32),
            pltpu.VMEM((8, 3 * D), F32),
            pltpu.VMEM((part_a.buffer, 128), F32),
            pltpu.VMEM((16, 512), F32),
            pltpu.VMEM((4, 14 * 16, 128), F32),
            pltpu.VMEM((8, 512), F32),
            pltpu.VMEM((1, D, 256), BF16),
            pltpu.VMEM((1, 2 * D, 256), BF16),
            pltpu.VMEM((4, rows, 3 * D), BF16),
            pltpu.VMEM((4, rows, D), BF16),
            pltpu.VMEM((4, rows, D), BF16),
            pltpu.VMEM((4, rows, D), F32),
            pltpu.SemaphoreType.DMA((2,)),
        ]
        + [
            pltpu.SemaphoreType.DMA,
            pltpu.SemaphoreType.DMA((3,)),
            pltpu.SemaphoreType.DMA((3,)),
        ]
        * 5
        + chain_scratch,
        compiler_params=pltpu.CompilerParams(
            collective_id=3, has_side_effects=True, vmem_limit_bytes=VMEM_LIMIT
        ),
        name="attend_back",
    )(
        *saved,
        by_window(d_mixed),
        probs,
        inverse,
        keys_back,
        query_tab,
        query_back,
        by_window(x),
        by_window(d_res),
        wqkv,
        vecs,
        *blocks,
        out,
        g_proj,
        g_vec2,
        jnp.asarray(fine),
        jnp.asarray(coarse),
    )
    grad_a = grad_a.reshape(-1)[: part_a.length]
    grad_b = grad_b.reshape(-1)[: part.length]
    return grad_a, grad_b, output, dx


def to_blocks(part, chains, flat):
    for device in range(part.devices):
        at = part.start(device)
        for places, out in chains:
            out[places[device]] = flat[at : at + out.shape[1], :].astype(BF16)
            at += out.shape[1]


def pack(
    part, chains, one_fine, one_coarse,
    g_bias, g_qkv, g_vec1, g_proj, g_vec2, flat, table, shifted, line,
):
    row, lane = divmod(ATTN_VECTORS[0], 128)
    flat[4608:, :] = jnp.zeros((flat.shape[0] - 4608, 128), F32)
    put_matrix(flat, 0, g_qkv)
    put_matrix(flat, 3456, g_proj)
    vectors = [
        g_vec1[1:2, :D],
        g_vec1[2:3, :D],
        g_vec1[0:1, :D],
        g_vec1[0:1, 2 * D :],
        g_vec2[4:5, :D],
    ]
    pieces = [v[:, j * 128 : (j + 1) * 128] for v in vectors for j in range(3)]
    pieces += [jnp.zeros((1, 128), F32)]
    flat[row : row + 16, :] += shift_lanes(jnp.concatenate(pieces, axis=0), lane, True)
    for h in range(HEADS):
        table[...] = jnp.zeros_like(table)
        for half in range(2):
            turned = g_bias[h, half].T
            for y in range(WIN):
                for at, length, source in bias_runs(half, WIN * half + y):
                    table[0:14, source : source + length] += turned[
                        y * 14 : y * 14 + 14, at : at + length
                    ]
        for c in range(4):
            shifted[c, pl.ds(h, 14, stride=16), :] = table[0:14, c * 128 : (c + 1) * 128]
    high, low = split_float(jnp.concatenate([shifted[c] for c in range(3)], axis=1))
    moved_fine = dot_t(high, one_fine[...]) + dot_t(low, one_fine[...])
    high, low = split_float(shifted[3])
    moved_coarse = dot_t(high, one_coarse[...]) + dot_t(low, one_coarse[...])
    g_fine = jnp.zeros((16, 384), F32)
    g_coarse = jnp.zeros((16, 256), F32)
    for qx in range(14):
        at = slice(qx * 16, qx * 16 + 16)
        g_fine += pltpu.roll(moved_fine[at], (384 - qx) % 384, 1)
        g_coarse += pltpu.roll(moved_coarse[at], (256 - qx // 2) % 256, 1)
    for t, h, length, row, lane, count in table_lines():
        line[...] = jnp.zeros_like(line)
        line[0:1, lane : lane + length] = (g_fine, g_coarse)[t][h : h + 1, :length]
        for c in range(count):
            flat[row + c : row + c + 1, :] += line[0:1, c * 128 : (c + 1) * 128]
    to_blocks(part, chains, flat)


def adamw(master, first, second, grads):
    first_new = beta_one * first + (1.0 - beta_one) * grads
    second_new = beta_two * second + (1.0 - beta_two) * grads * grads
    first_hat = first_new / (1.0 - beta_one**STEP)
    second_hat = second_new / (1.0 - beta_two**STEP)
    master_new = master - learn_rate * (
        first_hat / (jnp.sqrt(second_hat) + adam_eps) + decay_rate * master
    )
    return (first_new, second_new, master_new)


def body(
    tokens, cotangent, attn_master, attn_first, attn_second, mlp_master, mlp_first, mlp_second
):
    n_dp, n_grp = lax.axis_size("dp"), lax.axis_size("grp")
    order = bit_order(n_dp, n_grp)
    chain_places = [place_list(o, n_dp, n_grp) for o in (order, other_order(order))]
    part_a = Part(n_dp * n_grp, attn_master.shape[0])
    part_b = Part(n_dp * n_grp, mlp_master.shape[0])
    images = tokens.shape[1] // 4 // SEQ
    wqkv, wproj, vecs_a, bias, x, blocks_b = gather_params(
        part_a, part_b, order, chain_places, attn_master, mlp_master, tokens[0]
    )
    mixed, probs, *saved, inverse, cot, blocks_b = attend(
        order, x, cotangent[0], blocks_b, wqkv, vecs_a, bias, images
    )
    mixed = mixed.reshape(-1, D)
    out, d_res, d_mixed, *sums_b, g_proj, g_vec2 = mlp(
        part_b, chain_places, cot, mixed, x, wproj, vecs_a, blocks_b
    )
    grad_a, grad_b, output, dx = attend_back(
        part_a, part_b, order, chain_places, saved, d_mixed, probs, inverse, x, d_res, wqkv,
        vecs_a, sums_b, out, g_proj, g_vec2,
    )
    attn_new = adamw(attn_master, attn_first, attn_second, grad_a)
    mlp_new = adamw(mlp_master, mlp_first, mlp_second, grad_b)
    input_grad = dx.reshape(-1, D).astype(F32)
    return (output[None], input_grad[None], *attn_new, *mlp_new)


def solution(mesh):
    flat_spec = P(("dp", "grp"))
    token_spec = P("dp", "grp", None)
    placed = (token_spec, token_spec) + (flat_spec,) * 6
    return jax.shard_map(
        body, mesh=mesh, in_specs=placed, out_specs=placed, check_vma=False
    )
```
